32 devices in a mesh: fsdp: 4 (over y, x), ctx: 4 (over z), tp: 2 (over core).
Axes of the slice: x: 2, y: 2, z: 4, core: 2. Of those that a mesh axis runs over, the one named last changes fastest.
Arguments:
- tokens: bfloat16 [4, 1024, 1536], P('fsdp', 'ctx'), may hold values from -6 to 6
- attn_norm: float32 [1536], replicated, may hold values from 0.5 to 1.5
- attention_params: bfloat16 [1536, 2, 1792], P('fsdp', 'tp')
- ffn_norm: float32 [1536], replicated, may hold values from 0.5 to 1.5
- expert_weights: bfloat16 [1536, 8, 3, 768], P('fsdp', None, None, 'tp'), may hold values from -0.15625 to 0.15625
- gate_values: float32 [4, 1024, 4], P('fsdp', 'ctx'), may hold values from 0.5 to 1.5
- routes: int32 [4, 1024, 4], P('fsdp', 'ctx'), may hold values from 0 to 7, all different within a row
- slot_order: int32 [4, 1024], P('fsdp', 'ctx'), may hold values from 0 to 255, as said below
- cotangent: bfloat16 [4, 1024, 1536], P('fsdp', 'ctx'), may hold values from -6 to 6
Outputs:
- layer_out: bfloat16 [4, 1024, 1536], P('fsdp', 'ctx')
- tokens_grad: bfloat16 [4, 1024, 1536], P('fsdp', 'ctx')
- attn_weights_grad: float32 [1536, 2, 1792], P('fsdp', 'tp')
- expert_weights_grad: float32 [1536, 8, 3, 768], P('fsdp', None, None, 'tp')
- attn_norm_grad: float32 [1536], replicated
- ffn_norm_grad: float32 [1536], replicated
- gate_grad: float32 [4, 1024, 4], P('fsdp', 'ctx')
The draws below stay inside these ranges and needn't reach their ends.
Inputs may be any that keep to these rules, and one draw needn't show every extreme that they name: `slot_order`: within each group of 1 sequence and one block of 256 positions the values are a permutation of the group's ranks, read with sequences first and positions second. `routes`: the 4 experts of a token are different.
All inputs are finite; a program needn't handle non-finite values.
Results may differ from the reference program's by a relative error of at most 0.018.
Values may be sent and summed in bfloat16 or wider, within the bound.
A program may use at most 256 MiB of HBM per device.

```python
import math
import jax
import jax.numpy as jnp
from jax import lax

MODEL_DIM = 1536
KEY_VALUE_HEADS = 2
HEAD_DIM = 128
H = 768
TOP = 4
EXPERTS = 8
BLOCK = 256
SEQ_DEV = 1
SEQS = 4
LENGTH = 1024
QUERY_PER_GROUP = 6
CAP = 160


def draw_attention_params(key, part):
    column_list = (2 * QUERY_PER_GROUP + 2) * HEAD_DIM
    array_shape = (MODEL_DIM, KEY_VALUE_HEADS, column_list)
    base = jax.random.normal(key, array_shape, jnp.float32)
    column = jnp.arange(column_list)
    factor = jnp.where(column < (QUERY_PER_GROUP + 1) * HEAD_DIM, math.sqrt(2.5), 1.0) / math.sqrt(MODEL_DIM)
    return (base * factor[None, None, :]).astype(jnp.bfloat16)


def draw_slot_order(key, part):
    group_size = SEQ_DEV * BLOCK
    blocks = LENGTH // BLOCK
    group_count = SEQS // SEQ_DEV * blocks
    keys = jax.random.split(key, group_count)
    ranks = jax.vmap(lambda sub_key: jax.random.permutation(sub_key, group_size))(keys)
    ranks = ranks.reshape(SEQS // SEQ_DEV, blocks, SEQ_DEV, BLOCK)
    return jnp.transpose(ranks, (0, 2, 1, 3)).reshape(SEQS, LENGTH).astype(jnp.int32)


def levels(key, dims, cuts, least, largest):
    gain, own = 1.0, jax.random.fold_in(key, 6)
    for dim, parts in cuts:
        draws = jnp.exp(jax.random.uniform(jax.random.fold_in(own, dim), (parts,), jnp.float32, least / len(cuts), largest / len(cuts)))
        gain = gain * jnp.repeat(draws, dims[dim] // parts).reshape([-1 if axis == dim else 1 for axis in range(len(dims))])
    return gain


def different_ones(own_key, rows, count, top, lift):
    order = jax.random.permutation(jax.random.fold_in(own_key, 1), count)
    pull = order
    for power in range(3):
        pull = pull * pull // count
    pull = pull * lift // count
    tickets = jax.random.randint(jax.random.fold_in(own_key, 2), (rows, count), 0, 4096) + pull
    sure = jax.random.permutation(jax.random.fold_in(own_key, 3), rows)[jnp.arange(count) % rows]
    tickets = jnp.where(jnp.arange(rows)[:, None] == sure[None, :], 1 << 14, tickets)
    priority = tickets * count + jnp.arange(count)
    return lax.top_k(priority.astype(jnp.int32), top)[1].astype(jnp.int32)


def centred(rng, dims, width, limit, cuts=(), kind=jnp.bfloat16):
    values = jax.random.normal(rng, dims, jnp.float32) * width
    if len(cuts) > 0:
        values = levels(rng, dims, cuts, -0.22, 0.18) * values
    return jnp.clip(values, min=-limit, max=limit).astype(kind)


def setup_inputs(seed: int = 0) -> dict:
    key_list = jax.random.split(jax.random.key(seed), 10)
    tokens = centred(key_list[0], (SEQS, LENGTH, MODEL_DIM), 1.0, 6.0, ((0, 4), (1, 4)))
    attn_norm = jnp.clip(1.0 + 0.1 * jax.random.normal(key_list[1], (MODEL_DIM,), jnp.float32), 0.5, 1.5)
    attention_params = draw_attention_params(jax.random.fold_in(key_list[9], 71), 0)
    ffn_norm = jnp.clip(1.0 + 0.1 * jax.random.normal(key_list[3], (MODEL_DIM,), jnp.float32), 0.5, 1.5)
    expert_weights = centred(key_list[4], (MODEL_DIM, EXPERTS, 3, H), MODEL_DIM ** -0.5, 0.15625, ((0, 4), (3, 2)))
    gate_values = jnp.clip(0.5 + 1.0 * jax.random.uniform(key_list[5], (SEQS, LENGTH, TOP), jnp.float32) ** levels(key_list[5], (SEQS, LENGTH, TOP), ((0, 4), (1, 4)), -0.2, 0.2), 0.5, 1.5)
    routes = different_ones(key_list[6], SEQS * LENGTH, EXPERTS, TOP, 4096).reshape((SEQS, LENGTH, TOP))
    slot_order = draw_slot_order(jax.random.fold_in(key_list[9], 71), 0)
    cotangent = centred(key_list[8], (SEQS, LENGTH, MODEL_DIM), 1.0, 6.0, ((0, 4), (1, 4)))
    return dict(tokens=tokens, attn_norm=attn_norm, attention_params=attention_params, ffn_norm=ffn_norm, expert_weights=expert_weights, gate_values=gate_values, routes=routes, slot_order=slot_order, cotangent=cotangent)


@jax.custom_vjp
def low(v):
    return lax.optimization_barrier(v.astype(jnp.bfloat16)).astype(jnp.float32)

@jax.custom_vjp
def low_back(v):
    return v

def low_keep(v):
    return (low(v), None)

def low_pass(kept, grad):
    return (grad,)

def back_keep(v):
    return (v, None)

def back_low(kept, grad):
    return (low(grad),)
low.defvjp(low_keep, low_pass)
low_back.defvjp(back_keep, back_low)
eps = 1e-06
theta_base = 1000000.0
highest_precision = lax.Precision.HIGHEST

def rms_scale(source, gain_vec):
    return source * lax.rsqrt(lax.optimization_barrier(jnp.mean(source * source, axis=-1, keepdims=True)) + eps) * gain_vec

def angle_tables(positions):
    frequency = theta_base ** (-(jnp.arange(HEAD_DIM // 2, dtype=jnp.float32) * 2.0) / HEAD_DIM)
    angles = positions.astype(jnp.float32)[:, None] * frequency[None, :]
    return (jnp.cos(angles), jnp.sin(angles))

def rotate(source, cosine_table, sine_table):
    half_size = source.shape[-1] // 2
    front_half = source[..., :half_size]
    back_half = source[..., half_size:]
    return jnp.concatenate([front_half * cosine_table - back_half * sine_table, back_half * cosine_table + front_half * sine_table], axis=-1)

def slot_tables(route_rows, rank_rows):
    tok_count = route_rows.shape[0]
    inverse = jnp.zeros((tok_count,), jnp.int32).at[rank_rows].set(jnp.arange(tok_count, dtype=jnp.int32))
    ranked = route_rows[inverse].reshape(-1)
    onehot = (ranked[:, None] == jnp.arange(EXPERTS, dtype=jnp.int32)[None, :]).astype(jnp.int32)
    before = jnp.cumsum(onehot, axis=0) - onehot
    slot_ranked = lax.optimization_barrier(jnp.sum(before * onehot, axis=1)).reshape(tok_count, TOP)
    slots = slot_ranked[rank_rows]
    kept_pair = slots < CAP
    pair_slot = jnp.where(kept_pair, route_rows * CAP + slots, EXPERTS * CAP).astype(jnp.int32)
    owners = jnp.broadcast_to(jnp.arange(tok_count, dtype=jnp.int32)[:, None], (tok_count, TOP))
    slot_token = jnp.full((EXPERTS * CAP,), tok_count, jnp.int32).at[pair_slot.reshape(-1)].set(owners.reshape(-1), mode='drop')
    return (kept_pair, pair_slot, slot_token)

def attend_sequence(item_args):
    queries, key_rows, value_rows = item_args
    scores = low_back(jnp.einsum('qhgd,khd->hgqk', queries, key_rows, precision=highest_precision) * HEAD_DIM ** (-0.5))
    block_ids = jnp.arange(queries.shape[0], dtype=jnp.int32) // BLOCK
    allowed = block_ids[None, :] <= block_ids[:, None]
    scores = jnp.where(allowed, scores, -1e+30)
    attn_probs = jax.nn.softmax(scores, axis=-1)
    return jnp.einsum('hgqk,khd->qhgd', low(attn_probs), value_rows, precision=highest_precision)

def expert_group(normed, gate_rows, kept_pair, pair_slot, slot_token, expert_weights):
    model_width = normed.shape[1]
    padded = jnp.concatenate([normed, jnp.zeros((1, model_width), normed.dtype)], axis=0)
    inputs = padded[slot_token].reshape(EXPERTS, CAP, model_width)
    gate_act = low_back(jnp.einsum('ecd,deh->ech', inputs, expert_weights[:, :, 0], precision=highest_precision))
    up_act = low_back(jnp.einsum('ecd,deh->ech', inputs, expert_weights[:, :, 1], precision=highest_precision))
    hidden = low(jax.nn.silu(gate_act) * up_act)
    expert_out = low_back(jnp.einsum('ech,deh->ecd', hidden, expert_weights[:, :, 2], precision=highest_precision))
    out_pad = jnp.concatenate([expert_out.reshape(EXPERTS * CAP, model_width), jnp.zeros((1, model_width), expert_out.dtype)], axis=0)
    picked = out_pad[pair_slot]
    weighting = gate_rows * kept_pair.astype(gate_rows.dtype)
    return lax.optimization_barrier(jnp.sum(picked * weighting[:, :, None], axis=1))

def layer_forward(tokens, attn_norm, attention_params, ffn_norm, expert_weights, gate_values, tables):
    kept_pair, pair_slot, slot_token = tables
    sequence_count, sequence_length, model_width = tokens.shape
    input_columns = (QUERY_PER_GROUP + 2) * HEAD_DIM
    first_normed = low(rms_scale(tokens, attn_norm))
    projected_rows = low_back(jnp.einsum('ayz,zgi->aygi', first_normed, attention_params[:, :, :input_columns], precision=highest_precision))
    projected_rows = projected_rows.reshape(sequence_count, sequence_length, KEY_VALUE_HEADS, QUERY_PER_GROUP + 2, HEAD_DIM)
    cosine_table, sine_table = angle_tables(jnp.arange(sequence_length, dtype=jnp.int32))
    cos_wide = cosine_table[None, :, None, None, :]
    sin_wide = sine_table[None, :, None, None, :]
    queries = low(rotate(projected_rows[:, :, :, :QUERY_PER_GROUP], cos_wide, sin_wide))
    key_rows = low(rotate(projected_rows[:, :, :, QUERY_PER_GROUP:QUERY_PER_GROUP + 1], cos_wide, sin_wide))[:, :, :, 0]
    value_rows = low(projected_rows[:, :, :, QUERY_PER_GROUP + 1])
    mixed_heads = lax.map(jax.checkpoint(attend_sequence), (queries, key_rows, value_rows))
    mixed_heads = low(low_back(mixed_heads)).reshape(sequence_count, sequence_length, KEY_VALUE_HEADS, QUERY_PER_GROUP * HEAD_DIM)
    attention_output = low_back(jnp.einsum('vnue,wue->vnw', mixed_heads, attention_params[:, :, input_columns:], precision=highest_precision))
    residual = tokens + attention_output
    normed_two = low(rms_scale(residual, ffn_norm))
    blocks = sequence_length // BLOCK
    grouped = normed_two.reshape(sequence_count, blocks, BLOCK, model_width).transpose(1, 0, 2, 3)
    grouped = grouped.reshape(blocks, sequence_count * BLOCK, model_width)
    gate_groups = gate_values.reshape(sequence_count, blocks, BLOCK, TOP).transpose(1, 0, 2, 3)
    gate_groups = gate_groups.reshape(blocks, sequence_count * BLOCK, TOP)
    moe = jax.vmap(expert_group, in_axes=(0, 0, 0, 0, 0, None))(grouped, gate_groups, kept_pair, pair_slot, slot_token, expert_weights)
    moe = moe.reshape(blocks, sequence_count, BLOCK, model_width).transpose(1, 0, 2, 3)
    return residual + moe.reshape(sequence_count, sequence_length, model_width)

def reference(tokens, attn_norm, attention_params, ffn_norm, expert_weights, gate_values, routes, slot_order, cotangent):
    step_count = SEQS // SEQ_DEV
    blocks = LENGTH // BLOCK
    group_size = SEQ_DEV * BLOCK
    route_groups = routes.reshape(step_count, SEQ_DEV, blocks, BLOCK, TOP).transpose(0, 2, 1, 3, 4)
    route_groups = route_groups.reshape(step_count, blocks, group_size, TOP)
    rank_groups = slot_order.reshape(step_count, SEQ_DEV, blocks, BLOCK).transpose(0, 2, 1, 3)
    rank_groups = rank_groups.reshape(step_count, blocks, group_size)
    kept_pair, pair_slot, slot_token = jax.vmap(jax.vmap(slot_tables))(route_groups, rank_groups)
    norm_one = attn_norm.astype(jnp.float32)
    attn_full = attention_params.astype(jnp.float32)
    norm_two = ffn_norm.astype(jnp.float32)
    expert_full = expert_weights.astype(jnp.float32)

    def group_step(grad_sums, item_args):
        token_group, gate_group, cot_group, kept_rows, slot_rows, owner_rows = item_args

        def forward_fn(tok_in, norm_in, attn_in, ffn_in, expert_in, gate_in):
            return layer_forward(tok_in, norm_in, attn_in, ffn_in, expert_in, gate_in, (kept_rows, slot_rows, owner_rows))
        result, pullback = jax.vjp(forward_fn, token_group.astype(jnp.float32), norm_one, attn_full, norm_two, expert_full, gate_group.astype(jnp.float32))
        grads = pullback(cot_group.astype(jnp.float32))
        new_sums = (grad_sums[0] + grads[1], grad_sums[1] + grads[2], grad_sums[2] + grads[3], grad_sums[3] + grads[4])
        return (new_sums, (result.astype(jnp.bfloat16), grads[0].astype(jnp.bfloat16), grads[5]))
    start_sums = (jnp.zeros_like(norm_one), jnp.zeros_like(attn_full), jnp.zeros_like(norm_two), jnp.zeros_like(expert_full))
    grad_sums, (outputs, input_grads, gate_grads) = lax.scan(group_step, start_sums, (tokens.reshape(step_count, SEQ_DEV, LENGTH, MODEL_DIM), gate_values.reshape(step_count, SEQ_DEV, LENGTH, TOP), cotangent.reshape(step_count, SEQ_DEV, LENGTH, MODEL_DIM), kept_pair, pair_slot, slot_token))
    return (outputs.reshape(SEQS, LENGTH, MODEL_DIM), input_grads.reshape(SEQS, LENGTH, MODEL_DIM), grad_sums[1], grad_sums[3], grad_sums[0], grad_sums[2], gate_grads.reshape(SEQS, LENGTH, TOP))
```

```python
import jax
import jax.numpy as jnp
from jax import lax
from jax.experimental import pallas as pl
from jax.experimental.pallas import tpu as pltpu
from jax.sharding import PartitionSpec as P

HEAD_DIM = 128
TOP = 4
EXPERTS = 8
QUERY_PER_GROUP = 6
CAP = 160


eps = 1e-06
theta_base = 1000000.0


def angle_tables(positions):
    frequency = theta_base ** (-(jnp.arange(HEAD_DIM // 2, dtype=jnp.float32) * 2.0) / HEAD_DIM)
    angles = positions.astype(jnp.float32)[:, None] * frequency[None, :]
    return (jnp.cos(angles), jnp.sin(angles))


def rotate(source, cosine_table, sine_table):
    half_size = source.shape[-1] // 2
    front_half = source[..., :half_size]
    back_half = source[..., half_size:]
    return jnp.concatenate(
        [
            front_half * cosine_table - back_half * sine_table,
            back_half * cosine_table + front_half * sine_table,
        ],
        axis=-1,
    )


def norm_back(source, inv_rms, gain_vec, upstream):
    scaled = upstream * gain_vec
    inner_sum = jnp.mean(scaled * source, axis=-1, keepdims=True)
    d_source = inv_rms * scaled - source * inv_rms * inv_rms * inv_rms * inner_sum
    return (d_source, jnp.sum(upstream * source * inv_rms, axis=0))


def slot_tables(route_rows, rank_rows):
    tok_count = route_rows.shape[0]
    inverse = (
        jnp.zeros((tok_count,), jnp.int32).at[rank_rows].set(jnp.arange(tok_count, dtype=jnp.int32))
    )
    ranked = route_rows[inverse].reshape(-1)
    onehot = (ranked[:, None] == jnp.arange(EXPERTS, dtype=jnp.int32)[None, :]).astype(jnp.int32)
    before = jnp.cumsum(onehot, axis=0) - onehot
    slot_ranked = jnp.sum(before * onehot, axis=1).reshape(tok_count, TOP)
    slots = slot_ranked[rank_rows]
    kept_pair = slots < CAP
    pair_slot = jnp.where(kept_pair, route_rows * CAP + slots, EXPERTS * CAP)
    owners = jnp.broadcast_to(jnp.arange(tok_count, dtype=jnp.int32)[:, None], (tok_count, TOP))
    slot_token = (
        jnp.full((EXPERTS * CAP,), tok_count, jnp.int32)
        .at[pair_slot.reshape(-1)]
        .set(owners.reshape(-1), mode="drop")
    )
    return (kept_pair, pair_slot, slot_token)


def attend_forward(queries, key_rows, value_rows, allowed):
    scores = jnp.einsum(
        "qhgd,khd->hgqk", queries, key_rows, preferred_element_type=jnp.float32
    ) * HEAD_DIM ** (-0.5)
    scores = jnp.where(allowed, scores, -1e30)
    row_max = jnp.max(scores, axis=-1, keepdims=True)
    expd = jnp.exp(scores - row_max)
    row_total = jnp.sum(expd, axis=-1, keepdims=True)
    attn_probs = (expd / row_total).astype(jnp.bfloat16)
    mixed_heads = jnp.einsum(
        "hgqk,khd->qhgd", attn_probs, value_rows, preferred_element_type=jnp.float32
    )
    return (mixed_heads.astype(jnp.bfloat16), row_max + jnp.log(row_total))


def attend_backward(queries, key_rows, value_rows, allowed, log_total, d_mixed):
    scores = jnp.einsum(
        "qhgd,khd->hgqk", queries, key_rows, preferred_element_type=jnp.float32
    ) * HEAD_DIM ** (-0.5)
    scores = jnp.where(allowed, scores, -1e30)
    attn_probs = jnp.exp(scores - log_total)
    low_probs = attn_probs.astype(jnp.bfloat16)
    d_probs = jnp.einsum("qhgd,khd->hgqk", d_mixed, value_rows, preferred_element_type=jnp.float32)
    inner_sum = jnp.sum(attn_probs * d_probs, axis=-1, keepdims=True)
    d_scores = (attn_probs * (d_probs - inner_sum)).astype(jnp.bfloat16)
    d_queries = jnp.einsum(
        "hgqk,khd->qhgd", d_scores, key_rows, preferred_element_type=jnp.float32
    ) * HEAD_DIM ** (-0.5)
    d_keys = jnp.einsum(
        "hgqk,qhgd->khd", d_scores, queries, preferred_element_type=jnp.float32
    ) * HEAD_DIM ** (-0.5)
    d_values = jnp.einsum("hgqk,qhgd->khd", low_probs, d_mixed, preferred_element_type=jnp.float32)
    return (d_queries, d_keys, d_values)


def body(
    tokens,
    attn_norm,
    attention_params,
    ffn_norm,
    expert_weights,
    gate_values,
    routes,
    slot_order,
    cotangent,
):
    sequence_count, block_len, model_width = tokens.shape
    tok_count = sequence_count * block_len
    kv_loc = attention_params.shape[1]
    input_columns = (QUERY_PER_GROUP + 2) * HEAD_DIM
    ctx_size = lax.axis_size("ctx")
    ctx_place = lax.axis_index("ctx")
    sequence_length = block_len * ctx_size
    whole_attn, whole_expert = (
        lax.all_gather(attention_params, "fsdp", axis=0, tiled=True),
        lax.all_gather(expert_weights, "fsdp", axis=0, tiled=True),
    )
    positions = ctx_place * block_len + jnp.arange(block_len, dtype=jnp.int32)
    cosine_table, sine_table = angle_tables(positions)
    cosine_table = jnp.tile(cosine_table, (sequence_count, 1))
    sine_table = jnp.tile(sine_table, (sequence_count, 1))
    cos_four = cosine_table[:, None, None, :]
    sin_four = sine_table[:, None, None, :]
    cos_three = cosine_table[:, None, :]
    sin_three = sine_table[:, None, :]
    allowed = (jnp.arange(sequence_length, dtype=jnp.int32) // block_len <= ctx_place)[
        None, None, None, :
    ]
    tok_float = tokens.reshape(tok_count, model_width).astype(jnp.float32)
    inv_one = lax.rsqrt(jnp.mean(tok_float * tok_float, axis=-1, keepdims=True) + eps)
    first_normed = (tok_float * inv_one * attn_norm).astype(jnp.bfloat16)
    projected_rows = jnp.einsum(
        "td,dhc->thc",
        first_normed,
        whole_attn[:, :, :input_columns],
        preferred_element_type=jnp.float32,
    ).reshape(tok_count, kv_loc, QUERY_PER_GROUP + 2, HEAD_DIM)
    queries = rotate(projected_rows[:, :, :QUERY_PER_GROUP], cos_four, sin_four).astype(
        jnp.bfloat16
    )
    key_rows = rotate(projected_rows[:, :, QUERY_PER_GROUP], cos_three, sin_three).astype(
        jnp.bfloat16
    )
    value_rows = projected_rows[:, :, QUERY_PER_GROUP + 1].astype(jnp.bfloat16)
    key_all, value_all = (
        lax.all_gather(
            key_rows.reshape(sequence_count, block_len, kv_loc, HEAD_DIM), "ctx", axis=1, tiled=True
        ),
        lax.all_gather(
            value_rows.reshape(sequence_count, block_len, kv_loc, HEAD_DIM),
            "ctx",
            axis=1,
            tiled=True,
        ),
    )
    query_seq = queries.reshape(sequence_count, block_len, kv_loc, QUERY_PER_GROUP, HEAD_DIM)
    mixed_heads, log_total = lax.map(
        lambda item_args: attend_forward(item_args[0], item_args[1], item_args[2], allowed),
        (query_seq, key_all, value_all),
    )
    mixed_flat = mixed_heads.reshape(tok_count, kv_loc, QUERY_PER_GROUP * HEAD_DIM)
    attn_part = jnp.einsum(
        "thc,dhc->td",
        mixed_flat,
        whole_attn[:, :, input_columns:],
        preferred_element_type=jnp.float32,
    )
    attn_sum = lax.psum(attn_part, "tp")
    residual = tok_float + attn_sum
    inv_two = lax.rsqrt(jnp.mean(residual * residual, axis=-1, keepdims=True) + eps)
    normed_two = (residual * inv_two * ffn_norm).astype(jnp.bfloat16)
    kept_pair, pair_slot, slot_token = slot_tables(
        routes.reshape(tok_count, TOP), slot_order.reshape(tok_count)
    )
    kept_float = kept_pair.astype(jnp.float32)
    gate_kept = gate_values.reshape(tok_count, TOP) * kept_float
    slot_gate = (
        jnp.zeros((EXPERTS * CAP,), jnp.float32)
        .at[pair_slot.reshape(-1)]
        .set(gate_kept.reshape(-1), mode="drop")
    )
    padded = jnp.concatenate([normed_two, jnp.zeros((1, model_width), jnp.bfloat16)], axis=0)
    inputs = padded[slot_token].reshape(EXPERTS, CAP, model_width)
    gate_act = jnp.einsum(
        "ecd,deh->ech", inputs, whole_expert[:, :, 0], preferred_element_type=jnp.float32
    )
    up_act = jnp.einsum(
        "ecd,deh->ech", inputs, whole_expert[:, :, 1], preferred_element_type=jnp.float32
    )
    gate_sigmoid = jax.nn.sigmoid(gate_act)
    active = gate_act * gate_sigmoid
    hidden = (active * up_act).astype(jnp.bfloat16)
    expert_out = jnp.einsum(
        "ech,deh->ecd", hidden, whole_expert[:, :, 2], preferred_element_type=jnp.float32
    )
    out_pad = jnp.concatenate(
        [expert_out.reshape(EXPERTS * CAP, model_width), jnp.zeros((1, model_width), jnp.float32)],
        axis=0,
    )
    picked = out_pad[pair_slot]
    moe_part = jnp.sum(picked * gate_kept[:, :, None], axis=1)
    moe = lax.psum(moe_part.astype(jnp.bfloat16), "tp").astype(jnp.float32)
    layer_out = (
        (residual + moe).astype(jnp.bfloat16).reshape(sequence_count, block_len, model_width)
    )
    grad_out = cotangent.reshape(tok_count, model_width).astype(jnp.float32)
    gate_part = jnp.sum(picked * grad_out[:, None, :], axis=-1) * kept_float
    grad_pad = jnp.concatenate([grad_out, jnp.zeros((1, model_width), jnp.float32)], axis=0)
    d_expert = (
        (grad_pad[slot_token] * slot_gate[:, None])
        .astype(jnp.bfloat16)
        .reshape(EXPERTS, CAP, model_width)
    )
    d_hidden = jnp.einsum(
        "ecd,deh->ech", d_expert, whole_expert[:, :, 2], preferred_element_type=jnp.float32
    )
    silu_slope = gate_sigmoid * (1.0 + gate_act * (1.0 - gate_sigmoid))
    d_gate_act = (d_hidden * up_act * silu_slope).astype(jnp.bfloat16)
    d_up_act = (d_hidden * active).astype(jnp.bfloat16)
    d_inputs = jnp.einsum(
        "ech,deh->ecd", d_gate_act, whole_expert[:, :, 0], preferred_element_type=jnp.float32
    )
    d_inputs = d_inputs + jnp.einsum(
        "ech,deh->ecd", d_up_act, whole_expert[:, :, 1], preferred_element_type=jnp.float32
    )
    d_in_pad = jnp.concatenate(
        [d_inputs.reshape(EXPERTS * CAP, model_width), jnp.zeros((1, model_width), jnp.float32)],
        axis=0,
    )
    d_normed_part = jnp.sum(d_in_pad[pair_slot], axis=1)
    d_normed_two, gate_grad = lax.psum((d_normed_part, gate_part), "tp")
    d_resid_norm, gain_two = norm_back(residual, inv_two, ffn_norm, d_normed_two)
    d_residual = grad_out + d_resid_norm
    d_attn = d_residual.astype(jnp.bfloat16)
    d_mixed = jnp.einsum(
        "td,dhc->thc", d_attn, whole_attn[:, :, input_columns:], preferred_element_type=jnp.float32
    ).astype(jnp.bfloat16)
    d_mixed_seq = d_mixed.reshape(sequence_count, block_len, kv_loc, QUERY_PER_GROUP, HEAD_DIM)
    d_queries, d_key_all, d_value_all = lax.map(
        lambda item_args: attend_backward(
            item_args[0], item_args[1], item_args[2], allowed, item_args[3], item_args[4]
        ),
        (query_seq, key_all, value_all, log_total, d_mixed_seq),
    )
    d_keys, d_values = (
        lax.psum_scatter(
            d_key_all.astype(jnp.bfloat16), "ctx", scatter_dimension=1, tiled=True
        ).astype(jnp.float32),
        lax.psum_scatter(
            d_value_all.astype(jnp.bfloat16), "ctx", scatter_dimension=1, tiled=True
        ).astype(jnp.float32),
    )
    d_queries = rotate(
        d_queries.reshape(tok_count, kv_loc, QUERY_PER_GROUP, HEAD_DIM), cos_four, -sin_four
    )
    d_keys = rotate(d_keys.reshape(tok_count, kv_loc, HEAD_DIM), cos_three, -sin_three)
    d_values = d_values.reshape(tok_count, kv_loc, HEAD_DIM)
    d_projected = jnp.concatenate([d_queries, d_keys[:, :, None], d_values[:, :, None]], axis=2)
    d_projected = d_projected.astype(jnp.bfloat16).reshape(tok_count, kv_loc, input_columns)
    d_normed_local = jnp.einsum(
        "thc,dhc->td",
        d_projected,
        whole_attn[:, :, :input_columns],
        preferred_element_type=jnp.float32,
    )
    d_normed_one = lax.psum(d_normed_local.astype(jnp.bfloat16), "tp").astype(jnp.float32)
    d_tok_norm, gain_one = norm_back(tok_float, inv_one, attn_norm, d_normed_one)
    tokens_grad = (
        (d_residual + d_tok_norm)
        .astype(jnp.bfloat16)
        .reshape(sequence_count, block_len, model_width)
    )
    gain_one, gain_two = lax.psum((gain_one, gain_two), ("fsdp", "ctx"))
    in_term = jnp.einsum(
        "td,thc->dhc", first_normed, d_projected, preferred_element_type=jnp.float32
    )
    out_term = jnp.einsum("td,thc->dhc", d_attn, mixed_flat, preferred_element_type=jnp.float32)
    attn_grad = lax.psum_scatter(
        jnp.concatenate([in_term, out_term], axis=2),
        ("fsdp", "ctx"),
        scatter_dimension=0,
        tiled=True,
    )
    gate_term = jnp.einsum("ecd,ech->deh", inputs, d_gate_act, preferred_element_type=jnp.float32)
    up_term = jnp.einsum("ecd,ech->deh", inputs, d_up_act, preferred_element_type=jnp.float32)
    down_term = jnp.einsum("ecd,ech->deh", d_expert, hidden, preferred_element_type=jnp.float32)
    expert_grad = lax.psum_scatter(
        jnp.stack([gate_term, up_term, down_term], axis=2),
        ("fsdp", "ctx"),
        scatter_dimension=0,
        tiled=True,
    )
    attn_grad, expert_grad = (
        lax.all_gather(attn_grad.astype(jnp.bfloat16), "ctx", axis=0, tiled=True).astype(
            attn_grad.dtype
        ),
        lax.all_gather(expert_grad.astype(jnp.bfloat16), "ctx", axis=0, tiled=True).astype(
            expert_grad.dtype
        ),
    )
    return (
        layer_out,
        tokens_grad,
        attn_grad,
        expert_grad,
        gain_one,
        gain_two,
        gate_grad.reshape(sequence_count, block_len, TOP),
    )


MESH_ID = pl.DeviceIdType.MESH
MIB = 2**20


def rel_perm(size, r):
    return [(i, i ^ r) for i in range(size)]


def from_rel(value, r):
    return lax.ppermute(value, "fsdp", rel_perm(lax.axis_size("fsdp"), r))


def swap_core(value):
    return lax.ppermute(value, "tp", [(0, 1), (1, 0)])


def shift_ctx(value, step):
    size = lax.axis_size("ctx")
    pairs = [(i, i + step) for i in range(size) if 0 <= i + step < size]
    return lax.ppermute(value, "ctx", pairs)


def sum_ctx(value):
    place = lax.axis_index("ctx")
    inner = (place == 1) | (place == 2)
    arrived = lax.ppermute(value, "ctx", [(0, 1), (3, 2)])
    pair = jnp.where(
        inner, value.astype(jnp.float32) + arrived.astype(jnp.float32), value.astype(jnp.float32)
    ).astype(jnp.bfloat16)
    across = lax.ppermute(pair, "ctx", [(1, 2), (2, 1)])
    total = (pair.astype(jnp.float32) + across.astype(jnp.float32)).astype(jnp.bfloat16)
    back = lax.ppermute(total, "ctx", [(1, 0), (2, 3)])
    return jnp.where(inner, total, back)


def expert_order(place):
    row = jnp.arange(128, dtype=jnp.int32)
    expert = (((row // 32) ^ place) * 2) + (row // 16) % 2
    source = (row % 16) * 8 + expert
    return (source[:, None] == row[None, :]).astype(jnp.bfloat16)


def split_kernel(order_ref, in_ref, out_ref):
    depth = in_ref.shape[0]
    for m in range(3):
        for k in range(depth // 16):
            block = in_ref[pl.ds(k * 16, 16), m].reshape(128, in_ref.shape[3])
            moved = jnp.dot(order_ref[...], block, preferred_element_type=jnp.float32)
            moved = moved.astype(jnp.bfloat16).reshape(8, 16, in_ref.shape[3])
            out_ref[:, m, pl.ds(k * 16, 16), :] = moved


def split_experts(weights, order):
    rows, _, experts, width = weights.shape
    step = 64
    return pl.pallas_call(
        split_kernel,
        grid=(rows // step,),
        in_specs=[
            pl.BlockSpec((128, 128), lambda i: (0, 0)),
            pl.BlockSpec((step, 3, experts, width), lambda i: (i, 0, 0, 0)),
        ],
        out_specs=pl.BlockSpec((experts, 3, step, width), lambda i: (0, 0, i, 0)),
        out_shape=jax.ShapeDtypeStruct((experts, 3, rows, width), jnp.bfloat16),
        compiler_params=pltpu.CompilerParams(vmem_limit_bytes=40 * MIB),
        name="split_experts",
    )(order, weights)


def join_kernel(order_ref, in_ref, out_ref):
    width = in_ref.shape[3]
    for m in range(3):
        for k in range(in_ref.shape[2] // 16):
            block = in_ref[:, m, pl.ds(k * 16, 16), :].reshape(128, width)
            moved = jnp.dot(order_ref[...], block, preferred_element_type=jnp.float32)
            out_ref[pl.ds(k * 16, 16), m] = moved.reshape(16, 8, width)


def join_experts(grads, order):
    experts, _, rows, width = grads.shape
    step = 64
    return pl.pallas_call(
        join_kernel,
        grid=(rows // step,),
        in_specs=[
            pl.BlockSpec((128, 128), lambda i: (0, 0)),
            pl.BlockSpec((experts, 3, step, width), lambda i: (0, 0, i, 0)),
        ],
        out_specs=pl.BlockSpec((step, 3, experts, width), lambda i: (i, 0, 0, 0)),
        out_shape=jax.ShapeDtypeStruct((rows, 3, experts, width), jnp.float32),
        compiler_params=pltpu.CompilerParams(vmem_limit_bytes=40 * MIB),
        name="join_experts",
    )(order, grads)


NT = (((1,), (1,)), ((), ()))
TN = (((0,), (0,)), ((), ()))


def dot_f32(a, b, dims=(((1,), (0,)), ((), ()))):
    return lax.dot_general(a, b, dims, preferred_element_type=jnp.float32)


def block_probs(place_ref, keys, query):
    scores = dot_f32(keys, query, NT) * HEAD_DIM ** (-0.5)
    block = lax.broadcasted_iota(jnp.int32, scores.shape, 0) // query.shape[0]
    scores = jnp.where(block <= place_ref[0], scores, -1e30)
    expd = jnp.exp(scores - jnp.max(scores, axis=0, keepdims=True))
    return expd * (1.0 / jnp.sum(expd, axis=0, keepdims=True))


def attend_kernel(place_ref, q_ref, k_ref, v_ref, out_ref):
    keys = k_ref[...]
    vals = v_ref[...]
    for g in range(QUERY_PER_GROUP):
        cols = pl.ds(g * HEAD_DIM, HEAD_DIM)
        probs = block_probs(place_ref, keys, q_ref[:, cols]).astype(jnp.bfloat16)
        out_ref[:, cols] = dot_f32(probs, vals, TN).astype(jnp.bfloat16)


def attend_back_kernel(place_ref, q_ref, k_ref, v_ref, dm_ref, dq_ref, dk_ref, dv_ref):
    keys = k_ref[...]
    vals = v_ref[...]
    scale = HEAD_DIM ** (-0.5)
    dk_ref[...] = jnp.zeros_like(dk_ref)
    dv_ref[...] = jnp.zeros_like(dv_ref)
    for g in range(QUERY_PER_GROUP):
        cols = pl.ds(g * HEAD_DIM, HEAD_DIM)
        query = q_ref[:, cols]
        d_mixed = dm_ref[:, cols]
        probs = block_probs(place_ref, keys, query)
        d_probs = dot_f32(vals, d_mixed, NT)
        inner = jnp.sum(probs * d_probs, axis=0, keepdims=True)
        d_scores = (probs * (d_probs - inner)).astype(jnp.bfloat16)
        dq_ref[:, cols] = dot_f32(d_scores, keys, TN) * scale
        dk_ref[...] += dot_f32(d_scores, query) * scale
        dv_ref[...] += dot_f32(probs.astype(jnp.bfloat16), d_mixed)


def attend(place, q, k, v):
    return pl.pallas_call(
        attend_kernel,
        in_specs=[pl.BlockSpec(memory_space=pltpu.SMEM)]
        + [pl.BlockSpec(memory_space=pltpu.VMEM)] * 3,
        out_specs=pl.BlockSpec(memory_space=pltpu.VMEM),
        out_shape=jax.ShapeDtypeStruct(q.shape, jnp.bfloat16),
        compiler_params=pltpu.CompilerParams(vmem_limit_bytes=40 * MIB),
        name="attend",
    )(place, q, k, v)


def attend_back(place, q, k, v, d_mixed):
    return pl.pallas_call(
        attend_back_kernel,
        in_specs=[pl.BlockSpec(memory_space=pltpu.SMEM)]
        + [pl.BlockSpec(memory_space=pltpu.VMEM)] * 4,
        out_specs=[pl.BlockSpec(memory_space=pltpu.VMEM)] * 3,
        out_shape=[
            jax.ShapeDtypeStruct(q.shape, jnp.float32),
            jax.ShapeDtypeStruct(k.shape, jnp.float32),
            jax.ShapeDtypeStruct(v.shape, jnp.float32),
        ],
        compiler_params=pltpu.CompilerParams(vmem_limit_bytes=40 * MIB),
        name="attend_back",
    )(place, q, k, v, d_mixed)


def spread_rows(half):
    mine = jnp.stack([half] + [from_rel(half, r) for r in range(1, 4)])
    return jnp.stack([mine, swap_core(mine)])


def gather_sum(parts):
    own, other = parts[0], parts[1].astype(jnp.bfloat16)
    both = own + swap_core(other).astype(jnp.float32)
    total = both[0]
    for r in range(1, 4):
        total = total + from_rel(both[r].astype(jnp.bfloat16), r).astype(jnp.float32)
    return total


def join_halves(core, half):
    other = swap_core(half)
    first = jnp.where(core == 0, half, other)
    second = jnp.where(core == 0, other, half)
    return jnp.concatenate([first, second], axis=0)


def body_fast(
    tokens,
    attn_norm,
    attention_params,
    ffn_norm,
    expert_weights,
    gate_values,
    routes,
    slot_order,
    cotangent,
):
    sequence_count, block_len, model_width = tokens.shape
    count = sequence_count * block_len
    half = count // 2
    own_experts = EXPERTS // 4
    input_columns = (QUERY_PER_GROUP + 2) * HEAD_DIM
    query_columns = QUERY_PER_GROUP * HEAD_DIM
    f = lax.axis_index("fsdp")
    z = lax.axis_index("ctx")
    core = lax.axis_index("tp")
    shard = attention_params.shape[0]
    f32, bf16 = jnp.float32, jnp.bfloat16

    def my_half(value):
        return lax.dynamic_slice_in_dim(value, core * half, half, 0)

    attn_own = attention_params[:, 0, :]
    attn_x, attn_y = from_rel(attn_own, 1), from_rel(attn_own, 2)
    cut = shard // 2
    attn_d = jnp.concatenate([from_rel(attn_x[:cut], 2), from_rel(attn_y[cut:], 1)], axis=0)
    place_order = jnp.arange(4, dtype=jnp.int32) ^ f
    whole_attn = jnp.stack([attn_own, attn_x, attn_y, attn_d])[place_order].reshape(
        4 * shard, attention_params.shape[2]
    )
    attn_in, attn_out = whole_attn[:, :input_columns], whole_attn[:, input_columns:]

    order = expert_order(f)
    pieces = split_experts(jnp.transpose(expert_weights, (0, 2, 1, 3)), order)
    pieces = pieces.reshape(4, own_experts, 3, shard, expert_weights.shape[3])
    arrived = [pieces[0]] + [from_rel(pieces[r], r) for r in range(1, 4)]
    whole_expert = jnp.stack(arrived, axis=2)
    whole_expert = jnp.take(whole_expert, place_order, axis=2).reshape(
        own_experts, 3, 4 * shard, expert_weights.shape[3]
    )

    route_rows, rank_rows = routes.reshape(count, TOP), slot_order.reshape(count)
    gates = gate_values.reshape(count, TOP)
    chosen = route_rows[:, :, None] == jnp.arange(EXPERTS, dtype=jnp.int32)
    member = jnp.any(chosen, axis=1)
    ahead = rank_rows[None, :] < rank_rows[:, None]
    slots = dot_f32(ahead.astype(bf16), member.astype(bf16))
    kept = member & (slots < CAP - 0.5)
    weight = jnp.sum(jnp.where(chosen, gates[:, :, None], 0.0), axis=1) * kept.astype(f32)
    weight_rows = weight.T.reshape(4, own_experts, 2, half)
    weight_rows = weight_rows[place_order]
    weights_in = jnp.stack(
        [weight_rows[0]] + [from_rel(weight_rows[r], r) for r in range(1, 4)]
    )
    weights_in = jnp.where(core == 0, weights_in, weights_in[:, :, ::-1])
    weights_in = jnp.transpose(weights_in, (1, 2, 0, 3)).reshape(own_experts, 8 * half)

    positions = z * block_len + jnp.arange(block_len, dtype=jnp.int32)
    cosine, sine = angle_tables(positions)
    cos_three, sin_three = cosine[:, None, :], sine[:, None, :]
    tok_float = tokens.reshape(count, model_width).astype(f32)
    inv_one = lax.rsqrt(jnp.mean(tok_float * tok_float, axis=-1, keepdims=True) + eps)
    first_normed = (tok_float * inv_one * attn_norm).astype(bf16)
    projected = dot_f32(first_normed, attn_in).reshape(count, QUERY_PER_GROUP + 2, HEAD_DIM)
    turned = rotate(projected[:, : QUERY_PER_GROUP + 1], cos_three, sin_three).astype(bf16)
    queries = turned[:, :QUERY_PER_GROUP].reshape(count, query_columns)
    key_value = jnp.concatenate(
        [turned[:, QUERY_PER_GROUP], projected[:, QUERY_PER_GROUP + 1].astype(bf16)], axis=1
    )
    kv_all = jnp.concatenate([key_value] + [shift_ctx(key_value, s) for s in range(1, 4)], axis=0)
    key_all, value_all = kv_all[:, :HEAD_DIM], kv_all[:, HEAD_DIM:]
    place = jnp.reshape(z, (1,)).astype(jnp.int32)
    mixed = attend(place, queries, key_all, value_all)
    attn_part = dot_f32(mixed, attn_out, NT)
    other_rows = lax.dynamic_slice_in_dim(attn_part, (1 - core) * half, half, 0)
    residual = my_half(tok_float) + (my_half(attn_part) + swap_core(other_rows))
    inv_two = lax.rsqrt(jnp.mean(residual * residual, axis=-1, keepdims=True) + eps)
    normed_two = (residual * inv_two * ffn_norm).astype(bf16)

    grad_out = cotangent.reshape(count, model_width)
    inputs = spread_rows(normed_two).reshape(8 * half, model_width)
    upstream = spread_rows(my_half(grad_out)).reshape(8 * half, model_width)
    moe_parts = 0.0
    d_normed_parts = 0.0
    gate_parts = []
    expert_grads = []
    for e in range(own_experts):
        gate_act = dot_f32(inputs, whole_expert[e, 0])
        up_act = dot_f32(inputs, whole_expert[e, 1])
        d_plain = dot_f32(upstream, whole_expert[e, 2])
        gate_sigmoid = jax.nn.sigmoid(gate_act)
        active = gate_act * gate_sigmoid
        hidden = active * up_act
        scale = weights_in[e][:, None]
        hidden_low = (hidden * scale).astype(bf16)
        gate_parts.append(jnp.sum(hidden * d_plain, axis=1))
        d_hidden = d_plain * scale
        silu_slope = gate_sigmoid * (1.0 + gate_act * (1.0 - gate_sigmoid))
        d_gate = (d_hidden * up_act * silu_slope).astype(bf16)
        d_up = (d_hidden * active).astype(bf16)
        moe_parts = moe_parts + dot_f32(hidden_low, whole_expert[e, 2], NT)
        d_normed_parts = (
            d_normed_parts
            + dot_f32(d_gate, whole_expert[e, 0], NT)
            + dot_f32(d_up, whole_expert[e, 1], NT)
        )
        expert_grads.append(
            jnp.stack(
                [
                    dot_f32(inputs, d_gate, TN).astype(bf16),
                    dot_f32(inputs, d_up, TN).astype(bf16),
                    dot_f32(upstream, hidden_low, TN).astype(bf16),
                ]
            )
        )
    d_normed_two = gather_sum(d_normed_parts.reshape(2, 4, half, model_width))
    moe = gather_sum(moe_parts.reshape(2, 4, half, model_width))
    layer_out = join_halves(core, (residual + moe).astype(bf16))

    gate_rows = jnp.stack(gate_parts).reshape(own_experts, 2, 4, half)
    gate_rows = gate_rows[:, 0] + swap_core(gate_rows[:, 1])
    gate_rows = jnp.stack(
        [gate_rows[:, 0]] + [from_rel(gate_rows[:, r], r) for r in range(1, 4)]
    )
    gate_rows = join_halves(core, gate_rows.reshape(EXPERTS, half).T)
    rel_ids = (place_order[:, None] * own_experts + jnp.arange(own_experts)).reshape(EXPERTS)
    kept_rel = kept[:, rel_ids]
    picked = (route_rows[:, :, None] == rel_ids) & kept_rel[:, None, :]
    gate_grad = jnp.sum(jnp.where(picked, gate_rows[:, None, :], 0.0), axis=-1)

    d_resid_norm, gain_two = norm_back(residual, inv_two, ffn_norm, d_normed_two)
    d_residual = my_half(grad_out).astype(f32) + d_resid_norm
    d_attn = join_halves(core, d_residual.astype(bf16))
    d_mixed = dot_f32(d_attn, attn_out).astype(bf16)
    d_queries, d_key_all, d_value_all = attend_back(place, queries, key_all, value_all, d_mixed)
    d_kv = jnp.concatenate([d_key_all, d_value_all], axis=1).reshape(4, count, 2 * HEAD_DIM)
    d_key_value = d_kv[0]
    for s in range(1, 4):
        d_key_value = d_key_value + shift_ctx(d_kv[s].astype(bf16), -s).astype(f32)
    d_turned = jnp.concatenate([d_queries, d_key_value[:, :HEAD_DIM]], axis=1)
    d_turned = rotate(
        d_turned.reshape(count, QUERY_PER_GROUP + 1, HEAD_DIM), cos_three, -sin_three
    ).reshape(count, query_columns + HEAD_DIM)
    d_projected = jnp.concatenate([d_turned, d_key_value[:, HEAD_DIM:]], axis=1).astype(bf16)
    d_normed_local = dot_f32(d_projected, attn_in, NT)
    other_rows = lax.dynamic_slice_in_dim(d_normed_local, (1 - core) * half, half, 0)
    d_normed_one = my_half(d_normed_local) + swap_core(other_rows.astype(bf16)).astype(f32)
    d_tok_norm, gain_one = norm_back(my_half(tok_float), my_half(inv_one), attn_norm, d_normed_one)
    tokens_grad = join_halves(core, (d_residual + d_tok_norm).astype(bf16))
    gains = lax.psum(jnp.stack([gain_one, gain_two]), ("fsdp", "ctx", "tp"))

    attn_grad = jnp.concatenate(
        [dot_f32(first_normed, d_projected, TN), dot_f32(d_attn, mixed, TN)], axis=1
    ).reshape(4, shard, -1)[place_order]
    attn_sum = attn_grad[0]
    for r in range(1, 4):
        attn_sum = attn_sum + from_rel(attn_grad[r].astype(bf16), r).astype(f32)
    attn_total = sum_ctx(attn_sum.astype(bf16)).astype(f32)[:, None, :]

    finals = []
    for e in range(own_experts):
        total = sum_ctx(expert_grads[e]).reshape(3, 4, shard, -1)
        total = jnp.take(total, place_order, axis=1)
        finals.append(
            jnp.stack([total[:, 0]] + [from_rel(total[:, r], r) for r in range(1, 4)])
        )
    finals = jnp.stack(finals, axis=1).reshape(EXPERTS, 3, shard, -1)
    expert_grad = jnp.transpose(join_experts(finals, order.T), (0, 2, 1, 3))
    return (
        layer_out.reshape(sequence_count, block_len, model_width),
        tokens_grad.reshape(sequence_count, block_len, model_width),
        attn_total,
        expert_grad,
        gains[0],
        gains[1],
        gate_grad.reshape(sequence_count, block_len, TOP),
    )


def solution(mesh):
    in_specs = (
        P("fsdp", "ctx", None),
        P(),
        P("fsdp", "tp", None),
        P(),
        P("fsdp", None, None, "tp"),
        P("fsdp", "ctx", None),
        P("fsdp", "ctx", None),
        P("fsdp", "ctx"),
        P("fsdp", "ctx", None),
    )
    out_specs = (
        P("fsdp", "ctx", None),
        P("fsdp", "ctx", None),
        P("fsdp", "tp", None),
        P("fsdp", None, None, "tp"),
        P(),
        P(),
        P("fsdp", "ctx", None),
    )
    four = mesh.shape["fsdp"] == 4 and mesh.shape["ctx"] == 4 and mesh.shape["tp"] == 2
    body_fn = body_fast if four else body
    return jax.shard_map(body_fn, mesh=mesh, in_specs=in_specs, out_specs=out_specs, check_vma=False)
```

```python
import jax
import jax.numpy as jnp
from jax import lax
import numpy as np
from jax.experimental import pallas as pl
from jax.experimental.pallas import tpu as pltpu
from jax.sharding import PartitionSpec as P

HEAD_DIM = 128
TOP = 4
EXPERTS = 8
QUERY_PER_GROUP = 6
CAP = 160


eps = 1e-06
theta_base = 1000000.0


def angle_tables(positions):
    frequency = theta_base ** (-(jnp.arange(HEAD_DIM // 2, dtype=jnp.float32) * 2.0) / HEAD_DIM)
    angles = positions.astype(jnp.float32)[:, None] * frequency[None, :]
    return (jnp.cos(angles), jnp.sin(angles))


def rotate(source, cosine_table, sine_table):
    half_size = source.shape[-1] // 2
    front_half = source[..., :half_size]
    back_half = source[..., half_size:]
    return jnp.concatenate(
        [
            front_half * cosine_table - back_half * sine_table,
            back_half * cosine_table + front_half * sine_table,
        ],
        axis=-1,
    )


def norm_back(source, inv_rms, gain_vec, upstream):
    scaled = upstream * gain_vec
    inner_sum = jnp.mean(scaled * source, axis=-1, keepdims=True)
    d_source = inv_rms * scaled - source * inv_rms * inv_rms * inv_rms * inner_sum
    return (d_source, jnp.sum(upstream * source * inv_rms, axis=0))


def slot_tables(route_rows, rank_rows):
    tok_count = route_rows.shape[0]
    inverse = (
        jnp.zeros((tok_count,), jnp.int32).at[rank_rows].set(jnp.arange(tok_count, dtype=jnp.int32))
    )
    ranked = route_rows[inverse].reshape(-1)
    onehot = (ranked[:, None] == jnp.arange(EXPERTS, dtype=jnp.int32)[None, :]).astype(jnp.int32)
    before = jnp.cumsum(onehot, axis=0) - onehot
    slot_ranked = jnp.sum(before * onehot, axis=1).reshape(tok_count, TOP)
    slots = slot_ranked[rank_rows]
    kept_pair = slots < CAP
    pair_slot = jnp.where(kept_pair, route_rows * CAP + slots, EXPERTS * CAP)
    owners = jnp.broadcast_to(jnp.arange(tok_count, dtype=jnp.int32)[:, None], (tok_count, TOP))
    slot_token = (
        jnp.full((EXPERTS * CAP,), tok_count, jnp.int32)
        .at[pair_slot.reshape(-1)]
        .set(owners.reshape(-1), mode="drop")
    )
    return (kept_pair, pair_slot, slot_token)


def attend_forward(queries, key_rows, value_rows, allowed):
    scores = jnp.einsum(
        "qhgd,khd->hgqk", queries, key_rows, preferred_element_type=jnp.float32
    ) * HEAD_DIM ** (-0.5)
    scores = jnp.where(allowed, scores, -1e30)
    row_max = jnp.max(scores, axis=-1, keepdims=True)
    expd = jnp.exp(scores - row_max)
    row_total = jnp.sum(expd, axis=-1, keepdims=True)
    attn_probs = (expd / row_total).astype(jnp.bfloat16)
    mixed_heads = jnp.einsum(
        "hgqk,khd->qhgd", attn_probs, value_rows, preferred_element_type=jnp.float32
    )
    return (mixed_heads.astype(jnp.bfloat16), row_max + jnp.log(row_total))


def attend_backward(queries, key_rows, value_rows, allowed, log_total, d_mixed):
    scores = jnp.einsum(
        "qhgd,khd->hgqk", queries, key_rows, preferred_element_type=jnp.float32
    ) * HEAD_DIM ** (-0.5)
    scores = jnp.where(allowed, scores, -1e30)
    attn_probs = jnp.exp(scores - log_total)
    low_probs = attn_probs.astype(jnp.bfloat16)
    d_probs = jnp.einsum("qhgd,khd->hgqk", d_mixed, value_rows, preferred_element_type=jnp.float32)
    inner_sum = jnp.sum(attn_probs * d_probs, axis=-1, keepdims=True)
    d_scores = (attn_probs * (d_probs - inner_sum)).astype(jnp.bfloat16)
    d_queries = jnp.einsum(
        "hgqk,khd->qhgd", d_scores, key_rows, preferred_element_type=jnp.float32
    ) * HEAD_DIM ** (-0.5)
    d_keys = jnp.einsum(
        "hgqk,qhgd->khd", d_scores, queries, preferred_element_type=jnp.float32
    ) * HEAD_DIM ** (-0.5)
    d_values = jnp.einsum("hgqk,qhgd->khd", low_probs, d_mixed, preferred_element_type=jnp.float32)
    return (d_queries, d_keys, d_values)


def body(
    tokens,
    attn_norm,
    attention_params,
    ffn_norm,
    expert_weights,
    gate_values,
    routes,
    slot_order,
    cotangent,
):
    sequence_count, block_len, model_width = tokens.shape
    tok_count = sequence_count * block_len
    kv_loc = attention_params.shape[1]
    input_columns = (QUERY_PER_GROUP + 2) * HEAD_DIM
    ctx_size = lax.axis_size("ctx")
    ctx_place = lax.axis_index("ctx")
    sequence_length = block_len * ctx_size
    whole_attn, whole_expert = (
        lax.all_gather(attention_params, "fsdp", axis=0, tiled=True),
        lax.all_gather(expert_weights, "fsdp", axis=0, tiled=True),
    )
    positions = ctx_place * block_len + jnp.arange(block_len, dtype=jnp.int32)
    cosine_table, sine_table = angle_tables(positions)
    cosine_table = jnp.tile(cosine_table, (sequence_count, 1))
    sine_table = jnp.tile(sine_table, (sequence_count, 1))
    cos_four = cosine_table[:, None, None, :]
    sin_four = sine_table[:, None, None, :]
    cos_three = cosine_table[:, None, :]
    sin_three = sine_table[:, None, :]
    allowed = (jnp.arange(sequence_length, dtype=jnp.int32) // block_len <= ctx_place)[
        None, None, None, :
    ]
    tok_float = tokens.reshape(tok_count, model_width).astype(jnp.float32)
    inv_one = lax.rsqrt(jnp.mean(tok_float * tok_float, axis=-1, keepdims=True) + eps)
    first_normed = (tok_float * inv_one * attn_norm).astype(jnp.bfloat16)
    projected_rows = jnp.einsum(
        "td,dhc->thc",
        first_normed,
        whole_attn[:, :, :input_columns],
        preferred_element_type=jnp.float32,
    ).reshape(tok_count, kv_loc, QUERY_PER_GROUP + 2, HEAD_DIM)
    queries = rotate(projected_rows[:, :, :QUERY_PER_GROUP], cos_four, sin_four).astype(
        jnp.bfloat16
    )
    key_rows = rotate(projected_rows[:, :, QUERY_PER_GROUP], cos_three, sin_three).astype(
        jnp.bfloat16
    )
    value_rows = projected_rows[:, :, QUERY_PER_GROUP + 1].astype(jnp.bfloat16)
    key_all, value_all = (
        lax.all_gather(
            key_rows.reshape(sequence_count, block_len, kv_loc, HEAD_DIM), "ctx", axis=1, tiled=True
        ),
        lax.all_gather(
            value_rows.reshape(sequence_count, block_len, kv_loc, HEAD_DIM),
            "ctx",
            axis=1,
            tiled=True,
        ),
    )
    query_seq = queries.reshape(sequence_count, block_len, kv_loc, QUERY_PER_GROUP, HEAD_DIM)
    mixed_heads, log_total = lax.map(
        lambda item_args: attend_forward(item_args[0], item_args[1], item_args[2], allowed),
        (query_seq, key_all, value_all),
    )
    mixed_flat = mixed_heads.reshape(tok_count, kv_loc, QUERY_PER_GROUP * HEAD_DIM)
    attn_part = jnp.einsum(
        "thc,dhc->td",
        mixed_flat,
        whole_attn[:, :, input_columns:],
        preferred_element_type=jnp.float32,
    )
    attn_sum = lax.psum(attn_part, "tp")
    residual = tok_float + attn_sum
    inv_two = lax.rsqrt(jnp.mean(residual * residual, axis=-1, keepdims=True) + eps)
    normed_two = (residual * inv_two * ffn_norm).astype(jnp.bfloat16)
    kept_pair, pair_slot, slot_token = slot_tables(
        routes.reshape(tok_count, TOP), slot_order.reshape(tok_count)
    )
    kept_float = kept_pair.astype(jnp.float32)
    gate_kept = gate_values.reshape(tok_count, TOP) * kept_float
    slot_gate = (
        jnp.zeros((EXPERTS * CAP,), jnp.float32)
        .at[pair_slot.reshape(-1)]
        .set(gate_kept.reshape(-1), mode="drop")
    )
    padded = jnp.concatenate([normed_two, jnp.zeros((1, model_width), jnp.bfloat16)], axis=0)
    inputs = padded[slot_token].reshape(EXPERTS, CAP, model_width)
    gate_act = jnp.einsum(
        "ecd,deh->ech", inputs, whole_expert[:, :, 0], preferred_element_type=jnp.float32
    )
    up_act = jnp.einsum(
        "ecd,deh->ech", inputs, whole_expert[:, :, 1], preferred_element_type=jnp.float32
    )
    gate_sigmoid = jax.nn.sigmoid(gate_act)
    active = gate_act * gate_sigmoid
    hidden = (active * up_act).astype(jnp.bfloat16)
    expert_out = jnp.einsum(
        "ech,deh->ecd", hidden, whole_expert[:, :, 2], preferred_element_type=jnp.float32
    )
    out_pad = jnp.concatenate(
        [expert_out.reshape(EXPERTS * CAP, model_width), jnp.zeros((1, model_width), jnp.float32)],
        axis=0,
    )
    picked = out_pad[pair_slot]
    moe_part = jnp.sum(picked * gate_kept[:, :, None], axis=1)
    moe = lax.psum(moe_part.astype(jnp.bfloat16), "tp").astype(jnp.float32)
    layer_out = (
        (residual + moe).astype(jnp.bfloat16).reshape(sequence_count, block_len, model_width)
    )
    grad_out = cotangent.reshape(tok_count, model_width).astype(jnp.float32)
    gate_part = jnp.sum(picked * grad_out[:, None, :], axis=-1) * kept_float
    grad_pad = jnp.concatenate([grad_out, jnp.zeros((1, model_width), jnp.float32)], axis=0)
    d_expert = (
        (grad_pad[slot_token] * slot_gate[:, None])
        .astype(jnp.bfloat16)
        .reshape(EXPERTS, CAP, model_width)
    )
    d_hidden = jnp.einsum(
        "ecd,deh->ech", d_expert, whole_expert[:, :, 2], preferred_element_type=jnp.float32
    )
    silu_slope = gate_sigmoid * (1.0 + gate_act * (1.0 - gate_sigmoid))
    d_gate_act = (d_hidden * up_act * silu_slope).astype(jnp.bfloat16)
    d_up_act = (d_hidden * active).astype(jnp.bfloat16)
    d_inputs = jnp.einsum(
        "ech,deh->ecd", d_gate_act, whole_expert[:, :, 0], preferred_element_type=jnp.float32
    )
    d_inputs = d_inputs + jnp.einsum(
        "ech,deh->ecd", d_up_act, whole_expert[:, :, 1], preferred_element_type=jnp.float32
    )
    d_in_pad = jnp.concatenate(
        [d_inputs.reshape(EXPERTS * CAP, model_width), jnp.zeros((1, model_width), jnp.float32)],
        axis=0,
    )
    d_normed_part = jnp.sum(d_in_pad[pair_slot], axis=1)
    d_normed_two, gate_grad = lax.psum((d_normed_part, gate_part), "tp")
    d_resid_norm, gain_two = norm_back(residual, inv_two, ffn_norm, d_normed_two)
    d_residual = grad_out + d_resid_norm
    d_attn = d_residual.astype(jnp.bfloat16)
    d_mixed = jnp.einsum(
        "td,dhc->thc", d_attn, whole_attn[:, :, input_columns:], preferred_element_type=jnp.float32
    ).astype(jnp.bfloat16)
    d_mixed_seq = d_mixed.reshape(sequence_count, block_len, kv_loc, QUERY_PER_GROUP, HEAD_DIM)
    d_queries, d_key_all, d_value_all = lax.map(
        lambda item_args: attend_backward(
            item_args[0], item_args[1], item_args[2], allowed, item_args[3], item_args[4]
        ),
        (query_seq, key_all, value_all, log_total, d_mixed_seq),
    )
    d_keys, d_values = (
        lax.psum_scatter(
            d_key_all.astype(jnp.bfloat16), "ctx", scatter_dimension=1, tiled=True
        ).astype(jnp.float32),
        lax.psum_scatter(
            d_value_all.astype(jnp.bfloat16), "ctx", scatter_dimension=1, tiled=True
        ).astype(jnp.float32),
    )
    d_queries = rotate(
        d_queries.reshape(tok_count, kv_loc, QUERY_PER_GROUP, HEAD_DIM), cos_four, -sin_four
    )
    d_keys = rotate(d_keys.reshape(tok_count, kv_loc, HEAD_DIM), cos_three, -sin_three)
    d_values = d_values.reshape(tok_count, kv_loc, HEAD_DIM)
    d_projected = jnp.concatenate([d_queries, d_keys[:, :, None], d_values[:, :, None]], axis=2)
    d_projected = d_projected.astype(jnp.bfloat16).reshape(tok_count, kv_loc, input_columns)
    d_normed_local = jnp.einsum(
        "thc,dhc->td",
        d_projected,
        whole_attn[:, :, :input_columns],
        preferred_element_type=jnp.float32,
    )
    d_normed_one = lax.psum(d_normed_local.astype(jnp.bfloat16), "tp").astype(jnp.float32)
    d_tok_norm, gain_one = norm_back(tok_float, inv_one, attn_norm, d_normed_one)
    tokens_grad = (
        (d_residual + d_tok_norm)
        .astype(jnp.bfloat16)
        .reshape(sequence_count, block_len, model_width)
    )
    gain_one, gain_two = lax.psum((gain_one, gain_two), ("fsdp", "ctx"))
    in_term = jnp.einsum(
        "td,thc->dhc", first_normed, d_projected, preferred_element_type=jnp.float32
    )
    out_term = jnp.einsum("td,thc->dhc", d_attn, mixed_flat, preferred_element_type=jnp.float32)
    attn_grad = lax.psum_scatter(
        jnp.concatenate([in_term, out_term], axis=2),
        ("fsdp", "ctx"),
        scatter_dimension=0,
        tiled=True,
    )
    gate_term = jnp.einsum("ecd,ech->deh", inputs, d_gate_act, preferred_element_type=jnp.float32)
    up_term = jnp.einsum("ecd,ech->deh", inputs, d_up_act, preferred_element_type=jnp.float32)
    down_term = jnp.einsum("ecd,ech->deh", d_expert, hidden, preferred_element_type=jnp.float32)
    expert_grad = lax.psum_scatter(
        jnp.stack([gate_term, up_term, down_term], axis=2),
        ("fsdp", "ctx"),
        scatter_dimension=0,
        tiled=True,
    )
    attn_grad, expert_grad = (
        lax.all_gather(attn_grad.astype(jnp.bfloat16), "ctx", axis=0, tiled=True).astype(
            attn_grad.dtype
        ),
        lax.all_gather(expert_grad.astype(jnp.bfloat16), "ctx", axis=0, tiled=True).astype(
            expert_grad.dtype
        ),
    )
    return (
        layer_out,
        tokens_grad,
        attn_grad,
        expert_grad,
        gain_one,
        gain_two,
        gate_grad.reshape(sequence_count, block_len, TOP),
    )


MESH_ID = pl.DeviceIdType.MESH
MIB = 2**20


def rel_perm(size, r):
    return [(i, i ^ r) for i in range(size)]


def from_rel(value, r):
    return lax.ppermute(value, "fsdp", rel_perm(lax.axis_size("fsdp"), r))


def swap_core(value):
    return lax.ppermute(value, "tp", [(0, 1), (1, 0)])


def shift_ctx(value, step):
    size = lax.axis_size("ctx")
    pairs = [(i, i + step) for i in range(size) if 0 <= i + step < size]
    return lax.ppermute(value, "ctx", pairs)


def sum_ctx(value):
    place = lax.axis_index("ctx")
    inner = (place == 1) | (place == 2)
    arrived = lax.ppermute(value, "ctx", [(0, 1), (3, 2)])
    pair = jnp.where(
        inner, value.astype(jnp.float32) + arrived.astype(jnp.float32), value.astype(jnp.float32)
    ).astype(jnp.bfloat16)
    across = lax.ppermute(pair, "ctx", [(1, 2), (2, 1)])
    total = (pair.astype(jnp.float32) + across.astype(jnp.float32)).astype(jnp.bfloat16)
    back = lax.ppermute(total, "ctx", [(1, 0), (2, 3)])
    return jnp.where(inner, total, back)


def expert_order(place):
    row = jnp.arange(128, dtype=jnp.int32)
    expert = (((row // 32) ^ place) * 2) + (row // 16) % 2
    source = (row % 16) * 8 + expert
    return (source[:, None] == row[None, :]).astype(jnp.bfloat16)


def split_kernel(order_ref, in_ref, out_ref):
    depth = in_ref.shape[0]
    for m in range(3):
        for k in range(depth // 16):
            block = in_ref[pl.ds(k * 16, 16), m].reshape(128, in_ref.shape[3])
            moved = jnp.dot(order_ref[...], block, preferred_element_type=jnp.float32)
            moved = moved.astype(jnp.bfloat16).reshape(8, 16, in_ref.shape[3])
            out_ref[:, m, pl.ds(k * 16, 16), :] = moved


def split_experts(weights, order):
    rows, _, experts, width = weights.shape
    step = 64
    return pl.pallas_call(
        split_kernel,
        grid=(rows // step,),
        in_specs=[
            pl.BlockSpec((128, 128), lambda i: (0, 0)),
            pl.BlockSpec((step, 3, experts, width), lambda i: (i, 0, 0, 0)),
        ],
        out_specs=pl.BlockSpec((experts, 3, step, width), lambda i: (0, 0, i, 0)),
        out_shape=jax.ShapeDtypeStruct((experts, 3, rows, width), jnp.bfloat16),
        compiler_params=pltpu.CompilerParams(vmem_limit_bytes=40 * MIB),
        name="split_experts",
    )(order, weights)


def join_kernel(order_ref, in_ref, out_ref):
    width = in_ref.shape[3]
    for m in range(3):
        for k in range(in_ref.shape[2] // 16):
            block = in_ref[:, m, pl.ds(k * 16, 16), :].reshape(128, width)
            moved = jnp.dot(order_ref[...], block, preferred_element_type=jnp.float32)
            out_ref[pl.ds(k * 16, 16), m] = moved.reshape(16, 8, width)


def join_experts(grads, order):
    experts, _, rows, width = grads.shape
    step = 64
    return pl.pallas_call(
        join_kernel,
        grid=(rows // step,),
        in_specs=[
            pl.BlockSpec((128, 128), lambda i: (0, 0)),
            pl.BlockSpec((experts, 3, step, width), lambda i: (0, 0, i, 0)),
        ],
        out_specs=pl.BlockSpec((step, 3, experts, width), lambda i: (i, 0, 0, 0)),
        out_shape=jax.ShapeDtypeStruct((rows, 3, experts, width), jnp.float32),
        compiler_params=pltpu.CompilerParams(vmem_limit_bytes=40 * MIB),
        name="join_experts",
    )(order, grads)


NT = (((1,), (1,)), ((), ()))
TN = (((0,), (0,)), ((), ()))


def dot_f32(a, b, dims=(((1,), (0,)), ((), ()))):
    return lax.dot_general(a, b, dims, preferred_element_type=jnp.float32)


def block_probs(last, keys, query):
    scores = dot_f32(keys, query, NT) * HEAD_DIM ** (-0.5)
    block = lax.broadcasted_iota(jnp.int32, scores.shape, 0) // query.shape[0]
    scores = jnp.where(block <= last, scores, -1e30)
    expd = jnp.exp(scores - jnp.max(scores, axis=0, keepdims=True))
    return expd * (1.0 / jnp.sum(expd, axis=0, keepdims=True))


def attend_kernel(place_ref, q_ref, k_ref, v_ref, out_ref):
    keys = k_ref[...]
    vals = v_ref[...]
    for g in range(QUERY_PER_GROUP):
        cols = pl.ds(g * HEAD_DIM, HEAD_DIM)
        probs = block_probs(place_ref[0], keys, q_ref[:, cols]).astype(jnp.bfloat16)
        out_ref[:, cols] = dot_f32(probs, vals, TN).astype(jnp.bfloat16)


def attend_back_kernel(place_ref, q_ref, k_ref, v_ref, dm_ref, dq_ref, dk_ref, dv_ref):
    keys = k_ref[...]
    vals = v_ref[...]
    scale = HEAD_DIM ** (-0.5)
    dk_ref[...] = jnp.zeros_like(dk_ref)
    dv_ref[...] = jnp.zeros_like(dv_ref)
    for g in range(QUERY_PER_GROUP):
        cols = pl.ds(g * HEAD_DIM, HEAD_DIM)
        query = q_ref[:, cols]
        d_mixed = dm_ref[:, cols]
        probs = block_probs(place_ref[0], keys, query)
        d_probs = dot_f32(vals, d_mixed, NT)
        inner = jnp.sum(probs * d_probs, axis=0, keepdims=True)
        d_scores = (probs * (d_probs - inner)).astype(jnp.bfloat16)
        dq_ref[:, cols] = dot_f32(d_scores, keys, TN) * scale
        dk_ref[...] += dot_f32(d_scores, query) * scale
        dv_ref[...] += dot_f32(probs.astype(jnp.bfloat16), d_mixed)


def attend(place, q, k, v):
    return pl.pallas_call(
        attend_kernel,
        in_specs=[pl.BlockSpec(memory_space=pltpu.SMEM)]
        + [pl.BlockSpec(memory_space=pltpu.VMEM)] * 3,
        out_specs=pl.BlockSpec(memory_space=pltpu.VMEM),
        out_shape=jax.ShapeDtypeStruct(q.shape, jnp.bfloat16),
        compiler_params=pltpu.CompilerParams(vmem_limit_bytes=40 * MIB),
        name="attend",
    )(place, q, k, v)


def attend_back(place, q, k, v, d_mixed):
    return pl.pallas_call(
        attend_back_kernel,
        in_specs=[pl.BlockSpec(memory_space=pltpu.SMEM)]
        + [pl.BlockSpec(memory_space=pltpu.VMEM)] * 4,
        out_specs=[pl.BlockSpec(memory_space=pltpu.VMEM)] * 3,
        out_shape=[
            jax.ShapeDtypeStruct(q.shape, jnp.float32),
            jax.ShapeDtypeStruct(k.shape, jnp.float32),
            jax.ShapeDtypeStruct(v.shape, jnp.float32),
        ],
        compiler_params=pltpu.CompilerParams(vmem_limit_bytes=40 * MIB),
        name="attend_back",
    )(place, q, k, v, d_mixed)


def gather_sum(parts, f, core):
    own, other = parts[core], parts[1 - core].astype(jnp.bfloat16)
    both = own + swap_core(other).astype(jnp.float32)
    total = both[f]
    for r in range(1, 4):
        total = total + from_rel(both[f ^ r].astype(jnp.bfloat16), r).astype(jnp.float32)
    return total


def join_halves(core, half):
    other = swap_core(half)
    first = jnp.where(core == 0, half, other)
    second = jnp.where(core == 0, other, half)
    return jnp.concatenate([first, second], axis=0)


def place():
    return lax.axis_index("fsdp"), lax.axis_index("ctx"), lax.axis_index("tp")


def plane_peers(f):
    return f + 1 - 2 * lax.rem(f, 2), lax.rem(f + 2, 4), 3 - f


def rows_of(index, size):
    return pl.ds(pl.multiple_of(index * size, size), size)


def greet(devices):
    barrier = pltpu.get_barrier_semaphore()
    for device in devices:
        pl.semaphore_signal(barrier, inc=1, device_id=device, device_id_type=MESH_ID)
    pl.semaphore_wait(barrier, len(devices))


def turn(value, cosine, sine):
    return value * cosine + pltpu.roll(value, HEAD_DIM // 2, 1) * sine


def front_kernel(
    tok_ref,
    gain_one_ref,
    gain_two_ref,
    freq_ref,
    routes_ref,
    gates_ref,
    order_ref,
    attn_hbm,
    pieces_hbm,
    cot_hbm,
    xn_ref,
    q_ref,
    kv_ref,
    mixed_ref,
    res_ref,
    wl_ref,
    wa_hbm,
    w_hbm,
    x_hbm,
    dy_hbm,
    wa,
    part,
    part_in,
    low_half,
    send,
    recv,
    local,
):
    f, z, c = place()
    fx, fy, fd = plane_peers(f)
    count, width = tok_ref.shape
    half = count // 2
    shard = attn_hbm.shape[0]
    cut = shard // 2
    in_cols = (QUERY_PER_GROUP + 2) * HEAD_DIM
    ins = pl.ds(0, in_cols)
    outs = pl.ds(in_cols, attn_hbm.shape[1] - in_cols)

    def at(fsdp=f, ctx=z, tp=c):
        return {"fsdp": fsdp, "ctx": ctx, "tp": tp}

    def remote(src, dst, k, device):
        return pltpu.make_async_remote_copy(
            src_ref=src,
            dst_ref=dst,
            send_sem=send.at[k],
            recv_sem=recv.at[k],
            device_id=device,
            device_id_type=MESH_ID,
        )

    plane = [at(fx), at(fy), at(fd)]
    rel = [fx, fy, fd]
    line = [at(ctx=lax.rem(z + s, 4)) for s in range(1, 4)]
    sibling = at(tp=1 - c)
    greet(plane + line + [sibling])

    mine = rows_of(f, shard)
    owned = pltpu.make_async_copy(attn_hbm, wa.at[mine], local.at[0])
    owned.start()
    in_x = remote(attn_hbm.at[:, ins], wa.at[mine, ins], 0, at(fx))
    in_y = remote(attn_hbm.at[:, ins], wa.at[mine, ins], 1, at(fy))
    in_x.start()
    in_y.start()

    rank = jnp.broadcast_to(order_ref[...].astype(jnp.float32), (count, count))
    ahead = jnp.where(rank.T < rank, 1.0, 0.0).astype(jnp.bfloat16)
    expert = lax.broadcasted_iota(jnp.int32, (128, count), 0)
    member = jnp.zeros((128, count), jnp.float32)
    gate = jnp.zeros((128, count), jnp.float32)
    for j in range(TOP):
        hit = jnp.broadcast_to(routes_ref[j : j + 1, :], (128, count)) == expert
        member = jnp.where(hit, 1.0, member)
        gate = jnp.where(hit, jnp.broadcast_to(gates_ref[j : j + 1, :], (128, count)), gate)
    slots = dot_f32(member.astype(jnp.bfloat16), ahead)
    gate = jnp.where(slots < CAP - 0.5, gate, 0.0)
    wl_ref[f] = gate[:EXPERTS]
    gate_copies = [remote(wl_ref.at[f], wl_ref.at[f], 2 + i, plane[i]) for i in range(3)]
    for copy in gate_copies:
        copy.start()

    own_w = pltpu.make_async_copy(pieces_hbm.at[0], w_hbm.at[:, :, mine, :], local.at[1])
    own_w.start()
    own_dy = [
        pltpu.make_async_copy(
            cot_hbm.at[pl.ds(i * half, half)], dy_hbm.at[i, f], local.at[2 + i]
        )
        for i in range(2)
    ]
    for copy in own_dy:
        copy.start()

    tok = tok_ref[...].astype(jnp.float32)
    inv = lax.rsqrt(jnp.mean(tok * tok, axis=-1, keepdims=True) + eps)
    xn_ref[...] = (tok * inv * gain_one_ref[...]).astype(jnp.bfloat16)
    position = z * count + lax.broadcasted_iota(jnp.int32, (count, HEAD_DIM), 0)
    angle = position.astype(jnp.float32) * freq_ref[...]
    cosine = jnp.cos(angle)
    lane = lax.broadcasted_iota(jnp.int32, (count, HEAD_DIM), 1)
    sine = jnp.where(lane < HEAD_DIM // 2, -jnp.sin(angle), jnp.sin(angle))

    top, low = rows_of(2 * fx, cut), rows_of(2 * fy + 1, cut)
    in_x.wait_recv()
    in_xy = remote(wa.at[top, ins], wa.at[top, ins], 5, at(fy))
    in_xy.start()
    in_y.wait_recv()
    in_yx = remote(wa.at[low, ins], wa.at[low, ins], 6, at(fx))
    in_yx.start()
    out_x = remote(attn_hbm.at[:, outs], wa.at[mine, outs], 7, at(fx))
    out_y = remote(attn_hbm.at[:, outs], wa.at[mine, outs], 8, at(fy))
    out_x.start()
    out_y.start()
    owned.wait()
    in_xy.wait_recv()
    in_yx.wait_recv()

    normed = xn_ref[...]
    for h in range(QUERY_PER_GROUP + 2):
        cols = pl.ds(h * HEAD_DIM, HEAD_DIM)
        if h % 2 == 0:
            pair = dot_f32(normed, wa[:, pl.ds(h * HEAD_DIM, 2 * HEAD_DIM)])
        value = pair[:, (h % 2) * HEAD_DIM : (h % 2 + 1) * HEAD_DIM]
        if h <= QUERY_PER_GROUP:
            value = turn(value, cosine, sine)
        if h < QUERY_PER_GROUP:
            q_ref[:, cols] = value.astype(jnp.bfloat16)
        else:
            kv_ref[0, :, pl.ds((h - QUERY_PER_GROUP) * HEAD_DIM, HEAD_DIM)] = value.astype(
                jnp.bfloat16
            )
    kv_copies = [remote(kv_ref.at[0], kv_ref.at[s], 8 + s, line[s - 1]) for s in range(1, 4)]
    for s in range(1, 4):

        @pl.when(z + s < 4)
        def _(s=s):
            kv_copies[s - 1].start()

        @pl.when(z < s)
        def _(s=s):
            kv_ref[s] = jnp.zeros(kv_ref.shape[1:], jnp.bfloat16)

    out_x.wait_recv()
    out_xy = remote(wa.at[top, outs], wa.at[top, outs], 12, at(fy))
    out_xy.start()
    out_y.wait_recv()
    out_yx = remote(wa.at[low, outs], wa.at[low, outs], 13, at(fx))
    out_yx.start()

    w_copies = []
    for m in range(3):
        for i in range(3):
            w_copies.append(
                remote(
                    pieces_hbm.at[i + 1, :, m], w_hbm.at[:, m, mine, :], 14 + 3 * m + i, plane[i]
                )
            )
    for copy in w_copies:
        copy.start()
    dy_copies = [
        remote(cot_hbm.at[rows_of(c, half)], dy_hbm.at[c, f], 23 + i, plane[i]) for i in range(3)
    ]
    for copy in dy_copies:
        copy.start()

    for s in range(1, 4):

        @pl.when(z >= s)
        def _(s=s):
            kv_copies[s - 1].wait_recv()

    keys = kv_ref[:, :, pl.ds(0, HEAD_DIM)].reshape(4 * count, HEAD_DIM)
    vals = kv_ref[:, :, pl.ds(HEAD_DIM, HEAD_DIM)].reshape(4 * count, HEAD_DIM)
    for g in range(QUERY_PER_GROUP):
        cols = pl.ds(g * HEAD_DIM, HEAD_DIM)
        probs = block_probs(z, keys, q_ref[:, cols]).astype(jnp.bfloat16)
        mixed_ref[:, cols] = dot_f32(probs, vals, TN).astype(jnp.bfloat16)

    out_xy.wait_recv()
    out_yx.wait_recv()
    store_wa = pltpu.make_async_copy(wa, wa_hbm, local.at[4])
    store_wa.start()
    for s in range(width // 256):
        cols = pl.ds(s * 256, 256)
        part[:, cols] = dot_f32(mixed_ref[...], wa[cols, outs], NT)
    swap = remote(part.at[rows_of(1 - c, half)], part_in, 26, sibling)
    swap.start()
    swap.wait_recv()
    my_rows = rows_of(c, half)
    residual = tok_ref[my_rows, :].astype(jnp.float32) + (part[my_rows, :] + part_in[...])
    res_ref[...] = residual
    inv = lax.rsqrt(jnp.mean(residual * residual, axis=-1, keepdims=True) + eps)
    low_half[...] = (residual * inv * gain_two_ref[...]).astype(jnp.bfloat16)
    own_x = pltpu.make_async_copy(low_half, x_hbm.at[c, f], local.at[5])
    own_x.start()
    x_copies = [remote(low_half, x_hbm.at[c, f], 27 + i, plane[i]) for i in range(3)]
    for copy in x_copies:
        copy.start()
    sib_x = [remote(low_half, x_hbm.at[c, f], 30, sibling)]
    sib_x[0].start()

    sib_dy = []
    for i in range(3):
        dy_copies[i].wait_recv()
        sib_dy.append(remote(dy_hbm.at[c, rel[i]], dy_hbm.at[c, rel[i]], 31 + i, sibling))
        sib_dy[i].start()
    for i in range(3):
        x_copies[i].wait_recv()
        sib_x.append(remote(x_hbm.at[c, rel[i]], x_hbm.at[c, rel[i]], 34 + i, sibling))
        sib_x[i + 1].start()

    for copy in w_copies + gate_copies + sib_dy + sib_x:
        copy.wait_recv()
    for s in range(1, 4):

        @pl.when(z + s < 4)
        def _(s=s):
            kv_copies[s - 1].wait_send()

    for copy in [in_x, in_y, in_xy, in_yx, out_x, out_y, out_xy, out_yx, swap]:
        copy.wait_send()
    for copy in w_copies + gate_copies + dy_copies + x_copies + sib_dy + sib_x:
        copy.wait_send()
    for copy in [own_w, own_x, store_wa] + own_dy:
        copy.wait()


def front(tok, gain_one, gain_two, routes, gates, order, attn_own, pieces, cot):
    count, width = tok.shape
    half = count // 2
    shard, columns = attn_own.shape
    experts, hidden = pieces.shape[1], pieces.shape[4]
    i = np.arange(HEAD_DIM // 2, dtype=np.float32)
    freq = (theta_base ** (-(i * 2.0) / HEAD_DIM)).astype(np.float32)
    freq = jnp.asarray(np.concatenate([freq, freq])[None, :])
    vmem, hbm = pl.BlockSpec(memory_space=pltpu.VMEM), pl.BlockSpec(memory_space=pl.ANY)
    bf16, f32 = jnp.bfloat16, jnp.float32
    shape = jax.ShapeDtypeStruct
    return pl.pallas_call(
        front_kernel,
        in_specs=[vmem] * 7 + [hbm] * 3,
        out_specs=[vmem] * 6 + [hbm] * 4,
        out_shape=[
            shape((count, width), bf16),
            shape((count, QUERY_PER_GROUP * HEAD_DIM), bf16),
            shape((4, count, 2 * HEAD_DIM), bf16),
            shape((count, QUERY_PER_GROUP * HEAD_DIM), bf16),
            shape((half, width), f32),
            shape((4, EXPERTS, count), f32),
            shape((4 * shard, columns), bf16),
            shape((experts, 3, 4 * shard, hidden), bf16),
            shape((2, 4, half, width), bf16),
            shape((2, 4, half, width), bf16),
        ],
        scratch_shapes=[
            pltpu.VMEM((4 * shard, columns), bf16),
            pltpu.VMEM((count, width), f32),
            pltpu.VMEM((half, width), f32),
            pltpu.VMEM((half, width), bf16),
            pltpu.SemaphoreType.DMA((37,)),
            pltpu.SemaphoreType.DMA((37,)),
            pltpu.SemaphoreType.DMA((6,)),
        ],
        compiler_params=pltpu.CompilerParams(
            collective_id=0, has_side_effects=True, vmem_limit_bytes=48 * MIB
        ),
        name="front",
    )(tok, gain_one, gain_two, freq, routes, gates, order, attn_own, pieces, cot)


def body_fast(
    tokens,
    attn_norm,
    attention_params,
    ffn_norm,
    expert_weights,
    gate_values,
    routes,
    slot_order,
    cotangent,
):
    sequence_count, block_len, model_width = tokens.shape
    count = sequence_count * block_len
    half = count // 2
    own_experts = EXPERTS // 4
    input_columns = (QUERY_PER_GROUP + 2) * HEAD_DIM
    query_columns = QUERY_PER_GROUP * HEAD_DIM
    f = lax.axis_index("fsdp")
    z = lax.axis_index("ctx")
    core = lax.axis_index("tp")
    shard = attention_params.shape[0]
    f32, bf16 = jnp.float32, jnp.bfloat16

    def my_half(value):
        return lax.dynamic_slice_in_dim(value, core * half, half, 0)

    place_order = jnp.arange(4, dtype=jnp.int32) ^ f
    order = expert_order(f)
    pieces = split_experts(jnp.transpose(expert_weights, (0, 2, 1, 3)), order)
    pieces = jnp.transpose(
        pieces.reshape(4, own_experts, 3, shard, expert_weights.shape[3]), (0, 1, 2, 3, 4)
    )
    tok_low = tokens.reshape(count, model_width)
    grad_out = cotangent.reshape(count, model_width)
    first_normed, queries, kv_all, mixed, residual, gate_table, whole_attn, whole_expert, x, dy = front(
        tok_low,
        attn_norm[None, :],
        ffn_norm[None, :],
        routes.reshape(count, TOP).T,
        gate_values.reshape(count, TOP).T,
        slot_order.reshape(1, count),
        attention_params[:, 0, :],
        pieces,
        grad_out,
    )
    inputs = x.reshape(8 * half, model_width)
    upstream = dy.reshape(8 * half, model_width)
    attn_in, attn_out = whole_attn[:, :input_columns], whole_attn[:, input_columns:]
    weights_in = lax.dynamic_slice_in_dim(gate_table, f * own_experts, own_experts, 1)
    weights_in = jnp.transpose(weights_in.reshape(4, own_experts, 2, half), (1, 2, 0, 3))
    weights_in = weights_in.reshape(own_experts, 8 * half)
    kept = gate_table[f].T != 0.0
    route_rows = routes.reshape(count, TOP)
    kv_all = kv_all.reshape(4 * count, 2 * HEAD_DIM)
    key_all, value_all = kv_all[:, :HEAD_DIM], kv_all[:, HEAD_DIM:]
    tok_float = tok_low.astype(f32)
    inv_one = lax.rsqrt(jnp.mean(tok_float * tok_float, axis=-1, keepdims=True) + eps)
    inv_two = lax.rsqrt(jnp.mean(residual * residual, axis=-1, keepdims=True) + eps)
    positions = z * block_len + jnp.arange(block_len, dtype=jnp.int32)
    cosine, sine = angle_tables(positions)
    cos_three, sin_three = cosine[:, None, :], sine[:, None, :]
    place = jnp.reshape(z, (1,)).astype(jnp.int32)

    moe_parts = 0.0
    d_normed_parts = 0.0
    gate_parts = []
    expert_grads = []
    for e in range(own_experts):
        gate_act = dot_f32(inputs, whole_expert[e, 0])
        up_act = dot_f32(inputs, whole_expert[e, 1])
        d_plain = dot_f32(upstream, whole_expert[e, 2])
        gate_sigmoid = jax.nn.sigmoid(gate_act)
        active = gate_act * gate_sigmoid
        hidden = active * up_act
        scale = weights_in[e][:, None]
        hidden_low = (hidden * scale).astype(bf16)
        gate_parts.append(jnp.sum(hidden * d_plain, axis=1))
        d_hidden = d_plain * scale
        silu_slope = gate_sigmoid * (1.0 + gate_act * (1.0 - gate_sigmoid))
        d_gate = (d_hidden * up_act * silu_slope).astype(bf16)
        d_up = (d_hidden * active).astype(bf16)
        moe_parts = moe_parts + dot_f32(hidden_low, whole_expert[e, 2], NT)
        d_normed_parts = (
            d_normed_parts
            + dot_f32(d_gate, whole_expert[e, 0], NT)
            + dot_f32(d_up, whole_expert[e, 1], NT)
        )
        expert_grads.append(
            jnp.stack(
                [
                    dot_f32(inputs, d_gate, TN).astype(bf16),
                    dot_f32(inputs, d_up, TN).astype(bf16),
                    dot_f32(upstream, hidden_low, TN).astype(bf16),
                ]
            )
        )
    d_normed_two = gather_sum(d_normed_parts.reshape(2, 4, half, model_width), f, core)
    moe = gather_sum(moe_parts.reshape(2, 4, half, model_width), f, core)
    layer_out = join_halves(core, (residual + moe).astype(bf16))

    gate_rows = jnp.stack(gate_parts).reshape(own_experts, 2, 4, half)
    gate_rows = jnp.take(gate_rows, core, 1) + swap_core(jnp.take(gate_rows, 1 - core, 1))
    gate_rows = jnp.stack(
        [gate_rows[:, f]] + [from_rel(gate_rows[:, f ^ r], r) for r in range(1, 4)]
    )
    gate_rows = join_halves(core, gate_rows.reshape(EXPERTS, half).T)
    rel_ids = (place_order[:, None] * own_experts + jnp.arange(own_experts)).reshape(EXPERTS)
    kept_rel = kept[:, rel_ids]
    picked = (route_rows[:, :, None] == rel_ids) & kept_rel[:, None, :]
    gate_grad = jnp.sum(jnp.where(picked, gate_rows[:, None, :], 0.0), axis=-1)

    d_resid_norm, gain_two = norm_back(residual, inv_two, ffn_norm, d_normed_two)
    d_residual = my_half(grad_out).astype(f32) + d_resid_norm
    d_attn = join_halves(core, d_residual.astype(bf16))
    d_mixed = dot_f32(d_attn, attn_out).astype(bf16)
    d_queries, d_key_all, d_value_all = attend_back(place, queries, key_all, value_all, d_mixed)
    d_kv = jnp.concatenate([d_key_all, d_value_all], axis=1).reshape(4, count, 2 * HEAD_DIM)
    d_key_value = d_kv[0]
    for s in range(1, 4):
        d_key_value = d_key_value + shift_ctx(d_kv[s].astype(bf16), -s).astype(f32)
    d_turned = jnp.concatenate([d_queries, d_key_value[:, :HEAD_DIM]], axis=1)
    d_turned = rotate(
        d_turned.reshape(count, QUERY_PER_GROUP + 1, HEAD_DIM), cos_three, -sin_three
    ).reshape(count, query_columns + HEAD_DIM)
    d_projected = jnp.concatenate([d_turned, d_key_value[:, HEAD_DIM:]], axis=1).astype(bf16)
    d_normed_local = dot_f32(d_projected, attn_in, NT)
    other_rows = lax.dynamic_slice_in_dim(d_normed_local, (1 - core) * half, half, 0)
    d_normed_one = my_half(d_normed_local) + swap_core(other_rows.astype(bf16)).astype(f32)
    d_tok_norm, gain_one = norm_back(my_half(tok_float), my_half(inv_one), attn_norm, d_normed_one)
    tokens_grad = join_halves(core, (d_residual + d_tok_norm).astype(bf16))
    gains = jnp.stack([gain_one, gain_two])
    gains = gains + swap_core(gains)
    for axis, r in (("fsdp", 1), ("fsdp", 2), ("ctx", 1), ("ctx", 2)):
        gains = gains + lax.ppermute(gains, axis, rel_perm(4, r))

    attn_grad = jnp.concatenate(
        [dot_f32(first_normed, d_projected, TN), dot_f32(d_attn, mixed, TN)], axis=1
    ).reshape(4, shard, -1)[place_order]
    attn_sum = attn_grad[0]
    for r in range(1, 4):
        attn_sum = attn_sum + from_rel(attn_grad[r].astype(bf16), r).astype(f32)
    attn_total = sum_ctx(attn_sum.astype(bf16)).astype(f32)[:, None, :]

    finals = []
    for e in range(own_experts):
        total = sum_ctx(expert_grads[e]).reshape(3, 4, shard, -1)
        total = jnp.take(total, place_order, axis=1)
        finals.append(
            jnp.stack([total[:, 0]] + [from_rel(total[:, r], r) for r in range(1, 4)])
        )
    finals = jnp.stack(finals, axis=1).reshape(EXPERTS, 3, shard, -1)
    expert_grad = jnp.transpose(join_experts(finals, order.T), (0, 2, 1, 3))
    return (
        layer_out.reshape(sequence_count, block_len, model_width),
        tokens_grad.reshape(sequence_count, block_len, model_width),
        attn_total,
        expert_grad,
        gains[0],
        gains[1],
        gate_grad.reshape(sequence_count, block_len, TOP),
    )


def solution(mesh):
    in_specs = (
        P("fsdp", "ctx", None),
        P(),
        P("fsdp", "tp", None),
        P(),
        P("fsdp", None, None, "tp"),
        P("fsdp", "ctx", None),
        P("fsdp", "ctx", None),
        P("fsdp", "ctx"),
        P("fsdp", "ctx", None),
    )
    out_specs = (
        P("fsdp", "ctx", None),
        P("fsdp", "ctx", None),
        P("fsdp", "tp", None),
        P("fsdp", None, None, "tp"),
        P(),
        P(),
        P("fsdp", "ctx", None),
    )
    four = mesh.shape["fsdp"] == 4 and mesh.shape["ctx"] == 4 and mesh.shape["tp"] == 2
    body_fn = body_fast if four else body
    return jax.shard_map(body_fn, mesh=mesh, in_specs=in_specs, out_specs=out_specs, check_vma=False)
```

```python
import jax
import jax.numpy as jnp
from jax import lax
import numpy as np
from jax.experimental import pallas as pl
from jax.experimental.pallas import tpu as pltpu
from jax.sharding import PartitionSpec as P

HEAD_DIM = 128
TOP = 4
EXPERTS = 8
QUERY_PER_GROUP = 6
CAP = 160


eps = 1e-06
theta_base = 1000000.0


def angle_tables(positions):
    frequency = theta_base ** (-(jnp.arange(HEAD_DIM // 2, dtype=jnp.float32) * 2.0) / HEAD_DIM)
    angles = positions.astype(jnp.float32)[:, None] * frequency[None, :]
    return (jnp.cos(angles), jnp.sin(angles))


def rotate(source, cosine_table, sine_table):
    half_size = source.shape[-1] // 2
    front_half = source[..., :half_size]
    back_half = source[..., half_size:]
    return jnp.concatenate(
        [
            front_half * cosine_table - back_half * sine_table,
            back_half * cosine_table + front_half * sine_table,
        ],
        axis=-1,
    )


def norm_back(source, inv_rms, gain_vec, upstream):
    scaled = upstream * gain_vec
    inner_sum = jnp.mean(scaled * source, axis=-1, keepdims=True)
    d_source = inv_rms * scaled - source * inv_rms * inv_rms * inv_rms * inner_sum
    return (d_source, jnp.sum(upstream * source * inv_rms, axis=0))


def slot_tables(route_rows, rank_rows):
    tok_count = route_rows.shape[0]
    inverse = (
        jnp.zeros((tok_count,), jnp.int32).at[rank_rows].set(jnp.arange(tok_count, dtype=jnp.int32))
    )
    ranked = route_rows[inverse].reshape(-1)
    onehot = (ranked[:, None] == jnp.arange(EXPERTS, dtype=jnp.int32)[None, :]).astype(jnp.int32)
    before = jnp.cumsum(onehot, axis=0) - onehot
    slot_ranked = jnp.sum(before * onehot, axis=1).reshape(tok_count, TOP)
    slots = slot_ranked[rank_rows]
    kept_pair = slots < CAP
    pair_slot = jnp.where(kept_pair, route_rows * CAP + slots, EXPERTS * CAP)
    owners = jnp.broadcast_to(jnp.arange(tok_count, dtype=jnp.int32)[:, None], (tok_count, TOP))
    slot_token = (
        jnp.full((EXPERTS * CAP,), tok_count, jnp.int32)
        .at[pair_slot.reshape(-1)]
        .set(owners.reshape(-1), mode="drop")
    )
    return (kept_pair, pair_slot, slot_token)


def attend_forward(queries, key_rows, value_rows, allowed):
    scores = jnp.einsum(
        "qhgd,khd->hgqk", queries, key_rows, preferred_element_type=jnp.float32
    ) * HEAD_DIM ** (-0.5)
    scores = jnp.where(allowed, scores, -1e30)
    row_max = jnp.max(scores, axis=-1, keepdims=True)
    expd = jnp.exp(scores - row_max)
    row_total = jnp.sum(expd, axis=-1, keepdims=True)
    attn_probs = (expd / row_total).astype(jnp.bfloat16)
    mixed_heads = jnp.einsum(
        "hgqk,khd->qhgd", attn_probs, value_rows, preferred_element_type=jnp.float32
    )
    return (mixed_heads.astype(jnp.bfloat16), row_max + jnp.log(row_total))


def attend_backward(queries, key_rows, value_rows, allowed, log_total, d_mixed):
    scores = jnp.einsum(
        "qhgd,khd->hgqk", queries, key_rows, preferred_element_type=jnp.float32
    ) * HEAD_DIM ** (-0.5)
    scores = jnp.where(allowed, scores, -1e30)
    attn_probs = jnp.exp(scores - log_total)
    low_probs = attn_probs.astype(jnp.bfloat16)
    d_probs = jnp.einsum("qhgd,khd->hgqk", d_mixed, value_rows, preferred_element_type=jnp.float32)
    inner_sum = jnp.sum(attn_probs * d_probs, axis=-1, keepdims=True)
    d_scores = (attn_probs * (d_probs - inner_sum)).astype(jnp.bfloat16)
    d_queries = jnp.einsum(
        "hgqk,khd->qhgd", d_scores, key_rows, preferred_element_type=jnp.float32
    ) * HEAD_DIM ** (-0.5)
    d_keys = jnp.einsum(
        "hgqk,qhgd->khd", d_scores, queries, preferred_element_type=jnp.float32
    ) * HEAD_DIM ** (-0.5)
    d_values = jnp.einsum("hgqk,qhgd->khd", low_probs, d_mixed, preferred_element_type=jnp.float32)
    return (d_queries, d_keys, d_values)


def body(
    tokens,
    attn_norm,
    attention_params,
    ffn_norm,
    expert_weights,
    gate_values,
    routes,
    slot_order,
    cotangent,
):
    sequence_count, block_len, model_width = tokens.shape
    tok_count = sequence_count * block_len
    kv_loc = attention_params.shape[1]
    input_columns = (QUERY_PER_GROUP + 2) * HEAD_DIM
    ctx_size = lax.axis_size("ctx")
    ctx_place = lax.axis_index("ctx")
    sequence_length = block_len * ctx_size
    whole_attn, whole_expert = (
        lax.all_gather(attention_params, "fsdp", axis=0, tiled=True),
        lax.all_gather(expert_weights, "fsdp", axis=0, tiled=True),
    )
    positions = ctx_place * block_len + jnp.arange(block_len, dtype=jnp.int32)
    cosine_table, sine_table = angle_tables(positions)
    cosine_table = jnp.tile(cosine_table, (sequence_count, 1))
    sine_table = jnp.tile(sine_table, (sequence_count, 1))
    cos_four = cosine_table[:, None, None, :]
    sin_four = sine_table[:, None, None, :]
    cos_three = cosine_table[:, None, :]
    sin_three = sine_table[:, None, :]
    allowed = (jnp.arange(sequence_length, dtype=jnp.int32) // block_len <= ctx_place)[
        None, None, None, :
    ]
    tok_float = tokens.reshape(tok_count, model_width).astype(jnp.float32)
    inv_one = lax.rsqrt(jnp.mean(tok_float * tok_float, axis=-1, keepdims=True) + eps)
    first_normed = (tok_float * inv_one * attn_norm).astype(jnp.bfloat16)
    projected_rows = jnp.einsum(
        "td,dhc->thc",
        first_normed,
        whole_attn[:, :, :input_columns],
        preferred_element_type=jnp.float32,
    ).reshape(tok_count, kv_loc, QUERY_PER_GROUP + 2, HEAD_DIM)
    queries = rotate(projected_rows[:, :, :QUERY_PER_GROUP], cos_four, sin_four).astype(
        jnp.bfloat16
    )
    key_rows = rotate(projected_rows[:, :, QUERY_PER_GROUP], cos_three, sin_three).astype(
        jnp.bfloat16
    )
    value_rows = projected_rows[:, :, QUERY_PER_GROUP + 1].astype(jnp.bfloat16)
    key_all, value_all = (
        lax.all_gather(
            key_rows.reshape(sequence_count, block_len, kv_loc, HEAD_DIM), "ctx", axis=1, tiled=True
        ),
        lax.all_gather(
            value_rows.reshape(sequence_count, block_len, kv_loc, HEAD_DIM),
            "ctx",
            axis=1,
            tiled=True,
        ),
    )
    query_seq = queries.reshape(sequence_count, block_len, kv_loc, QUERY_PER_GROUP, HEAD_DIM)
    mixed_heads, log_total = lax.map(
        lambda item_args: attend_forward(item_args[0], item_args[1], item_args[2], allowed),
        (query_seq, key_all, value_all),
    )
    mixed_flat = mixed_heads.reshape(tok_count, kv_loc, QUERY_PER_GROUP * HEAD_DIM)
    attn_part = jnp.einsum(
        "thc,dhc->td",
        mixed_flat,
        whole_attn[:, :, input_columns:],
        preferred_element_type=jnp.float32,
    )
    attn_sum = lax.psum(attn_part, "tp")
    residual = tok_float + attn_sum
    inv_two = lax.rsqrt(jnp.mean(residual * residual, axis=-1, keepdims=True) + eps)
    normed_two = (residual * inv_two * ffn_norm).astype(jnp.bfloat16)
    kept_pair, pair_slot, slot_token = slot_tables(
        routes.reshape(tok_count, TOP), slot_order.reshape(tok_count)
    )
    kept_float = kept_pair.astype(jnp.float32)
    gate_kept = gate_values.reshape(tok_count, TOP) * kept_float
    slot_gate = (
        jnp.zeros((EXPERTS * CAP,), jnp.float32)
        .at[pair_slot.reshape(-1)]
        .set(gate_kept.reshape(-1), mode="drop")
    )
    padded = jnp.concatenate([normed_two, jnp.zeros((1, model_width), jnp.bfloat16)], axis=0)
    inputs = padded[slot_token].reshape(EXPERTS, CAP, model_width)
    gate_act = jnp.einsum(
        "ecd,deh->ech", inputs, whole_expert[:, :, 0], preferred_element_type=jnp.float32
    )
    up_act = jnp.einsum(
        "ecd,deh->ech", inputs, whole_expert[:, :, 1], preferred_element_type=jnp.float32
    )
    gate_sigmoid = jax.nn.sigmoid(gate_act)
    active = gate_act * gate_sigmoid
    hidden = (active * up_act).astype(jnp.bfloat16)
    expert_out = jnp.einsum(
        "ech,deh->ecd", hidden, whole_expert[:, :, 2], preferred_element_type=jnp.float32
    )
    out_pad = jnp.concatenate(
        [expert_out.reshape(EXPERTS * CAP, model_width), jnp.zeros((1, model_width), jnp.float32)],
        axis=0,
    )
    picked = out_pad[pair_slot]
    moe_part = jnp.sum(picked * gate_kept[:, :, None], axis=1)
    moe = lax.psum(moe_part.astype(jnp.bfloat16), "tp").astype(jnp.float32)
    layer_out = (
        (residual + moe).astype(jnp.bfloat16).reshape(sequence_count, block_len, model_width)
    )
    grad_out = cotangent.reshape(tok_count, model_width).astype(jnp.float32)
    gate_part = jnp.sum(picked * grad_out[:, None, :], axis=-1) * kept_float
    grad_pad = jnp.concatenate([grad_out, jnp.zeros((1, model_width), jnp.float32)], axis=0)
    d_expert = (
        (grad_pad[slot_token] * slot_gate[:, None])
        .astype(jnp.bfloat16)
        .reshape(EXPERTS, CAP, model_width)
    )
    d_hidden = jnp.einsum(
        "ecd,deh->ech", d_expert, whole_expert[:, :, 2], preferred_element_type=jnp.float32
    )
    silu_slope = gate_sigmoid * (1.0 + gate_act * (1.0 - gate_sigmoid))
    d_gate_act = (d_hidden * up_act * silu_slope).astype(jnp.bfloat16)
    d_up_act = (d_hidden * active).astype(jnp.bfloat16)
    d_inputs = jnp.einsum(
        "ech,deh->ecd", d_gate_act, whole_expert[:, :, 0], preferred_element_type=jnp.float32
    )
    d_inputs = d_inputs + jnp.einsum(
        "ech,deh->ecd", d_up_act, whole_expert[:, :, 1], preferred_element_type=jnp.float32
    )
    d_in_pad = jnp.concatenate(
        [d_inputs.reshape(EXPERTS * CAP, model_width), jnp.zeros((1, model_width), jnp.float32)],
        axis=0,
    )
    d_normed_part = jnp.sum(d_in_pad[pair_slot], axis=1)
    d_normed_two, gate_grad = lax.psum((d_normed_part, gate_part), "tp")
    d_resid_norm, gain_two = norm_back(residual, inv_two, ffn_norm, d_normed_two)
    d_residual = grad_out + d_resid_norm
    d_attn = d_residual.astype(jnp.bfloat16)
    d_mixed = jnp.einsum(
        "td,dhc->thc", d_attn, whole_attn[:, :, input_columns:], preferred_element_type=jnp.float32
    ).astype(jnp.bfloat16)
    d_mixed_seq = d_mixed.reshape(sequence_count, block_len, kv_loc, QUERY_PER_GROUP, HEAD_DIM)
    d_queries, d_key_all, d_value_all = lax.map(
        lambda item_args: attend_backward(
            item_args[0], item_args[1], item_args[2], allowed, item_args[3], item_args[4]
        ),
        (query_seq, key_all, value_all, log_total, d_mixed_seq),
    )
    d_keys, d_values = (
        lax.psum_scatter(
            d_key_all.astype(jnp.bfloat16), "ctx", scatter_dimension=1, tiled=True
        ).astype(jnp.float32),
        lax.psum_scatter(
            d_value_all.astype(jnp.bfloat16), "ctx", scatter_dimension=1, tiled=True
        ).astype(jnp.float32),
    )
    d_queries = rotate(
        d_queries.reshape(tok_count, kv_loc, QUERY_PER_GROUP, HEAD_DIM), cos_four, -sin_four
    )
    d_keys = rotate(d_keys.reshape(tok_count, kv_loc, HEAD_DIM), cos_three, -sin_three)
    d_values = d_values.reshape(tok_count, kv_loc, HEAD_DIM)
    d_projected = jnp.concatenate([d_queries, d_keys[:, :, None], d_values[:, :, None]], axis=2)
    d_projected = d_projected.astype(jnp.bfloat16).reshape(tok_count, kv_loc, input_columns)
    d_normed_local = jnp.einsum(
        "thc,dhc->td",
        d_projected,
        whole_attn[:, :, :input_columns],
        preferred_element_type=jnp.float32,
    )
    d_normed_one = lax.psum(d_normed_local.astype(jnp.bfloat16), "tp").astype(jnp.float32)
    d_tok_norm, gain_one = norm_back(tok_float, inv_one, attn_norm, d_normed_one)
    tokens_grad = (
        (d_residual + d_tok_norm)
        .astype(jnp.bfloat16)
        .reshape(sequence_count, block_len, model_width)
    )
    gain_one, gain_two = lax.psum((gain_one, gain_two), ("fsdp", "ctx"))
    in_term = jnp.einsum(
        "td,thc->dhc", first_normed, d_projected, preferred_element_type=jnp.float32
    )
    out_term = jnp.einsum("td,thc->dhc", d_attn, mixed_flat, preferred_element_type=jnp.float32)
    attn_grad = lax.psum_scatter(
        jnp.concatenate([in_term, out_term], axis=2),
        ("fsdp", "ctx"),
        scatter_dimension=0,
        tiled=True,
    )
    gate_term = jnp.einsum("ecd,ech->deh", inputs, d_gate_act, preferred_element_type=jnp.float32)
    up_term = jnp.einsum("ecd,ech->deh", inputs, d_up_act, preferred_element_type=jnp.float32)
    down_term = jnp.einsum("ecd,ech->deh", d_expert, hidden, preferred_element_type=jnp.float32)
    expert_grad = lax.psum_scatter(
        jnp.stack([gate_term, up_term, down_term], axis=2),
        ("fsdp", "ctx"),
        scatter_dimension=0,
        tiled=True,
    )
    attn_grad, expert_grad = (
        lax.all_gather(attn_grad.astype(jnp.bfloat16), "ctx", axis=0, tiled=True).astype(
            attn_grad.dtype
        ),
        lax.all_gather(expert_grad.astype(jnp.bfloat16), "ctx", axis=0, tiled=True).astype(
            expert_grad.dtype
        ),
    )
    return (
        layer_out,
        tokens_grad,
        attn_grad,
        expert_grad,
        gain_one,
        gain_two,
        gate_grad.reshape(sequence_count, block_len, TOP),
    )


MESH_ID = pl.DeviceIdType.MESH
MIB = 2**20


def expert_order(place):
    row = jnp.arange(128, dtype=jnp.int32)
    expert = (((row // 32) ^ place) * 2) + (row // 16) % 2
    source = (row % 16) * 8 + expert
    return (source[:, None] == row[None, :]).astype(jnp.bfloat16)


def split_kernel(order_ref, in_ref, out_ref):
    depth = in_ref.shape[0]
    for m in range(3):
        for k in range(depth // 16):
            block = in_ref[pl.ds(k * 16, 16), m].reshape(128, in_ref.shape[3])
            moved = jnp.dot(order_ref[...], block, preferred_element_type=jnp.float32)
            moved = moved.astype(jnp.bfloat16).reshape(8, 16, in_ref.shape[3])
            out_ref[:, m, pl.ds(k * 16, 16), :] = moved


def split_experts(weights, order):
    rows, _, experts, width = weights.shape
    step = 64
    return pl.pallas_call(
        split_kernel,
        grid=(rows // step,),
        in_specs=[
            pl.BlockSpec((128, 128), lambda i: (0, 0)),
            pl.BlockSpec((step, 3, experts, width), lambda i: (i, 0, 0, 0)),
        ],
        out_specs=pl.BlockSpec((experts, 3, step, width), lambda i: (0, 0, i, 0)),
        out_shape=jax.ShapeDtypeStruct((experts, 3, rows, width), jnp.bfloat16),
        compiler_params=pltpu.CompilerParams(vmem_limit_bytes=40 * MIB),
        name="split_experts",
    )(order, weights)


def join_kernel(order_ref, in_ref, out_ref):
    width = in_ref.shape[3]
    for m in range(3):
        for k in range(in_ref.shape[2] // 16):
            block = in_ref[:, m, pl.ds(k * 16, 16), :].reshape(128, width)
            moved = jnp.dot(order_ref[...], block, preferred_element_type=jnp.float32)
            out_ref[pl.ds(k * 16, 16), m] = moved.reshape(16, 8, width)


def join_experts(grads, order):
    experts, _, rows, width = grads.shape
    step = 64
    return pl.pallas_call(
        join_kernel,
        grid=(rows // step,),
        in_specs=[
            pl.BlockSpec((128, 128), lambda i: (0, 0)),
            pl.BlockSpec((experts, 3, step, width), lambda i: (0, 0, i, 0)),
        ],
        out_specs=pl.BlockSpec((step, 3, experts, width), lambda i: (i, 0, 0, 0)),
        out_shape=jax.ShapeDtypeStruct((rows, 3, experts, width), jnp.float32),
        compiler_params=pltpu.CompilerParams(vmem_limit_bytes=40 * MIB),
        name="join_experts",
    )(order, grads)


NT = (((1,), (1,)), ((), ()))
TN = (((0,), (0,)), ((), ()))


def dot_f32(a, b, dims=(((1,), (0,)), ((), ()))):
    return lax.dot_general(a, b, dims, preferred_element_type=jnp.float32)


def block_probs(last, keys, query):
    scores = dot_f32(keys, query, NT) * HEAD_DIM ** (-0.5)
    block = lax.broadcasted_iota(jnp.int32, scores.shape, 0) // query.shape[0]
    scores = jnp.where(block <= last, scores, -1e30)
    expd = jnp.exp(scores - jnp.max(scores, axis=0, keepdims=True))
    return expd * (1.0 / jnp.sum(expd, axis=0, keepdims=True))


def place():
    return lax.axis_index("fsdp"), lax.axis_index("ctx"), lax.axis_index("tp")


def plane_peers(f):
    return f + 1 - 2 * lax.rem(f, 2), lax.rem(f + 2, 4), 3 - f


def rows_of(index, size):
    return pl.ds(pl.multiple_of(index * size, size), size)


def greet(devices):
    barrier = pltpu.get_barrier_semaphore()
    for device in devices:
        pl.semaphore_signal(barrier, inc=1, device_id=device, device_id_type=MESH_ID)
    pl.semaphore_wait(barrier, len(devices))


def turn(value, cosine, sine):
    return value * cosine + pltpu.roll(value, HEAD_DIM // 2, 1) * sine


def frequencies():
    i = np.arange(HEAD_DIM // 2, dtype=np.float32)
    freq = (theta_base ** (-(i * 2.0) / HEAD_DIM)).astype(np.float32)
    return jnp.asarray(np.concatenate([freq, freq])[None, :])


def front_kernel(
    tok_ref,
    gain_one_ref,
    gain_two_ref,
    freq_ref,
    routes_ref,
    gates_ref,
    order_ref,
    attn_hbm,
    pieces_hbm,
    cot_hbm,
    xn_ref,
    q_ref,
    kv_ref,
    mixed_ref,
    res_ref,
    wl_ref,
    wa_hbm,
    w_hbm,
    x_hbm,
    dy_hbm,
    wa,
    part,
    part_in,
    low_half,
    send,
    recv,
    local,
):
    f, z, c = place()
    fx, fy, fd = plane_peers(f)
    count, width = tok_ref.shape
    half = count // 2
    shard = attn_hbm.shape[0]
    cut = shard // 2
    in_cols = (QUERY_PER_GROUP + 2) * HEAD_DIM
    ins = pl.ds(0, in_cols)
    outs = pl.ds(in_cols, attn_hbm.shape[1] - in_cols)

    def at(fsdp=f, ctx=z, tp=c):
        return {"fsdp": fsdp, "ctx": ctx, "tp": tp}

    def remote(src, dst, k, device):
        return pltpu.make_async_remote_copy(
            src_ref=src,
            dst_ref=dst,
            send_sem=send.at[k],
            recv_sem=recv.at[k],
            device_id=device,
            device_id_type=MESH_ID,
        )

    plane = [at(fx), at(fy), at(fd)]
    rel = [fx, fy, fd]
    line = [at(ctx=lax.rem(z + s, 4)) for s in range(1, 4)]
    sibling = at(tp=1 - c)
    greet(plane + line + [sibling])

    mine = rows_of(f, shard)
    owned = pltpu.make_async_copy(attn_hbm, wa.at[mine], local.at[0])
    owned.start()
    in_x = remote(attn_hbm.at[:, ins], wa.at[mine, ins], 0, at(fx))
    in_y = remote(attn_hbm.at[:, ins], wa.at[mine, ins], 1, at(fy))
    in_x.start()
    in_y.start()

    rank = jnp.broadcast_to(order_ref[...].astype(jnp.float32), (count, count))
    ahead = jnp.where(rank.T < rank, 1.0, 0.0).astype(jnp.bfloat16)
    expert = lax.broadcasted_iota(jnp.int32, (128, count), 0)
    member = jnp.zeros((128, count), jnp.float32)
    gate = jnp.zeros((128, count), jnp.float32)
    for j in range(TOP):
        hit = jnp.broadcast_to(routes_ref[j : j + 1, :], (128, count)) == expert
        member = jnp.where(hit, 1.0, member)
        gate = jnp.where(hit, jnp.broadcast_to(gates_ref[j : j + 1, :], (128, count)), gate)
    slots = dot_f32(member.astype(jnp.bfloat16), ahead)
    gate = jnp.where(slots < CAP - 0.5, gate, 0.0)
    wl_ref[f] = gate[:EXPERTS]
    gate_copies = [remote(wl_ref.at[f], wl_ref.at[f], 2 + i, plane[i]) for i in range(3)]
    for copy in gate_copies:
        copy.start()

    own_w = pltpu.make_async_copy(pieces_hbm.at[0], w_hbm.at[:, :, mine, :], local.at[1])
    own_w.start()
    own_dy = [
        pltpu.make_async_copy(
            cot_hbm.at[pl.ds(i * half, half)], dy_hbm.at[i, f], local.at[2 + i]
        )
        for i in range(2)
    ]
    for copy in own_dy:
        copy.start()

    tok = tok_ref[...].astype(jnp.float32)
    inv = lax.rsqrt(jnp.mean(tok * tok, axis=-1, keepdims=True) + eps)
    xn_ref[...] = (tok * inv * gain_one_ref[...]).astype(jnp.bfloat16)
    position = z * count + lax.broadcasted_iota(jnp.int32, (count, HEAD_DIM), 0)
    angle = position.astype(jnp.float32) * freq_ref[...]
    cosine = jnp.cos(angle)
    lane = lax.broadcasted_iota(jnp.int32, (count, HEAD_DIM), 1)
    sine = jnp.where(lane < HEAD_DIM // 2, -jnp.sin(angle), jnp.sin(angle))

    top, low = rows_of(2 * fx, cut), rows_of(2 * fy + 1, cut)
    in_x.wait_recv()
    in_xy = remote(wa.at[top, ins], wa.at[top, ins], 5, at(fy))
    in_xy.start()
    in_y.wait_recv()
    in_yx = remote(wa.at[low, ins], wa.at[low, ins], 6, at(fx))
    in_yx.start()
    out_x = remote(attn_hbm.at[:, outs], wa.at[mine, outs], 7, at(fx))
    out_y = remote(attn_hbm.at[:, outs], wa.at[mine, outs], 8, at(fy))
    out_x.start()
    out_y.start()
    owned.wait()
    in_xy.wait_recv()
    in_yx.wait_recv()

    normed = xn_ref[...]
    for h in range(QUERY_PER_GROUP + 2):
        cols = pl.ds(h * HEAD_DIM, HEAD_DIM)
        if h % 2 == 0:
            pair = dot_f32(normed, wa[:, pl.ds(h * HEAD_DIM, 2 * HEAD_DIM)])
        value = pair[:, (h % 2) * HEAD_DIM : (h % 2 + 1) * HEAD_DIM]
        if h <= QUERY_PER_GROUP:
            value = turn(value, cosine, sine)
        if h < QUERY_PER_GROUP:
            q_ref[:, cols] = value.astype(jnp.bfloat16)
        else:
            kv_ref[0, :, pl.ds((h - QUERY_PER_GROUP) * HEAD_DIM, HEAD_DIM)] = value.astype(
                jnp.bfloat16
            )
    kv_copies = [remote(kv_ref.at[0], kv_ref.at[s], 8 + s, line[s - 1]) for s in range(1, 4)]
    for s in range(1, 4):

        @pl.when(z + s < 4)
        def _(s=s):
            kv_copies[s - 1].start()

        @pl.when(z < s)
        def _(s=s):
            kv_ref[s] = jnp.zeros(kv_ref.shape[1:], jnp.bfloat16)

    out_x.wait_recv()
    out_xy = remote(wa.at[top, outs], wa.at[top, outs], 12, at(fy))
    out_xy.start()
    out_y.wait_recv()
    out_yx = remote(wa.at[low, outs], wa.at[low, outs], 13, at(fx))
    out_yx.start()

    w_copies = []
    for m in range(3):
        for i in range(3):
            w_copies.append(
                remote(
                    pieces_hbm.at[i + 1, :, m], w_hbm.at[:, m, mine, :], 14 + 3 * m + i, plane[i]
                )
            )
    for copy in w_copies:
        copy.start()
    dy_copies = [
        remote(cot_hbm.at[rows_of(c, half)], dy_hbm.at[c, f], 23 + i, plane[i]) for i in range(3)
    ]
    for copy in dy_copies:
        copy.start()

    for s in range(1, 4):

        @pl.when(z >= s)
        def _(s=s):
            kv_copies[s - 1].wait_recv()

    keys = kv_ref[:, :, pl.ds(0, HEAD_DIM)].reshape(4 * count, HEAD_DIM)
    vals = kv_ref[:, :, pl.ds(HEAD_DIM, HEAD_DIM)].reshape(4 * count, HEAD_DIM)
    for g in range(QUERY_PER_GROUP):
        cols = pl.ds(g * HEAD_DIM, HEAD_DIM)
        probs = block_probs(z, keys, q_ref[:, cols]).astype(jnp.bfloat16)
        mixed_ref[:, cols] = dot_f32(probs, vals, TN).astype(jnp.bfloat16)

    out_xy.wait_recv()
    out_yx.wait_recv()
    store_wa = pltpu.make_async_copy(wa, wa_hbm, local.at[4])
    store_wa.start()
    for s in range(width // 256):
        cols = pl.ds(s * 256, 256)
        part[:, cols] = dot_f32(mixed_ref[...], wa[cols, outs], NT)
    swap = remote(part.at[rows_of(1 - c, half)], part_in, 26, sibling)
    swap.start()
    swap.wait_recv()
    my_rows = rows_of(c, half)
    residual = tok_ref[my_rows, :].astype(jnp.float32) + (part[my_rows, :] + part_in[...])
    res_ref[...] = residual
    inv = lax.rsqrt(jnp.mean(residual * residual, axis=-1, keepdims=True) + eps)
    low_half[...] = (residual * inv * gain_two_ref[...]).astype(jnp.bfloat16)
    own_x = pltpu.make_async_copy(low_half, x_hbm.at[c, f], local.at[5])
    own_x.start()
    x_copies = [remote(low_half, x_hbm.at[c, f], 27 + i, plane[i]) for i in range(3)]
    for copy in x_copies:
        copy.start()
    sib_x = [remote(low_half, x_hbm.at[c, f], 30, sibling)]
    sib_x[0].start()

    sib_dy = []
    for i in range(3):
        dy_copies[i].wait_recv()
        sib_dy.append(remote(dy_hbm.at[c, rel[i]], dy_hbm.at[c, rel[i]], 31 + i, sibling))
        sib_dy[i].start()
    for i in range(3):
        x_copies[i].wait_recv()
        sib_x.append(remote(x_hbm.at[c, rel[i]], x_hbm.at[c, rel[i]], 34 + i, sibling))
        sib_x[i + 1].start()

    for copy in w_copies + gate_copies + sib_dy + sib_x:
        copy.wait_recv()
    for s in range(1, 4):

        @pl.when(z + s < 4)
        def _(s=s):
            kv_copies[s - 1].wait_send()

    for copy in [in_x, in_y, in_xy, in_yx, out_x, out_y, out_xy, out_yx, swap]:
        copy.wait_send()
    for copy in w_copies + gate_copies + dy_copies + x_copies + sib_dy + sib_x:
        copy.wait_send()
    for copy in [own_w, own_x, store_wa] + own_dy:
        copy.wait()


def front(tok, gain_one, gain_two, routes, gates, order, attn_own, pieces, cot):
    count, width = tok.shape
    half = count // 2
    shard, columns = attn_own.shape
    experts, hidden = pieces.shape[1], pieces.shape[4]
    vmem, hbm = pl.BlockSpec(memory_space=pltpu.VMEM), pl.BlockSpec(memory_space=pl.ANY)
    bf16, f32 = jnp.bfloat16, jnp.float32
    shape = jax.ShapeDtypeStruct
    return pl.pallas_call(
        front_kernel,
        in_specs=[vmem] * 7 + [hbm] * 3,
        out_specs=[vmem] * 6 + [hbm] * 4,
        out_shape=[
            shape((count, width), bf16),
            shape((count, QUERY_PER_GROUP * HEAD_DIM), bf16),
            shape((4, count, 2 * HEAD_DIM), bf16),
            shape((count, QUERY_PER_GROUP * HEAD_DIM), bf16),
            shape((half, width), f32),
            shape((4, EXPERTS, count), f32),
            shape((4 * shard, columns), bf16),
            shape((experts, 3, 4 * shard, hidden), bf16),
            shape((2, 4, half, width), bf16),
            shape((2, 4, half, width), bf16),
        ],
        scratch_shapes=[
            pltpu.VMEM((4 * shard, columns), bf16),
            pltpu.VMEM((count, width), f32),
            pltpu.VMEM((half, width), f32),
            pltpu.VMEM((half, width), bf16),
            pltpu.SemaphoreType.DMA((37,)),
            pltpu.SemaphoreType.DMA((37,)),
            pltpu.SemaphoreType.DMA((6,)),
        ],
        compiler_params=pltpu.CompilerParams(
            collective_id=0, has_side_effects=True, vmem_limit_bytes=48 * MIB
        ),
        name="front",
    )(tok, gain_one, gain_two, frequencies(), routes, gates, order, attn_own, pieces, cot)


def moe_kernel(
    x_hbm, dy_hbm, w_hbm, wl_ref, ge_hbm, dn_ref, mo_ref, gg_ref, x, dy, wgu, wd, gu, hid, ge, scales, sem, out_sem
):
    f = lax.axis_index("fsdp")
    tokens, width = x.shape
    hidden = w_hbm.shape[3]
    half = tokens // 8
    tile = 2 * half
    own = w_hbm.shape[0]
    loads = [pltpu.make_async_copy(x_hbm, x, sem.at[0])]
    for e in range(own):
        for m in range(2):
            loads.append(
                pltpu.make_async_copy(
                    w_hbm.at[e, m], wgu.at[:, pl.ds((2 * e + m) * hidden, hidden)], sem.at[1 + 3 * e + m]
                )
            )
    loads.append(pltpu.make_async_copy(dy_hbm, dy, sem.at[7]))
    for e in range(own):
        loads.append(
            pltpu.make_async_copy(w_hbm.at[e, 2], wd.at[:, pl.ds(e * hidden, hidden)], sem.at[3 + 3 * e])
        )
    for copy in loads:
        copy.start()
    lane = lax.broadcasted_iota(jnp.int32, (half, 128), 1)
    for b in range(8):
        rows = wl_ref[b % 4, :, pl.ds((b // 4) * half, half)]
        rows = jnp.concatenate([rows, jnp.zeros((128 - EXPERTS, half), jnp.float32)], axis=0)
        scales[pl.ds(b * half, half), :] = rows.T
    for copy in loads:
        copy.wait()

    lanes = lax.broadcasted_iota(jnp.int32, (tile, 128), 1)

    def step(i, _):
        rows = pl.ds(pl.multiple_of(i * tile, tile), tile)
        acts = dot_f32(x[rows, :], wgu[...])
        plain = dot_f32(dy[rows, :], wd[...])
        table = scales[rows, :]
        sums = jnp.zeros((tile, 128), jnp.float32)
        for e in range(own):
            gate_act = acts[:, 2 * e * hidden : (2 * e + 1) * hidden]
            up_act = acts[:, (2 * e + 1) * hidden : (2 * e + 2) * hidden]
            d_plain = plain[:, e * hidden : (e + 1) * hidden]
            here = lanes == own * f + e
            scale = jnp.sum(jnp.where(here, table, 0.0), axis=1, keepdims=True)
            sigmoid = 1.0 / (1.0 + jnp.exp(-gate_act))
            active = gate_act * sigmoid
            act = active * up_act
            total = jnp.sum(act * d_plain, axis=1, keepdims=True)
            sums = jnp.where(here, jnp.where(scale != 0.0, total, 0.0), sums)
            d_hidden = d_plain * scale
            slope = sigmoid * (1.0 + gate_act * (1.0 - sigmoid))
            hid[rows, pl.ds(e * hidden, hidden)] = (act * scale).astype(jnp.bfloat16)
            gu[rows, pl.ds(2 * e * hidden, hidden)] = (d_hidden * up_act * slope).astype(jnp.bfloat16)
            gu[rows, pl.ds((2 * e + 1) * hidden, hidden)] = (d_hidden * active).astype(jnp.bfloat16)
        gg_ref[rows, :] = sums
        return 0

    lax.fori_loop(0, tokens // tile, step, 0)

    block = width // 4

    def grad_step(s, _):
        cols = pl.ds(pl.multiple_of(s * block, 128), block)
        inner = dot_f32(x[:, cols], gu[...], TN).astype(jnp.bfloat16)
        outer = dot_f32(dy[:, cols], hid[...], TN).astype(jnp.bfloat16)
        for e in range(own):
            for m in range(2):
                k = 2 * e + m
                ge[3 * e + m, cols, :] = inner[:, k * hidden : (k + 1) * hidden]
            ge[3 * e + 2, cols, :] = outer[:, e * hidden : (e + 1) * hidden]
        return 0

    lax.fori_loop(0, 4, grad_step, 0)
    store = pltpu.make_async_copy(ge, ge_hbm, out_sem)
    store.start()

    def down_step(i, _):
        rows = pl.ds(pl.multiple_of(i * tile, tile), tile)
        dn_ref[rows, :] = dot_f32(gu[rows, :], wgu[...], NT).astype(jnp.bfloat16)
        mo_ref[rows, :] = dot_f32(hid[rows, :], wd[...], NT).astype(jnp.bfloat16)
        return 0

    lax.fori_loop(0, tokens // tile, down_step, 0)
    store.wait()


def moe_layer(x, dy, weights, gate_table):
    tokens, width = x.shape
    own, _, _, hidden = weights.shape
    vmem, hbm = pl.BlockSpec(memory_space=pltpu.VMEM), pl.BlockSpec(memory_space=pl.ANY)
    bf16, f32 = jnp.bfloat16, jnp.float32
    shape = jax.ShapeDtypeStruct
    return pl.pallas_call(
        moe_kernel,
        in_specs=[hbm] * 3 + [vmem],
        out_specs=[hbm, vmem, vmem, vmem],
        out_shape=[
            shape((3 * own, width, hidden), bf16),
            shape((tokens, width), bf16),
            shape((tokens, width), bf16),
            shape((tokens, 128), f32),
        ],
        scratch_shapes=[
            pltpu.VMEM((tokens, width), bf16),
            pltpu.VMEM((tokens, width), bf16),
            pltpu.VMEM((width, 2 * own * hidden), bf16),
            pltpu.VMEM((width, own * hidden), bf16),
            pltpu.VMEM((tokens, 2 * own * hidden), bf16),
            pltpu.VMEM((tokens, own * hidden), bf16),
            pltpu.VMEM((3 * own, width, hidden), bf16),
            pltpu.VMEM((tokens, 128), f32),
            pltpu.SemaphoreType.DMA((8,)),
            pltpu.SemaphoreType.DMA,
        ],
        compiler_params=pltpu.CompilerParams(vmem_limit_bytes=58 * MIB),
        name="experts",
    )(x, dy, weights, gate_table)


def rear_kernel(
    res_ref,
    xn_ref,
    q_ref,
    kv_ref,
    mixed_ref,
    gain_one_ref,
    gain_two_ref,
    freq_ref,
    tok_hbm,
    cot_hbm,
    ge_hbm,
    dn_hbm,
    mo_hbm,
    gg_hbm,
    wa_hbm,
    layer_ref,
    tokgrad_ref,
    gains_ref,
    gate_ref,
    attn_hbm,
    fin_hbm,
    ge,
    r1,
    r2,
    wa,
    dn_own,
    dn_in,
    dn_got,
    mo_own,
    mo_in,
    mo_got,
    gg_own,
    gg_in,
    gg_sum,
    gg_got,
    dres,
    dattn,
    dmixed,
    dproj,
    dkv,
    dkv_low,
    dkv_got,
    d1,
    d1_low,
    d1_in,
    ga,
    ra,
    a1,
    a2,
    gacc,
    gin,
    tok_half,
    cot_half,
    send,
    recv,
    local,
    z_out,
    z_across,
    z_back,
    z_r1,
    z_r2,
    f_out,
    f_in,
):
    f, z, c = place()
    fx, fy, fd = plane_peers(f)
    rel = [f, fx, fy, fd]
    f32, bf16 = jnp.float32, jnp.bfloat16
    count, width = tok_hbm.shape
    half = count // 2
    shard = attn_hbm.shape[0]
    in_cols = (QUERY_PER_GROUP + 2) * HEAD_DIM
    q_cols = QUERY_PER_GROUP * HEAD_DIM
    ins = pl.ds(0, in_cols)
    outs = pl.ds(in_cols, attn_hbm.shape[1] - in_cols)
    scale = HEAD_DIM ** (-0.5)

    def at(fsdp=f, ctx=z, tp=c):
        return {"fsdp": fsdp, "ctx": ctx, "tp": tp}

    def copy_to(src, dst, send_sem, recv_sem, device):
        return pltpu.make_async_remote_copy(
            src_ref=src,
            dst_ref=dst,
            send_sem=send_sem,
            recv_sem=recv_sem,
            device_id=device,
            device_id_type=MESH_ID,
        )

    def remote(src, dst, k, device):
        return copy_to(src, dst, send.at[k], recv.at[k], device)

    plane = [at(fx), at(fy), at(fd)]
    line = [at(ctx=lax.rem(z + s, 4)) for s in range(1, 4)]
    sibling = at(tp=1 - c)
    partner = at(ctx=z + 1 - 2 * lax.rem(z, 2))
    opposite = at(ctx=3 - z)
    inner = (z == 1) | (z == 2)
    outer = (z == 0) | (z == 3)

    loads = [pltpu.make_async_copy(ge_hbm, ge, local.at[0])]
    loads.append(pltpu.make_async_copy(dn_hbm.at[c], dn_own, local.at[1]))
    loads.append(pltpu.make_async_copy(gg_hbm.at[c], gg_own, local.at[2]))
    loads.append(pltpu.make_async_copy(wa_hbm, wa, local.at[3]))
    loads.append(pltpu.make_async_copy(mo_hbm.at[c], mo_own, local.at[4]))
    loads.append(pltpu.make_async_copy(tok_hbm.at[rows_of(c, half)], tok_half, local.at[5]))
    loads.append(pltpu.make_async_copy(cot_hbm.at[rows_of(c, half)], cot_half, local.at[6]))
    for copy in loads:
        copy.start()
    greet(plane + line + [sibling])
    dn_swap = remote(dn_hbm.at[1 - c], dn_in, 0, sibling)
    gg_swap = remote(gg_hbm.at[1 - c], gg_in, 1, sibling)
    mo_swap = remote(mo_hbm.at[1 - c], mo_in, 2, sibling)
    dn_swap.start()
    gg_swap.start()
    mo_swap.start()

    mats = ge.shape[0]
    n_expert = 4 * mats
    n_attn = 4
    n_all = n_expert + n_attn
    a_rows = shard // n_attn

    def chunk(k):
        if k < n_expert:
            j, r = k // 4, k % 4
            rows = rows_of(rel[r], shard)
            return ge.at[j, rows], r1.at[j, rows], r2.at[j, rows]
        rows = pl.ds((k - n_expert) * a_rows, a_rows)
        return ra.at[0, rows], a1.at[rows], a2.at[rows]

    def add_into(dst, left, right):
        size = dst.shape[0] // 6

        def body(i, _):
            rows = pl.ds(pl.multiple_of(i * size, size), size)
            dst[rows, :] = (left[rows, :].astype(f32) + right[rows, :].astype(f32)).astype(bf16)
            return 0

        lax.fori_loop(0, 6, body, 0)

    def first(k):
        own, one, _ = chunk(k)
        return copy_to(own, one, z_out.at[k], z_r1.at[k], partner)

    def across(k):
        own, _, two = chunk(k)
        return copy_to(own, two, z_across.at[k], z_r2.at[k], opposite)

    def back(k):
        _, one, _ = chunk(k)
        return copy_to(one, one, z_back.at[k], z_r1.at[k], partner)

    def final(k):
        _, one, _ = chunk(k)
        j, r = k // 4, k % 4
        if r == 0:
            return pltpu.make_async_copy(one, fin_hbm.at[0, j], f_out.at[k])
        return copy_to(one, fin_hbm.at[r, j], f_out.at[k], f_in.at[k], plane[r - 1])

    def z_step(i):
        if i < n_all:

            @pl.when(outer)
            def _():
                if i >= 2:
                    first(i - 2).wait_send()
                first(i).start()

        if 1 <= i <= n_all:
            k = i - 1

            @pl.when(inner)
            def _():
                own, one, _ = chunk(k)
                first(k).wait_recv()
                add_into(own, own, one)
                across(k).start()

        if 2 <= i <= n_all + 1:
            k = i - 2

            @pl.when(inner)
            def _():
                own, one, two = chunk(k)
                across(k).wait_recv()
                add_into(one, own, two)
                back(k).start()
                if k < n_expert:
                    final(k).start()

        if 3 <= i <= n_all + 2:
            k = i - 3

            @pl.when(outer)
            def _():
                back(k).wait_recv()
                if k < n_expert:
                    final(k).start()

    loads[0].wait()
    z_step(0)
    loads[5].wait()
    loads[6].wait()

    loads[1].wait()
    loads[2].wait()
    gg_swap.wait_recv()
    gg_sum[...] = gg_own[...] + gg_in[...]
    dn_swap.wait_recv()
    for g in range(4):
        dn_own[g] = (dn_own[g].astype(f32) + dn_in[g].astype(f32)).astype(bf16)
    dn_out = [remote(dn_own.at[rel[i + 1]], dn_got.at[i], 3 + i, plane[i]) for i in range(3)]
    gg_out = [remote(gg_sum.at[rel[i + 1]], gg_got.at[i], 6 + i, plane[i]) for i in range(3)]
    for copy in dn_out + gg_out:
        copy.start()
    z_step(1)
    loads[4].wait()
    mo_swap.wait_recv()
    for g in range(4):
        mo_own[g] = (mo_own[g].astype(f32) + mo_in[g].astype(f32)).astype(bf16)
    mo_out = [remote(mo_own.at[rel[i + 1]], mo_got.at[i], 9 + i, plane[i]) for i in range(3)]
    for copy in mo_out:
        copy.start()
    z_step(2)
    for copy in dn_out:
        copy.wait_recv()
    d_two = dn_own[f].astype(f32)
    for i in range(3):
        d_two = d_two + dn_got[i].astype(f32)
    residual = res_ref[...]
    inv = lax.rsqrt(jnp.mean(residual * residual, axis=-1, keepdims=True) + eps)
    scaled = d_two * gain_two_ref[...]
    inside = jnp.mean(scaled * residual, axis=-1, keepdims=True)
    d_norm = inv * scaled - residual * (inv * inv * inv * inside)
    gacc[0] = jnp.zeros(gacc.shape[1:], f32)
    gacc[0, 1:2, :] = jnp.sum(d_two * residual * inv, axis=0, keepdims=True)
    my_rows = rows_of(c, half)
    d_res = cot_half[...].astype(f32) + d_norm
    dres[...] = d_res
    dattn[my_rows, :] = d_res.astype(bf16)
    da_swap = remote(dattn.at[my_rows], dattn.at[my_rows], 12, sibling)
    da_swap.start()
    loads[3].wait()
    z_step(3)
    da_swap.wait_recv()
    dmixed[...] = dot_f32(dattn[...], wa[:, outs]).astype(bf16)
    z_step(4)

    position = z * count + lax.broadcasted_iota(jnp.int32, (count, HEAD_DIM), 0)
    angle = position.astype(f32) * freq_ref[...]
    cosine = jnp.cos(angle)
    lane = lax.broadcasted_iota(jnp.int32, (count, HEAD_DIM), 1)
    sine = jnp.where(lane < HEAD_DIM // 2, jnp.sin(angle), -jnp.sin(angle))
    keys = kv_ref[:, :, pl.ds(0, HEAD_DIM)].reshape(4 * count, HEAD_DIM)
    vals = kv_ref[:, :, pl.ds(HEAD_DIM, HEAD_DIM)].reshape(4 * count, HEAD_DIM)
    key_cols, val_cols = pl.ds(0, HEAD_DIM), pl.ds(HEAD_DIM, HEAD_DIM)
    dkv[...] = jnp.zeros_like(dkv)
    for g in range(QUERY_PER_GROUP):
        cols = pl.ds(g * HEAD_DIM, HEAD_DIM)
        query = q_ref[:, cols]
        d_mix = dmixed[:, cols]
        probs = block_probs(z, keys, query)
        d_probs = dot_f32(vals, d_mix, NT)
        inside = jnp.sum(probs * d_probs, axis=0, keepdims=True)
        d_scores = (probs * (d_probs - inside)).astype(bf16)
        d_query = dot_f32(d_scores, keys, TN) * scale
        dproj[:, cols] = turn(d_query, cosine, sine).astype(bf16)
        dkv[:, key_cols] += dot_f32(d_scores, query) * scale
        dkv[:, val_cols] += dot_f32(probs.astype(bf16), d_mix)
        if g % 2 == 1:
            z_step(5 + g // 2)
    dkv_low[...] = dkv[...].reshape(dkv_low.shape).astype(bf16)
    dkv_out = [
        remote(dkv_low.at[s], dkv_got.at[s - 1], 12 + s, at(ctx=lax.rem(z + 4 - s, 4)))
        for s in range(1, 4)
    ]
    for s in range(1, 4):

        @pl.when(z >= s)
        def _(s=s):
            dkv_out[s - 1].start()

    def weight_grad(left, right, cols):
        def body(i, _):
            rows = pl.ds(pl.multiple_of(i * 256, 256), 256)
            ga[rows, cols] = dot_f32(left[:, rows], right, TN).astype(bf16)
            return 0

        lax.fori_loop(0, width // 256, body, 0)

    def send_grad(cols, k):
        copies = [
            remote(ga.at[rows_of(rel[i + 1], shard), cols], ra.at[i, :, cols], k + i, plane[i])
            for i in range(3)
        ]
        for copy in copies:
            copy.start()
        return copies

    weight_grad(dattn, mixed_ref[...], outs)
    ga_copies = send_grad(outs, 16)
    z_step(8)
    q_part = pl.ds(0, q_cols)
    weight_grad(xn_ref, dproj[:, q_part], q_part)
    ga_copies += send_grad(q_part, 19)
    z_step(9)
    for s in range(1, 4):

        @pl.when(z + s < 4)
        def _(s=s):
            dkv_out[s - 1].wait_recv()
            dkv[0:count, :] += dkv_got[s - 1].astype(f32)

    kv_part = pl.ds(q_cols, 2 * HEAD_DIM)
    dproj[:, pl.ds(q_cols, HEAD_DIM)] = turn(dkv[0:count, key_cols], cosine, sine).astype(bf16)
    dproj[:, pl.ds(q_cols + HEAD_DIM, HEAD_DIM)] = dkv[0:count, val_cols].astype(bf16)
    weight_grad(xn_ref, dproj[:, kv_part], kv_part)
    ga_copies += send_grad(kv_part, 22)
    z_step(10)

    for s in range(width // 256):
        rows = pl.ds(s * 256, 256)
        d1[:, rows] = dot_f32(dproj[my_rows, :], wa[rows, ins], NT)
        d1_low[:, rows] = dot_f32(dproj[rows_of(1 - c, half), :], wa[rows, ins], NT).astype(bf16)
    d1_swap = remote(d1_low, d1_in, 25, sibling)
    d1_swap.start()
    z_step(11)
    d1_swap.wait_recv()
    d_one = d1[...] + d1_in[...].astype(f32)
    tok = tok_half[...].astype(f32)
    inv = lax.rsqrt(jnp.mean(tok * tok, axis=-1, keepdims=True) + eps)
    scaled = d_one * gain_one_ref[...]
    inside = jnp.mean(scaled * tok, axis=-1, keepdims=True)
    d_norm = inv * scaled - tok * (inv * inv * inv * inside)
    gacc[0, 0:1, :] = jnp.sum(d_one * tok * inv, axis=0, keepdims=True)
    tokgrad_ref[my_rows, :] = (dres[...] + d_norm).astype(bf16)
    tg_swap = remote(tokgrad_ref.at[my_rows], tokgrad_ref.at[my_rows], 26, sibling)
    tg_swap.start()
    z_step(12)

    for copy in mo_out + gg_out:
        copy.wait_recv()
    moe = mo_own[f].astype(f32)
    gates = gg_sum[f]
    for i in range(3):
        moe = moe + mo_got[i].astype(f32)
        gates = gates + gg_got[i]
    layer_ref[my_rows, :] = (res_ref[...] + moe).astype(bf16)
    gate_ref[my_rows, :] = gates
    lo_swap = remote(layer_ref.at[my_rows], layer_ref.at[my_rows], 27, sibling)
    gt_swap = remote(gate_ref.at[my_rows], gate_ref.at[my_rows], 28, sibling)
    lo_swap.start()
    gt_swap.start()
    z_step(13)

    stages = [sibling, at(fx), at(fy), partner, at(ctx=lax.rem(z + 2, 4))]
    gain_copies = [remote(gacc.at[i], gin.at[i], 29 + i, stages[i]) for i in range(5)]
    for i in range(5):
        gain_copies[i].start()
        z_step(14 + i)
        gain_copies[i].wait_recv()
        total = gacc[i] + gin[i]
        if i < 4:
            gacc[i + 1] = total
        else:
            gains_ref[...] = total

    for i in range(19, n_expert):
        z_step(i)
    for copy in ga_copies:
        copy.wait_recv()

    def attn_sum(i, _):
        size = shard // 8
        here = pl.ds(pl.multiple_of(i * size, size), size)
        total = ga[pl.ds(pl.multiple_of(f * shard + i * size, size), size), :].astype(f32)
        for r in range(3):
            total = total + ra[r, here, :].astype(f32)
        ra[0, here, :] = total.astype(bf16)
        return 0

    lax.fori_loop(0, 8, attn_sum, 0)
    for i in range(n_expert, n_all + 3):
        z_step(i)
    store = pltpu.make_async_copy(a1, attn_hbm, local.at[0])
    store.start()

    store.wait()
    for k in range(n_all):

        @pl.when(outer)
        def _(k=k):
            if k >= n_all - 2:
                first(k).wait_send()

        @pl.when(inner)
        def _(k=k):
            across(k).wait_send()
            back(k).wait_send()

    for k in range(n_expert):
        if k % 4 == 0:
            final(k).wait()
        else:
            final(k).wait_send()
            final(k).wait_recv()
    for s in range(1, 4):

        @pl.when(z >= s)
        def _(s=s):
            dkv_out[s - 1].wait_send()

    for copy in [tg_swap, lo_swap, gt_swap]:
        copy.wait_recv()
    swaps = [dn_swap, gg_swap, mo_swap, da_swap, d1_swap, tg_swap, lo_swap, gt_swap]
    for copy in swaps + dn_out + gg_out + mo_out + ga_copies + gain_copies:
        copy.wait_send()


def rear(tok, cot, res, xn, q, kv, mixed, gain_one, gain_two, ge, dn, mo, gg, wa):
    count, width = tok.shape
    half = count // 2
    columns = wa.shape[1]
    shard = width // 4
    mats, _, hidden = ge.shape
    q_cols = q.shape[1]
    vmem, hbm = pl.BlockSpec(memory_space=pltpu.VMEM), pl.BlockSpec(memory_space=pl.ANY)
    bf16, f32 = jnp.bfloat16, jnp.float32
    shape = jax.ShapeDtypeStruct
    dma = pltpu.SemaphoreType.DMA
    n_all = 4 * mats + 4
    return pl.pallas_call(
        rear_kernel,
        in_specs=[vmem] * 8 + [hbm] * 7,
        out_specs=[vmem] * 4 + [hbm] * 2,
        out_shape=[
            shape((count, width), bf16),
            shape((count, width), bf16),
            shape((8, width), f32),
            shape((count, 128), f32),
            shape((shard, columns), bf16),
            shape((4, mats, shard, hidden), bf16),
        ],
        scratch_shapes=[
            pltpu.VMEM((mats, width, hidden), bf16),
            pltpu.VMEM((mats, width, hidden), bf16),
            pltpu.VMEM((mats, width, hidden), bf16),
            pltpu.VMEM((width, columns), bf16),
            pltpu.VMEM((4, half, width), bf16),
            pltpu.VMEM((4, half, width), bf16),
            pltpu.VMEM((3, half, width), bf16),
            pltpu.VMEM((4, half, width), bf16),
            pltpu.VMEM((4, half, width), bf16),
            pltpu.VMEM((3, half, width), bf16),
            pltpu.VMEM((4, half, 128), f32),
            pltpu.VMEM((4, half, 128), f32),
            pltpu.VMEM((4, half, 128), f32),
            pltpu.VMEM((3, half, 128), f32),
            pltpu.VMEM((half, width), f32),
            pltpu.VMEM((count, width), bf16),
            pltpu.VMEM((count, q_cols), bf16),
            pltpu.VMEM((count, q_cols + 2 * HEAD_DIM), bf16),
            pltpu.VMEM((4 * count, 2 * HEAD_DIM), f32),
            pltpu.VMEM((4, count, 2 * HEAD_DIM), bf16),
            pltpu.VMEM((3, count, 2 * HEAD_DIM), bf16),
            pltpu.VMEM((half, width), f32),
            pltpu.VMEM((half, width), bf16),
            pltpu.VMEM((half, width), bf16),
            pltpu.VMEM((width, columns), bf16),
            pltpu.VMEM((3, shard, columns), bf16),
            pltpu.VMEM((shard, columns), bf16),
            pltpu.VMEM((shard, columns), bf16),
            pltpu.VMEM((5, 8, width), f32),
            pltpu.VMEM((5, 8, width), f32),
            pltpu.VMEM((half, width), bf16),
            pltpu.VMEM((half, width), bf16),
            dma((34,)),
            dma((34,)),
            dma((7,)),
            dma((n_all,)),
            dma((n_all,)),
            dma((n_all,)),
            dma((n_all,)),
            dma((n_all,)),
            dma((4 * mats,)),
            dma((4 * mats,)),
        ],
        compiler_params=pltpu.CompilerParams(
            collective_id=1, has_side_effects=True, vmem_limit_bytes=62 * MIB
        ),
        name="rear",
    )(res, xn, q, kv, mixed, gain_one, gain_two, frequencies(), tok, cot, ge, dn, mo, gg, wa)


def body_fast(
    tokens,
    attn_norm,
    attention_params,
    ffn_norm,
    expert_weights,
    gate_values,
    routes,
    slot_order,
    cotangent,
):
    sequence_count, block_len, model_width = tokens.shape
    count = sequence_count * block_len
    half = count // 2
    own_experts = EXPERTS // 4
    f = lax.axis_index("fsdp")
    shard, hidden = attention_params.shape[0], expert_weights.shape[3]
    order = expert_order(f)
    pieces = split_experts(jnp.transpose(expert_weights, (0, 2, 1, 3)), order)
    pieces = pieces.reshape(4, own_experts, 3, shard, hidden)
    tok = tokens.reshape(count, model_width)
    cot = cotangent.reshape(count, model_width)
    gain_one, gain_two = attn_norm[None, :], ffn_norm[None, :]
    route_rows = routes.reshape(count, TOP)
    normed, queries, kv, mixed, residual, gate_table, whole_attn, whole_expert, x, dy = front(
        tok,
        gain_one,
        gain_two,
        route_rows.T,
        gate_values.reshape(count, TOP).T,
        slot_order.reshape(1, count),
        attention_params[:, 0, :],
        pieces,
        cot,
    )
    grads, d_normed, moe, gate_parts = moe_layer(
        x.reshape(8 * half, model_width), dy.reshape(8 * half, model_width), whole_expert, gate_table
    )
    layer_out, tokens_grad, gains, gate_rows, attn_grad, finals = rear(
        tok,
        cot,
        residual,
        normed,
        queries,
        kv,
        mixed,
        gain_one,
        gain_two,
        grads,
        d_normed.reshape(2, 4, half, model_width),
        moe.reshape(2, 4, half, model_width),
        gate_parts.reshape(2, 4, half, 128),
        whole_attn,
    )
    picked = route_rows[:, :, None] == jnp.arange(EXPERTS, dtype=jnp.int32)
    gate_grad = jnp.sum(jnp.where(picked, gate_rows[:, None, :EXPERTS], 0.0), axis=-1)
    finals = finals.reshape(EXPERTS, 3, shard, hidden)
    expert_grad = jnp.transpose(join_experts(finals, order.T), (0, 2, 1, 3))
    return (
        layer_out.reshape(sequence_count, block_len, model_width),
        tokens_grad.reshape(sequence_count, block_len, model_width),
        attn_grad.astype(jnp.float32)[:, None, :],
        expert_grad,
        gains[0],
        gains[1],
        gate_grad.reshape(sequence_count, block_len, TOP),
    )


def solution(mesh):
    in_specs = (
        P("fsdp", "ctx", None),
        P(),
        P("fsdp", "tp", None),
        P(),
        P("fsdp", None, None, "tp"),
        P("fsdp", "ctx", None),
        P("fsdp", "ctx", None),
        P("fsdp", "ctx"),
        P("fsdp", "ctx", None),
    )
    out_specs = (
        P("fsdp", "ctx", None),
        P("fsdp", "ctx", None),
        P("fsdp", "tp", None),
        P("fsdp", None, None, "tp"),
        P(),
        P(),
        P("fsdp", "ctx", None),
    )
    four = mesh.shape["fsdp"] == 4 and mesh.shape["ctx"] == 4 and mesh.shape["tp"] == 2
    body_fn = body_fast if four else body
    return jax.shard_map(body_fn, mesh=mesh, in_specs=in_specs, out_specs=out_specs, check_vma=False)
```

```python
import jax
import jax.numpy as jnp
from jax import lax
import numpy as np
from jax.experimental import pallas as pl
from jax.experimental.pallas import tpu as pltpu
from jax.sharding import PartitionSpec as P

HEAD_DIM = 128
TOP = 4
EXPERTS = 8
QUERY_PER_GROUP = 6
CAP = 160


eps = 1e-06
theta_base = 1000000.0


def angle_tables(positions):
    frequency = theta_base ** (-(jnp.arange(HEAD_DIM // 2, dtype=jnp.float32) * 2.0) / HEAD_DIM)
    angles = positions.astype(jnp.float32)[:, None] * frequency[None, :]
    return (jnp.cos(angles), jnp.sin(angles))


def rotate(source, cosine_table, sine_table):
    half_size = source.shape[-1] // 2
    front_half = source[..., :half_size]
    back_half = source[..., half_size:]
    return jnp.concatenate(
        [
            front_half * cosine_table - back_half * sine_table,
            back_half * cosine_table + front_half * sine_table,
        ],
        axis=-1,
    )


def norm_back(source, inv_rms, gain_vec, upstream):
    scaled = upstream * gain_vec
    inner_sum = jnp.mean(scaled * source, axis=-1, keepdims=True)
    d_source = inv_rms * scaled - source * inv_rms * inv_rms * inv_rms * inner_sum
    return (d_source, jnp.sum(upstream * source * inv_rms, axis=0))


def slot_tables(route_rows, rank_rows):
    tok_count = route_rows.shape[0]
    inverse = (
        jnp.zeros((tok_count,), jnp.int32).at[rank_rows].set(jnp.arange(tok_count, dtype=jnp.int32))
    )
    ranked = route_rows[inverse].reshape(-1)
    onehot = (ranked[:, None] == jnp.arange(EXPERTS, dtype=jnp.int32)[None, :]).astype(jnp.int32)
    before = jnp.cumsum(onehot, axis=0) - onehot
    slot_ranked = jnp.sum(before * onehot, axis=1).reshape(tok_count, TOP)
    slots = slot_ranked[rank_rows]
    kept_pair = slots < CAP
    pair_slot = jnp.where(kept_pair, route_rows * CAP + slots, EXPERTS * CAP)
    owners = jnp.broadcast_to(jnp.arange(tok_count, dtype=jnp.int32)[:, None], (tok_count, TOP))
    slot_token = (
        jnp.full((EXPERTS * CAP,), tok_count, jnp.int32)
        .at[pair_slot.reshape(-1)]
        .set(owners.reshape(-1), mode="drop")
    )
    return (kept_pair, pair_slot, slot_token)


def attend_forward(queries, key_rows, value_rows, allowed):
    scores = jnp.einsum(
        "qhgd,khd->hgqk", queries, key_rows, preferred_element_type=jnp.float32
    ) * HEAD_DIM ** (-0.5)
    scores = jnp.where(allowed, scores, -1e30)
    row_max = jnp.max(scores, axis=-1, keepdims=True)
    expd = jnp.exp(scores - row_max)
    row_total = jnp.sum(expd, axis=-1, keepdims=True)
    attn_probs = (expd / row_total).astype(jnp.bfloat16)
    mixed_heads = jnp.einsum(
        "hgqk,khd->qhgd", attn_probs, value_rows, preferred_element_type=jnp.float32
    )
    return (mixed_heads.astype(jnp.bfloat16), row_max + jnp.log(row_total))


def attend_backward(queries, key_rows, value_rows, allowed, log_total, d_mixed):
    scores = jnp.einsum(
        "qhgd,khd->hgqk", queries, key_rows, preferred_element_type=jnp.float32
    ) * HEAD_DIM ** (-0.5)
    scores = jnp.where(allowed, scores, -1e30)
    attn_probs = jnp.exp(scores - log_total)
    low_probs = attn_probs.astype(jnp.bfloat16)
    d_probs = jnp.einsum("qhgd,khd->hgqk", d_mixed, value_rows, preferred_element_type=jnp.float32)
    inner_sum = jnp.sum(attn_probs * d_probs, axis=-1, keepdims=True)
    d_scores = (attn_probs * (d_probs - inner_sum)).astype(jnp.bfloat16)
    d_queries = jnp.einsum(
        "hgqk,khd->qhgd", d_scores, key_rows, preferred_element_type=jnp.float32
    ) * HEAD_DIM ** (-0.5)
    d_keys = jnp.einsum(
        "hgqk,qhgd->khd", d_scores, queries, preferred_element_type=jnp.float32
    ) * HEAD_DIM ** (-0.5)
    d_values = jnp.einsum("hgqk,qhgd->khd", low_probs, d_mixed, preferred_element_type=jnp.float32)
    return (d_queries, d_keys, d_values)


def body(
    tokens,
    attn_norm,
    attention_params,
    ffn_norm,
    expert_weights,
    gate_values,
    routes,
    slot_order,
    cotangent,
):
    sequence_count, block_len, model_width = tokens.shape
    tok_count = sequence_count * block_len
    kv_loc = attention_params.shape[1]
    input_columns = (QUERY_PER_GROUP + 2) * HEAD_DIM
    ctx_size = lax.axis_size("ctx")
    ctx_place = lax.axis_index("ctx")
    sequence_length = block_len * ctx_size
    whole_attn, whole_expert = (
        lax.all_gather(attention_params, "fsdp", axis=0, tiled=True),
        lax.all_gather(expert_weights, "fsdp", axis=0, tiled=True),
    )
    positions = ctx_place * block_len + jnp.arange(block_len, dtype=jnp.int32)
    cosine_table, sine_table = angle_tables(positions)
    cosine_table = jnp.tile(cosine_table, (sequence_count, 1))
    sine_table = jnp.tile(sine_table, (sequence_count, 1))
    cos_four = cosine_table[:, None, None, :]
    sin_four = sine_table[:, None, None, :]
    cos_three = cosine_table[:, None, :]
    sin_three = sine_table[:, None, :]
    allowed = (jnp.arange(sequence_length, dtype=jnp.int32) // block_len <= ctx_place)[
        None, None, None, :
    ]
    tok_float = tokens.reshape(tok_count, model_width).astype(jnp.float32)
    inv_one = lax.rsqrt(jnp.mean(tok_float * tok_float, axis=-1, keepdims=True) + eps)
    first_normed = (tok_float * inv_one * attn_norm).astype(jnp.bfloat16)
    projected_rows = jnp.einsum(
        "td,dhc->thc",
        first_normed,
        whole_attn[:, :, :input_columns],
        preferred_element_type=jnp.float32,
    ).reshape(tok_count, kv_loc, QUERY_PER_GROUP + 2, HEAD_DIM)
    queries = rotate(projected_rows[:, :, :QUERY_PER_GROUP], cos_four, sin_four).astype(
        jnp.bfloat16
    )
    key_rows = rotate(projected_rows[:, :, QUERY_PER_GROUP], cos_three, sin_three).astype(
        jnp.bfloat16
    )
    value_rows = projected_rows[:, :, QUERY_PER_GROUP + 1].astype(jnp.bfloat16)
    key_all, value_all = (
        lax.all_gather(
            key_rows.reshape(sequence_count, block_len, kv_loc, HEAD_DIM), "ctx", axis=1, tiled=True
        ),
        lax.all_gather(
            value_rows.reshape(sequence_count, block_len, kv_loc, HEAD_DIM),
            "ctx",
            axis=1,
            tiled=True,
        ),
    )
    query_seq = queries.reshape(sequence_count, block_len, kv_loc, QUERY_PER_GROUP, HEAD_DIM)
    mixed_heads, log_total = lax.map(
        lambda item_args: attend_forward(item_args[0], item_args[1], item_args[2], allowed),
        (query_seq, key_all, value_all),
    )
    mixed_flat = mixed_heads.reshape(tok_count, kv_loc, QUERY_PER_GROUP * HEAD_DIM)
    attn_part = jnp.einsum(
        "thc,dhc->td",
        mixed_flat,
        whole_attn[:, :, input_columns:],
        preferred_element_type=jnp.float32,
    )
    attn_sum = lax.psum(attn_part, "tp")
    residual = tok_float + attn_sum
    inv_two = lax.rsqrt(jnp.mean(residual * residual, axis=-1, keepdims=True) + eps)
    normed_two = (residual * inv_two * ffn_norm).astype(jnp.bfloat16)
    kept_pair, pair_slot, slot_token = slot_tables(
        routes.reshape(tok_count, TOP), slot_order.reshape(tok_count)
    )
    kept_float = kept_pair.astype(jnp.float32)
    gate_kept = gate_values.reshape(tok_count, TOP) * kept_float
    slot_gate = (
        jnp.zeros((EXPERTS * CAP,), jnp.float32)
        .at[pair_slot.reshape(-1)]
        .set(gate_kept.reshape(-1), mode="drop")
    )
    padded = jnp.concatenate([normed_two, jnp.zeros((1, model_width), jnp.bfloat16)], axis=0)
    inputs = padded[slot_token].reshape(EXPERTS, CAP, model_width)
    gate_act = jnp.einsum(
        "ecd,deh->ech", inputs, whole_expert[:, :, 0], preferred_element_type=jnp.float32
    )
    up_act = jnp.einsum(
        "ecd,deh->ech", inputs, whole_expert[:, :, 1], preferred_element_type=jnp.float32
    )
    gate_sigmoid = jax.nn.sigmoid(gate_act)
    active = gate_act * gate_sigmoid
    hidden = (active * up_act).astype(jnp.bfloat16)
    expert_out = jnp.einsum(
        "ech,deh->ecd", hidden, whole_expert[:, :, 2], preferred_element_type=jnp.float32
    )
    out_pad = jnp.concatenate(
        [expert_out.reshape(EXPERTS * CAP, model_width), jnp.zeros((1, model_width), jnp.float32)],
        axis=0,
    )
    picked = out_pad[pair_slot]
    moe_part = jnp.sum(picked * gate_kept[:, :, None], axis=1)
    moe = lax.psum(moe_part.astype(jnp.bfloat16), "tp").astype(jnp.float32)
    layer_out = (
        (residual + moe).astype(jnp.bfloat16).reshape(sequence_count, block_len, model_width)
    )
    grad_out = cotangent.reshape(tok_count, model_width).astype(jnp.float32)
    gate_part = jnp.sum(picked * grad_out[:, None, :], axis=-1) * kept_float
    grad_pad = jnp.concatenate([grad_out, jnp.zeros((1, model_width), jnp.float32)], axis=0)
    d_expert = (
        (grad_pad[slot_token] * slot_gate[:, None])
        .astype(jnp.bfloat16)
        .reshape(EXPERTS, CAP, model_width)
    )
    d_hidden = jnp.einsum(
        "ecd,deh->ech", d_expert, whole_expert[:, :, 2], preferred_element_type=jnp.float32
    )
    silu_slope = gate_sigmoid * (1.0 + gate_act * (1.0 - gate_sigmoid))
    d_gate_act = (d_hidden * up_act * silu_slope).astype(jnp.bfloat16)
    d_up_act = (d_hidden * active).astype(jnp.bfloat16)
    d_inputs = jnp.einsum(
        "ech,deh->ecd", d_gate_act, whole_expert[:, :, 0], preferred_element_type=jnp.float32
    )
    d_inputs = d_inputs + jnp.einsum(
        "ech,deh->ecd", d_up_act, whole_expert[:, :, 1], preferred_element_type=jnp.float32
    )
    d_in_pad = jnp.concatenate(
        [d_inputs.reshape(EXPERTS * CAP, model_width), jnp.zeros((1, model_width), jnp.float32)],
        axis=0,
    )
    d_normed_part = jnp.sum(d_in_pad[pair_slot], axis=1)
    d_normed_two, gate_grad = lax.psum((d_normed_part, gate_part), "tp")
    d_resid_norm, gain_two = norm_back(residual, inv_two, ffn_norm, d_normed_two)
    d_residual = grad_out + d_resid_norm
    d_attn = d_residual.astype(jnp.bfloat16)
    d_mixed = jnp.einsum(
        "td,dhc->thc", d_attn, whole_attn[:, :, input_columns:], preferred_element_type=jnp.float32
    ).astype(jnp.bfloat16)
    d_mixed_seq = d_mixed.reshape(sequence_count, block_len, kv_loc, QUERY_PER_GROUP, HEAD_DIM)
    d_queries, d_key_all, d_value_all = lax.map(
        lambda item_args: attend_backward(
            item_args[0], item_args[1], item_args[2], allowed, item_args[3], item_args[4]
        ),
        (query_seq, key_all, value_all, log_total, d_mixed_seq),
    )
    d_keys, d_values = (
        lax.psum_scatter(
            d_key_all.astype(jnp.bfloat16), "ctx", scatter_dimension=1, tiled=True
        ).astype(jnp.float32),
        lax.psum_scatter(
            d_value_all.astype(jnp.bfloat16), "ctx", scatter_dimension=1, tiled=True
        ).astype(jnp.float32),
    )
    d_queries = rotate(
        d_queries.reshape(tok_count, kv_loc, QUERY_PER_GROUP, HEAD_DIM), cos_four, -sin_four
    )
    d_keys = rotate(d_keys.reshape(tok_count, kv_loc, HEAD_DIM), cos_three, -sin_three)
    d_values = d_values.reshape(tok_count, kv_loc, HEAD_DIM)
    d_projected = jnp.concatenate([d_queries, d_keys[:, :, None], d_values[:, :, None]], axis=2)
    d_projected = d_projected.astype(jnp.bfloat16).reshape(tok_count, kv_loc, input_columns)
    d_normed_local = jnp.einsum(
        "thc,dhc->td",
        d_projected,
        whole_attn[:, :, :input_columns],
        preferred_element_type=jnp.float32,
    )
    d_normed_one = lax.psum(d_normed_local.astype(jnp.bfloat16), "tp").astype(jnp.float32)
    d_tok_norm, gain_one = norm_back(tok_float, inv_one, attn_norm, d_normed_one)
    tokens_grad = (
        (d_residual + d_tok_norm)
        .astype(jnp.bfloat16)
        .reshape(sequence_count, block_len, model_width)
    )
    gain_one, gain_two = lax.psum((gain_one, gain_two), ("fsdp", "ctx"))
    in_term = jnp.einsum(
        "td,thc->dhc", first_normed, d_projected, preferred_element_type=jnp.float32
    )
    out_term = jnp.einsum("td,thc->dhc", d_attn, mixed_flat, preferred_element_type=jnp.float32)
    attn_grad = lax.psum_scatter(
        jnp.concatenate([in_term, out_term], axis=2),
        ("fsdp", "ctx"),
        scatter_dimension=0,
        tiled=True,
    )
    gate_term = jnp.einsum("ecd,ech->deh", inputs, d_gate_act, preferred_element_type=jnp.float32)
    up_term = jnp.einsum("ecd,ech->deh", inputs, d_up_act, preferred_element_type=jnp.float32)
    down_term = jnp.einsum("ecd,ech->deh", d_expert, hidden, preferred_element_type=jnp.float32)
    expert_grad = lax.psum_scatter(
        jnp.stack([gate_term, up_term, down_term], axis=2),
        ("fsdp", "ctx"),
        scatter_dimension=0,
        tiled=True,
    )
    attn_grad, expert_grad = (
        lax.all_gather(attn_grad.astype(jnp.bfloat16), "ctx", axis=0, tiled=True).astype(
            attn_grad.dtype
        ),
        lax.all_gather(expert_grad.astype(jnp.bfloat16), "ctx", axis=0, tiled=True).astype(
            expert_grad.dtype
        ),
    )
    return (
        layer_out,
        tokens_grad,
        attn_grad,
        expert_grad,
        gain_one,
        gain_two,
        gate_grad.reshape(sequence_count, block_len, TOP),
    )


MESH_ID = pl.DeviceIdType.MESH
MIB = 2**20


def expert_order(place):
    row = jnp.arange(128, dtype=jnp.int32)
    expert = (((row // 32) ^ place) * 2) + (row // 16) % 2
    source = (row % 16) * 8 + expert
    return (source[:, None] == row[None, :]).astype(jnp.bfloat16)


def join_kernel(order_ref, in_ref, out_ref):
    width = in_ref.shape[3]
    for m in range(3):
        for k in range(in_ref.shape[2] // 16):
            block = in_ref[:, m, pl.ds(k * 16, 16), :].reshape(128, width)
            moved = jnp.dot(order_ref[...], block, preferred_element_type=jnp.float32)
            out_ref[pl.ds(k * 16, 16), m] = moved.reshape(16, 8, width)


def join_experts(grads, order):
    experts, _, rows, width = grads.shape
    step = 64
    return pl.pallas_call(
        join_kernel,
        grid=(rows // step,),
        in_specs=[
            pl.BlockSpec((128, 128), lambda i: (0, 0)),
            pl.BlockSpec((experts, 3, step, width), lambda i: (0, 0, i, 0)),
        ],
        out_specs=pl.BlockSpec((step, 3, experts, width), lambda i: (i, 0, 0, 0)),
        out_shape=jax.ShapeDtypeStruct((rows, 3, experts, width), jnp.float32),
        compiler_params=pltpu.CompilerParams(vmem_limit_bytes=40 * MIB),
        name="join_experts",
    )(order, grads)


NT = (((1,), (1,)), ((), ()))
TN = (((0,), (0,)), ((), ()))


def dot_f32(a, b, dims=(((1,), (0,)), ((), ()))):
    return lax.dot_general(a, b, dims, preferred_element_type=jnp.float32)


def block_probs(last, keys, query):
    scores = dot_f32(keys, query, NT) * HEAD_DIM ** (-0.5)
    block = lax.broadcasted_iota(jnp.int32, scores.shape, 0) // query.shape[0]
    scores = jnp.where(block <= last, scores, -1e30)
    expd = jnp.exp(scores - jnp.max(scores, axis=0, keepdims=True))
    return expd * (1.0 / jnp.sum(expd, axis=0, keepdims=True))


def place():
    return lax.axis_index("fsdp"), lax.axis_index("ctx"), lax.axis_index("tp")


def plane_peers(f):
    return f + 1 - 2 * lax.rem(f, 2), lax.rem(f + 2, 4), 3 - f


def rows_of(index, size):
    return pl.ds(pl.multiple_of(index * size, size), size)


def greet(devices):
    barrier = pltpu.get_barrier_semaphore()
    for device in devices:
        pl.semaphore_signal(barrier, inc=1, device_id=device, device_id_type=MESH_ID)
    pl.semaphore_wait(barrier, len(devices))


def turn(value, cosine, sine):
    return value * cosine + pltpu.roll(value, HEAD_DIM // 2, 1) * sine


def frequencies():
    i = np.arange(HEAD_DIM // 2, dtype=np.float32)
    freq = (theta_base ** (-(i * 2.0) / HEAD_DIM)).astype(np.float32)
    return jnp.asarray(np.concatenate([freq, freq])[None, :])


def front_kernel(
    tok_ref,
    gain_one_ref,
    gain_two_ref,
    freq_ref,
    routes_ref,
    gates_ref,
    order_ref,
    attn_hbm,
    experts_hbm,
    cot_hbm,
    xn_ref,
    q_ref,
    kv_ref,
    mixed_ref,
    res_ref,
    wl_ref,
    wa_hbm,
    w_hbm,
    x_hbm,
    dy_hbm,
    raw,
    pieces,
    wa,
    part,
    part_in,
    low_half,
    send,
    recv,
    local,
):
    f, z, c = place()
    fx, fy, fd = plane_peers(f)
    count, width = tok_ref.shape
    half = count // 2
    shard = attn_hbm.shape[0]
    cut = shard // 2
    in_cols = (QUERY_PER_GROUP + 2) * HEAD_DIM
    ins = pl.ds(0, in_cols)
    outs = pl.ds(in_cols, attn_hbm.shape[1] - in_cols)

    def at(fsdp=f, ctx=z, tp=c):
        return {"fsdp": fsdp, "ctx": ctx, "tp": tp}

    def remote(src, dst, k, device):
        return pltpu.make_async_remote_copy(
            src_ref=src,
            dst_ref=dst,
            send_sem=send.at[k],
            recv_sem=recv.at[k],
            device_id=device,
            device_id_type=MESH_ID,
        )

    plane = [at(fx), at(fy), at(fd)]
    rel = [fx, fy, fd]
    line = [at(ctx=lax.rem(z + s, 4)) for s in range(1, 4)]
    sibling = at(tp=1 - c)
    mine = rows_of(f, shard)
    load = pltpu.make_async_copy(experts_hbm, raw, local.at[6])
    load.start()
    greet(plane + line + [sibling])

    owned = pltpu.make_async_copy(attn_hbm, wa.at[mine], local.at[0])
    owned.start()
    in_x = remote(attn_hbm.at[:, ins], wa.at[mine, ins], 0, at(fx))
    in_y = remote(attn_hbm.at[:, ins], wa.at[mine, ins], 1, at(fy))
    in_x.start()
    in_y.start()

    rank = jnp.broadcast_to(order_ref[...].astype(jnp.float32), (count, count))
    ahead = jnp.where(rank.T < rank, 1.0, 0.0).astype(jnp.bfloat16)
    expert = lax.broadcasted_iota(jnp.int32, (128, count), 0)
    member = jnp.zeros((128, count), jnp.float32)
    gate = jnp.zeros((128, count), jnp.float32)
    for j in range(TOP):
        hit = jnp.broadcast_to(routes_ref[j : j + 1, :], (128, count)) == expert
        member = jnp.where(hit, 1.0, member)
        gate = jnp.where(hit, jnp.broadcast_to(gates_ref[j : j + 1, :], (128, count)), gate)
    slots = dot_f32(member.astype(jnp.bfloat16), ahead)
    gate = jnp.where(slots < CAP - 0.5, gate, 0.0)
    wl_ref[f] = gate[:EXPERTS]
    gate_copies = [remote(wl_ref.at[f], wl_ref.at[f], 2 + i, plane[i]) for i in range(3)]
    for copy in gate_copies:
        copy.start()

    own_dy = [
        pltpu.make_async_copy(
            cot_hbm.at[pl.ds(i * half, half)], dy_hbm.at[i, f], local.at[2 + i]
        )
        for i in range(2)
    ]
    for copy in own_dy:
        copy.start()

    row = lax.broadcasted_iota(jnp.int32, (128, 128), 0)
    column = lax.broadcasted_iota(jnp.int32, (128, 128), 1)
    owner = jnp.where(row < 64, jnp.where(row < 32, f, fx), jnp.where(row < 96, fy, fd))
    source = (row % 16) * 8 + owner * 2 + (row // 16) % 2
    order = jnp.where(source == column, 1.0, 0.0).astype(jnp.bfloat16)

    def split(m):
        def body(k, _):
            rows = pl.ds(pl.multiple_of(k * 16, 16), 16)
            block = raw[rows, m].reshape(128, raw.shape[3])
            moved = dot_f32(order, block).astype(jnp.bfloat16)
            pieces[:, m, rows, :] = moved.reshape(8, 16, raw.shape[3])
            return 0

        lax.fori_loop(0, shard // 16, body, 0)

    cut_rows = shard // 4
    from_rows = rows_of(z, cut_rows)
    to_rows = rows_of(4 * f + z, cut_rows)

    def quarter(m, i):
        return remote(
            pieces.at[pl.ds(2 * (i + 1), 2), m, from_rows],
            w_hbm.at[:, m, to_rows, :],
            37 + 3 * m + i,
            plane[i],
        )

    def hand_on(m, i):
        quarters[3 * m + i].wait_recv()
        here = w_hbm.at[:, m, rows_of(4 * rel[i] + z, cut_rows), :]
        copies = [remote(here, here, 43 + 9 * m + 3 * i + s, line[s]) for s in range(3)]
        for copy in copies:
            copy.start()
        return copies

    load.wait()
    split(0)
    quarters = [quarter(0, i) for i in range(3)]
    for copy in quarters:
        copy.start()

    tok = tok_ref[...].astype(jnp.float32)
    inv = lax.rsqrt(jnp.mean(tok * tok, axis=-1, keepdims=True) + eps)
    xn_ref[...] = (tok * inv * gain_one_ref[...]).astype(jnp.bfloat16)
    position = z * count + lax.broadcasted_iota(jnp.int32, (count, HEAD_DIM), 0)
    angle = position.astype(jnp.float32) * freq_ref[...]
    cosine = jnp.cos(angle)
    lane = lax.broadcasted_iota(jnp.int32, (count, HEAD_DIM), 1)
    sine = jnp.where(lane < HEAD_DIM // 2, -jnp.sin(angle), jnp.sin(angle))

    top, low = rows_of(2 * fx, cut), rows_of(2 * fy + 1, cut)
    in_x.wait_recv()
    in_xy = remote(wa.at[top, ins], wa.at[top, ins], 5, at(fy))
    in_xy.start()
    in_y.wait_recv()
    in_yx = remote(wa.at[low, ins], wa.at[low, ins], 6, at(fx))
    in_yx.start()
    out_x = remote(attn_hbm.at[:, outs], wa.at[mine, outs], 7, at(fx))
    out_y = remote(attn_hbm.at[:, outs], wa.at[mine, outs], 8, at(fy))
    split(1)
    quarters += [quarter(1, i) for i in range(3)]
    for copy in quarters[3:]:
        copy.start()
    out_x.start()
    out_y.start()
    handed = hand_on(0, 0) + hand_on(0, 1)
    split(2)
    own_w = pltpu.make_async_copy(pieces.at[pl.ds(0, 2)], w_hbm.at[:, :, mine, :], local.at[1])
    own_w.start()
    owned.wait()
    in_xy.wait_recv()
    in_yx.wait_recv()

    normed = xn_ref[...]
    for h in range(QUERY_PER_GROUP + 2):
        cols = pl.ds(h * HEAD_DIM, HEAD_DIM)
        if h % 2 == 0:
            pair = dot_f32(normed, wa[:, pl.ds(h * HEAD_DIM, 2 * HEAD_DIM)])
        value = pair[:, (h % 2) * HEAD_DIM : (h % 2 + 1) * HEAD_DIM]
        if h <= QUERY_PER_GROUP:
            value = turn(value, cosine, sine)
        if h < QUERY_PER_GROUP:
            q_ref[:, cols] = value.astype(jnp.bfloat16)
        else:
            kv_ref[0, :, pl.ds((h - QUERY_PER_GROUP) * HEAD_DIM, HEAD_DIM)] = value.astype(
                jnp.bfloat16
            )
    kv_copies = [remote(kv_ref.at[0], kv_ref.at[s], 8 + s, line[s - 1]) for s in range(1, 4)]
    for s in range(1, 4):

        @pl.when(z + s < 4)
        def _(s=s):
            kv_copies[s - 1].start()

        @pl.when(z < s)
        def _(s=s):
            kv_ref[s] = jnp.zeros(kv_ref.shape[1:], jnp.bfloat16)

    handed += hand_on(0, 2)
    out_x.wait_recv()
    out_xy = remote(wa.at[top, outs], wa.at[top, outs], 12, at(fy))
    out_xy.start()
    out_y.wait_recv()
    out_yx = remote(wa.at[low, outs], wa.at[low, outs], 13, at(fx))
    out_yx.start()

    w_copies = [
        remote(pieces.at[pl.ds(2 * (i + 1), 2), 2], w_hbm.at[:, 2, mine, :], 14 + i, plane[i])
        for i in range(3)
    ]
    for copy in w_copies:
        copy.start()
    dy_copies = [
        remote(cot_hbm.at[rows_of(c, half)], dy_hbm.at[c, f], 23 + i, plane[i]) for i in range(3)
    ]
    for copy in dy_copies:
        copy.start()
    for i in range(3):
        handed += hand_on(1, i)

    for s in range(1, 4):

        @pl.when(z >= s)
        def _(s=s):
            kv_copies[s - 1].wait_recv()

    keys = kv_ref[:, :, pl.ds(0, HEAD_DIM)].reshape(4 * count, HEAD_DIM)
    vals = kv_ref[:, :, pl.ds(HEAD_DIM, HEAD_DIM)].reshape(4 * count, HEAD_DIM)
    for g in range(QUERY_PER_GROUP):
        cols = pl.ds(g * HEAD_DIM, HEAD_DIM)
        probs = block_probs(z, keys, q_ref[:, cols]).astype(jnp.bfloat16)
        mixed_ref[:, cols] = dot_f32(probs, vals, TN).astype(jnp.bfloat16)

    out_xy.wait_recv()
    out_yx.wait_recv()
    store_wa = pltpu.make_async_copy(wa, wa_hbm, local.at[4])
    store_wa.start()
    for s in range(width // 256):
        cols = pl.ds(s * 256, 256)
        part[:, cols] = dot_f32(mixed_ref[...], wa[cols, outs], NT)
    swap = remote(part.at[rows_of(1 - c, half)], part_in, 26, sibling)
    swap.start()
    swap.wait_recv()
    my_rows = rows_of(c, half)
    residual = tok_ref[my_rows, :].astype(jnp.float32) + (part[my_rows, :] + part_in[...])
    res_ref[...] = residual
    inv = lax.rsqrt(jnp.mean(residual * residual, axis=-1, keepdims=True) + eps)
    low_half[...] = (residual * inv * gain_two_ref[...]).astype(jnp.bfloat16)
    own_x = pltpu.make_async_copy(low_half, x_hbm.at[c, f], local.at[5])
    own_x.start()
    x_copies = [remote(low_half, x_hbm.at[c, f], 27 + i, plane[i]) for i in range(3)]
    for copy in x_copies:
        copy.start()
    sib_x = [remote(low_half, x_hbm.at[c, f], 30, sibling)]
    sib_x[0].start()

    sib_dy = []
    for i in range(3):
        dy_copies[i].wait_recv()
        sib_dy.append(remote(dy_hbm.at[c, rel[i]], dy_hbm.at[c, rel[i]], 31 + i, sibling))
        sib_dy[i].start()
    for i in range(3):
        x_copies[i].wait_recv()
        sib_x.append(remote(x_hbm.at[c, rel[i]], x_hbm.at[c, rel[i]], 34 + i, sibling))
        sib_x[i + 1].start()

    for copy in w_copies + gate_copies + handed + sib_dy + sib_x:
        copy.wait_recv()
    for s in range(1, 4):

        @pl.when(z + s < 4)
        def _(s=s):
            kv_copies[s - 1].wait_send()

    for copy in [in_x, in_y, in_xy, in_yx, out_x, out_y, out_xy, out_yx, swap]:
        copy.wait_send()
    for copy in w_copies + quarters + handed + gate_copies + dy_copies + x_copies + sib_dy + sib_x:
        copy.wait_send()
    for copy in [own_w, own_x, store_wa] + own_dy:
        copy.wait()


def front(tok, gain_one, gain_two, routes, gates, order, attn_own, weights, cot):
    count, width = tok.shape
    half = count // 2
    shard, columns = attn_own.shape
    experts, hidden = EXPERTS // 4, weights.shape[3]
    vmem, hbm = pl.BlockSpec(memory_space=pltpu.VMEM), pl.BlockSpec(memory_space=pl.ANY)
    bf16, f32 = jnp.bfloat16, jnp.float32
    shape = jax.ShapeDtypeStruct
    return pl.pallas_call(
        front_kernel,
        in_specs=[vmem] * 7 + [hbm] * 3,
        out_specs=[vmem] * 6 + [hbm] * 4,
        out_shape=[
            shape((count, width), bf16),
            shape((count, QUERY_PER_GROUP * HEAD_DIM), bf16),
            shape((4, count, 2 * HEAD_DIM), bf16),
            shape((count, QUERY_PER_GROUP * HEAD_DIM), bf16),
            shape((half, width), f32),
            shape((4, EXPERTS, count), f32),
            shape((4 * shard, columns), bf16),
            shape((experts, 3, 4 * shard, hidden), bf16),
            shape((2, 4, half, width), bf16),
            shape((2, 4, half, width), bf16),
        ],
        scratch_shapes=[
            pltpu.VMEM(weights.shape, bf16),
            pltpu.VMEM((EXPERTS, 3, shard, hidden), bf16),
            pltpu.VMEM((4 * shard, columns), bf16),
            pltpu.VMEM((count, width), f32),
            pltpu.VMEM((half, width), f32),
            pltpu.VMEM((half, width), bf16),
            pltpu.SemaphoreType.DMA((61,)),
            pltpu.SemaphoreType.DMA((61,)),
            pltpu.SemaphoreType.DMA((7,)),
        ],
        compiler_params=pltpu.CompilerParams(
            collective_id=0, has_side_effects=True, vmem_limit_bytes=48 * MIB
        ),
        name="front",
    )(tok, gain_one, gain_two, frequencies(), routes, gates, order, attn_own, weights, cot)


def moe_kernel(
    x_hbm, dy_hbm, w_hbm, wl_ref, ge_hbm, dn_ref, mo_ref, gg_ref, x, dy, wgu, wd, gu, hid, ge, scales, sem, out_sem
):
    f = lax.axis_index("fsdp")
    tokens, width = x.shape
    hidden = w_hbm.shape[3]
    half = tokens // 8
    tile = 2 * half
    own = w_hbm.shape[0]
    loads = [pltpu.make_async_copy(x_hbm, x, sem.at[0])]
    for e in range(own):
        for m in range(2):
            loads.append(
                pltpu.make_async_copy(
                    w_hbm.at[e, m], wgu.at[:, pl.ds((2 * e + m) * hidden, hidden)], sem.at[1 + 3 * e + m]
                )
            )
    loads.append(pltpu.make_async_copy(dy_hbm, dy, sem.at[7]))
    for e in range(own):
        loads.append(
            pltpu.make_async_copy(w_hbm.at[e, 2], wd.at[:, pl.ds(e * hidden, hidden)], sem.at[3 + 3 * e])
        )
    for copy in loads:
        copy.start()
    lane = lax.broadcasted_iota(jnp.int32, (half, 128), 1)
    for b in range(8):
        rows = wl_ref[b % 4, :, pl.ds((b // 4) * half, half)]
        rows = jnp.concatenate([rows, jnp.zeros((128 - EXPERTS, half), jnp.float32)], axis=0)
        scales[pl.ds(b * half, half), :] = rows.T
    for copy in loads:
        copy.wait()

    lanes = lax.broadcasted_iota(jnp.int32, (tile, 128), 1)

    def step(i, _):
        rows = pl.ds(pl.multiple_of(i * tile, tile), tile)
        acts = dot_f32(x[rows, :], wgu[...])
        plain = dot_f32(dy[rows, :], wd[...])
        table = scales[rows, :]
        sums = jnp.zeros((tile, 128), jnp.float32)
        for e in range(own):
            gate_act = acts[:, 2 * e * hidden : (2 * e + 1) * hidden]
            up_act = acts[:, (2 * e + 1) * hidden : (2 * e + 2) * hidden]
            d_plain = plain[:, e * hidden : (e + 1) * hidden]
            here = lanes == own * f + e
            scale = jnp.sum(jnp.where(here, table, 0.0), axis=1, keepdims=True)
            sigmoid = 1.0 / (1.0 + jnp.exp(-gate_act))
            active = gate_act * sigmoid
            act = active * up_act
            total = jnp.sum(act * d_plain, axis=1, keepdims=True)
            sums = jnp.where(here, jnp.where(scale != 0.0, total, 0.0), sums)
            d_hidden = d_plain * scale
            slope = sigmoid * (1.0 + gate_act * (1.0 - sigmoid))
            hid[rows, pl.ds(e * hidden, hidden)] = (act * scale).astype(jnp.bfloat16)
            gu[rows, pl.ds(2 * e * hidden, hidden)] = (d_hidden * up_act * slope).astype(jnp.bfloat16)
            gu[rows, pl.ds((2 * e + 1) * hidden, hidden)] = (d_hidden * active).astype(jnp.bfloat16)
        gg_ref[rows, :] = sums
        return 0

    lax.fori_loop(0, tokens // tile, step, 0)

    block = width // 4

    def grad_step(s, _):
        cols = pl.ds(pl.multiple_of(s * block, 128), block)
        inner = dot_f32(x[:, cols], gu[...], TN).astype(jnp.bfloat16)
        outer = dot_f32(dy[:, cols], hid[...], TN).astype(jnp.bfloat16)
        for e in range(own):
            for m in range(2):
                k = 2 * e + m
                ge[3 * e + m, cols, :] = inner[:, k * hidden : (k + 1) * hidden]
            ge[3 * e + 2, cols, :] = outer[:, e * hidden : (e + 1) * hidden]
        return 0

    lax.fori_loop(0, 4, grad_step, 0)
    store = pltpu.make_async_copy(ge, ge_hbm, out_sem)
    store.start()

    def down_step(i, _):
        rows = pl.ds(pl.multiple_of(i * tile, tile), tile)
        dn_ref[rows, :] = dot_f32(gu[rows, :], wgu[...], NT).astype(jnp.bfloat16)
        mo_ref[rows, :] = dot_f32(hid[rows, :], wd[...], NT).astype(jnp.bfloat16)
        return 0

    lax.fori_loop(0, tokens // tile, down_step, 0)
    store.wait()


def moe_layer(x, dy, weights, gate_table):
    tokens, width = x.shape
    own, _, _, hidden = weights.shape
    vmem, hbm = pl.BlockSpec(memory_space=pltpu.VMEM), pl.BlockSpec(memory_space=pl.ANY)
    bf16, f32 = jnp.bfloat16, jnp.float32
    shape = jax.ShapeDtypeStruct
    return pl.pallas_call(
        moe_kernel,
        in_specs=[hbm] * 3 + [vmem],
        out_specs=[hbm, vmem, vmem, vmem],
        out_shape=[
            shape((3 * own, width, hidden), bf16),
            shape((tokens, width), bf16),
            shape((tokens, width), bf16),
            shape((tokens, 128), f32),
        ],
        scratch_shapes=[
            pltpu.VMEM((tokens, width), bf16),
            pltpu.VMEM((tokens, width), bf16),
            pltpu.VMEM((width, 2 * own * hidden), bf16),
            pltpu.VMEM((width, own * hidden), bf16),
            pltpu.VMEM((tokens, 2 * own * hidden), bf16),
            pltpu.VMEM((tokens, own * hidden), bf16),
            pltpu.VMEM((3 * own, width, hidden), bf16),
            pltpu.VMEM((tokens, 128), f32),
            pltpu.SemaphoreType.DMA((8,)),
            pltpu.SemaphoreType.DMA,
        ],
        compiler_params=pltpu.CompilerParams(vmem_limit_bytes=58 * MIB),
        name="experts",
    )(x, dy, weights, gate_table)


def rear_kernel(
    res_ref,
    xn_ref,
    q_ref,
    kv_ref,
    mixed_ref,
    gain_one_ref,
    gain_two_ref,
    freq_ref,
    tok_hbm,
    cot_hbm,
    ge_hbm,
    dn_hbm,
    mo_hbm,
    gg_hbm,
    wa_hbm,
    layer_ref,
    tokgrad_ref,
    gains_ref,
    gate_ref,
    attn_hbm,
    fin_hbm,
    ge,
    r1,
    r2,
    wa,
    dn_own,
    dn_in,
    dn_got,
    mo_own,
    mo_in,
    mo_got,
    gg_own,
    gg_in,
    gg_sum,
    gg_got,
    dres,
    dattn,
    dmixed,
    dproj,
    dkv,
    dkv_low,
    dkv_got,
    d1,
    d1_low,
    d1_in,
    ga,
    ra,
    a1,
    a2,
    gacc,
    gin,
    tok_half,
    cot_half,
    send,
    recv,
    local,
    z_out,
    z_across,
    z_back,
    z_r1,
    z_r2,
    f_out,
    f_in,
):
    f, z, c = place()
    fx, fy, fd = plane_peers(f)
    rel = [f, fx, fy, fd]
    f32, bf16 = jnp.float32, jnp.bfloat16
    count, width = tok_hbm.shape
    half = count // 2
    shard = attn_hbm.shape[0]
    in_cols = (QUERY_PER_GROUP + 2) * HEAD_DIM
    q_cols = QUERY_PER_GROUP * HEAD_DIM
    ins = pl.ds(0, in_cols)
    outs = pl.ds(in_cols, attn_hbm.shape[1] - in_cols)
    scale = HEAD_DIM ** (-0.5)

    def at(fsdp=f, ctx=z, tp=c):
        return {"fsdp": fsdp, "ctx": ctx, "tp": tp}

    def copy_to(src, dst, send_sem, recv_sem, device):
        return pltpu.make_async_remote_copy(
            src_ref=src,
            dst_ref=dst,
            send_sem=send_sem,
            recv_sem=recv_sem,
            device_id=device,
            device_id_type=MESH_ID,
        )

    def remote(src, dst, k, device):
        return copy_to(src, dst, send.at[k], recv.at[k], device)

    plane = [at(fx), at(fy), at(fd)]
    line = [at(ctx=lax.rem(z + s, 4)) for s in range(1, 4)]
    sibling = at(tp=1 - c)
    partner = at(ctx=z + 1 - 2 * lax.rem(z, 2))
    opposite = at(ctx=3 - z)
    inner = (z == 1) | (z == 2)
    outer = (z == 0) | (z == 3)

    loads = [pltpu.make_async_copy(ge_hbm, ge, local.at[0])]
    loads.append(pltpu.make_async_copy(dn_hbm.at[c], dn_own, local.at[1]))
    loads.append(pltpu.make_async_copy(gg_hbm.at[c], gg_own, local.at[2]))
    loads.append(pltpu.make_async_copy(wa_hbm, wa, local.at[3]))
    loads.append(pltpu.make_async_copy(mo_hbm.at[c], mo_own, local.at[4]))
    loads.append(pltpu.make_async_copy(tok_hbm.at[rows_of(c, half)], tok_half, local.at[5]))
    loads.append(pltpu.make_async_copy(cot_hbm.at[rows_of(c, half)], cot_half, local.at[6]))
    for copy in loads:
        copy.start()
    greet(plane + line + [sibling])
    dn_swap = remote(dn_hbm.at[1 - c], dn_in, 0, sibling)
    gg_swap = remote(gg_hbm.at[1 - c], gg_in, 1, sibling)
    mo_swap = remote(mo_hbm.at[1 - c], mo_in, 2, sibling)
    dn_swap.start()
    gg_swap.start()
    mo_swap.start()

    mats = ge.shape[0]
    n_expert = 4 * mats
    n_attn = 4
    n_all = n_expert + n_attn
    a_rows = shard // n_attn

    def chunk(k):
        if k < n_expert:
            j, r = k // 4, k % 4
            rows = rows_of(rel[r], shard)
            return ge.at[j, rows], r1.at[j, rows], r2.at[j, rows]
        rows = pl.ds((k - n_expert) * a_rows, a_rows)
        return ra.at[0, rows], a1.at[rows], a2.at[rows]

    def add_into(dst, left, right):
        size = dst.shape[0] // 6

        def body(i, _):
            rows = pl.ds(pl.multiple_of(i * size, size), size)
            dst[rows, :] = (left[rows, :].astype(f32) + right[rows, :].astype(f32)).astype(bf16)
            return 0

        lax.fori_loop(0, 6, body, 0)

    def first(k):
        own, one, _ = chunk(k)
        return copy_to(own, one, z_out.at[k], z_r1.at[k], partner)

    def across(k):
        own, _, two = chunk(k)
        return copy_to(own, two, z_across.at[k], z_r2.at[k], opposite)

    def back(k):
        _, one, _ = chunk(k)
        return copy_to(one, one, z_back.at[k], z_r1.at[k], partner)

    def final(k):
        _, one, _ = chunk(k)
        j, r = k // 4, k % 4
        if r == 0:
            return pltpu.make_async_copy(one, fin_hbm.at[0, j], f_out.at[k])
        return copy_to(one, fin_hbm.at[r, j], f_out.at[k], f_in.at[k], plane[r - 1])

    def z_step(i):
        if i < n_all:

            @pl.when(outer)
            def _():
                if i >= 2:
                    first(i - 2).wait_send()
                first(i).start()

        if 1 <= i <= n_all:
            k = i - 1

            @pl.when(inner)
            def _():
                own, one, _ = chunk(k)
                first(k).wait_recv()
                add_into(own, own, one)
                across(k).start()

        if 2 <= i <= n_all + 1:
            k = i - 2

            @pl.when(inner)
            def _():
                own, one, two = chunk(k)
                across(k).wait_recv()
                add_into(one, own, two)
                back(k).start()
                if k < n_expert:
                    final(k).start()

        if 3 <= i <= n_all + 2:
            k = i - 3

            @pl.when(outer)
            def _():
                back(k).wait_recv()
                if k < n_expert:
                    final(k).start()

    loads[0].wait()
    z_step(0)
    loads[5].wait()
    loads[6].wait()

    loads[1].wait()
    loads[2].wait()
    gg_swap.wait_recv()
    gg_sum[...] = gg_own[...] + gg_in[...]
    dn_swap.wait_recv()
    for g in range(4):
        dn_own[g] = (dn_own[g].astype(f32) + dn_in[g].astype(f32)).astype(bf16)
    dn_out = [remote(dn_own.at[rel[i + 1]], dn_got.at[i], 3 + i, plane[i]) for i in range(3)]
    gg_out = [remote(gg_sum.at[rel[i + 1]], gg_got.at[i], 6 + i, plane[i]) for i in range(3)]
    for copy in dn_out + gg_out:
        copy.start()
    z_step(1)
    loads[4].wait()
    mo_swap.wait_recv()
    for g in range(4):
        mo_own[g] = (mo_own[g].astype(f32) + mo_in[g].astype(f32)).astype(bf16)
    mo_out = [remote(mo_own.at[rel[i + 1]], mo_got.at[i], 9 + i, plane[i]) for i in range(3)]
    for copy in mo_out:
        copy.start()
    z_step(2)
    for copy in dn_out:
        copy.wait_recv()
    d_two = dn_own[f].astype(f32)
    for i in range(3):
        d_two = d_two + dn_got[i].astype(f32)
    residual = res_ref[...]
    inv = lax.rsqrt(jnp.mean(residual * residual, axis=-1, keepdims=True) + eps)
    scaled = d_two * gain_two_ref[...]
    inside = jnp.mean(scaled * residual, axis=-1, keepdims=True)
    d_norm = inv * scaled - residual * (inv * inv * inv * inside)
    gacc[0] = jnp.zeros(gacc.shape[1:], f32)
    gacc[0, 1:2, :] = jnp.sum(d_two * residual * inv, axis=0, keepdims=True)
    my_rows = rows_of(c, half)
    d_res = cot_half[...].astype(f32) + d_norm
    dres[...] = d_res
    dattn[my_rows, :] = d_res.astype(bf16)
    da_swap = remote(dattn.at[my_rows], dattn.at[my_rows], 12, sibling)
    da_swap.start()
    loads[3].wait()
    z_step(3)
    da_swap.wait_recv()
    dmixed[...] = dot_f32(dattn[...], wa[:, outs]).astype(bf16)
    z_step(4)

    position = z * count + lax.broadcasted_iota(jnp.int32, (count, HEAD_DIM), 0)
    angle = position.astype(f32) * freq_ref[...]
    cosine = jnp.cos(angle)
    lane = lax.broadcasted_iota(jnp.int32, (count, HEAD_DIM), 1)
    sine = jnp.where(lane < HEAD_DIM // 2, jnp.sin(angle), -jnp.sin(angle))
    keys = kv_ref[:, :, pl.ds(0, HEAD_DIM)].reshape(4 * count, HEAD_DIM)
    vals = kv_ref[:, :, pl.ds(HEAD_DIM, HEAD_DIM)].reshape(4 * count, HEAD_DIM)
    key_cols, val_cols = pl.ds(0, HEAD_DIM), pl.ds(HEAD_DIM, HEAD_DIM)
    dkv[...] = jnp.zeros_like(dkv)
    for g in range(QUERY_PER_GROUP):
        cols = pl.ds(g * HEAD_DIM, HEAD_DIM)
        query = q_ref[:, cols]
        d_mix = dmixed[:, cols]
        probs = block_probs(z, keys, query)
        d_probs = dot_f32(vals, d_mix, NT)
        inside = jnp.sum(probs * d_probs, axis=0, keepdims=True)
        d_scores = (probs * (d_probs - inside)).astype(bf16)
        d_query = dot_f32(d_scores, keys, TN) * scale
        dproj[:, cols] = turn(d_query, cosine, sine).astype(bf16)
        dkv[:, key_cols] += dot_f32(d_scores, query) * scale
        dkv[:, val_cols] += dot_f32(probs.astype(bf16), d_mix)
        if g % 2 == 1:
            z_step(5 + g // 2)
    dkv_low[...] = dkv[...].reshape(dkv_low.shape).astype(bf16)
    dkv_out = [
        remote(dkv_low.at[s], dkv_got.at[s - 1], 12 + s, at(ctx=lax.rem(z + 4 - s, 4)))
        for s in range(1, 4)
    ]
    for s in range(1, 4):

        @pl.when(z >= s)
        def _(s=s):
            dkv_out[s - 1].start()

    def weight_grad(left, right, cols):
        def body(i, _):
            rows = pl.ds(pl.multiple_of(i * 256, 256), 256)
            ga[rows, cols] = dot_f32(left[:, rows], right, TN).astype(bf16)
            return 0

        lax.fori_loop(0, width // 256, body, 0)

    def send_grad(cols, k):
        copies = [
            remote(ga.at[rows_of(rel[i + 1], shard), cols], ra.at[i, :, cols], k + i, plane[i])
            for i in range(3)
        ]
        for copy in copies:
            copy.start()
        return copies

    weight_grad(dattn, mixed_ref[...], outs)
    ga_copies = send_grad(outs, 16)
    z_step(8)
    q_part = pl.ds(0, q_cols)
    weight_grad(xn_ref, dproj[:, q_part], q_part)
    ga_copies += send_grad(q_part, 19)
    z_step(9)
    for s in range(1, 4):

        @pl.when(z + s < 4)
        def _(s=s):
            dkv_out[s - 1].wait_recv()
            dkv[0:count, :] += dkv_got[s - 1].astype(f32)

    kv_part = pl.ds(q_cols, 2 * HEAD_DIM)
    dproj[:, pl.ds(q_cols, HEAD_DIM)] = turn(dkv[0:count, key_cols], cosine, sine).astype(bf16)
    dproj[:, pl.ds(q_cols + HEAD_DIM, HEAD_DIM)] = dkv[0:count, val_cols].astype(bf16)
    weight_grad(xn_ref, dproj[:, kv_part], kv_part)
    ga_copies += send_grad(kv_part, 22)
    z_step(10)

    for s in range(width // 256):
        rows = pl.ds(s * 256, 256)
        d1[:, rows] = dot_f32(dproj[my_rows, :], wa[rows, ins], NT)
        d1_low[:, rows] = dot_f32(dproj[rows_of(1 - c, half), :], wa[rows, ins], NT).astype(bf16)
    d1_swap = remote(d1_low, d1_in, 25, sibling)
    d1_swap.start()
    z_step(11)
    d1_swap.wait_recv()
    d_one = d1[...] + d1_in[...].astype(f32)
    tok = tok_half[...].astype(f32)
    inv = lax.rsqrt(jnp.mean(tok * tok, axis=-1, keepdims=True) + eps)
    scaled = d_one * gain_one_ref[...]
    inside = jnp.mean(scaled * tok, axis=-1, keepdims=True)
    d_norm = inv * scaled - tok * (inv * inv * inv * inside)
    gacc[0, 0:1, :] = jnp.sum(d_one * tok * inv, axis=0, keepdims=True)
    tokgrad_ref[my_rows, :] = (dres[...] + d_norm).astype(bf16)
    tg_swap = remote(tokgrad_ref.at[my_rows], tokgrad_ref.at[my_rows], 26, sibling)
    tg_swap.start()
    z_step(12)

    for copy in mo_out + gg_out:
        copy.wait_recv()
    moe = mo_own[f].astype(f32)
    gates = gg_sum[f]
    for i in range(3):
        moe = moe + mo_got[i].astype(f32)
        gates = gates + gg_got[i]
    layer_ref[my_rows, :] = (res_ref[...] + moe).astype(bf16)
    gate_ref[my_rows, :] = gates
    lo_swap = remote(layer_ref.at[my_rows], layer_ref.at[my_rows], 27, sibling)
    gt_swap = remote(gate_ref.at[my_rows], gate_ref.at[my_rows], 28, sibling)
    lo_swap.start()
    gt_swap.start()
    z_step(13)

    stages = [sibling, at(fx), at(fy), partner, at(ctx=lax.rem(z + 2, 4))]
    gain_copies = [remote(gacc.at[i], gin.at[i], 29 + i, stages[i]) for i in range(5)]
    for i in range(5):
        gain_copies[i].start()
        z_step(14 + i)
        gain_copies[i].wait_recv()
        total = gacc[i] + gin[i]
        if i < 4:
            gacc[i + 1] = total
        else:
            gains_ref[...] = total

    for i in range(19, n_expert):
        z_step(i)
    for copy in ga_copies:
        copy.wait_recv()

    def attn_sum(i, _):
        size = shard // 8
        here = pl.ds(pl.multiple_of(i * size, size), size)
        total = ga[pl.ds(pl.multiple_of(f * shard + i * size, size), size), :].astype(f32)
        for r in range(3):
            total = total + ra[r, here, :].astype(f32)
        ra[0, here, :] = total.astype(bf16)
        return 0

    lax.fori_loop(0, 8, attn_sum, 0)
    for i in range(n_expert, n_all + 3):
        z_step(i)
    store = pltpu.make_async_copy(a1, attn_hbm, local.at[0])
    store.start()

    store.wait()
    for k in range(n_all):

        @pl.when(outer)
        def _(k=k):
            if k >= n_all - 2:
                first(k).wait_send()

        @pl.when(inner)
        def _(k=k):
            across(k).wait_send()
            back(k).wait_send()

    for k in range(n_expert):
        if k % 4 == 0:
            final(k).wait()
        else:
            final(k).wait_send()
            final(k).wait_recv()
    for s in range(1, 4):

        @pl.when(z >= s)
        def _(s=s):
            dkv_out[s - 1].wait_send()

    for copy in [tg_swap, lo_swap, gt_swap]:
        copy.wait_recv()
    swaps = [dn_swap, gg_swap, mo_swap, da_swap, d1_swap, tg_swap, lo_swap, gt_swap]
    for copy in swaps + dn_out + gg_out + mo_out + ga_copies + gain_copies:
        copy.wait_send()


def rear(tok, cot, res, xn, q, kv, mixed, gain_one, gain_two, ge, dn, mo, gg, wa):
    count, width = tok.shape
    half = count // 2
    columns = wa.shape[1]
    shard = width // 4
    mats, _, hidden = ge.shape
    q_cols = q.shape[1]
    vmem, hbm = pl.BlockSpec(memory_space=pltpu.VMEM), pl.BlockSpec(memory_space=pl.ANY)
    bf16, f32 = jnp.bfloat16, jnp.float32
    shape = jax.ShapeDtypeStruct
    dma = pltpu.SemaphoreType.DMA
    n_all = 4 * mats + 4
    return pl.pallas_call(
        rear_kernel,
        in_specs=[vmem] * 8 + [hbm] * 7,
        out_specs=[vmem] * 4 + [hbm] * 2,
        out_shape=[
            shape((count, width), bf16),
            shape((count, width), bf16),
            shape((8, width), f32),
            shape((count, 128), f32),
            shape((shard, columns), bf16),
            shape((4, mats, shard, hidden), bf16),
        ],
        scratch_shapes=[
            pltpu.VMEM((mats, width, hidden), bf16),
            pltpu.VMEM((mats, width, hidden), bf16),
            pltpu.VMEM((mats, width, hidden), bf16),
            pltpu.VMEM((width, columns), bf16),
            pltpu.VMEM((4, half, width), bf16),
            pltpu.VMEM((4, half, width), bf16),
            pltpu.VMEM((3, half, width), bf16),
            pltpu.VMEM((4, half, width), bf16),
            pltpu.VMEM((4, half, width), bf16),
            pltpu.VMEM((3, half, width), bf16),
            pltpu.VMEM((4, half, 128), f32),
            pltpu.VMEM((4, half, 128), f32),
            pltpu.VMEM((4, half, 128), f32),
            pltpu.VMEM((3, half, 128), f32),
            pltpu.VMEM((half, width), f32),
            pltpu.VMEM((count, width), bf16),
            pltpu.VMEM((count, q_cols), bf16),
            pltpu.VMEM((count, q_cols + 2 * HEAD_DIM), bf16),
            pltpu.VMEM((4 * count, 2 * HEAD_DIM), f32),
            pltpu.VMEM((4, count, 2 * HEAD_DIM), bf16),
            pltpu.VMEM((3, count, 2 * HEAD_DIM), bf16),
            pltpu.VMEM((half, width), f32),
            pltpu.VMEM((half, width), bf16),
            pltpu.VMEM((half, width), bf16),
            pltpu.VMEM((width, columns), bf16),
            pltpu.VMEM((3, shard, columns), bf16),
            pltpu.VMEM((shard, columns), bf16),
            pltpu.VMEM((shard, columns), bf16),
            pltpu.VMEM((5, 8, width), f32),
            pltpu.VMEM((5, 8, width), f32),
            pltpu.VMEM((half, width), bf16),
            pltpu.VMEM((half, width), bf16),
            dma((34,)),
            dma((34,)),
            dma((7,)),
            dma((n_all,)),
            dma((n_all,)),
            dma((n_all,)),
            dma((n_all,)),
            dma((n_all,)),
            dma((4 * mats,)),
            dma((4 * mats,)),
        ],
        compiler_params=pltpu.CompilerParams(
            collective_id=1, has_side_effects=True, vmem_limit_bytes=62 * MIB
        ),
        name="rear",
    )(res, xn, q, kv, mixed, gain_one, gain_two, frequencies(), tok, cot, ge, dn, mo, gg, wa)


def body_fast(
    tokens,
    attn_norm,
    attention_params,
    ffn_norm,
    expert_weights,
    gate_values,
    routes,
    slot_order,
    cotangent,
):
    sequence_count, block_len, model_width = tokens.shape
    count = sequence_count * block_len
    half = count // 2
    f = lax.axis_index("fsdp")
    shard, hidden = attention_params.shape[0], expert_weights.shape[3]
    tok = tokens.reshape(count, model_width)
    cot = cotangent.reshape(count, model_width)
    gain_one, gain_two = attn_norm[None, :], ffn_norm[None, :]
    route_rows = routes.reshape(count, TOP)
    normed, queries, kv, mixed, residual, gate_table, whole_attn, whole_expert, x, dy = front(
        tok,
        gain_one,
        gain_two,
        route_rows.T,
        gate_values.reshape(count, TOP).T,
        slot_order.reshape(1, count),
        attention_params[:, 0, :],
        jnp.transpose(expert_weights, (0, 2, 1, 3)),
        cot,
    )
    grads, d_normed, moe, gate_parts = moe_layer(
        x.reshape(8 * half, model_width), dy.reshape(8 * half, model_width), whole_expert, gate_table
    )
    layer_out, tokens_grad, gains, gate_rows, attn_grad, finals = rear(
        tok,
        cot,
        residual,
        normed,
        queries,
        kv,
        mixed,
        gain_one,
        gain_two,
        grads,
        d_normed.reshape(2, 4, half, model_width),
        moe.reshape(2, 4, half, model_width),
        gate_parts.reshape(2, 4, half, 128),
        whole_attn,
    )
    picked = route_rows[:, :, None] == jnp.arange(EXPERTS, dtype=jnp.int32)
    gate_grad = jnp.sum(jnp.where(picked, gate_rows[:, None, :EXPERTS], 0.0), axis=-1)
    finals = finals.reshape(EXPERTS, 3, shard, hidden)
    expert_grad = jnp.transpose(join_experts(finals, expert_order(f).T), (0, 2, 1, 3))
    return (
        layer_out.reshape(sequence_count, block_len, model_width),
        tokens_grad.reshape(sequence_count, block_len, model_width),
        attn_grad.astype(jnp.float32)[:, None, :],
        expert_grad,
        gains[0],
        gains[1],
        gate_grad.reshape(sequence_count, block_len, TOP),
    )


def solution(mesh):
    in_specs = (
        P("fsdp", "ctx", None),
        P(),
        P("fsdp", "tp", None),
        P(),
        P("fsdp", None, None, "tp"),
        P("fsdp", "ctx", None),
        P("fsdp", "ctx", None),
        P("fsdp", "ctx"),
        P("fsdp", "ctx", None),
    )
    out_specs = (
        P("fsdp", "ctx", None),
        P("fsdp", "ctx", None),
        P("fsdp", "tp", None),
        P("fsdp", None, None, "tp"),
        P(),
        P(),
        P("fsdp", "ctx", None),
    )
    four = mesh.shape["fsdp"] == 4 and mesh.shape["ctx"] == 4 and mesh.shape["tp"] == 2
    body_fn = body_fast if four else body
    return jax.shard_map(body_fn, mesh=mesh, in_specs=in_specs, out_specs=out_specs, check_vma=False)
```

```python
import jax
import jax.numpy as jnp
from jax import lax
import numpy as np
from jax.experimental import pallas as pl
from jax.experimental.pallas import tpu as pltpu
from jax.sharding import PartitionSpec as P

HEAD_DIM = 128
TOP = 4
EXPERTS = 8
QUERY_PER_GROUP = 6
CAP = 160


eps = 1e-06
theta_base = 1000000.0


def angle_tables(positions):
    frequency = theta_base ** (-(jnp.arange(HEAD_DIM // 2, dtype=jnp.float32) * 2.0) / HEAD_DIM)
    angles = positions.astype(jnp.float32)[:, None] * frequency[None, :]
    return (jnp.cos(angles), jnp.sin(angles))


def rotate(source, cosine_table, sine_table):
    half_size = source.shape[-1] // 2
    front_half = source[..., :half_size]
    back_half = source[..., half_size:]
    return jnp.concatenate(
        [
            front_half * cosine_table - back_half * sine_table,
            back_half * cosine_table + front_half * sine_table,
        ],
        axis=-1,
    )


def norm_back(source, inv_rms, gain_vec, upstream):
    scaled = upstream * gain_vec
    inner_sum = jnp.mean(scaled * source, axis=-1, keepdims=True)
    d_source = inv_rms * scaled - source * inv_rms * inv_rms * inv_rms * inner_sum
    return (d_source, jnp.sum(upstream * source * inv_rms, axis=0))


def slot_tables(route_rows, rank_rows):
    tok_count = route_rows.shape[0]
    inverse = (
        jnp.zeros((tok_count,), jnp.int32).at[rank_rows].set(jnp.arange(tok_count, dtype=jnp.int32))
    )
    ranked = route_rows[inverse].reshape(-1)
    onehot = (ranked[:, None] == jnp.arange(EXPERTS, dtype=jnp.int32)[None, :]).astype(jnp.int32)
    before = jnp.cumsum(onehot, axis=0) - onehot
    slot_ranked = jnp.sum(before * onehot, axis=1).reshape(tok_count, TOP)
    slots = slot_ranked[rank_rows]
    kept_pair = slots < CAP
    pair_slot = jnp.where(kept_pair, route_rows * CAP + slots, EXPERTS * CAP)
    owners = jnp.broadcast_to(jnp.arange(tok_count, dtype=jnp.int32)[:, None], (tok_count, TOP))
    slot_token = (
        jnp.full((EXPERTS * CAP,), tok_count, jnp.int32)
        .at[pair_slot.reshape(-1)]
        .set(owners.reshape(-1), mode="drop")
    )
    return (kept_pair, pair_slot, slot_token)


def attend_forward(queries, key_rows, value_rows, allowed):
    scores = jnp.einsum(
        "qhgd,khd->hgqk", queries, key_rows, preferred_element_type=jnp.float32
    ) * HEAD_DIM ** (-0.5)
    scores = jnp.where(allowed, scores, -1e30)
    row_max = jnp.max(scores, axis=-1, keepdims=True)
    expd = jnp.exp(scores - row_max)
    row_total = jnp.sum(expd, axis=-1, keepdims=True)
    attn_probs = (expd / row_total).astype(jnp.bfloat16)
    mixed_heads = jnp.einsum(
        "hgqk,khd->qhgd", attn_probs, value_rows, preferred_element_type=jnp.float32
    )
    return (mixed_heads.astype(jnp.bfloat16), row_max + jnp.log(row_total))


def attend_backward(queries, key_rows, value_rows, allowed, log_total, d_mixed):
    scores = jnp.einsum(
        "qhgd,khd->hgqk", queries, key_rows, preferred_element_type=jnp.float32
    ) * HEAD_DIM ** (-0.5)
    scores = jnp.where(allowed, scores, -1e30)
    attn_probs = jnp.exp(scores - log_total)
    low_probs = attn_probs.astype(jnp.bfloat16)
    d_probs = jnp.einsum("qhgd,khd->hgqk", d_mixed, value_rows, preferred_element_type=jnp.float32)
    inner_sum = jnp.sum(attn_probs * d_probs, axis=-1, keepdims=True)
    d_scores = (attn_probs * (d_probs - inner_sum)).astype(jnp.bfloat16)
    d_queries = jnp.einsum(
        "hgqk,khd->qhgd", d_scores, key_rows, preferred_element_type=jnp.float32
    ) * HEAD_DIM ** (-0.5)
    d_keys = jnp.einsum(
        "hgqk,qhgd->khd", d_scores, queries, preferred_element_type=jnp.float32
    ) * HEAD_DIM ** (-0.5)
    d_values = jnp.einsum("hgqk,qhgd->khd", low_probs, d_mixed, preferred_element_type=jnp.float32)
    return (d_queries, d_keys, d_values)


def body(
    tokens,
    attn_norm,
    attention_params,
    ffn_norm,
    expert_weights,
    gate_values,
    routes,
    slot_order,
    cotangent,
):
    sequence_count, block_len, model_width = tokens.shape
    tok_count = sequence_count * block_len
    kv_loc = attention_params.shape[1]
    input_columns = (QUERY_PER_GROUP + 2) * HEAD_DIM
    ctx_size = lax.axis_size("ctx")
    ctx_place = lax.axis_index("ctx")
    sequence_length = block_len * ctx_size
    whole_attn, whole_expert = (
        lax.all_gather(attention_params, "fsdp", axis=0, tiled=True),
        lax.all_gather(expert_weights, "fsdp", axis=0, tiled=True),
    )
    positions = ctx_place * block_len + jnp.arange(block_len, dtype=jnp.int32)
    cosine_table, sine_table = angle_tables(positions)
    cosine_table = jnp.tile(cosine_table, (sequence_count, 1))
    sine_table = jnp.tile(sine_table, (sequence_count, 1))
    cos_four = cosine_table[:, None, None, :]
    sin_four = sine_table[:, None, None, :]
    cos_three = cosine_table[:, None, :]
    sin_three = sine_table[:, None, :]
    allowed = (jnp.arange(sequence_length, dtype=jnp.int32) // block_len <= ctx_place)[
        None, None, None, :
    ]
    tok_float = tokens.reshape(tok_count, model_width).astype(jnp.float32)
    inv_one = lax.rsqrt(jnp.mean(tok_float * tok_float, axis=-1, keepdims=True) + eps)
    first_normed = (tok_float * inv_one * attn_norm).astype(jnp.bfloat16)
    projected_rows = jnp.einsum(
        "td,dhc->thc",
        first_normed,
        whole_attn[:, :, :input_columns],
        preferred_element_type=jnp.float32,
    ).reshape(tok_count, kv_loc, QUERY_PER_GROUP + 2, HEAD_DIM)
    queries = rotate(projected_rows[:, :, :QUERY_PER_GROUP], cos_four, sin_four).astype(
        jnp.bfloat16
    )
    key_rows = rotate(projected_rows[:, :, QUERY_PER_GROUP], cos_three, sin_three).astype(
        jnp.bfloat16
    )
    value_rows = projected_rows[:, :, QUERY_PER_GROUP + 1].astype(jnp.bfloat16)
    key_all, value_all = (
        lax.all_gather(
            key_rows.reshape(sequence_count, block_len, kv_loc, HEAD_DIM), "ctx", axis=1, tiled=True
        ),
        lax.all_gather(
            value_rows.reshape(sequence_count, block_len, kv_loc, HEAD_DIM),
            "ctx",
            axis=1,
            tiled=True,
        ),
    )
    query_seq = queries.reshape(sequence_count, block_len, kv_loc, QUERY_PER_GROUP, HEAD_DIM)
    mixed_heads, log_total = lax.map(
        lambda item_args: attend_forward(item_args[0], item_args[1], item_args[2], allowed),
        (query_seq, key_all, value_all),
    )
    mixed_flat = mixed_heads.reshape(tok_count, kv_loc, QUERY_PER_GROUP * HEAD_DIM)
    attn_part = jnp.einsum(
        "thc,dhc->td",
        mixed_flat,
        whole_attn[:, :, input_columns:],
        preferred_element_type=jnp.float32,
    )
    attn_sum = lax.psum(attn_part, "tp")
    residual = tok_float + attn_sum
    inv_two = lax.rsqrt(jnp.mean(residual * residual, axis=-1, keepdims=True) + eps)
    normed_two = (residual * inv_two * ffn_norm).astype(jnp.bfloat16)
    kept_pair, pair_slot, slot_token = slot_tables(
        routes.reshape(tok_count, TOP), slot_order.reshape(tok_count)
    )
    kept_float = kept_pair.astype(jnp.float32)
    gate_kept = gate_values.reshape(tok_count, TOP) * kept_float
    slot_gate = (
        jnp.zeros((EXPERTS * CAP,), jnp.float32)
        .at[pair_slot.reshape(-1)]
        .set(gate_kept.reshape(-1), mode="drop")
    )
    padded = jnp.concatenate([normed_two, jnp.zeros((1, model_width), jnp.bfloat16)], axis=0)
    inputs = padded[slot_token].reshape(EXPERTS, CAP, model_width)
    gate_act = jnp.einsum(
        "ecd,deh->ech", inputs, whole_expert[:, :, 0], preferred_element_type=jnp.float32
    )
    up_act = jnp.einsum(
        "ecd,deh->ech", inputs, whole_expert[:, :, 1], preferred_element_type=jnp.float32
    )
    gate_sigmoid = jax.nn.sigmoid(gate_act)
    active = gate_act * gate_sigmoid
    hidden = (active * up_act).astype(jnp.bfloat16)
    expert_out = jnp.einsum(
        "ech,deh->ecd", hidden, whole_expert[:, :, 2], preferred_element_type=jnp.float32
    )
    out_pad = jnp.concatenate(
        [expert_out.reshape(EXPERTS * CAP, model_width), jnp.zeros((1, model_width), jnp.float32)],
        axis=0,
    )
    picked = out_pad[pair_slot]
    moe_part = jnp.sum(picked * gate_kept[:, :, None], axis=1)
    moe = lax.psum(moe_part.astype(jnp.bfloat16), "tp").astype(jnp.float32)
    layer_out = (
        (residual + moe).astype(jnp.bfloat16).reshape(sequence_count, block_len, model_width)
    )
    grad_out = cotangent.reshape(tok_count, model_width).astype(jnp.float32)
    gate_part = jnp.sum(picked * grad_out[:, None, :], axis=-1) * kept_float
    grad_pad = jnp.concatenate([grad_out, jnp.zeros((1, model_width), jnp.float32)], axis=0)
    d_expert = (
        (grad_pad[slot_token] * slot_gate[:, None])
        .astype(jnp.bfloat16)
        .reshape(EXPERTS, CAP, model_width)
    )
    d_hidden = jnp.einsum(
        "ecd,deh->ech", d_expert, whole_expert[:, :, 2], preferred_element_type=jnp.float32
    )
    silu_slope = gate_sigmoid * (1.0 + gate_act * (1.0 - gate_sigmoid))
    d_gate_act = (d_hidden * up_act * silu_slope).astype(jnp.bfloat16)
    d_up_act = (d_hidden * active).astype(jnp.bfloat16)
    d_inputs = jnp.einsum(
        "ech,deh->ecd", d_gate_act, whole_expert[:, :, 0], preferred_element_type=jnp.float32
    )
    d_inputs = d_inputs + jnp.einsum(
        "ech,deh->ecd", d_up_act, whole_expert[:, :, 1], preferred_element_type=jnp.float32
    )
    d_in_pad = jnp.concatenate(
        [d_inputs.reshape(EXPERTS * CAP, model_width), jnp.zeros((1, model_width), jnp.float32)],
        axis=0,
    )
    d_normed_part = jnp.sum(d_in_pad[pair_slot], axis=1)
    d_normed_two, gate_grad = lax.psum((d_normed_part, gate_part), "tp")
    d_resid_norm, gain_two = norm_back(residual, inv_two, ffn_norm, d_normed_two)
    d_residual = grad_out + d_resid_norm
    d_attn = d_residual.astype(jnp.bfloat16)
    d_mixed = jnp.einsum(
        "td,dhc->thc", d_attn, whole_attn[:, :, input_columns:], preferred_element_type=jnp.float32
    ).astype(jnp.bfloat16)
    d_mixed_seq = d_mixed.reshape(sequence_count, block_len, kv_loc, QUERY_PER_GROUP, HEAD_DIM)
    d_queries, d_key_all, d_value_all = lax.map(
        lambda item_args: attend_backward(
            item_args[0], item_args[1], item_args[2], allowed, item_args[3], item_args[4]
        ),
        (query_seq, key_all, value_all, log_total, d_mixed_seq),
    )
    d_keys, d_values = (
        lax.psum_scatter(
            d_key_all.astype(jnp.bfloat16), "ctx", scatter_dimension=1, tiled=True
        ).astype(jnp.float32),
        lax.psum_scatter(
            d_value_all.astype(jnp.bfloat16), "ctx", scatter_dimension=1, tiled=True
        ).astype(jnp.float32),
    )
    d_queries = rotate(
        d_queries.reshape(tok_count, kv_loc, QUERY_PER_GROUP, HEAD_DIM), cos_four, -sin_four
    )
    d_keys = rotate(d_keys.reshape(tok_count, kv_loc, HEAD_DIM), cos_three, -sin_three)
    d_values = d_values.reshape(tok_count, kv_loc, HEAD_DIM)
    d_projected = jnp.concatenate([d_queries, d_keys[:, :, None], d_values[:, :, None]], axis=2)
    d_projected = d_projected.astype(jnp.bfloat16).reshape(tok_count, kv_loc, input_columns)
    d_normed_local = jnp.einsum(
        "thc,dhc->td",
        d_projected,
        whole_attn[:, :, :input_columns],
        preferred_element_type=jnp.float32,
    )
    d_normed_one = lax.psum(d_normed_local.astype(jnp.bfloat16), "tp").astype(jnp.float32)
    d_tok_norm, gain_one = norm_back(tok_float, inv_one, attn_norm, d_normed_one)
    tokens_grad = (
        (d_residual + d_tok_norm)
        .astype(jnp.bfloat16)
        .reshape(sequence_count, block_len, model_width)
    )
    gain_one, gain_two = lax.psum((gain_one, gain_two), ("fsdp", "ctx"))
    in_term = jnp.einsum(
        "td,thc->dhc", first_normed, d_projected, preferred_element_type=jnp.float32
    )
    out_term = jnp.einsum("td,thc->dhc", d_attn, mixed_flat, preferred_element_type=jnp.float32)
    attn_grad = lax.psum_scatter(
        jnp.concatenate([in_term, out_term], axis=2),
        ("fsdp", "ctx"),
        scatter_dimension=0,
        tiled=True,
    )
    gate_term = jnp.einsum("ecd,ech->deh", inputs, d_gate_act, preferred_element_type=jnp.float32)
    up_term = jnp.einsum("ecd,ech->deh", inputs, d_up_act, preferred_element_type=jnp.float32)
    down_term = jnp.einsum("ecd,ech->deh", d_expert, hidden, preferred_element_type=jnp.float32)
    expert_grad = lax.psum_scatter(
        jnp.stack([gate_term, up_term, down_term], axis=2),
        ("fsdp", "ctx"),
        scatter_dimension=0,
        tiled=True,
    )
    attn_grad, expert_grad = (
        lax.all_gather(attn_grad.astype(jnp.bfloat16), "ctx", axis=0, tiled=True).astype(
            attn_grad.dtype
        ),
        lax.all_gather(expert_grad.astype(jnp.bfloat16), "ctx", axis=0, tiled=True).astype(
            expert_grad.dtype
        ),
    )
    return (
        layer_out,
        tokens_grad,
        attn_grad,
        expert_grad,
        gain_one,
        gain_two,
        gate_grad.reshape(sequence_count, block_len, TOP),
    )


MESH_ID = pl.DeviceIdType.MESH
MIB = 2**20


def expert_order(place):
    row = jnp.arange(128, dtype=jnp.int32)
    expert = (((row // 32) ^ place) * 2) + (row // 16) % 2
    source = (row % 16) * 8 + expert
    return (source[:, None] == row[None, :]).astype(jnp.bfloat16)


def join_kernel(order_ref, in_ref, out_ref):
    width = in_ref.shape[3]
    for m in range(3):
        for k in range(in_ref.shape[2] // 16):
            block = in_ref[:, m, pl.ds(k * 16, 16), :].reshape(128, width)
            moved = jnp.dot(order_ref[...], block, preferred_element_type=jnp.float32)
            out_ref[pl.ds(k * 16, 16), m] = moved.reshape(16, 8, width)


def join_experts(grads, order):
    experts, _, rows, width = grads.shape
    step = 64
    return pl.pallas_call(
        join_kernel,
        grid=(rows // step,),
        in_specs=[
            pl.BlockSpec((128, 128), lambda i: (0, 0)),
            pl.BlockSpec((experts, 3, step, width), lambda i: (0, 0, i, 0)),
        ],
        out_specs=pl.BlockSpec((step, 3, experts, width), lambda i: (i, 0, 0, 0)),
        out_shape=jax.ShapeDtypeStruct((rows, 3, experts, width), jnp.float32),
        compiler_params=pltpu.CompilerParams(vmem_limit_bytes=40 * MIB),
        name="join_experts",
    )(order, grads)


NT = (((1,), (1,)), ((), ()))
TN = (((0,), (0,)), ((), ()))


def dot_f32(a, b, dims=(((1,), (0,)), ((), ()))):
    return lax.dot_general(a, b, dims, preferred_element_type=jnp.float32)


def block_probs(last, keys, query):
    scores = dot_f32(keys, query, NT) * HEAD_DIM ** (-0.5)
    block = lax.broadcasted_iota(jnp.int32, scores.shape, 0) // query.shape[0]
    scores = jnp.where(block <= last, scores, -1e30)
    expd = jnp.exp(scores - jnp.max(scores, axis=0, keepdims=True))
    return expd * (1.0 / jnp.sum(expd, axis=0, keepdims=True))


def place():
    return lax.axis_index("fsdp"), lax.axis_index("ctx"), lax.axis_index("tp")


def plane_peers(f):
    return f + 1 - 2 * lax.rem(f, 2), lax.rem(f + 2, 4), 3 - f


def rows_of(index, size):
    return pl.ds(pl.multiple_of(index * size, size), size)


def greet(devices):
    barrier = pltpu.get_barrier_semaphore()
    for device in devices:
        pl.semaphore_signal(barrier, inc=1, device_id=device, device_id_type=MESH_ID)
    pl.semaphore_wait(barrier, len(devices))


def turn(value, cosine, sine):
    return value * cosine + pltpu.roll(value, HEAD_DIM // 2, 1) * sine


def frequencies():
    i = np.arange(HEAD_DIM // 2, dtype=np.float32)
    freq = (theta_base ** (-(i * 2.0) / HEAD_DIM)).astype(np.float32)
    return jnp.asarray(np.concatenate([freq, freq])[None, :])


def front_kernel(
    tok_ref,
    gain_one_ref,
    gain_two_ref,
    freq_ref,
    routes_ref,
    gates_ref,
    order_ref,
    attn_hbm,
    experts_hbm,
    cot_hbm,
    xn_ref,
    q_ref,
    kv_ref,
    mixed_ref,
    res_ref,
    wl_ref,
    wa_hbm,
    w_hbm,
    x_hbm,
    dy_hbm,
    raw,
    pieces,
    wa,
    part,
    part_in,
    low_half,
    send,
    recv,
    local,
):
    f, z, c = place()
    fx, fy, fd = plane_peers(f)
    count, width = tok_ref.shape
    half = count // 2
    shard = attn_hbm.shape[0]
    cut = shard // 2
    in_cols = (QUERY_PER_GROUP + 2) * HEAD_DIM
    ins = pl.ds(0, in_cols)
    outs = pl.ds(in_cols, attn_hbm.shape[1] - in_cols)

    def at(fsdp=f, ctx=z, tp=c):
        return {"fsdp": fsdp, "ctx": ctx, "tp": tp}

    def remote(src, dst, k, device):
        return pltpu.make_async_remote_copy(
            src_ref=src,
            dst_ref=dst,
            send_sem=send.at[k],
            recv_sem=recv.at[k],
            device_id=device,
            device_id_type=MESH_ID,
        )

    plane = [at(fx), at(fy), at(fd)]
    rel = [fx, fy, fd]
    line = [at(ctx=lax.rem(z + s, 4)) for s in range(1, 4)]
    sibling = at(tp=1 - c)
    mine = rows_of(f, shard)
    load = pltpu.make_async_copy(experts_hbm, raw, local.at[6])
    load.start()
    greet(plane + line + [sibling])

    owned = pltpu.make_async_copy(attn_hbm, wa.at[mine], local.at[0])
    owned.start()
    in_x = remote(attn_hbm.at[:, ins], wa.at[mine, ins], 0, at(fx))
    in_y = remote(attn_hbm.at[:, ins], wa.at[mine, ins], 1, at(fy))
    in_x.start()
    in_y.start()

    rank = jnp.broadcast_to(order_ref[...].astype(jnp.float32), (count, count))
    ahead = jnp.where(rank.T < rank, 1.0, 0.0).astype(jnp.bfloat16)
    expert = lax.broadcasted_iota(jnp.int32, (128, count), 0)
    member = jnp.zeros((128, count), jnp.float32)
    gate = jnp.zeros((128, count), jnp.float32)
    for j in range(TOP):
        hit = jnp.broadcast_to(routes_ref[j : j + 1, :], (128, count)) == expert
        member = jnp.where(hit, 1.0, member)
        gate = jnp.where(hit, jnp.broadcast_to(gates_ref[j : j + 1, :], (128, count)), gate)
    slots = dot_f32(member.astype(jnp.bfloat16), ahead)
    gate = jnp.where(slots < CAP - 0.5, gate, 0.0)
    wl_ref[f] = gate[:EXPERTS]
    gate_copies = [remote(wl_ref.at[f], wl_ref.at[f], 2 + i, plane[i]) for i in range(3)]
    for copy in gate_copies:
        copy.start()

    own_dy = [
        pltpu.make_async_copy(
            cot_hbm.at[pl.ds(i * half, half)], dy_hbm.at[i, f], local.at[2 + i]
        )
        for i in range(2)
    ]
    for copy in own_dy:
        copy.start()

    row = lax.broadcasted_iota(jnp.int32, (128, 128), 0)
    column = lax.broadcasted_iota(jnp.int32, (128, 128), 1)
    owner = jnp.where(row < 64, jnp.where(row < 32, f, fx), jnp.where(row < 96, fy, fd))
    source = (row % 16) * 8 + owner * 2 + (row // 16) % 2
    order = jnp.where(source == column, 1.0, 0.0).astype(jnp.bfloat16)

    def split(m):
        def body(k, _):
            rows = pl.ds(pl.multiple_of(k * 16, 16), 16)
            block = raw[rows, m].reshape(128, raw.shape[3])
            moved = dot_f32(order, block).astype(jnp.bfloat16)
            pieces[:, m, rows, :] = moved.reshape(8, 16, raw.shape[3])
            return 0

        lax.fori_loop(0, shard // 16, body, 0)

    cut_rows = shard // 4
    from_rows = rows_of(z, cut_rows)
    to_rows = rows_of(4 * f + z, cut_rows)

    def quarter(m, i):
        return remote(
            pieces.at[pl.ds(2 * (i + 1), 2), m, from_rows],
            w_hbm.at[:, m, to_rows, :],
            37 + 3 * m + i,
            plane[i],
        )

    def hand_on(m, i):
        quarters[3 * m + i].wait_recv()
        here = w_hbm.at[:, m, rows_of(4 * rel[i] + z, cut_rows), :]
        copies = [remote(here, here, 43 + 9 * m + 3 * i + s, line[s]) for s in range(3)]
        for copy in copies:
            copy.start()
        return copies

    load.wait()
    split(0)
    quarters = [quarter(0, i) for i in range(3)]
    for copy in quarters:
        copy.start()

    tok = tok_ref[...].astype(jnp.float32)
    inv = lax.rsqrt(jnp.mean(tok * tok, axis=-1, keepdims=True) + eps)
    xn_ref[...] = (tok * inv * gain_one_ref[...]).astype(jnp.bfloat16)
    position = z * count + lax.broadcasted_iota(jnp.int32, (count, HEAD_DIM), 0)
    angle = position.astype(jnp.float32) * freq_ref[...]
    cosine = jnp.cos(angle)
    lane = lax.broadcasted_iota(jnp.int32, (count, HEAD_DIM), 1)
    sine = jnp.where(lane < HEAD_DIM // 2, -jnp.sin(angle), jnp.sin(angle))

    top, low = rows_of(2 * fx, cut), rows_of(2 * fy + 1, cut)
    in_x.wait_recv()
    in_xy = remote(wa.at[top, ins], wa.at[top, ins], 5, at(fy))
    in_xy.start()
    in_y.wait_recv()
    in_yx = remote(wa.at[low, ins], wa.at[low, ins], 6, at(fx))
    in_yx.start()
    out_x = remote(attn_hbm.at[:, outs], wa.at[mine, outs], 7, at(fx))
    out_y = remote(attn_hbm.at[:, outs], wa.at[mine, outs], 8, at(fy))
    split(1)
    quarters += [quarter(1, i) for i in range(3)]
    for copy in quarters[3:]:
        copy.start()
    out_x.start()
    out_y.start()
    handed = hand_on(0, 0) + hand_on(0, 1)
    split(2)
    own_w = pltpu.make_async_copy(pieces.at[pl.ds(0, 2)], w_hbm.at[:, :, mine, :], local.at[1])
    own_w.start()
    owned.wait()
    in_xy.wait_recv()
    in_yx.wait_recv()

    normed = xn_ref[...]
    for h in range(QUERY_PER_GROUP + 2):
        cols = pl.ds(h * HEAD_DIM, HEAD_DIM)
        if h % 2 == 0:
            pair = dot_f32(normed, wa[:, pl.ds(h * HEAD_DIM, 2 * HEAD_DIM)])
        value = pair[:, (h % 2) * HEAD_DIM : (h % 2 + 1) * HEAD_DIM]
        if h <= QUERY_PER_GROUP:
            value = turn(value, cosine, sine)
        if h < QUERY_PER_GROUP:
            q_ref[:, cols] = value.astype(jnp.bfloat16)
        else:
            kv_ref[0, :, pl.ds((h - QUERY_PER_GROUP) * HEAD_DIM, HEAD_DIM)] = value.astype(
                jnp.bfloat16
            )
    kv_copies = [remote(kv_ref.at[0], kv_ref.at[s], 8 + s, line[s - 1]) for s in range(1, 4)]
    for s in range(1, 4):

        @pl.when(z + s < 4)
        def _(s=s):
            kv_copies[s - 1].start()

        @pl.when(z < s)
        def _(s=s):
            kv_ref[s] = jnp.zeros(kv_ref.shape[1:], jnp.bfloat16)

    handed += hand_on(0, 2)
    out_x.wait_recv()
    out_xy = remote(wa.at[top, outs], wa.at[top, outs], 12, at(fy))
    out_xy.start()
    out_y.wait_recv()
    out_yx = remote(wa.at[low, outs], wa.at[low, outs], 13, at(fx))
    out_yx.start()

    w_copies = [
        remote(pieces.at[pl.ds(2 * (i + 1), 2), 2], w_hbm.at[:, 2, mine, :], 14 + i, plane[i])
        for i in range(3)
    ]
    for copy in w_copies:
        copy.start()
    dy_copies = [
        remote(cot_hbm.at[rows_of(c, half)], dy_hbm.at[c, f], 23 + i, plane[i]) for i in range(3)
    ]
    for copy in dy_copies:
        copy.start()
    for i in range(3):
        handed += hand_on(1, i)

    for s in range(1, 4):

        @pl.when(z >= s)
        def _(s=s):
            kv_copies[s - 1].wait_recv()

    keys = kv_ref[:, :, pl.ds(0, HEAD_DIM)].reshape(4 * count, HEAD_DIM)
    vals = kv_ref[:, :, pl.ds(HEAD_DIM, HEAD_DIM)].reshape(4 * count, HEAD_DIM)
    for g in range(QUERY_PER_GROUP):
        cols = pl.ds(g * HEAD_DIM, HEAD_DIM)
        probs = block_probs(z, keys, q_ref[:, cols]).astype(jnp.bfloat16)
        mixed_ref[:, cols] = dot_f32(probs, vals, TN).astype(jnp.bfloat16)

    out_xy.wait_recv()
    out_yx.wait_recv()
    store_wa = pltpu.make_async_copy(wa, wa_hbm, local.at[4])
    store_wa.start()
    for s in range(width // 256):
        cols = pl.ds(s * 256, 256)
        part[:, cols] = dot_f32(mixed_ref[...], wa[cols, outs], NT)
    swap = remote(part.at[rows_of(1 - c, half)], part_in, 26, sibling)
    swap.start()
    swap.wait_recv()
    my_rows = rows_of(c, half)
    residual = tok_ref[my_rows, :].astype(jnp.float32) + (part[my_rows, :] + part_in[...])
    res_ref[...] = residual
    inv = lax.rsqrt(jnp.mean(residual * residual, axis=-1, keepdims=True) + eps)
    low_half[...] = (residual * inv * gain_two_ref[...]).astype(jnp.bfloat16)
    own_x = pltpu.make_async_copy(low_half, x_hbm.at[c, f], local.at[5])
    own_x.start()
    x_copies = [remote(low_half, x_hbm.at[c, f], 27 + i, plane[i]) for i in range(3)]
    for copy in x_copies:
        copy.start()
    sib_x = [remote(low_half, x_hbm.at[c, f], 30, sibling)]
    sib_x[0].start()

    sib_dy = []
    for i in range(3):
        dy_copies[i].wait_recv()
        sib_dy.append(remote(dy_hbm.at[c, rel[i]], dy_hbm.at[c, rel[i]], 31 + i, sibling))
        sib_dy[i].start()
    for i in range(3):
        x_copies[i].wait_recv()
        sib_x.append(remote(x_hbm.at[c, rel[i]], x_hbm.at[c, rel[i]], 34 + i, sibling))
        sib_x[i + 1].start()

    for copy in w_copies + gate_copies + handed + sib_dy + sib_x:
        copy.wait_recv()
    for s in range(1, 4):

        @pl.when(z + s < 4)
        def _(s=s):
            kv_copies[s - 1].wait_send()

    for copy in [in_x, in_y, in_xy, in_yx, out_x, out_y, out_xy, out_yx, swap]:
        copy.wait_send()
    for copy in w_copies + quarters + handed + gate_copies + dy_copies + x_copies + sib_dy + sib_x:
        copy.wait_send()
    for copy in [own_w, own_x, store_wa] + own_dy:
        copy.wait()


def front(tok, gain_one, gain_two, routes, gates, order, attn_own, weights, cot):
    count, width = tok.shape
    half = count // 2
    shard, columns = attn_own.shape
    experts, hidden = EXPERTS // 4, weights.shape[3]
    vmem, hbm = pl.BlockSpec(memory_space=pltpu.VMEM), pl.BlockSpec(memory_space=pl.ANY)
    bf16, f32 = jnp.bfloat16, jnp.float32
    shape = jax.ShapeDtypeStruct
    return pl.pallas_call(
        front_kernel,
        in_specs=[vmem] * 7 + [hbm] * 3,
        out_specs=[vmem] * 6 + [hbm] * 4,
        out_shape=[
            shape((count, width), bf16),
            shape((count, QUERY_PER_GROUP * HEAD_DIM), bf16),
            shape((4, count, 2 * HEAD_DIM), bf16),
            shape((count, QUERY_PER_GROUP * HEAD_DIM), bf16),
            shape((half, width), f32),
            shape((4, EXPERTS, count), f32),
            shape((4 * shard, columns), bf16),
            shape((experts, 3, 4 * shard, hidden), bf16),
            shape((2, 4, half, width), bf16),
            shape((2, 4, half, width), bf16),
        ],
        scratch_shapes=[
            pltpu.VMEM(weights.shape, bf16),
            pltpu.VMEM((EXPERTS, 3, shard, hidden), bf16),
            pltpu.VMEM((4 * shard, columns), bf16),
            pltpu.VMEM((count, width), f32),
            pltpu.VMEM((half, width), f32),
            pltpu.VMEM((half, width), bf16),
            pltpu.SemaphoreType.DMA((61,)),
            pltpu.SemaphoreType.DMA((61,)),
            pltpu.SemaphoreType.DMA((7,)),
        ],
        compiler_params=pltpu.CompilerParams(
            collective_id=0, has_side_effects=True, vmem_limit_bytes=48 * MIB
        ),
        name="front",
    )(tok, gain_one, gain_two, frequencies(), routes, gates, order, attn_own, weights, cot)


def moe_kernel(
    x_hbm, dy_hbm, w_hbm, wl_ref, ge_hbm, dn_ref, mo_ref, gg_ref, x, dy, wgu, wd, gu, hid, ge, scales, sem, out_sem
):
    f = lax.axis_index("fsdp")
    tokens, width = x.shape
    hidden = w_hbm.shape[3]
    half = tokens // 8
    tile = 2 * half
    own = w_hbm.shape[0]
    loads = [pltpu.make_async_copy(x_hbm, x, sem.at[0])]
    for e in range(own):
        for m in range(2):
            loads.append(
                pltpu.make_async_copy(
                    w_hbm.at[e, m], wgu.at[:, pl.ds((2 * e + m) * hidden, hidden)], sem.at[1 + 3 * e + m]
                )
            )
    loads.append(pltpu.make_async_copy(dy_hbm, dy, sem.at[7]))
    for e in range(own):
        loads.append(
            pltpu.make_async_copy(w_hbm.at[e, 2], wd.at[:, pl.ds(e * hidden, hidden)], sem.at[3 + 3 * e])
        )
    for copy in loads:
        copy.start()
    lane = lax.broadcasted_iota(jnp.int32, (half, 128), 1)
    for b in range(8):
        rows = wl_ref[b % 4, :, pl.ds((b // 4) * half, half)]
        rows = jnp.concatenate([rows, jnp.zeros((128 - EXPERTS, half), jnp.float32)], axis=0)
        scales[pl.ds(b * half, half), :] = rows.T
    for copy in loads:
        copy.wait()

    lanes = lax.broadcasted_iota(jnp.int32, (tile, 128), 1)

    def step(i, _):
        rows = pl.ds(pl.multiple_of(i * tile, tile), tile)
        acts = dot_f32(x[rows, :], wgu[...])
        plain = dot_f32(dy[rows, :], wd[...])
        table = scales[rows, :]
        sums = jnp.zeros((tile, 128), jnp.float32)
        for e in range(own):
            gate_act = acts[:, 2 * e * hidden : (2 * e + 1) * hidden]
            up_act = acts[:, (2 * e + 1) * hidden : (2 * e + 2) * hidden]
            d_plain = plain[:, e * hidden : (e + 1) * hidden]
            here = lanes == own * f + e
            scale = jnp.sum(jnp.where(here, table, 0.0), axis=1, keepdims=True)
            sigmoid = 1.0 / (1.0 + jnp.exp(-gate_act))
            active = gate_act * sigmoid
            act = active * up_act
            total = jnp.sum(act * d_plain, axis=1, keepdims=True)
            sums = jnp.where(here, jnp.where(scale != 0.0, total, 0.0), sums)
            d_hidden = d_plain * scale
            slope = sigmoid * (1.0 + gate_act * (1.0 - sigmoid))
            hid[rows, pl.ds(e * hidden, hidden)] = (act * scale).astype(jnp.bfloat16)
            gu[rows, pl.ds(2 * e * hidden, hidden)] = (d_hidden * up_act * slope).astype(jnp.bfloat16)
            gu[rows, pl.ds((2 * e + 1) * hidden, hidden)] = (d_hidden * active).astype(jnp.bfloat16)
        gg_ref[rows, :] = sums
        return 0

    lax.fori_loop(0, tokens // tile, step, 0)

    block = width // 4

    def grad_step(s, _):
        cols = pl.ds(pl.multiple_of(s * block, 128), block)
        inner = dot_f32(x[:, cols], gu[...], TN).astype(jnp.bfloat16)
        outer = dot_f32(dy[:, cols], hid[...], TN).astype(jnp.bfloat16)
        for e in range(own):
            for m in range(2):
                k = 2 * e + m
                ge[3 * e + m, cols, :] = inner[:, k * hidden : (k + 1) * hidden]
            ge[3 * e + 2, cols, :] = outer[:, e * hidden : (e + 1) * hidden]
        return 0

    lax.fori_loop(0, 4, grad_step, 0)
    store = pltpu.make_async_copy(ge, ge_hbm, out_sem)
    store.start()

    def down_step(i, _):
        rows = pl.ds(pl.multiple_of(i * tile, tile), tile)
        dn_ref[rows, :] = dot_f32(gu[rows, :], wgu[...], NT).astype(jnp.bfloat16)
        mo_ref[rows, :] = dot_f32(hid[rows, :], wd[...], NT).astype(jnp.bfloat16)
        return 0

    lax.fori_loop(0, tokens // tile, down_step, 0)
    store.wait()


def moe_layer(x, dy, weights, gate_table):
    tokens, width = x.shape
    own, _, _, hidden = weights.shape
    vmem, hbm = pl.BlockSpec(memory_space=pltpu.VMEM), pl.BlockSpec(memory_space=pl.ANY)
    bf16, f32 = jnp.bfloat16, jnp.float32
    shape = jax.ShapeDtypeStruct
    return pl.pallas_call(
        moe_kernel,
        in_specs=[hbm] * 3 + [vmem],
        out_specs=[hbm, vmem, vmem, vmem],
        out_shape=[
            shape((3 * own, width, hidden), bf16),
            shape((tokens, width), bf16),
            shape((tokens, width), bf16),
            shape((tokens, 128), f32),
        ],
        scratch_shapes=[
            pltpu.VMEM((tokens, width), bf16),
            pltpu.VMEM((tokens, width), bf16),
            pltpu.VMEM((width, 2 * own * hidden), bf16),
            pltpu.VMEM((width, own * hidden), bf16),
            pltpu.VMEM((tokens, 2 * own * hidden), bf16),
            pltpu.VMEM((tokens, own * hidden), bf16),
            pltpu.VMEM((3 * own, width, hidden), bf16),
            pltpu.VMEM((tokens, 128), f32),
            pltpu.SemaphoreType.DMA((8,)),
            pltpu.SemaphoreType.DMA,
        ],
        compiler_params=pltpu.CompilerParams(vmem_limit_bytes=58 * MIB),
        name="experts",
    )(x, dy, weights, gate_table)


def rear_kernel(
    res_ref,
    xn_ref,
    q_ref,
    kv_ref,
    mixed_ref,
    gain_one_ref,
    gain_two_ref,
    freq_ref,
    tok_hbm,
    cot_hbm,
    ge_hbm,
    dn_hbm,
    mo_hbm,
    gg_hbm,
    wa_hbm,
    layer_ref,
    tokgrad_ref,
    gains_ref,
    gate_ref,
    attn_hbm,
    fin_hbm,
    ge,
    r1,
    r2,
    wa,
    dn_own,
    dn_in,
    dn_got,
    mo_own,
    mo_in,
    mo_got,
    gg_own,
    gg_in,
    gg_sum,
    gg_got,
    dres,
    dattn,
    dmixed,
    dproj,
    dkv,
    dkv_low,
    dkv_got,
    d1,
    d1_low,
    d1_in,
    ga,
    ra,
    a1,
    a2,
    gacc,
    gin,
    tok_half,
    cot_half,
    send,
    recv,
    local,
    z_out,
    z_across,
    z_back,
    z_r1,
    z_r2,
    f_out,
    f_in,
):
    f, z, c = place()
    fx, fy, fd = plane_peers(f)
    rel = [f, fx, fy, fd]
    f32, bf16 = jnp.float32, jnp.bfloat16
    count, width = tok_hbm.shape
    half = count // 2
    shard = attn_hbm.shape[0]
    in_cols = (QUERY_PER_GROUP + 2) * HEAD_DIM
    q_cols = QUERY_PER_GROUP * HEAD_DIM
    ins = pl.ds(0, in_cols)
    outs = pl.ds(in_cols, attn_hbm.shape[1] - in_cols)
    scale = HEAD_DIM ** (-0.5)

    def at(fsdp=f, ctx=z, tp=c):
        return {"fsdp": fsdp, "ctx": ctx, "tp": tp}

    def copy_to(src, dst, send_sem, recv_sem, device):
        return pltpu.make_async_remote_copy(
            src_ref=src,
            dst_ref=dst,
            send_sem=send_sem,
            recv_sem=recv_sem,
            device_id=device,
            device_id_type=MESH_ID,
        )

    def remote(src, dst, k, device):
        return copy_to(src, dst, send.at[k], recv.at[k], device)

    plane = [at(fx), at(fy), at(fd)]
    line = [at(ctx=lax.rem(z + s, 4)) for s in range(1, 4)]
    sibling = at(tp=1 - c)
    partner = at(ctx=z + 1 - 2 * lax.rem(z, 2))
    opposite = at(ctx=3 - z)
    inner = (z == 1) | (z == 2)
    outer = (z == 0) | (z == 3)

    loads = [pltpu.make_async_copy(ge_hbm, ge, local.at[0])]
    loads.append(pltpu.make_async_copy(dn_hbm.at[c], dn_own, local.at[1]))
    loads.append(pltpu.make_async_copy(gg_hbm.at[c], gg_own, local.at[2]))
    loads.append(pltpu.make_async_copy(wa_hbm, wa, local.at[3]))
    loads.append(pltpu.make_async_copy(mo_hbm.at[c], mo_own, local.at[4]))
    loads.append(pltpu.make_async_copy(tok_hbm.at[rows_of(c, half)], tok_half, local.at[5]))
    loads.append(pltpu.make_async_copy(cot_hbm.at[rows_of(c, half)], cot_half, local.at[6]))
    for copy in loads:
        copy.start()
    greet(plane + line + [sibling])
    dn_swap = remote(dn_hbm.at[1 - c], dn_in, 0, sibling)
    gg_swap = remote(gg_hbm.at[1 - c], gg_in, 1, sibling)
    mo_swap = remote(mo_hbm.at[1 - c], mo_in, 2, sibling)
    dn_swap.start()
    gg_swap.start()
    mo_swap.start()

    mats = ge.shape[0]
    n_expert = 4 * mats
    n_attn = 8
    n_all = n_expert + n_attn
    a_rows = shard // n_attn

    def chunk(k):
        if k < n_expert:
            j, r = k // 4, k % 4
            rows = rows_of(rel[r], shard)
            return ge.at[j, rows], r1.at[j, rows], r2.at[j, rows]
        rows = pl.ds((k - n_expert) * a_rows, a_rows)
        return ra.at[0, rows], a1.at[rows], a2.at[rows]

    def add_into(dst, left, right):
        size = dst.shape[0] // 3 if dst.shape[0] < 64 else 64

        def body(i, _):
            rows = pl.ds(pl.multiple_of(i * size, size), size)
            dst[rows, :] = (left[rows, :].astype(f32) + right[rows, :].astype(f32)).astype(bf16)
            return 0

        lax.fori_loop(0, dst.shape[0] // size, body, 0)

    def first(k):
        own, one, _ = chunk(k)
        return copy_to(own, one, z_out.at[k], z_r1.at[k], partner)

    def across(k):
        own, _, two = chunk(k)
        return copy_to(own, two, z_across.at[k], z_r2.at[k], opposite)

    def back(k):
        _, one, _ = chunk(k)
        return copy_to(one, one, z_back.at[k], z_r1.at[k], partner)

    def final(k):
        _, one, _ = chunk(k)
        j, r = k // 4, k % 4
        if r == 0:
            return pltpu.make_async_copy(one, fin_hbm.at[0, j], f_out.at[k])
        return copy_to(one, fin_hbm.at[r, j], f_out.at[k], f_in.at[k], plane[r - 1])

    pending = []
    pace = 2
    lag_b, lag_c, window = 3, 7, 3

    def z_step(i):
        for copy in pending[:pace]:
            copy.start()
        del pending[:pace]
        if i < n_all:

            @pl.when(outer)
            def _():
                if i >= window:
                    first(i - window).wait_send()
                first(i).start()

        if 1 <= i <= n_all:
            k = i - 1

            @pl.when(inner)
            def _():
                own, one, _ = chunk(k)
                first(k).wait_recv()
                add_into(own, own, one)
                across(k).start()

        if lag_b <= i < n_all + lag_b:
            k = i - lag_b

            @pl.when(inner)
            def _():
                own, one, two = chunk(k)
                across(k).wait_recv()
                add_into(one, own, two)
                back(k).start()
                if k < n_expert:
                    final(k).start()

        if lag_c <= i < n_all + lag_c:
            k = i - lag_c

            @pl.when(outer)
            def _():
                back(k).wait_recv()
                if k < n_expert:
                    final(k).start()

    steps = iter(range(n_all + max(lag_b, lag_c)))

    def go_on(count=1):
        for _ in range(count):
            z_step(next(steps))

    loads[0].wait()
    go_on()
    loads[5].wait()
    loads[6].wait()

    loads[1].wait()
    loads[2].wait()
    gg_swap.wait_recv()
    gg_sum[...] = gg_own[...] + gg_in[...]
    dn_swap.wait_recv()
    for g in range(4):
        dn_own[g] = (dn_own[g].astype(f32) + dn_in[g].astype(f32)).astype(bf16)
    dn_out = [remote(dn_own.at[rel[i + 1]], dn_got.at[i], 3 + i, plane[i]) for i in range(3)]
    gg_out = [remote(gg_sum.at[rel[i + 1]], gg_got.at[i], 6 + i, plane[i]) for i in range(3)]
    for copy in dn_out + gg_out:
        copy.start()
    go_on(3)
    for copy in dn_out:
        copy.wait_recv()
    loads[4].wait()
    mo_swap.wait_recv()
    for g in range(4):
        mo_own[g] = (mo_own[g].astype(f32) + mo_in[g].astype(f32)).astype(bf16)
    mo_out = [remote(mo_own.at[rel[i + 1]], mo_got.at[i], 9 + i, plane[i]) for i in range(3)]
    for copy in mo_out:
        copy.start()
    d_two = dn_own[f].astype(f32)
    for i in range(3):
        d_two = d_two + dn_got[i].astype(f32)
    residual = res_ref[...]
    inv = lax.rsqrt(jnp.mean(residual * residual, axis=-1, keepdims=True) + eps)
    scaled = d_two * gain_two_ref[...]
    inside = jnp.mean(scaled * residual, axis=-1, keepdims=True)
    d_norm = inv * scaled - residual * (inv * inv * inv * inside)
    gacc[0] = jnp.zeros(gacc.shape[1:], f32)
    gacc[0, 1:2, :] = jnp.sum(d_two * residual * inv, axis=0, keepdims=True)
    my_rows = rows_of(c, half)
    d_res = cot_half[...].astype(f32) + d_norm
    dres[...] = d_res
    dattn[my_rows, :] = d_res.astype(bf16)
    da_swap = remote(dattn.at[my_rows], dattn.at[my_rows], 12, sibling)
    da_swap.start()
    loads[3].wait()
    go_on()
    da_swap.wait_recv()
    dmixed[...] = dot_f32(dattn[...], wa[:, outs]).astype(bf16)
    go_on()

    position = z * count + lax.broadcasted_iota(jnp.int32, (count, HEAD_DIM), 0)
    angle = position.astype(f32) * freq_ref[...]
    cosine = jnp.cos(angle)
    lane = lax.broadcasted_iota(jnp.int32, (count, HEAD_DIM), 1)
    sine = jnp.where(lane < HEAD_DIM // 2, jnp.sin(angle), -jnp.sin(angle))
    keys = kv_ref[:, :, pl.ds(0, HEAD_DIM)].reshape(4 * count, HEAD_DIM)
    vals = kv_ref[:, :, pl.ds(HEAD_DIM, HEAD_DIM)].reshape(4 * count, HEAD_DIM)
    key_cols, val_cols = pl.ds(0, HEAD_DIM), pl.ds(HEAD_DIM, HEAD_DIM)
    dkv[...] = jnp.zeros_like(dkv)
    for g in range(QUERY_PER_GROUP):
        cols = pl.ds(g * HEAD_DIM, HEAD_DIM)
        query = q_ref[:, cols]
        d_mix = dmixed[:, cols]
        probs = block_probs(z, keys, query)
        d_probs = dot_f32(vals, d_mix, NT)
        inside = jnp.sum(probs * d_probs, axis=0, keepdims=True)
        d_scores = (probs * (d_probs - inside)).astype(bf16)
        d_query = dot_f32(d_scores, keys, TN) * scale
        dproj[:, cols] = turn(d_query, cosine, sine).astype(bf16)
        dkv[:, key_cols] += dot_f32(d_scores, query) * scale
        dkv[:, val_cols] += dot_f32(probs.astype(bf16), d_mix)
        if g % 2 == 1:
            go_on()
    dkv_low[...] = dkv[...].reshape(dkv_low.shape).astype(bf16)
    dkv_out = [
        remote(dkv_low.at[s], dkv_got.at[s - 1], 12 + s, at(ctx=lax.rem(z + 4 - s, 4)))
        for s in range(1, 4)
    ]
    for s in range(1, 4):

        @pl.when(z >= s)
        def _(s=s):
            dkv_out[s - 1].start()

    def weight_grad(left, right, cols):
        def body(i, _):
            rows = pl.ds(pl.multiple_of(i * 256, 256), 256)
            ga[rows, cols] = dot_f32(left[:, rows], right, TN).astype(bf16)
            return 0

        lax.fori_loop(0, width // 256, body, 0)

    def send_grad(cols, k):
        third = shard // 3
        copies = []
        for p in range(1 if cols.size < q_cols else 3):
            size = shard if cols.size < q_cols else third
            for i in range(3):
                rows = pl.ds(pl.multiple_of(rel[i + 1] * shard + p * size, size), size)
                copies.append(
                    remote(
                        ga.at[rows, cols],
                        ra.at[i, pl.ds(p * size, size), cols],
                        k + 3 * p + i,
                        plane[i],
                    )
                )
        pending.extend(copies)
        return copies

    weight_grad(dattn, mixed_ref[...], outs)
    ga_copies = send_grad(outs, 34)
    go_on()
    q_part = pl.ds(0, q_cols)
    weight_grad(xn_ref, dproj[:, q_part], q_part)
    ga_copies += send_grad(q_part, 43)
    go_on()
    for s in range(1, 4):

        @pl.when(z + s < 4)
        def _(s=s):
            dkv_out[s - 1].wait_recv()
            dkv[0:count, :] += dkv_got[s - 1].astype(f32)

    kv_part = pl.ds(q_cols, 2 * HEAD_DIM)
    dproj[:, pl.ds(q_cols, HEAD_DIM)] = turn(dkv[0:count, key_cols], cosine, sine).astype(bf16)
    dproj[:, pl.ds(q_cols + HEAD_DIM, HEAD_DIM)] = dkv[0:count, val_cols].astype(bf16)
    weight_grad(xn_ref, dproj[:, kv_part], kv_part)
    ga_copies += send_grad(kv_part, 16)
    go_on()

    for s in range(width // 256):
        rows = pl.ds(s * 256, 256)
        d1[:, rows] = dot_f32(dproj[my_rows, :], wa[rows, ins], NT)
        d1_low[:, rows] = dot_f32(dproj[rows_of(1 - c, half), :], wa[rows, ins], NT).astype(bf16)
    d1_swap = remote(d1_low, d1_in, 25, sibling)
    d1_swap.start()
    go_on()
    d1_swap.wait_recv()
    d_one = d1[...] + d1_in[...].astype(f32)
    tok = tok_half[...].astype(f32)
    inv = lax.rsqrt(jnp.mean(tok * tok, axis=-1, keepdims=True) + eps)
    scaled = d_one * gain_one_ref[...]
    inside = jnp.mean(scaled * tok, axis=-1, keepdims=True)
    d_norm = inv * scaled - tok * (inv * inv * inv * inside)
    gacc[0, 0:1, :] = jnp.sum(d_one * tok * inv, axis=0, keepdims=True)
    tokgrad_ref[my_rows, :] = (dres[...] + d_norm).astype(bf16)
    tg_swap = remote(tokgrad_ref.at[my_rows], tokgrad_ref.at[my_rows], 26, sibling)
    tg_swap.start()
    go_on()

    for copy in mo_out + gg_out:
        copy.wait_recv()
    moe = mo_own[f].astype(f32)
    gates = gg_sum[f]
    for i in range(3):
        moe = moe + mo_got[i].astype(f32)
        gates = gates + gg_got[i]
    layer_ref[my_rows, :] = (res_ref[...] + moe).astype(bf16)
    gate_ref[my_rows, :] = gates
    lo_swap = remote(layer_ref.at[my_rows], layer_ref.at[my_rows], 27, sibling)
    gt_swap = remote(gate_ref.at[my_rows], gate_ref.at[my_rows], 28, sibling)
    lo_swap.start()
    gt_swap.start()
    go_on()

    stages = [sibling, at(fx), at(fy), partner, at(ctx=lax.rem(z + 2, 4))]
    gain_copies = [remote(gacc.at[i], gin.at[i], 29 + i, stages[i]) for i in range(5)]
    for i in range(5):
        gain_copies[i].start()
        go_on()
        gain_copies[i].wait_recv()
        total = gacc[i] + gin[i]
        if i < 4:
            gacc[i + 1] = total
        else:
            gains_ref[...] = total

    while (i := next(steps)) < n_expert - 1:
        z_step(i)
    z_step(i)
    for copy in pending:
        copy.start()
    del pending[:]
    for copy in ga_copies:
        copy.wait_recv()

    def attn_sum(i, _):
        size = shard // 8
        here = pl.ds(pl.multiple_of(i * size, size), size)
        total = ga[pl.ds(pl.multiple_of(f * shard + i * size, size), size), :].astype(f32)
        for r in range(3):
            total = total + ra[r, here, :].astype(f32)
        ra[0, here, :] = total.astype(bf16)
        return 0

    lax.fori_loop(0, 8, attn_sum, 0)
    for i in steps:
        z_step(i)
    store = pltpu.make_async_copy(a1, attn_hbm, local.at[0])
    store.start()

    store.wait()
    for k in range(n_all):

        @pl.when(outer)
        def _(k=k):
            if k >= n_all - window:
                first(k).wait_send()

        @pl.when(inner)
        def _(k=k):
            across(k).wait_send()
            back(k).wait_send()

    for k in range(n_expert):
        if k % 4 == 0:
            final(k).wait()
        else:
            final(k).wait_send()
            final(k).wait_recv()
    for s in range(1, 4):

        @pl.when(z >= s)
        def _(s=s):
            dkv_out[s - 1].wait_send()

    for copy in [tg_swap, lo_swap, gt_swap]:
        copy.wait_recv()
    swaps = [dn_swap, gg_swap, mo_swap, da_swap, d1_swap, tg_swap, lo_swap, gt_swap]
    for copy in swaps + dn_out + gg_out + mo_out + ga_copies + gain_copies:
        copy.wait_send()


def rear(tok, cot, res, xn, q, kv, mixed, gain_one, gain_two, ge, dn, mo, gg, wa):
    count, width = tok.shape
    half = count // 2
    columns = wa.shape[1]
    shard = width // 4
    mats, _, hidden = ge.shape
    q_cols = q.shape[1]
    vmem, hbm = pl.BlockSpec(memory_space=pltpu.VMEM), pl.BlockSpec(memory_space=pl.ANY)
    bf16, f32 = jnp.bfloat16, jnp.float32
    shape = jax.ShapeDtypeStruct
    dma = pltpu.SemaphoreType.DMA
    n_all = 4 * mats + 8
    return pl.pallas_call(
        rear_kernel,
        in_specs=[vmem] * 8 + [hbm] * 7,
        out_specs=[vmem] * 4 + [hbm] * 2,
        out_shape=[
            shape((count, width), bf16),
            shape((count, width), bf16),
            shape((8, width), f32),
            shape((count, 128), f32),
            shape((shard, columns), bf16),
            shape((4, mats, shard, hidden), bf16),
        ],
        scratch_shapes=[
            pltpu.VMEM((mats, width, hidden), bf16),
            pltpu.VMEM((mats, width, hidden), bf16),
            pltpu.VMEM((mats, width, hidden), bf16),
            pltpu.VMEM((width, columns), bf16),
            pltpu.VMEM((4, half, width), bf16),
            pltpu.VMEM((4, half, width), bf16),
            pltpu.VMEM((3, half, width), bf16),
            pltpu.VMEM((4, half, width), bf16),
            pltpu.VMEM((4, half, width), bf16),
            pltpu.VMEM((3, half, width), bf16),
            pltpu.VMEM((4, half, 128), f32),
            pltpu.VMEM((4, half, 128), f32),
            pltpu.VMEM((4, half, 128), f32),
            pltpu.VMEM((3, half, 128), f32),
            pltpu.VMEM((half, width), f32),
            pltpu.VMEM((count, width), bf16),
            pltpu.VMEM((count, q_cols), bf16),
            pltpu.VMEM((count, q_cols + 2 * HEAD_DIM), bf16),
            pltpu.VMEM((4 * count, 2 * HEAD_DIM), f32),
            pltpu.VMEM((4, count, 2 * HEAD_DIM), bf16),
            pltpu.VMEM((3, count, 2 * HEAD_DIM), bf16),
            pltpu.VMEM((half, width), f32),
            pltpu.VMEM((half, width), bf16),
            pltpu.VMEM((half, width), bf16),
            pltpu.VMEM((width, columns), bf16),
            pltpu.VMEM((3, shard, columns), bf16),
            pltpu.VMEM((shard, columns), bf16),
            pltpu.VMEM((shard, columns), bf16),
            pltpu.VMEM((5, 8, width), f32),
            pltpu.VMEM((5, 8, width), f32),
            pltpu.VMEM((half, width), bf16),
            pltpu.VMEM((half, width), bf16),
            dma((52,)),
            dma((52,)),
            dma((7,)),
            dma((n_all,)),
            dma((n_all,)),
            dma((n_all,)),
            dma((n_all,)),
            dma((n_all,)),
            dma((4 * mats,)),
            dma((4 * mats,)),
        ],
        compiler_params=pltpu.CompilerParams(
            collective_id=1, has_side_effects=True, vmem_limit_bytes=62 * MIB
        ),
        name="rear",
    )(res, xn, q, kv, mixed, gain_one, gain_two, frequencies(), tok, cot, ge, dn, mo, gg, wa)


def body_fast(
    tokens,
    attn_norm,
    attention_params,
    ffn_norm,
    expert_weights,
    gate_values,
    routes,
    slot_order,
    cotangent,
):
    sequence_count, block_len, model_width = tokens.shape
    count = sequence_count * block_len
    half = count // 2
    f = lax.axis_index("fsdp")
    shard, hidden = attention_params.shape[0], expert_weights.shape[3]
    tok = tokens.reshape(count, model_width)
    cot = cotangent.reshape(count, model_width)
    gain_one, gain_two = attn_norm[None, :], ffn_norm[None, :]
    route_rows = routes.reshape(count, TOP)
    normed, queries, kv, mixed, residual, gate_table, whole_attn, whole_expert, x, dy = front(
        tok,
        gain_one,
        gain_two,
        route_rows.T,
        gate_values.reshape(count, TOP).T,
        slot_order.reshape(1, count),
        attention_params[:, 0, :],
        jnp.transpose(expert_weights, (0, 2, 1, 3)),
        cot,
    )
    grads, d_normed, moe, gate_parts = moe_layer(
        x.reshape(8 * half, model_width), dy.reshape(8 * half, model_width), whole_expert, gate_table
    )
    layer_out, tokens_grad, gains, gate_rows, attn_grad, finals = rear(
        tok,
        cot,
        residual,
        normed,
        queries,
        kv,
        mixed,
        gain_one,
        gain_two,
        grads,
        d_normed.reshape(2, 4, half, model_width),
        moe.reshape(2, 4, half, model_width),
        gate_parts.reshape(2, 4, half, 128),
        whole_attn,
    )
    picked = route_rows[:, :, None] == jnp.arange(EXPERTS, dtype=jnp.int32)
    gate_grad = jnp.sum(jnp.where(picked, gate_rows[:, None, :EXPERTS], 0.0), axis=-1)
    finals = finals.reshape(EXPERTS, 3, shard, hidden)
    expert_grad = jnp.transpose(join_experts(finals, expert_order(f).T), (0, 2, 1, 3))
    return (
        layer_out.reshape(sequence_count, block_len, model_width),
        tokens_grad.reshape(sequence_count, block_len, model_width),
        attn_grad.astype(jnp.float32)[:, None, :],
        expert_grad,
        gains[0],
        gains[1],
        gate_grad.reshape(sequence_count, block_len, TOP),
    )


def solution(mesh):
    in_specs = (
        P("fsdp", "ctx", None),
        P(),
        P("fsdp", "tp", None),
        P(),
        P("fsdp", None, None, "tp"),
        P("fsdp", "ctx", None),
        P("fsdp", "ctx", None),
        P("fsdp", "ctx"),
        P("fsdp", "ctx", None),
    )
    out_specs = (
        P("fsdp", "ctx", None),
        P("fsdp", "ctx", None),
        P("fsdp", "tp", None),
        P("fsdp", None, None, "tp"),
        P(),
        P(),
        P("fsdp", "ctx", None),
    )
    four = mesh.shape["fsdp"] == 4 and mesh.shape["ctx"] == 4 and mesh.shape["tp"] == 2
    body_fn = body_fast if four else body
    return jax.shard_map(body_fn, mesh=mesh, in_specs=in_specs, out_specs=out_specs, check_vma=False)
```

```python
import jax
import jax.numpy as jnp
from jax import lax
import math
import numpy as np
from jax.experimental import pallas as pl
from jax.experimental.pallas import tpu as pltpu
from jax.sharding import PartitionSpec as P

HEAD_DIM = 128
TOP = 4
EXPERTS = 8
QUERY_PER_GROUP = 6
CAP = 160


eps = 1e-06
theta_base = 1000000.0


def angle_tables(positions):
    frequency = theta_base ** (-(jnp.arange(HEAD_DIM // 2, dtype=jnp.float32) * 2.0) / HEAD_DIM)
    angles = positions.astype(jnp.float32)[:, None] * frequency[None, :]
    return (jnp.cos(angles), jnp.sin(angles))


def rotate(source, cosine_table, sine_table):
    half_size = source.shape[-1] // 2
    front_half = source[..., :half_size]
    back_half = source[..., half_size:]
    return jnp.concatenate(
        [
            front_half * cosine_table - back_half * sine_table,
            back_half * cosine_table + front_half * sine_table,
        ],
        axis=-1,
    )


def norm_back(source, inv_rms, gain_vec, upstream):
    scaled = upstream * gain_vec
    inner_sum = jnp.mean(scaled * source, axis=-1, keepdims=True)
    d_source = inv_rms * scaled - source * inv_rms * inv_rms * inv_rms * inner_sum
    return (d_source, jnp.sum(upstream * source * inv_rms, axis=0))


def slot_tables(route_rows, rank_rows):
    tok_count = route_rows.shape[0]
    inverse = (
        jnp.zeros((tok_count,), jnp.int32).at[rank_rows].set(jnp.arange(tok_count, dtype=jnp.int32))
    )
    ranked = route_rows[inverse].reshape(-1)
    onehot = (ranked[:, None] == jnp.arange(EXPERTS, dtype=jnp.int32)[None, :]).astype(jnp.int32)
    before = jnp.cumsum(onehot, axis=0) - onehot
    slot_ranked = jnp.sum(before * onehot, axis=1).reshape(tok_count, TOP)
    slots = slot_ranked[rank_rows]
    kept_pair = slots < CAP
    pair_slot = jnp.where(kept_pair, route_rows * CAP + slots, EXPERTS * CAP)
    owners = jnp.broadcast_to(jnp.arange(tok_count, dtype=jnp.int32)[:, None], (tok_count, TOP))
    slot_token = (
        jnp.full((EXPERTS * CAP,), tok_count, jnp.int32)
        .at[pair_slot.reshape(-1)]
        .set(owners.reshape(-1), mode="drop")
    )
    return (kept_pair, pair_slot, slot_token)


def attend_forward(queries, key_rows, value_rows, allowed):
    scores = jnp.einsum(
        "qhgd,khd->hgqk", queries, key_rows, preferred_element_type=jnp.float32
    ) * HEAD_DIM ** (-0.5)
    scores = jnp.where(allowed, scores, -1e30)
    row_max = jnp.max(scores, axis=-1, keepdims=True)
    expd = jnp.exp(scores - row_max)
    row_total = jnp.sum(expd, axis=-1, keepdims=True)
    attn_probs = (expd / row_total).astype(jnp.bfloat16)
    mixed_heads = jnp.einsum(
        "hgqk,khd->qhgd", attn_probs, value_rows, preferred_element_type=jnp.float32
    )
    return (mixed_heads.astype(jnp.bfloat16), row_max + jnp.log(row_total))


def attend_backward(queries, key_rows, value_rows, allowed, log_total, d_mixed):
    scores = jnp.einsum(
        "qhgd,khd->hgqk", queries, key_rows, preferred_element_type=jnp.float32
    ) * HEAD_DIM ** (-0.5)
    scores = jnp.where(allowed, scores, -1e30)
    attn_probs = jnp.exp(scores - log_total)
    low_probs = attn_probs.astype(jnp.bfloat16)
    d_probs = jnp.einsum("qhgd,khd->hgqk", d_mixed, value_rows, preferred_element_type=jnp.float32)
    inner_sum = jnp.sum(attn_probs * d_probs, axis=-1, keepdims=True)
    d_scores = (attn_probs * (d_probs - inner_sum)).astype(jnp.bfloat16)
    d_queries = jnp.einsum(
        "hgqk,khd->qhgd", d_scores, key_rows, preferred_element_type=jnp.float32
    ) * HEAD_DIM ** (-0.5)
    d_keys = jnp.einsum(
        "hgqk,qhgd->khd", d_scores, queries, preferred_element_type=jnp.float32
    ) * HEAD_DIM ** (-0.5)
    d_values = jnp.einsum("hgqk,qhgd->khd", low_probs, d_mixed, preferred_element_type=jnp.float32)
    return (d_queries, d_keys, d_values)


def body(
    tokens,
    attn_norm,
    attention_params,
    ffn_norm,
    expert_weights,
    gate_values,
    routes,
    slot_order,
    cotangent,
):
    sequence_count, block_len, model_width = tokens.shape
    tok_count = sequence_count * block_len
    kv_loc = attention_params.shape[1]
    input_columns = (QUERY_PER_GROUP + 2) * HEAD_DIM
    ctx_size = lax.axis_size("ctx")
    ctx_place = lax.axis_index("ctx")
    sequence_length = block_len * ctx_size
    whole_attn, whole_expert = (
        lax.all_gather(attention_params, "fsdp", axis=0, tiled=True),
        lax.all_gather(expert_weights, "fsdp", axis=0, tiled=True),
    )
    positions = ctx_place * block_len + jnp.arange(block_len, dtype=jnp.int32)
    cosine_table, sine_table = angle_tables(positions)
    cosine_table = jnp.tile(cosine_table, (sequence_count, 1))
    sine_table = jnp.tile(sine_table, (sequence_count, 1))
    cos_four = cosine_table[:, None, None, :]
    sin_four = sine_table[:, None, None, :]
    cos_three = cosine_table[:, None, :]
    sin_three = sine_table[:, None, :]
    allowed = (jnp.arange(sequence_length, dtype=jnp.int32) // block_len <= ctx_place)[
        None, None, None, :
    ]
    tok_float = tokens.reshape(tok_count, model_width).astype(jnp.float32)
    inv_one = lax.rsqrt(jnp.mean(tok_float * tok_float, axis=-1, keepdims=True) + eps)
    first_normed = (tok_float * inv_one * attn_norm).astype(jnp.bfloat16)
    projected_rows = jnp.einsum(
        "td,dhc->thc",
        first_normed,
        whole_attn[:, :, :input_columns],
        preferred_element_type=jnp.float32,
    ).reshape(tok_count, kv_loc, QUERY_PER_GROUP + 2, HEAD_DIM)
    queries = rotate(projected_rows[:, :, :QUERY_PER_GROUP], cos_four, sin_four).astype(
        jnp.bfloat16
    )
    key_rows = rotate(projected_rows[:, :, QUERY_PER_GROUP], cos_three, sin_three).astype(
        jnp.bfloat16
    )
    value_rows = projected_rows[:, :, QUERY_PER_GROUP + 1].astype(jnp.bfloat16)
    key_all, value_all = (
        lax.all_gather(
            key_rows.reshape(sequence_count, block_len, kv_loc, HEAD_DIM), "ctx", axis=1, tiled=True
        ),
        lax.all_gather(
            value_rows.reshape(sequence_count, block_len, kv_loc, HEAD_DIM),
            "ctx",
            axis=1,
            tiled=True,
        ),
    )
    query_seq = queries.reshape(sequence_count, block_len, kv_loc, QUERY_PER_GROUP, HEAD_DIM)
    mixed_heads, log_total = lax.map(
        lambda item_args: attend_forward(item_args[0], item_args[1], item_args[2], allowed),
        (query_seq, key_all, value_all),
    )
    mixed_flat = mixed_heads.reshape(tok_count, kv_loc, QUERY_PER_GROUP * HEAD_DIM)
    attn_part = jnp.einsum(
        "thc,dhc->td",
        mixed_flat,
        whole_attn[:, :, input_columns:],
        preferred_element_type=jnp.float32,
    )
    attn_sum = lax.psum(attn_part, "tp")
    residual = tok_float + attn_sum
    inv_two = lax.rsqrt(jnp.mean(residual * residual, axis=-1, keepdims=True) + eps)
    normed_two = (residual * inv_two * ffn_norm).astype(jnp.bfloat16)
    kept_pair, pair_slot, slot_token = slot_tables(
        routes.reshape(tok_count, TOP), slot_order.reshape(tok_count)
    )
    kept_float = kept_pair.astype(jnp.float32)
    gate_kept = gate_values.reshape(tok_count, TOP) * kept_float
    slot_gate = (
        jnp.zeros((EXPERTS * CAP,), jnp.float32)
        .at[pair_slot.reshape(-1)]
        .set(gate_kept.reshape(-1), mode="drop")
    )
    padded = jnp.concatenate([normed_two, jnp.zeros((1, model_width), jnp.bfloat16)], axis=0)
    inputs = padded[slot_token].reshape(EXPERTS, CAP, model_width)
    gate_act = jnp.einsum(
        "ecd,deh->ech", inputs, whole_expert[:, :, 0], preferred_element_type=jnp.float32
    )
    up_act = jnp.einsum(
        "ecd,deh->ech", inputs, whole_expert[:, :, 1], preferred_element_type=jnp.float32
    )
    gate_sigmoid = jax.nn.sigmoid(gate_act)
    active = gate_act * gate_sigmoid
    hidden = (active * up_act).astype(jnp.bfloat16)
    expert_out = jnp.einsum(
        "ech,deh->ecd", hidden, whole_expert[:, :, 2], preferred_element_type=jnp.float32
    )
    out_pad = jnp.concatenate(
        [expert_out.reshape(EXPERTS * CAP, model_width), jnp.zeros((1, model_width), jnp.float32)],
        axis=0,
    )
    picked = out_pad[pair_slot]
    moe_part = jnp.sum(picked * gate_kept[:, :, None], axis=1)
    moe = lax.psum(moe_part.astype(jnp.bfloat16), "tp").astype(jnp.float32)
    layer_out = (
        (residual + moe).astype(jnp.bfloat16).reshape(sequence_count, block_len, model_width)
    )
    grad_out = cotangent.reshape(tok_count, model_width).astype(jnp.float32)
    gate_part = jnp.sum(picked * grad_out[:, None, :], axis=-1) * kept_float
    grad_pad = jnp.concatenate([grad_out, jnp.zeros((1, model_width), jnp.float32)], axis=0)
    d_expert = (
        (grad_pad[slot_token] * slot_gate[:, None])
        .astype(jnp.bfloat16)
        .reshape(EXPERTS, CAP, model_width)
    )
    d_hidden = jnp.einsum(
        "ecd,deh->ech", d_expert, whole_expert[:, :, 2], preferred_element_type=jnp.float32
    )
    silu_slope = gate_sigmoid * (1.0 + gate_act * (1.0 - gate_sigmoid))
    d_gate_act = (d_hidden * up_act * silu_slope).astype(jnp.bfloat16)
    d_up_act = (d_hidden * active).astype(jnp.bfloat16)
    d_inputs = jnp.einsum(
        "ech,deh->ecd", d_gate_act, whole_expert[:, :, 0], preferred_element_type=jnp.float32
    )
    d_inputs = d_inputs + jnp.einsum(
        "ech,deh->ecd", d_up_act, whole_expert[:, :, 1], preferred_element_type=jnp.float32
    )
    d_in_pad = jnp.concatenate(
        [d_inputs.reshape(EXPERTS * CAP, model_width), jnp.zeros((1, model_width), jnp.float32)],
        axis=0,
    )
    d_normed_part = jnp.sum(d_in_pad[pair_slot], axis=1)
    d_normed_two, gate_grad = lax.psum((d_normed_part, gate_part), "tp")
    d_resid_norm, gain_two = norm_back(residual, inv_two, ffn_norm, d_normed_two)
    d_residual = grad_out + d_resid_norm
    d_attn = d_residual.astype(jnp.bfloat16)
    d_mixed = jnp.einsum(
        "td,dhc->thc", d_attn, whole_attn[:, :, input_columns:], preferred_element_type=jnp.float32
    ).astype(jnp.bfloat16)
    d_mixed_seq = d_mixed.reshape(sequence_count, block_len, kv_loc, QUERY_PER_GROUP, HEAD_DIM)
    d_queries, d_key_all, d_value_all = lax.map(
        lambda item_args: attend_backward(
            item_args[0], item_args[1], item_args[2], allowed, item_args[3], item_args[4]
        ),
        (query_seq, key_all, value_all, log_total, d_mixed_seq),
    )
    d_keys, d_values = (
        lax.psum_scatter(
            d_key_all.astype(jnp.bfloat16), "ctx", scatter_dimension=1, tiled=True
        ).astype(jnp.float32),
        lax.psum_scatter(
            d_value_all.astype(jnp.bfloat16), "ctx", scatter_dimension=1, tiled=True
        ).astype(jnp.float32),
    )
    d_queries = rotate(
        d_queries.reshape(tok_count, kv_loc, QUERY_PER_GROUP, HEAD_DIM), cos_four, -sin_four
    )
    d_keys = rotate(d_keys.reshape(tok_count, kv_loc, HEAD_DIM), cos_three, -sin_three)
    d_values = d_values.reshape(tok_count, kv_loc, HEAD_DIM)
    d_projected = jnp.concatenate([d_queries, d_keys[:, :, None], d_values[:, :, None]], axis=2)
    d_projected = d_projected.astype(jnp.bfloat16).reshape(tok_count, kv_loc, input_columns)
    d_normed_local = jnp.einsum(
        "thc,dhc->td",
        d_projected,
        whole_attn[:, :, :input_columns],
        preferred_element_type=jnp.float32,
    )
    d_normed_one = lax.psum(d_normed_local.astype(jnp.bfloat16), "tp").astype(jnp.float32)
    d_tok_norm, gain_one = norm_back(tok_float, inv_one, attn_norm, d_normed_one)
    tokens_grad = (
        (d_residual + d_tok_norm)
        .astype(jnp.bfloat16)
        .reshape(sequence_count, block_len, model_width)
    )
    gain_one, gain_two = lax.psum((gain_one, gain_two), ("fsdp", "ctx"))
    in_term = jnp.einsum(
        "td,thc->dhc", first_normed, d_projected, preferred_element_type=jnp.float32
    )
    out_term = jnp.einsum("td,thc->dhc", d_attn, mixed_flat, preferred_element_type=jnp.float32)
    attn_grad = lax.psum_scatter(
        jnp.concatenate([in_term, out_term], axis=2),
        ("fsdp", "ctx"),
        scatter_dimension=0,
        tiled=True,
    )
    gate_term = jnp.einsum("ecd,ech->deh", inputs, d_gate_act, preferred_element_type=jnp.float32)
    up_term = jnp.einsum("ecd,ech->deh", inputs, d_up_act, preferred_element_type=jnp.float32)
    down_term = jnp.einsum("ecd,ech->deh", d_expert, hidden, preferred_element_type=jnp.float32)
    expert_grad = lax.psum_scatter(
        jnp.stack([gate_term, up_term, down_term], axis=2),
        ("fsdp", "ctx"),
        scatter_dimension=0,
        tiled=True,
    )
    attn_grad, expert_grad = (
        lax.all_gather(attn_grad.astype(jnp.bfloat16), "ctx", axis=0, tiled=True).astype(
            attn_grad.dtype
        ),
        lax.all_gather(expert_grad.astype(jnp.bfloat16), "ctx", axis=0, tiled=True).astype(
            expert_grad.dtype
        ),
    )
    return (
        layer_out,
        tokens_grad,
        attn_grad,
        expert_grad,
        gain_one,
        gain_two,
        gate_grad.reshape(sequence_count, block_len, TOP),
    )


MESH_ID = pl.DeviceIdType.MESH
MIB = 2**20


def expert_order(place):
    row = jnp.arange(128, dtype=jnp.int32)
    expert = (((row // 32) ^ place) * 2) + (row // 16) % 2
    source = (row % 16) * 8 + expert
    return (source[:, None] == row[None, :]).astype(jnp.bfloat16)


def join_kernel(order_ref, in_ref, attn_in_ref, out_ref, attn_out_ref):
    width = in_ref.shape[3]
    for m in range(3):
        for k in range(in_ref.shape[2] // 16):
            block = in_ref[:, m, pl.ds(k * 16, 16), :].reshape(128, width)
            moved = jnp.dot(order_ref[...], block, preferred_element_type=jnp.float32)
            out_ref[pl.ds(k * 16, 16), m] = moved.reshape(16, 8, width)
    rows, columns = attn_in_ref.shape
    parts = columns // 128
    for j in range(parts):
        part = attn_in_ref[:, pl.ds(j * 128, 128)].astype(jnp.float32)
        attn_out_ref[pl.ds(j, rows, stride=parts), :] = part


def join_experts(grads, attn_grad, order):
    experts, _, rows, width = grads.shape
    columns = attn_grad.shape[1]
    step = 64
    lines = step * columns // 128
    return pl.pallas_call(
        join_kernel,
        grid=(rows // step,),
        in_specs=[
            pl.BlockSpec((128, 128), lambda i: (0, 0)),
            pl.BlockSpec((experts, 3, step, width), lambda i: (0, 0, i, 0)),
            pl.BlockSpec((step, columns), lambda i: (i, 0)),
        ],
        out_specs=[
            pl.BlockSpec((step, 3, experts, width), lambda i: (i, 0, 0, 0)),
            pl.BlockSpec((lines, 128), lambda i: (i, 0)),
        ],
        out_shape=[
            jax.ShapeDtypeStruct((rows, 3, experts, width), jnp.float32),
            jax.ShapeDtypeStruct((rows * columns // 128, 128), jnp.float32),
        ],
        compiler_params=pltpu.CompilerParams(vmem_limit_bytes=60 * MIB),
        name="join_experts",
    )(order, grads, attn_grad)


NT = (((1,), (1,)), ((), ()))
TN = (((0,), (0,)), ((), ()))


def dot_f32(a, b, dims=(((1,), (0,)), ((), ()))):
    return lax.dot_general(a, b, dims, preferred_element_type=jnp.float32)


def block_probs(last, keys, query):
    scores = dot_f32(keys, query, NT) * HEAD_DIM ** (-0.5)
    block = lax.broadcasted_iota(jnp.int32, scores.shape, 0) // query.shape[0]
    scores = jnp.where(block <= last, scores, -1e30)
    expd = jnp.exp(scores - jnp.max(scores, axis=0, keepdims=True))
    return expd * (1.0 / jnp.sum(expd, axis=0, keepdims=True))


def place():
    return lax.axis_index("fsdp"), lax.axis_index("ctx"), lax.axis_index("tp")


def plane_peers(f):
    return f + 1 - 2 * lax.rem(f, 2), lax.rem(f + 2, 4), 3 - f


def rows_of(index, size):
    return pl.ds(pl.multiple_of(index * size, size), size)


def greet(devices):
    barrier = pltpu.get_barrier_semaphore()
    for device in devices:
        pl.semaphore_signal(barrier, inc=1, device_id=device, device_id_type=MESH_ID)
    pl.semaphore_wait(barrier, len(devices))


def turn(value, cosine, sine):
    return value * cosine + pltpu.roll(value, HEAD_DIM // 2, 1) * sine


def frequencies():
    i = np.arange(HEAD_DIM // 2, dtype=np.float32)
    freq = (theta_base ** (-(i * 2.0) / HEAD_DIM)).astype(np.float32)
    return jnp.asarray(np.concatenate([freq, freq])[None, :])


def front_kernel(
    tok_ref,
    gain_one_ref,
    gain_two_ref,
    freq_ref,
    routes_ref,
    gates_ref,
    order_ref,
    attn_hbm,
    experts_hbm,
    cot_hbm,
    xn_ref,
    q_ref,
    kv_ref,
    mixed_ref,
    res_ref,
    wl_ref,
    wa_hbm,
    w_hbm,
    x_hbm,
    dy_hbm,
    raw,
    pieces,
    wa,
    part,
    part_in,
    low_half,
    send,
    recv,
    local,
):
    f, z, c = place()
    fx, fy, fd = plane_peers(f)
    count, width = tok_ref.shape
    half = count // 2
    shard = attn_hbm.shape[0]
    cut = shard // 2
    in_cols = (QUERY_PER_GROUP + 2) * HEAD_DIM
    ins = pl.ds(0, in_cols)
    outs = pl.ds(in_cols, attn_hbm.shape[1] - in_cols)

    def at(fsdp=f, ctx=z, tp=c):
        return {"fsdp": fsdp, "ctx": ctx, "tp": tp}

    def remote(src, dst, k, device):
        return pltpu.make_async_remote_copy(
            src_ref=src,
            dst_ref=dst,
            send_sem=send.at[k],
            recv_sem=recv.at[k],
            device_id=device,
            device_id_type=MESH_ID,
        )

    plane = [at(fx), at(fy), at(fd)]
    rel = [fx, fy, fd]
    line = [at(ctx=lax.rem(z + s, 4)) for s in range(1, 4)]
    sibling = at(tp=1 - c)
    mine = rows_of(f, shard)
    load = pltpu.make_async_copy(experts_hbm, raw, local.at[6])
    load.start()
    greet(plane + line + [sibling])

    owned = pltpu.make_async_copy(attn_hbm, wa.at[mine], local.at[0])
    owned.start()
    in_x = remote(attn_hbm.at[:, ins], wa.at[mine, ins], 0, at(fx))
    in_y = remote(attn_hbm.at[:, ins], wa.at[mine, ins], 1, at(fy))
    in_x.start()
    in_y.start()

    rank = jnp.broadcast_to(order_ref[...].astype(jnp.float32), (count, count))
    ahead = jnp.where(rank.T < rank, 1.0, 0.0).astype(jnp.bfloat16)
    expert = lax.broadcasted_iota(jnp.int32, (128, count), 0)
    member = jnp.zeros((128, count), jnp.float32)
    gate = jnp.zeros((128, count), jnp.float32)
    for j in range(TOP):
        hit = jnp.broadcast_to(routes_ref[j : j + 1, :], (128, count)) == expert
        member = jnp.where(hit, 1.0, member)
        gate = jnp.where(hit, jnp.broadcast_to(gates_ref[j : j + 1, :], (128, count)), gate)
    slots = dot_f32(member.astype(jnp.bfloat16), ahead)
    gate = jnp.where(slots < CAP - 0.5, gate, 0.0)
    wl_ref[f] = gate[:EXPERTS]
    gate_copies = [remote(wl_ref.at[f], wl_ref.at[f], 2 + i, plane[i]) for i in range(3)]
    for copy in gate_copies:
        copy.start()

    own_dy = [
        pltpu.make_async_copy(
            cot_hbm.at[pl.ds(i * half, half)], dy_hbm.at[i, f], local.at[2 + i]
        )
        for i in range(2)
    ]
    for copy in own_dy:
        copy.start()

    row = lax.broadcasted_iota(jnp.int32, (128, 128), 0)
    column = lax.broadcasted_iota(jnp.int32, (128, 128), 1)
    owner = jnp.where(row < 64, jnp.where(row < 32, f, fx), jnp.where(row < 96, fy, fd))
    source = (row % 16) * 8 + owner * 2 + (row // 16) % 2
    order = jnp.where(source == column, 1.0, 0.0).astype(jnp.bfloat16)

    def split(m):
        def body(k, _):
            rows = pl.ds(pl.multiple_of(k * 16, 16), 16)
            block = raw[rows, m].reshape(128, raw.shape[3])
            moved = dot_f32(order, block).astype(jnp.bfloat16)
            pieces[:, m, rows, :] = moved.reshape(8, 16, raw.shape[3])
            return 0

        lax.fori_loop(0, shard // 16, body, 0)

    cut_rows = shard // 4
    from_rows = rows_of(z, cut_rows)
    to_rows = rows_of(4 * f + z, cut_rows)

    def quarter(m, i):
        return remote(
            pieces.at[pl.ds(2 * (i + 1), 2), m, from_rows],
            w_hbm.at[:, m, to_rows, :],
            37 + 3 * m + i,
            plane[i],
        )

    def hand_on(m, i):
        quarters[3 * m + i].wait_recv()
        here = w_hbm.at[:, m, rows_of(4 * rel[i] + z, cut_rows), :]
        copies = [remote(here, here, 43 + 9 * m + 3 * i + s, line[s]) for s in range(3)]
        for copy in copies:
            copy.start()
        return copies

    load.wait()
    split(0)
    quarters = [quarter(0, i) for i in range(3)]
    for copy in quarters:
        copy.start()

    tok = tok_ref[...].astype(jnp.float32)
    inv = lax.rsqrt(jnp.mean(tok * tok, axis=-1, keepdims=True) + eps)
    xn_ref[...] = (tok * inv * gain_one_ref[...]).astype(jnp.bfloat16)
    position = z * count + lax.broadcasted_iota(jnp.int32, (count, HEAD_DIM), 0)
    angle = position.astype(jnp.float32) * freq_ref[...]
    cosine = jnp.cos(angle)
    lane = lax.broadcasted_iota(jnp.int32, (count, HEAD_DIM), 1)
    sine = jnp.where(lane < HEAD_DIM // 2, -jnp.sin(angle), jnp.sin(angle))

    top, low = rows_of(2 * fx, cut), rows_of(2 * fy + 1, cut)
    in_x.wait_recv()
    in_xy = remote(wa.at[top, ins], wa.at[top, ins], 5, at(fy))
    in_xy.start()
    in_y.wait_recv()
    in_yx = remote(wa.at[low, ins], wa.at[low, ins], 6, at(fx))
    in_yx.start()
    out_x = remote(attn_hbm.at[:, outs], wa.at[mine, outs], 7, at(fx))
    out_y = remote(attn_hbm.at[:, outs], wa.at[mine, outs], 8, at(fy))
    split(1)
    quarters += [quarter(1, i) for i in range(3)]
    for copy in quarters[3:]:
        copy.start()
    out_x.start()
    out_y.start()
    handed = hand_on(0, 0) + hand_on(0, 1)
    split(2)
    own_w = pltpu.make_async_copy(pieces.at[pl.ds(0, 2)], w_hbm.at[:, :, mine, :], local.at[1])
    own_w.start()
    owned.wait()
    in_xy.wait_recv()
    in_yx.wait_recv()

    normed = xn_ref[...]
    for h in range(QUERY_PER_GROUP + 2):
        cols = pl.ds(h * HEAD_DIM, HEAD_DIM)
        if h % 2 == 0:
            pair = dot_f32(normed, wa[:, pl.ds(h * HEAD_DIM, 2 * HEAD_DIM)])
        value = pair[:, (h % 2) * HEAD_DIM : (h % 2 + 1) * HEAD_DIM]
        if h <= QUERY_PER_GROUP:
            value = turn(value, cosine, sine)
        if h < QUERY_PER_GROUP:
            q_ref[:, cols] = value.astype(jnp.bfloat16)
        else:
            kv_ref[0, :, pl.ds((h - QUERY_PER_GROUP) * HEAD_DIM, HEAD_DIM)] = value.astype(
                jnp.bfloat16
            )
    kv_copies = [remote(kv_ref.at[0], kv_ref.at[s], 8 + s, line[s - 1]) for s in range(1, 4)]
    for s in range(1, 4):

        @pl.when(z + s < 4)
        def _(s=s):
            kv_copies[s - 1].start()

        @pl.when(z < s)
        def _(s=s):
            kv_ref[s] = jnp.zeros(kv_ref.shape[1:], jnp.bfloat16)

    handed += hand_on(0, 2)
    out_x.wait_recv()
    out_xy = remote(wa.at[top, outs], wa.at[top, outs], 12, at(fy))
    out_xy.start()
    out_y.wait_recv()
    out_yx = remote(wa.at[low, outs], wa.at[low, outs], 13, at(fx))
    out_yx.start()

    w_copies = [
        remote(pieces.at[pl.ds(2 * (i + 1), 2), 2], w_hbm.at[:, 2, mine, :], 14 + i, plane[i])
        for i in range(3)
    ]
    for copy in w_copies:
        copy.start()
    dy_copies = [
        remote(cot_hbm.at[rows_of(c, half)], dy_hbm.at[c, f], 23 + i, plane[i]) for i in range(3)
    ]
    for copy in dy_copies:
        copy.start()
    for i in range(3):
        handed += hand_on(1, i)

    for s in range(1, 4):

        @pl.when(z >= s)
        def _(s=s):
            kv_copies[s - 1].wait_recv()

    keys = kv_ref[:, :, pl.ds(0, HEAD_DIM)].reshape(4 * count, HEAD_DIM)
    vals = kv_ref[:, :, pl.ds(HEAD_DIM, HEAD_DIM)].reshape(4 * count, HEAD_DIM)
    for g in range(QUERY_PER_GROUP):
        cols = pl.ds(g * HEAD_DIM, HEAD_DIM)
        probs = block_probs(z, keys, q_ref[:, cols]).astype(jnp.bfloat16)
        mixed_ref[:, cols] = dot_f32(probs, vals, TN).astype(jnp.bfloat16)

    out_xy.wait_recv()
    out_yx.wait_recv()
    store_wa = pltpu.make_async_copy(wa, wa_hbm, local.at[4])
    store_wa.start()
    for s in range(width // 256):
        cols = pl.ds(s * 256, 256)
        part[:, cols] = dot_f32(mixed_ref[...], wa[cols, outs], NT)
    swap = remote(part.at[rows_of(1 - c, half)], part_in, 26, sibling)
    swap.start()
    swap.wait_recv()
    my_rows = rows_of(c, half)
    residual = tok_ref[my_rows, :].astype(jnp.float32) + (part[my_rows, :] + part_in[...])
    res_ref[...] = residual
    inv = lax.rsqrt(jnp.mean(residual * residual, axis=-1, keepdims=True) + eps)
    low_half[...] = (residual * inv * gain_two_ref[...]).astype(jnp.bfloat16)
    own_x = pltpu.make_async_copy(low_half, x_hbm.at[c, f], local.at[5])
    own_x.start()
    x_copies = [remote(low_half, x_hbm.at[c, f], 27 + i, plane[i]) for i in range(3)]
    for copy in x_copies:
        copy.start()
    sib_x = [remote(low_half, x_hbm.at[c, f], 30, sibling)]
    sib_x[0].start()

    sib_dy = []
    for i in range(3):
        dy_copies[i].wait_recv()
        sib_dy.append(remote(dy_hbm.at[c, rel[i]], dy_hbm.at[c, rel[i]], 31 + i, sibling))
        sib_dy[i].start()
    for i in range(3):
        x_copies[i].wait_recv()
        sib_x.append(remote(x_hbm.at[c, rel[i]], x_hbm.at[c, rel[i]], 34 + i, sibling))
        sib_x[i + 1].start()

    for copy in w_copies + gate_copies + handed + sib_dy + sib_x:
        copy.wait_recv()
    for s in range(1, 4):

        @pl.when(z + s < 4)
        def _(s=s):
            kv_copies[s - 1].wait_send()

    for copy in [in_x, in_y, in_xy, in_yx, out_x, out_y, out_xy, out_yx, swap]:
        copy.wait_send()
    for copy in w_copies + quarters + handed + gate_copies + dy_copies + x_copies + sib_dy + sib_x:
        copy.wait_send()
    for copy in [own_w, own_x, store_wa] + own_dy:
        copy.wait()


def front(tok, gain_one, gain_two, routes, gates, order, attn_own, weights, cot):
    count, width = tok.shape
    half = count // 2
    shard, columns = attn_own.shape
    experts, hidden = EXPERTS // 4, weights.shape[3]
    vmem, hbm = pl.BlockSpec(memory_space=pltpu.VMEM), pl.BlockSpec(memory_space=pl.ANY)
    bf16, f32 = jnp.bfloat16, jnp.float32
    shape = jax.ShapeDtypeStruct
    return pl.pallas_call(
        front_kernel,
        in_specs=[vmem] * 7 + [hbm] * 3,
        out_specs=[vmem] * 6 + [hbm] * 4,
        out_shape=[
            shape((count, width), bf16),
            shape((count, QUERY_PER_GROUP * HEAD_DIM), bf16),
            shape((4, count, 2 * HEAD_DIM), bf16),
            shape((count, QUERY_PER_GROUP * HEAD_DIM), bf16),
            shape((half, width), f32),
            shape((4, EXPERTS, count), f32),
            shape((4 * shard, columns), bf16),
            shape((experts, 3, 4 * shard, hidden), bf16),
            shape((2, 4, half, width), bf16),
            shape((2, 4, half, width), bf16),
        ],
        scratch_shapes=[
            pltpu.VMEM(weights.shape, bf16),
            pltpu.VMEM((EXPERTS, 3, shard, hidden), bf16),
            pltpu.VMEM((4 * shard, columns), bf16),
            pltpu.VMEM((count, width), f32),
            pltpu.VMEM((half, width), f32),
            pltpu.VMEM((half, width), bf16),
            pltpu.SemaphoreType.DMA((61,)),
            pltpu.SemaphoreType.DMA((61,)),
            pltpu.SemaphoreType.DMA((7,)),
        ],
        compiler_params=pltpu.CompilerParams(
            collective_id=0, has_side_effects=True, vmem_limit_bytes=60 * MIB
        ),
        name="front",
    )(tok, gain_one, gain_two, frequencies(), routes, gates, order, attn_own, weights, cot)


def ctx_chunks(mats, shard):
    early = [(0, 0), (1, 0)]
    chunks = [(j, r, 0, shard) for j, r in early]
    chunks += [(j, r, 0, shard) for j in range(mats) for r in range(4) if (j, r) not in early]
    return chunks, [shard // 8] * 8


def rear_kernel(
    res_ref,
    xn_ref,
    q_ref,
    kv_ref,
    mixed_ref,
    gain_one_ref,
    gain_two_ref,
    freq_ref,
    tok_hbm,
    cot_hbm,
    x_hbm,
    dy_hbm,
    w_hbm,
    wl_ref,
    wa_hbm,
    layer_ref,
    tokgrad_ref,
    gains_ref,
    gate_ref,
    attn_hbm,
    fin_hbm,
    xy,
    wgu,
    wd,
    gu,
    hid,
    table,
    ge,
    r1,
    dn_in,
    dn_got,
    mo_in,
    mo_got,
    gg_in,
    gg_sum,
    gg_got,
    dres,
    dattn,
    dmixed,
    dproj,
    dkv,
    dkv_low,
    dkv_got,
    d1,
    d1_low,
    d1_in,
    ra,
    a1,
    gacc,
    gin,
    tok_half,
    cot_half,
    send,
    recv,
    local,
    z_out,
    z_across,
    z_back,
    z_r1,
    z_r2,
    f_out,
    f_in,
    credit,
):
    f, z, c = place()
    fx, fy, fd = plane_peers(f)
    rel = [f, fx, fy, fd]
    f32, bf16 = jnp.float32, jnp.bfloat16
    count, width = tok_hbm.shape
    half = count // 2
    shard = attn_hbm.shape[0]
    in_cols = (QUERY_PER_GROUP + 2) * HEAD_DIM
    q_cols = QUERY_PER_GROUP * HEAD_DIM
    ins = pl.ds(0, in_cols)
    outs = pl.ds(in_cols, attn_hbm.shape[1] - in_cols)
    scale = HEAD_DIM ** (-0.5)

    def at(fsdp=f, ctx=z, tp=c):
        return {"fsdp": fsdp, "ctx": ctx, "tp": tp}

    def copy_to(src, dst, send_sem, recv_sem, device):
        return pltpu.make_async_remote_copy(
            src_ref=src,
            dst_ref=dst,
            send_sem=send_sem,
            recv_sem=recv_sem,
            device_id=device,
            device_id_type=MESH_ID,
        )

    def remote(src, dst, k, device):
        return copy_to(src, dst, send.at[k], recv.at[k], device)

    plane = [at(fx), at(fy), at(fd)]
    line = [at(ctx=lax.rem(z + s, 4)) for s in range(1, 4)]
    sibling = at(tp=1 - c)
    partner = at(ctx=z + 1 - 2 * lax.rem(z, 2))
    opposite = at(ctx=3 - z)
    inner = (z == 1) | (z == 2)
    outer = (z == 0) | (z == 3)

    own = w_hbm.shape[0]
    hidden = w_hbm.shape[3]
    tokens = 8 * half
    tile = 2 * half
    loads = [pltpu.make_async_copy(x_hbm, xy.at[pl.ds(0, tokens)], local.at[0])]
    for e in range(own):
        for m in range(2):
            cols = pl.ds((2 * e + m) * hidden, hidden)
            loads.append(pltpu.make_async_copy(w_hbm.at[e, m], wgu.at[:, cols], local.at[1 + 2 * e + m]))
    loads.append(pltpu.make_async_copy(dy_hbm, xy.at[pl.ds(tokens, tokens)], local.at[5]))
    for e in range(own):
        cols = pl.ds(e * hidden, hidden)
        loads.append(pltpu.make_async_copy(w_hbm.at[e, 2], wd.at[:, cols], local.at[6 + e]))
    my_rows = rows_of(c, half)
    loads.append(pltpu.make_async_copy(tok_hbm.at[my_rows], tok_half, local.at[8]))
    loads.append(pltpu.make_async_copy(cot_hbm.at[my_rows], cot_half, local.at[9]))
    for copy in loads:
        copy.start()
    greet(plane + line + [sibling])
    for b in range(8):
        rows = wl_ref[b % 4, :, pl.ds((b // 4) * half, half)]
        rows = jnp.concatenate([rows, jnp.zeros((128 - EXPERTS, half), f32)], axis=0)
        table[pl.ds(b * half, half), :] = rows.T
    for copy in loads:
        copy.wait()

    lanes = lax.broadcasted_iota(jnp.int32, (tile, 128), 1)

    def act_step(i, _):
        rows = pl.ds(pl.multiple_of(i * tile, tile), tile)
        acts = dot_f32(xy[rows, :], wgu[...])
        plain = dot_f32(xy[pl.ds(pl.multiple_of(tokens + i * tile, tile), tile), :], wd[...])
        scales = table[rows, :]
        sums = jnp.zeros((tile, 128), f32)
        for e in range(own):
            gate_act = acts[:, 2 * e * hidden : (2 * e + 1) * hidden]
            up_act = acts[:, (2 * e + 1) * hidden : (2 * e + 2) * hidden]
            d_plain = plain[:, e * hidden : (e + 1) * hidden]
            here = lanes == own * f + e
            factor = jnp.sum(jnp.where(here, scales, 0.0), axis=1, keepdims=True)
            sigmoid = 1.0 / (1.0 + jnp.exp(-gate_act))
            active = gate_act * sigmoid
            act = active * up_act
            total = jnp.sum(act * d_plain, axis=1, keepdims=True)
            sums = jnp.where(here, jnp.where(factor != 0.0, total, 0.0), sums)
            d_hidden = d_plain * factor
            slope = sigmoid * (1.0 + gate_act * (1.0 - sigmoid))
            hid[rows, pl.ds(e * hidden, hidden)] = (act * factor).astype(bf16)
            gu[rows, pl.ds(2 * e * hidden, hidden)] = (d_hidden * up_act * slope).astype(bf16)
            gu[rows, pl.ds((2 * e + 1) * hidden, hidden)] = (d_hidden * active).astype(bf16)
        table[rows, :] = sums
        return 0

    lax.fori_loop(0, tokens // tile, act_step, 0)
    side, far = rows_of(c, 4 * half), rows_of(1 - c, 4 * half)
    gg_swap = remote(table.at[far], gg_in, 1, sibling)
    gg_swap.start()

    def grad_step(t, _):
        cols = pl.ds(pl.multiple_of(lax.rem(f + t, 4) * shard, 128), shard)
        into_in = dot_f32(xy[pl.ds(0, tokens), cols], gu[...], TN).astype(bf16)
        into_out = dot_f32(xy[pl.ds(tokens, tokens), cols], hid[...], TN).astype(bf16)
        for e in range(own):
            for m in range(2):
                k = 2 * e + m
                ge[3 * e + m, cols, :] = into_in[:, k * hidden : (k + 1) * hidden]
            ge[3 * e + 2, cols, :] = into_out[:, e * hidden : (e + 1) * hidden]
        return 0

    def down_step(i, _):
        rows = pl.ds(pl.multiple_of(i * tile, tile), tile)
        ra[rows, pl.ds(0, width)] = dot_f32(gu[rows, :], wgu[...], NT).astype(bf16)
        return 0

    def out_step(i, _):
        rows = pl.ds(pl.multiple_of(i * tile, tile), tile)
        xy[rows, :] = dot_f32(hid[rows, :], wd[...], NT).astype(bf16)
        return 0

    chunks, attn_rows = ctx_chunks(ge.shape[0], shard)
    n_expert = len(chunks)
    n_all = n_expert + len(attn_rows)

    def chunk(k):
        if k < n_expert:
            j, r, low, size = chunks[k]
            rows = pl.ds(pl.multiple_of(rel[r] * shard + low, 16), size)
            return ge.at[j, rows], r1.at[j, rows]
        rows = pl.ds(sum(attn_rows[: k - n_expert]), attn_rows[k - n_expert])
        return ra.at[rows], a1.at[rows]

    def add_into(dst, left, right):
        size = math.gcd(dst.shape[0], 64)

        def body(i, _):
            rows = pl.ds(pl.multiple_of(i * size, size), size)
            dst[rows, :] = (left[rows, :].astype(f32) + right[rows, :].astype(f32)).astype(bf16)
            return 0

        lax.fori_loop(0, dst.shape[0] // size, body, 0)

    def first(k):
        own, one = chunk(k)
        return copy_to(own, one, z_out.at[k], z_r1.at[k], partner)

    def across(k):
        own, one = chunk(k)
        return copy_to(own, one, z_across.at[k], z_r2.at[k], opposite)

    def back(k):
        _, one = chunk(k)
        return copy_to(one, one, z_back.at[k], z_r1.at[k], partner)

    def final(k):
        _, one = chunk(k)
        j, r, low, size = chunks[k]
        there = fin_hbm.at[r, j, pl.ds(low, size)]
        if r == 0:
            return pltpu.make_async_copy(one, there, f_out.at[k])
        return copy_to(one, there, f_out.at[k], f_in.at[k], plane[r - 1])

    pending, ready = [], []
    pace = 2
    lag_a, lag_b, lag_c, window = 1, 3, 6, 3

    def z_step(i):
        if i < n_all:

            @pl.when(outer)
            def _():
                if i >= window:
                    first(i - window).wait_send()
                first(i).start()

        if lag_a <= i < n_all + lag_a:
            k = i - lag_a

            @pl.when(inner)
            def _():
                own, one = chunk(k)
                first(k).wait_recv()
                add_into(own, own, one)
                pl.semaphore_signal(credit, inc=1, device_id=opposite, device_id_type=MESH_ID)

        if lag_a <= i < n_all + lag_a:
            k = i - lag_a

            @pl.when(inner)
            def _():
                pl.semaphore_wait(credit, 1)
                across(k).start()

        if lag_b <= i < n_all + lag_b:
            k = i - lag_b

            @pl.when(inner)
            def _():
                own, one = chunk(k)
                across(k).wait_recv()
                add_into(one, own, one)
                back(k).start()

        if lag_c <= i < n_all + lag_c:
            k = i - lag_c

            @pl.when(outer)
            def _():
                back(k).wait_recv()

            if k < n_expert:
                ready.append(k)

        for _ in range(pace):
            if pending:
                pending.pop(0).start()
            elif ready:
                final(ready.pop(0)).start()

    steps = iter(range(n_all + max(lag_b, lag_c)))

    def go_on(count=1):
        for _ in range(count):
            z_step(next(steps))

    wide = pl.ds(0, width)
    lax.fori_loop(0, 1, grad_step, 0)
    go_on()
    lax.fori_loop(2 * (1 - c), 2 * (1 - c) + 2, down_step, 0)
    dn_swap = remote(ra.at[far, wide], dn_in, 0, sibling)
    dn_swap.start()
    lax.fori_loop(2 * c, 2 * c + 2, down_step, 0)
    go_on()

    def both(ref, arrived):
        def body(i, _):
            rows = pl.ds(pl.multiple_of(c * 4 * half + i * half, half), half)
            here = pl.ds(pl.multiple_of(i * half, half), half)
            ref[rows, wide] = (ref[rows, wide].astype(f32) + arrived[here, :].astype(f32)).astype(bf16)
            return 0

        lax.fori_loop(0, 4, body, 0)

    def group(i):
        return rows_of(4 * c + i, half)

    gg_swap.wait_recv()
    gg_sum[...] = table[side, :] + gg_in[...]
    dn_swap.wait_recv()
    both(ra, dn_in)
    dn_out = [
        remote(ra.at[group(rel[i + 1]), wide], dn_got.at[i], 3 + i, plane[i]) for i in range(3)
    ]
    gg_out = [
        remote(gg_sum.at[rows_of(rel[i + 1], half)], gg_got.at[i], 6 + i, plane[i])
        for i in range(3)
    ]
    for copy in dn_out + gg_out:
        copy.start()
    lax.fori_loop(1, 4, grad_step, 0)
    go_on()
    lax.fori_loop(2 * (1 - c), 2 * (1 - c) + 2, out_step, 0)
    mo_swap = remote(xy.at[far], mo_in, 2, sibling)
    mo_swap.start()
    lax.fori_loop(2 * c, 2 * c + 2, out_step, 0)
    in_part, out_part = pl.ds(0, in_cols), pl.ds(0, q_cols)
    load_in = pltpu.make_async_copy(wa_hbm.at[:, ins], wgu.at[:, in_part], local.at[0])
    load_out = pltpu.make_async_copy(wa_hbm.at[:, outs], wd, local.at[1])
    load_out.start()
    load_in.start()
    go_on()
    for copy in dn_out:
        copy.wait_recv()
    for copy in dn_out + [dn_swap]:
        copy.wait_send()
    mo_swap.wait_recv()
    both(xy, mo_in)
    d_two = ra[group(f), wide].astype(f32)
    for i in range(3):
        d_two = d_two + dn_got[i].astype(f32)
    residual = res_ref[...]
    inv = lax.rsqrt(jnp.mean(residual * residual, axis=-1, keepdims=True) + eps)
    scaled = d_two * gain_two_ref[...]
    inside = jnp.mean(scaled * residual, axis=-1, keepdims=True)
    d_norm = inv * scaled - residual * (inv * inv * inv * inside)
    gacc[0] = jnp.zeros(gacc.shape[1:], f32)
    gacc[0, 1:2, :] = jnp.sum(d_two * residual * inv, axis=0, keepdims=True)
    d_res = cot_half[...].astype(f32) + d_norm
    dres[...] = d_res
    dattn[my_rows, :] = d_res.astype(bf16)
    da_swap = remote(dattn.at[my_rows], dattn.at[my_rows], 12, sibling)
    da_swap.start()
    mo_out = [remote(xy.at[group(rel[i + 1])], mo_got.at[i], 9 + i, plane[i]) for i in range(3)]
    for copy in mo_out:
        copy.start()
    load_out.wait()
    go_on()
    da_swap.wait_recv()
    dmixed[...] = dot_f32(dattn[...], wd[...]).astype(bf16)
    go_on()

    position = z * count + lax.broadcasted_iota(jnp.int32, (count, HEAD_DIM), 0)
    angle = position.astype(f32) * freq_ref[...]
    cosine = jnp.cos(angle)
    lane = lax.broadcasted_iota(jnp.int32, (count, HEAD_DIM), 1)
    sine = jnp.where(lane < HEAD_DIM // 2, jnp.sin(angle), -jnp.sin(angle))
    keys = kv_ref[:, :, pl.ds(0, HEAD_DIM)].reshape(4 * count, HEAD_DIM)
    vals = kv_ref[:, :, pl.ds(HEAD_DIM, HEAD_DIM)].reshape(4 * count, HEAD_DIM)
    key_cols, val_cols = pl.ds(0, HEAD_DIM), pl.ds(HEAD_DIM, HEAD_DIM)
    dkv[...] = jnp.zeros_like(dkv)
    for g in range(QUERY_PER_GROUP):
        cols = pl.ds(g * HEAD_DIM, HEAD_DIM)
        query = q_ref[:, cols]
        d_mix = dmixed[:, cols]
        probs = block_probs(z, keys, query)
        d_probs = dot_f32(vals, d_mix, NT)
        inside = jnp.sum(probs * d_probs, axis=0, keepdims=True)
        d_scores = (probs * (d_probs - inside)).astype(bf16)
        d_query = dot_f32(d_scores, keys, TN) * scale
        dproj[:, cols] = turn(d_query, cosine, sine).astype(bf16)
        dkv[:, key_cols] += dot_f32(d_scores, query) * scale
        dkv[:, val_cols] += dot_f32(probs.astype(bf16), d_mix)
        if g % 3 == 2:
            go_on()
    dkv_low[...] = dkv[...].reshape(dkv_low.shape).astype(bf16)
    dkv_out = [
        remote(dkv_low.at[s], dkv_got.at[s - 1], 12 + s, at(ctx=lax.rem(z + 4 - s, 4)))
        for s in range(1, 4)
    ]
    for s in range(1, 4):

        @pl.when(z >= s)
        def _(s=s):
            dkv_out[s - 1].start()

    low_rows = pl.ds(4 * shard, shard)

    def weight_grad(left, right, cols):
        def body(i, _):
            rows = pl.ds(pl.multiple_of(i * 256, 256), 256)
            xy[rows, cols] = dot_f32(left[:, rows], right, TN).astype(bf16)
            return 0

        lax.fori_loop(0, width // 256, body, 0)

    def send_grad(cols, into, k):
        third = shard // 3
        copies = []
        for p in range(3):
            for i in range(3):
                rows = pl.ds(pl.multiple_of(rel[i + 1] * shard + p * third, third), third)
                copies.append(
                    remote(
                        xy.at[rows, cols],
                        ra.at[pl.ds(i * shard + p * third, third), into],
                        k + 3 * p + i,
                        plane[i],
                    )
                )
        pending.extend(copies)
        return copies

    for copy in mo_out + gg_out:
        copy.wait_recv()
    moe = xy[group(f), :].astype(f32)
    gates = gg_sum[rows_of(f, half), :]
    for i in range(3):
        moe = moe + mo_got[i].astype(f32)
        gates = gates + gg_got[i]
    layer_ref[my_rows, :] = (res_ref[...] + moe).astype(bf16)
    gate_ref[my_rows, :] = gates
    lo_swap = remote(layer_ref.at[my_rows], layer_ref.at[my_rows], 27, sibling)
    gt_swap = remote(gate_ref.at[my_rows], gate_ref.at[my_rows], 28, sibling)
    lo_swap.start()
    gt_swap.start()
    for copy in mo_out + [mo_swap]:
        copy.wait_send()
    go_on()

    right_half = pl.ds(q_cols, q_cols)
    weight_grad(dattn, mixed_ref[...], right_half)
    ga_copies = send_grad(right_half, outs, 34)
    go_on()
    q_part = pl.ds(0, q_cols)
    weight_grad(xn_ref, dproj[:, q_part], q_part)
    ga_copies += send_grad(q_part, q_part, 43)
    go_on()
    for s in range(1, 4):

        @pl.when(z + s < 4)
        def _(s=s):
            dkv_out[s - 1].wait_recv()
            dkv[0:count, :] += dkv_got[s - 1].astype(f32)

    kv_part = pl.ds(q_cols, 2 * HEAD_DIM)
    dproj[:, pl.ds(q_cols, HEAD_DIM)] = turn(dkv[0:count, key_cols], cosine, sine).astype(bf16)
    dproj[:, pl.ds(q_cols + HEAD_DIM, HEAD_DIM)] = dkv[0:count, val_cols].astype(bf16)
    for s in range(4):
        block = dot_f32(xn_ref[:, pl.ds(s * shard, shard)], dproj[:, kv_part], TN)
        xy[low_rows, pl.ds(s * 2 * HEAD_DIM, 2 * HEAD_DIM)] = block.astype(bf16)
    kv_copies = [
        remote(
            xy.at[low_rows, rows_of(rel[i + 1], 2 * HEAD_DIM)],
            ra.at[pl.ds(i * shard, shard), kv_part],
            16 + i,
            plane[i],
        )
        for i in range(3)
    ]
    pending.extend(kv_copies)
    ga_copies += kv_copies
    go_on()

    load_in.wait()
    for s in range(width // 256):
        rows = pl.ds(s * 256, 256)
        d1[:, rows] = dot_f32(dproj[my_rows, :], wgu[rows, in_part], NT)
        d1_low[:, rows] = dot_f32(
            dproj[rows_of(1 - c, half), :], wgu[rows, in_part], NT
        ).astype(bf16)
    d1_swap = remote(d1_low, d1_in, 25, sibling)
    d1_swap.start()
    go_on()
    d1_swap.wait_recv()
    d_one = d1[...] + d1_in[...].astype(f32)
    tok = tok_half[...].astype(f32)
    inv = lax.rsqrt(jnp.mean(tok * tok, axis=-1, keepdims=True) + eps)
    scaled = d_one * gain_one_ref[...]
    inside = jnp.mean(scaled * tok, axis=-1, keepdims=True)
    d_norm = inv * scaled - tok * (inv * inv * inv * inside)
    gacc[0, 0:1, :] = jnp.sum(d_one * tok * inv, axis=0, keepdims=True)
    tokgrad_ref[my_rows, :] = (dres[...] + d_norm).astype(bf16)
    tg_swap = remote(tokgrad_ref.at[my_rows], tokgrad_ref.at[my_rows], 26, sibling)
    tg_swap.start()
    go_on()

    stages = [sibling, at(fx), at(fy), partner, at(ctx=lax.rem(z + 2, 4))]
    gain_copies = [remote(gacc.at[i], gin.at[i], 29 + i, stages[i]) for i in range(5)]
    for i in range(5):
        gain_copies[i].start()
        go_on()
        gain_copies[i].wait_recv()
        total = gacc[i] + gin[i]
        if i < 4:
            gacc[i + 1] = total
        else:
            gains_ref[...] = total

    while (i := next(steps)) < n_expert - 1:
        z_step(i)
    z_step(i)
    for copy in pending:
        copy.start()
    del pending[:]
    for copy in ga_copies:
        copy.wait_recv()

    def attn_sum(i, _):
        size = shard // 8
        here = pl.ds(pl.multiple_of(i * size, size), size)
        rows = pl.ds(pl.multiple_of(f * shard + i * size, size), size)
        low = pl.ds(pl.multiple_of(4 * shard + i * size, size), size)
        for cols, mine in (
            (q_part, xy[rows, q_part]),
            (kv_part, xy[low, rows_of(f, 2 * HEAD_DIM)]),
            (outs, xy[rows, right_half]),
        ):
            total = mine.astype(f32)
            for r in range(3):
                other = pl.ds(pl.multiple_of(r * shard + i * size, size), size)
                total = total + ra[other, cols].astype(f32)
            ra[here, cols] = total.astype(bf16)
        return 0

    lax.fori_loop(0, 8, attn_sum, 0)
    for i in steps:
        z_step(i)
    store = pltpu.make_async_copy(a1, attn_hbm, local.at[0])
    store.start()

    for k in ready:
        final(k).start()

    store.wait()
    for k in range(n_all):

        @pl.when(outer)
        def _(k=k):
            if k >= n_all - window:
                first(k).wait_send()

        @pl.when(inner)
        def _(k=k):
            across(k).wait_send()
            back(k).wait_send()

    for k in range(n_expert):
        if chunks[k][1] == 0:
            final(k).wait()
        else:
            final(k).wait_send()
            final(k).wait_recv()
    for s in range(1, 4):

        @pl.when(z >= s)
        def _(s=s):
            dkv_out[s - 1].wait_send()

    for copy in [tg_swap, lo_swap, gt_swap]:
        copy.wait_recv()
    swaps = [gg_swap, da_swap, d1_swap, tg_swap, lo_swap, gt_swap]
    for copy in swaps + gg_out + ga_copies + gain_copies:
        copy.wait_send()


def rear(res, xn, q, kv, mixed, gain_one, gain_two, tok, cot, x, dy, weights, gate_table, wa):
    count, width = tok.shape
    half = count // 2
    tokens = 8 * half
    columns = wa.shape[1]
    shard = width // 4
    own, _, _, hidden = weights.shape
    mats = 3 * own
    q_cols = q.shape[1]
    vmem, hbm = pl.BlockSpec(memory_space=pltpu.VMEM), pl.BlockSpec(memory_space=pl.ANY)
    bf16, f32 = jnp.bfloat16, jnp.float32
    shape = jax.ShapeDtypeStruct
    dma = pltpu.SemaphoreType.DMA
    chunks, attn_rows = ctx_chunks(mats, shard)
    n_expert, n_all = len(chunks), len(chunks) + len(attn_rows)
    return pl.pallas_call(
        rear_kernel,
        in_specs=[vmem] * 8 + [hbm] * 5 + [vmem, hbm],
        out_specs=[vmem] * 4 + [hbm] * 2,
        out_shape=[
            shape((count, width), bf16),
            shape((count, width), bf16),
            shape((8, width), f32),
            shape((count, 128), f32),
            shape((shard, columns), bf16),
            shape((4, mats, shard, hidden), bf16),
        ],
        scratch_shapes=[
            pltpu.VMEM((2 * tokens, width), bf16),
            pltpu.VMEM((width, 2 * own * hidden), bf16),
            pltpu.VMEM((width, own * hidden), bf16),
            pltpu.VMEM((tokens, width), bf16),
            pltpu.VMEM((tokens, own * hidden), bf16),
            pltpu.VMEM((tokens, 128), f32),
            pltpu.VMEM((mats, width, hidden), bf16),
            pltpu.VMEM((mats, width, hidden), bf16),
            pltpu.VMEM((4 * half, width), bf16),
            pltpu.VMEM((3, half, width), bf16),
            pltpu.VMEM((4 * half, width), bf16),
            pltpu.VMEM((3, half, width), bf16),
            pltpu.VMEM((4 * half, 128), f32),
            pltpu.VMEM((4 * half, 128), f32),
            pltpu.VMEM((3, half, 128), f32),
            pltpu.VMEM((half, width), f32),
            pltpu.VMEM((count, width), bf16),
            pltpu.VMEM((count, q_cols), bf16),
            pltpu.VMEM((count, q_cols + 2 * HEAD_DIM), bf16),
            pltpu.VMEM((4 * count, 2 * HEAD_DIM), f32),
            pltpu.VMEM((4, count, 2 * HEAD_DIM), bf16),
            pltpu.VMEM((3, count, 2 * HEAD_DIM), bf16),
            pltpu.VMEM((half, width), f32),
            pltpu.VMEM((half, width), bf16),
            pltpu.VMEM((half, width), bf16),
            pltpu.VMEM((3 * shard, columns), bf16),
            pltpu.VMEM((shard, columns), bf16),
            pltpu.VMEM((5, 8, width), f32),
            pltpu.VMEM((5, 8, width), f32),
            pltpu.VMEM((half, width), bf16),
            pltpu.VMEM((half, width), bf16),
            dma((52,)),
            dma((52,)),
            dma((10,)),
            dma((n_all,)),
            dma((n_all,)),
            dma((n_all,)),
            dma((n_all,)),
            dma((n_all,)),
            dma((n_expert,)),
            dma((n_expert,)),
            pltpu.SemaphoreType.REGULAR,
        ],
        compiler_params=pltpu.CompilerParams(
            collective_id=1, has_side_effects=True, vmem_limit_bytes=63 * MIB
        ),
        name="rear",
    )(
        res,
        xn,
        q,
        kv,
        mixed,
        gain_one,
        gain_two,
        frequencies(),
        tok,
        cot,
        x,
        dy,
        weights,
        gate_table,
        wa,
    )


def body_fast(
    tokens,
    attn_norm,
    attention_params,
    ffn_norm,
    expert_weights,
    gate_values,
    routes,
    slot_order,
    cotangent,
):
    sequence_count, block_len, model_width = tokens.shape
    count = sequence_count * block_len
    half = count // 2
    f = lax.axis_index("fsdp")
    shard, hidden = attention_params.shape[0], expert_weights.shape[3]
    tok = tokens.reshape(count, model_width)
    cot = cotangent.reshape(count, model_width)
    gain_one, gain_two = attn_norm[None, :], ffn_norm[None, :]
    route_rows = routes.reshape(count, TOP)
    normed, queries, kv, mixed, residual, gate_table, whole_attn, whole_expert, x, dy = front(
        tok,
        gain_one,
        gain_two,
        route_rows.T,
        gate_values.reshape(count, TOP).T,
        slot_order.reshape(1, count),
        attention_params[:, 0, :],
        jnp.transpose(expert_weights, (0, 2, 1, 3)),
        cot,
    )
    layer_out, tokens_grad, gains, gate_rows, attn_grad, finals = rear(
        residual,
        normed,
        queries,
        kv,
        mixed,
        gain_one,
        gain_two,
        tok,
        cot,
        x.reshape(8 * half, model_width),
        dy.reshape(8 * half, model_width),
        whole_expert,
        gate_table,
        whole_attn,
    )
    picked = route_rows[:, :, None] == jnp.arange(EXPERTS, dtype=jnp.int32)
    gate_grad = jnp.sum(jnp.where(picked, gate_rows[:, None, :EXPERTS], 0.0), axis=-1)
    finals = finals.reshape(EXPERTS, 3, shard, hidden)
    expert_grad, attn_lines = join_experts(finals, attn_grad, expert_order(f).T)
    expert_grad = jnp.transpose(expert_grad, (0, 2, 1, 3))
    return (
        layer_out.reshape(sequence_count, block_len, model_width),
        tokens_grad.reshape(sequence_count, block_len, model_width),
        attn_lines.reshape(shard, 1, attention_params.shape[2]),
        expert_grad,
        gains[0],
        gains[1],
        gate_grad.reshape(sequence_count, block_len, TOP),
    )


def solution(mesh):
    in_specs = (
        P("fsdp", "ctx", None),
        P(),
        P("fsdp", "tp", None),
        P(),
        P("fsdp", None, None, "tp"),
        P("fsdp", "ctx", None),
        P("fsdp", "ctx", None),
        P("fsdp", "ctx"),
        P("fsdp", "ctx", None),
    )
    out_specs = (
        P("fsdp", "ctx", None),
        P("fsdp", "ctx", None),
        P("fsdp", "tp", None),
        P("fsdp", None, None, "tp"),
        P(),
        P(),
        P("fsdp", "ctx", None),
    )
    four = mesh.shape["fsdp"] == 4 and mesh.shape["ctx"] == 4 and mesh.shape["tp"] == 2
    body_fn = body_fast if four else body
    return jax.shard_map(body_fn, mesh=mesh, in_specs=in_specs, out_specs=out_specs, check_vma=False)
```

```python
import jax
import jax.numpy as jnp
from jax import lax
import math
import numpy as np
from jax.experimental import pallas as pl
from jax.experimental.pallas import tpu as pltpu
from jax.sharding import PartitionSpec as P

HEAD_DIM = 128
TOP = 4
EXPERTS = 8
QUERY_PER_GROUP = 6
CAP = 160


eps = 1e-06
theta_base = 1000000.0


def angle_tables(positions):
    frequency = theta_base ** (-(jnp.arange(HEAD_DIM // 2, dtype=jnp.float32) * 2.0) / HEAD_DIM)
    angles = positions.astype(jnp.float32)[:, None] * frequency[None, :]
    return (jnp.cos(angles), jnp.sin(angles))


def rotate(source, cosine_table, sine_table):
    half_size = source.shape[-1] // 2
    front_half = source[..., :half_size]
    back_half = source[..., half_size:]
    return jnp.concatenate(
        [
            front_half * cosine_table - back_half * sine_table,
            back_half * cosine_table + front_half * sine_table,
        ],
        axis=-1,
    )


def norm_back(source, inv_rms, gain_vec, upstream):
    scaled = upstream * gain_vec
    inner_sum = jnp.mean(scaled * source, axis=-1, keepdims=True)
    d_source = inv_rms * scaled - source * inv_rms * inv_rms * inv_rms * inner_sum
    return (d_source, jnp.sum(upstream * source * inv_rms, axis=0))


def slot_tables(route_rows, rank_rows):
    tok_count = route_rows.shape[0]
    inverse = (
        jnp.zeros((tok_count,), jnp.int32).at[rank_rows].set(jnp.arange(tok_count, dtype=jnp.int32))
    )
    ranked = route_rows[inverse].reshape(-1)
    onehot = (ranked[:, None] == jnp.arange(EXPERTS, dtype=jnp.int32)[None, :]).astype(jnp.int32)
    before = jnp.cumsum(onehot, axis=0) - onehot
    slot_ranked = jnp.sum(before * onehot, axis=1).reshape(tok_count, TOP)
    slots = slot_ranked[rank_rows]
    kept_pair = slots < CAP
    pair_slot = jnp.where(kept_pair, route_rows * CAP + slots, EXPERTS * CAP)
    owners = jnp.broadcast_to(jnp.arange(tok_count, dtype=jnp.int32)[:, None], (tok_count, TOP))
    slot_token = (
        jnp.full((EXPERTS * CAP,), tok_count, jnp.int32)
        .at[pair_slot.reshape(-1)]
        .set(owners.reshape(-1), mode="drop")
    )
    return (kept_pair, pair_slot, slot_token)


def attend_forward(queries, key_rows, value_rows, allowed):
    scores = jnp.einsum(
        "qhgd,khd->hgqk", queries, key_rows, preferred_element_type=jnp.float32
    ) * HEAD_DIM ** (-0.5)
    scores = jnp.where(allowed, scores, -1e30)
    row_max = jnp.max(scores, axis=-1, keepdims=True)
    expd = jnp.exp(scores - row_max)
    row_total = jnp.sum(expd, axis=-1, keepdims=True)
    attn_probs = (expd / row_total).astype(jnp.bfloat16)
    mixed_heads = jnp.einsum(
        "hgqk,khd->qhgd", attn_probs, value_rows, preferred_element_type=jnp.float32
    )
    return (mixed_heads.astype(jnp.bfloat16), row_max + jnp.log(row_total))


def attend_backward(queries, key_rows, value_rows, allowed, log_total, d_mixed):
    scores = jnp.einsum(
        "qhgd,khd->hgqk", queries, key_rows, preferred_element_type=jnp.float32
    ) * HEAD_DIM ** (-0.5)
    scores = jnp.where(allowed, scores, -1e30)
    attn_probs = jnp.exp(scores - log_total)
    low_probs = attn_probs.astype(jnp.bfloat16)
    d_probs = jnp.einsum("qhgd,khd->hgqk", d_mixed, value_rows, preferred_element_type=jnp.float32)
    inner_sum = jnp.sum(attn_probs * d_probs, axis=-1, keepdims=True)
    d_scores = (attn_probs * (d_probs - inner_sum)).astype(jnp.bfloat16)
    d_queries = jnp.einsum(
        "hgqk,khd->qhgd", d_scores, key_rows, preferred_element_type=jnp.float32
    ) * HEAD_DIM ** (-0.5)
    d_keys = jnp.einsum(
        "hgqk,qhgd->khd", d_scores, queries, preferred_element_type=jnp.float32
    ) * HEAD_DIM ** (-0.5)
    d_values = jnp.einsum("hgqk,qhgd->khd", low_probs, d_mixed, preferred_element_type=jnp.float32)
    return (d_queries, d_keys, d_values)


def body(
    tokens,
    attn_norm,
    attention_params,
    ffn_norm,
    expert_weights,
    gate_values,
    routes,
    slot_order,
    cotangent,
):
    sequence_count, block_len, model_width = tokens.shape
    tok_count = sequence_count * block_len
    kv_loc = attention_params.shape[1]
    input_columns = (QUERY_PER_GROUP + 2) * HEAD_DIM
    ctx_size = lax.axis_size("ctx")
    ctx_place = lax.axis_index("ctx")
    sequence_length = block_len * ctx_size
    whole_attn, whole_expert = (
        lax.all_gather(attention_params, "fsdp", axis=0, tiled=True),
        lax.all_gather(expert_weights, "fsdp", axis=0, tiled=True),
    )
    positions = ctx_place * block_len + jnp.arange(block_len, dtype=jnp.int32)
    cosine_table, sine_table = angle_tables(positions)
    cosine_table = jnp.tile(cosine_table, (sequence_count, 1))
    sine_table = jnp.tile(sine_table, (sequence_count, 1))
    cos_four = cosine_table[:, None, None, :]
    sin_four = sine_table[:, None, None, :]
    cos_three = cosine_table[:, None, :]
    sin_three = sine_table[:, None, :]
    allowed = (jnp.arange(sequence_length, dtype=jnp.int32) // block_len <= ctx_place)[
        None, None, None, :
    ]
    tok_float = tokens.reshape(tok_count, model_width).astype(jnp.float32)
    inv_one = lax.rsqrt(jnp.mean(tok_float * tok_float, axis=-1, keepdims=True) + eps)
    first_normed = (tok_float * inv_one * attn_norm).astype(jnp.bfloat16)
    projected_rows = jnp.einsum(
        "td,dhc->thc",
        first_normed,
        whole_attn[:, :, :input_columns],
        preferred_element_type=jnp.float32,
    ).reshape(tok_count, kv_loc, QUERY_PER_GROUP + 2, HEAD_DIM)
    queries = rotate(projected_rows[:, :, :QUERY_PER_GROUP], cos_four, sin_four).astype(
        jnp.bfloat16
    )
    key_rows = rotate(projected_rows[:, :, QUERY_PER_GROUP], cos_three, sin_three).astype(
        jnp.bfloat16
    )
    value_rows = projected_rows[:, :, QUERY_PER_GROUP + 1].astype(jnp.bfloat16)
    key_all, value_all = (
        lax.all_gather(
            key_rows.reshape(sequence_count, block_len, kv_loc, HEAD_DIM), "ctx", axis=1, tiled=True
        ),
        lax.all_gather(
            value_rows.reshape(sequence_count, block_len, kv_loc, HEAD_DIM),
            "ctx",
            axis=1,
            tiled=True,
        ),
    )
    query_seq = queries.reshape(sequence_count, block_len, kv_loc, QUERY_PER_GROUP, HEAD_DIM)
    mixed_heads, log_total = lax.map(
        lambda item_args: attend_forward(item_args[0], item_args[1], item_args[2], allowed),
        (query_seq, key_all, value_all),
    )
    mixed_flat = mixed_heads.reshape(tok_count, kv_loc, QUERY_PER_GROUP * HEAD_DIM)
    attn_part = jnp.einsum(
        "thc,dhc->td",
        mixed_flat,
        whole_attn[:, :, input_columns:],
        preferred_element_type=jnp.float32,
    )
    attn_sum = lax.psum(attn_part, "tp")
    residual = tok_float + attn_sum
    inv_two = lax.rsqrt(jnp.mean(residual * residual, axis=-1, keepdims=True) + eps)
    normed_two = (residual * inv_two * ffn_norm).astype(jnp.bfloat16)
    kept_pair, pair_slot, slot_token = slot_tables(
        routes.reshape(tok_count, TOP), slot_order.reshape(tok_count)
    )
    kept_float = kept_pair.astype(jnp.float32)
    gate_kept = gate_values.reshape(tok_count, TOP) * kept_float
    slot_gate = (
        jnp.zeros((EXPERTS * CAP,), jnp.float32)
        .at[pair_slot.reshape(-1)]
        .set(gate_kept.reshape(-1), mode="drop")
    )
    padded = jnp.concatenate([normed_two, jnp.zeros((1, model_width), jnp.bfloat16)], axis=0)
    inputs = padded[slot_token].reshape(EXPERTS, CAP, model_width)
    gate_act = jnp.einsum(
        "ecd,deh->ech", inputs, whole_expert[:, :, 0], preferred_element_type=jnp.float32
    )
    up_act = jnp.einsum(
        "ecd,deh->ech", inputs, whole_expert[:, :, 1], preferred_element_type=jnp.float32
    )
    gate_sigmoid = jax.nn.sigmoid(gate_act)
    active = gate_act * gate_sigmoid
    hidden = (active * up_act).astype(jnp.bfloat16)
    expert_out = jnp.einsum(
        "ech,deh->ecd", hidden, whole_expert[:, :, 2], preferred_element_type=jnp.float32
    )
    out_pad = jnp.concatenate(
        [expert_out.reshape(EXPERTS * CAP, model_width), jnp.zeros((1, model_width), jnp.float32)],
        axis=0,
    )
    picked = out_pad[pair_slot]
    moe_part = jnp.sum(picked * gate_kept[:, :, None], axis=1)
    moe = lax.psum(moe_part.astype(jnp.bfloat16), "tp").astype(jnp.float32)
    layer_out = (
        (residual + moe).astype(jnp.bfloat16).reshape(sequence_count, block_len, model_width)
    )
    grad_out = cotangent.reshape(tok_count, model_width).astype(jnp.float32)
    gate_part = jnp.sum(picked * grad_out[:, None, :], axis=-1) * kept_float
    grad_pad = jnp.concatenate([grad_out, jnp.zeros((1, model_width), jnp.float32)], axis=0)
    d_expert = (
        (grad_pad[slot_token] * slot_gate[:, None])
        .astype(jnp.bfloat16)
        .reshape(EXPERTS, CAP, model_width)
    )
    d_hidden = jnp.einsum(
        "ecd,deh->ech", d_expert, whole_expert[:, :, 2], preferred_element_type=jnp.float32
    )
    silu_slope = gate_sigmoid * (1.0 + gate_act * (1.0 - gate_sigmoid))
    d_gate_act = (d_hidden * up_act * silu_slope).astype(jnp.bfloat16)
    d_up_act = (d_hidden * active).astype(jnp.bfloat16)
    d_inputs = jnp.einsum(
        "ech,deh->ecd", d_gate_act, whole_expert[:, :, 0], preferred_element_type=jnp.float32
    )
    d_inputs = d_inputs + jnp.einsum(
        "ech,deh->ecd", d_up_act, whole_expert[:, :, 1], preferred_element_type=jnp.float32
    )
    d_in_pad = jnp.concatenate(
        [d_inputs.reshape(EXPERTS * CAP, model_width), jnp.zeros((1, model_width), jnp.float32)],
        axis=0,
    )
    d_normed_part = jnp.sum(d_in_pad[pair_slot], axis=1)
    d_normed_two, gate_grad = lax.psum((d_normed_part, gate_part), "tp")
    d_resid_norm, gain_two = norm_back(residual, inv_two, ffn_norm, d_normed_two)
    d_residual = grad_out + d_resid_norm
    d_attn = d_residual.astype(jnp.bfloat16)
    d_mixed = jnp.einsum(
        "td,dhc->thc", d_attn, whole_attn[:, :, input_columns:], preferred_element_type=jnp.float32
    ).astype(jnp.bfloat16)
    d_mixed_seq = d_mixed.reshape(sequence_count, block_len, kv_loc, QUERY_PER_GROUP, HEAD_DIM)
    d_queries, d_key_all, d_value_all = lax.map(
        lambda item_args: attend_backward(
            item_args[0], item_args[1], item_args[2], allowed, item_args[3], item_args[4]
        ),
        (query_seq, key_all, value_all, log_total, d_mixed_seq),
    )
    d_keys, d_values = (
        lax.psum_scatter(
            d_key_all.astype(jnp.bfloat16), "ctx", scatter_dimension=1, tiled=True
        ).astype(jnp.float32),
        lax.psum_scatter(
            d_value_all.astype(jnp.bfloat16), "ctx", scatter_dimension=1, tiled=True
        ).astype(jnp.float32),
    )
    d_queries = rotate(
        d_queries.reshape(tok_count, kv_loc, QUERY_PER_GROUP, HEAD_DIM), cos_four, -sin_four
    )
    d_keys = rotate(d_keys.reshape(tok_count, kv_loc, HEAD_DIM), cos_three, -sin_three)
    d_values = d_values.reshape(tok_count, kv_loc, HEAD_DIM)
    d_projected = jnp.concatenate([d_queries, d_keys[:, :, None], d_values[:, :, None]], axis=2)
    d_projected = d_projected.astype(jnp.bfloat16).reshape(tok_count, kv_loc, input_columns)
    d_normed_local = jnp.einsum(
        "thc,dhc->td",
        d_projected,
        whole_attn[:, :, :input_columns],
        preferred_element_type=jnp.float32,
    )
    d_normed_one = lax.psum(d_normed_local.astype(jnp.bfloat16), "tp").astype(jnp.float32)
    d_tok_norm, gain_one = norm_back(tok_float, inv_one, attn_norm, d_normed_one)
    tokens_grad = (
        (d_residual + d_tok_norm)
        .astype(jnp.bfloat16)
        .reshape(sequence_count, block_len, model_width)
    )
    gain_one, gain_two = lax.psum((gain_one, gain_two), ("fsdp", "ctx"))
    in_term = jnp.einsum(
        "td,thc->dhc", first_normed, d_projected, preferred_element_type=jnp.float32
    )
    out_term = jnp.einsum("td,thc->dhc", d_attn, mixed_flat, preferred_element_type=jnp.float32)
    attn_grad = lax.psum_scatter(
        jnp.concatenate([in_term, out_term], axis=2),
        ("fsdp", "ctx"),
        scatter_dimension=0,
        tiled=True,
    )
    gate_term = jnp.einsum("ecd,ech->deh", inputs, d_gate_act, preferred_element_type=jnp.float32)
    up_term = jnp.einsum("ecd,ech->deh", inputs, d_up_act, preferred_element_type=jnp.float32)
    down_term = jnp.einsum("ecd,ech->deh", d_expert, hidden, preferred_element_type=jnp.float32)
    expert_grad = lax.psum_scatter(
        jnp.stack([gate_term, up_term, down_term], axis=2),
        ("fsdp", "ctx"),
        scatter_dimension=0,
        tiled=True,
    )
    attn_grad, expert_grad = (
        lax.all_gather(attn_grad.astype(jnp.bfloat16), "ctx", axis=0, tiled=True).astype(
            attn_grad.dtype
        ),
        lax.all_gather(expert_grad.astype(jnp.bfloat16), "ctx", axis=0, tiled=True).astype(
            expert_grad.dtype
        ),
    )
    return (
        layer_out,
        tokens_grad,
        attn_grad,
        expert_grad,
        gain_one,
        gain_two,
        gate_grad.reshape(sequence_count, block_len, TOP),
    )


MESH_ID = pl.DeviceIdType.MESH
MIB = 2**20


def expert_order(place):
    row = jnp.arange(128, dtype=jnp.int32)
    expert = (((row // 32) ^ place) * 2) + (row // 16) % 2
    source = (row % 16) * 8 + expert
    return (source[:, None] == row[None, :]).astype(jnp.bfloat16)


def join_kernel(order_ref, in_ref, attn_in_ref, out_ref, attn_out_ref):
    width = in_ref.shape[3]
    for m in range(3):
        for k in range(in_ref.shape[2] // 16):
            block = in_ref[:, m, pl.ds(k * 16, 16), :].reshape(128, width)
            moved = jnp.dot(order_ref[...], block, preferred_element_type=jnp.float32)
            out_ref[pl.ds(k * 16, 16), m] = moved.reshape(16, 8, width)
    rows, columns = attn_in_ref.shape
    parts = columns // 128
    for j in range(parts):
        part = attn_in_ref[:, pl.ds(j * 128, 128)].astype(jnp.float32)
        attn_out_ref[pl.ds(j, rows, stride=parts), :] = part


def join_experts(grads, attn_grad, order):
    experts, _, rows, width = grads.shape
    columns = attn_grad.shape[1]
    step = 128
    lines = step * columns // 128
    return pl.pallas_call(
        join_kernel,
        grid=(rows // step,),
        in_specs=[
            pl.BlockSpec((128, 128), lambda i: (0, 0)),
            pl.BlockSpec((experts, 3, step, width), lambda i: (0, 0, i, 0)),
            pl.BlockSpec((step, columns), lambda i: (i, 0)),
        ],
        out_specs=[
            pl.BlockSpec((step, 3, experts, width), lambda i: (i, 0, 0, 0)),
            pl.BlockSpec((lines, 128), lambda i: (i, 0)),
        ],
        out_shape=[
            jax.ShapeDtypeStruct((rows, 3, experts, width), jnp.float32),
            jax.ShapeDtypeStruct((rows * columns // 128, 128), jnp.float32),
        ],
        compiler_params=pltpu.CompilerParams(vmem_limit_bytes=60 * MIB),
        name="join_experts",
    )(order, grads, attn_grad)


NT = (((1,), (1,)), ((), ()))
TN = (((0,), (0,)), ((), ()))


def dot_f32(a, b, dims=(((1,), (0,)), ((), ()))):
    return lax.dot_general(a, b, dims, preferred_element_type=jnp.float32)


def block_probs(last, keys, query):
    scores = dot_f32(keys, query, NT) * HEAD_DIM ** (-0.5)
    block = lax.broadcasted_iota(jnp.int32, scores.shape, 0) // query.shape[0]
    scores = jnp.where(block <= last, scores, -1e30)
    expd = jnp.exp(scores - jnp.max(scores, axis=0, keepdims=True))
    return expd * (1.0 / jnp.sum(expd, axis=0, keepdims=True))


def place():
    return lax.axis_index("fsdp"), lax.axis_index("ctx"), lax.axis_index("tp")


def plane_peers(f):
    return f + 1 - 2 * lax.rem(f, 2), lax.rem(f + 2, 4), 3 - f


def rows_of(index, size):
    return pl.ds(pl.multiple_of(index * size, size), size)


def greet(devices):
    barrier = pltpu.get_barrier_semaphore()
    for device in devices:
        pl.semaphore_signal(barrier, inc=1, device_id=device, device_id_type=MESH_ID)
    pl.semaphore_wait(barrier, len(devices))


def turn(value, cosine, sine):
    return value * cosine + pltpu.roll(value, HEAD_DIM // 2, 1) * sine


def frequencies():
    i = np.arange(HEAD_DIM // 2, dtype=np.float32)
    freq = (theta_base ** (-(i * 2.0) / HEAD_DIM)).astype(np.float32)
    return jnp.asarray(np.concatenate([freq, freq])[None, :])


def front_kernel(
    tok_ref,
    gain_one_ref,
    gain_two_ref,
    freq_ref,
    routes_ref,
    gates_ref,
    order_ref,
    attn_hbm,
    experts_hbm,
    cot_hbm,
    xn_ref,
    q_ref,
    kv_ref,
    mixed_ref,
    res_ref,
    wl_ref,
    wa_hbm,
    w_hbm,
    x_hbm,
    dy_hbm,
    raw,
    pieces,
    wa,
    part,
    part_in,
    low_half,
    send,
    recv,
    local,
):
    f, z, c = place()
    fx, fy, fd = plane_peers(f)
    count, width = tok_ref.shape
    half = count // 2
    shard = attn_hbm.shape[0]
    cut = shard // 2
    in_cols = (QUERY_PER_GROUP + 2) * HEAD_DIM
    ins = pl.ds(0, in_cols)
    outs = pl.ds(in_cols, attn_hbm.shape[1] - in_cols)

    def at(fsdp=f, ctx=z, tp=c):
        return {"fsdp": fsdp, "ctx": ctx, "tp": tp}

    def remote(src, dst, k, device):
        return pltpu.make_async_remote_copy(
            src_ref=src,
            dst_ref=dst,
            send_sem=send.at[k],
            recv_sem=recv.at[k],
            device_id=device,
            device_id_type=MESH_ID,
        )

    plane = [at(fx), at(fy), at(fd)]
    rel = [fx, fy, fd]
    line = [at(ctx=lax.rem(z + s, 4)) for s in range(1, 4)]
    sibling = at(tp=1 - c)
    mine = rows_of(f, shard)
    load = pltpu.make_async_copy(experts_hbm, raw, local.at[6])
    load.start()
    greet(plane + line + [sibling])

    owned = pltpu.make_async_copy(attn_hbm, wa.at[mine], local.at[0])
    owned.start()
    in_x = remote(attn_hbm.at[:, ins], wa.at[mine, ins], 0, at(fx))
    in_y = remote(attn_hbm.at[:, ins], wa.at[mine, ins], 1, at(fy))
    in_x.start()
    in_y.start()

    rank = jnp.broadcast_to(order_ref[...].astype(jnp.float32), (count, count))
    ahead = jnp.where(rank.T < rank, 1.0, 0.0).astype(jnp.bfloat16)
    expert = lax.broadcasted_iota(jnp.int32, (128, count), 0)
    member = jnp.zeros((128, count), jnp.float32)
    gate = jnp.zeros((128, count), jnp.float32)
    for j in range(TOP):
        hit = jnp.broadcast_to(routes_ref[j : j + 1, :], (128, count)) == expert
        member = jnp.where(hit, 1.0, member)
        gate = jnp.where(hit, jnp.broadcast_to(gates_ref[j : j + 1, :], (128, count)), gate)
    slots = dot_f32(member.astype(jnp.bfloat16), ahead)
    gate = jnp.where(slots < CAP - 0.5, gate, 0.0)
    wl_ref[f] = gate[:EXPERTS]
    gate_copies = [remote(wl_ref.at[f], wl_ref.at[f], 2 + i, plane[i]) for i in range(3)]
    for copy in gate_copies:
        copy.start()

    own_dy = [
        pltpu.make_async_copy(
            cot_hbm.at[pl.ds(i * half, half)], dy_hbm.at[i, f], local.at[2 + i]
        )
        for i in range(2)
    ]
    for copy in own_dy:
        copy.start()

    row = lax.broadcasted_iota(jnp.int32, (128, 128), 0)
    column = lax.broadcasted_iota(jnp.int32, (128, 128), 1)
    owner = jnp.where(row < 64, jnp.where(row < 32, f, fx), jnp.where(row < 96, fy, fd))
    source = (row % 16) * 8 + owner * 2 + (row // 16) % 2
    order = jnp.where(source == column, 1.0, 0.0).astype(jnp.bfloat16)

    def split(m):
        def body(k, _):
            rows = pl.ds(pl.multiple_of(k * 16, 16), 16)
            block = raw[rows, m].reshape(128, raw.shape[3])
            moved = dot_f32(order, block).astype(jnp.bfloat16)
            pieces[:, m, rows, :] = moved.reshape(8, 16, raw.shape[3])
            return 0

        lax.fori_loop(0, shard // 16, body, 0)

    cut_rows = shard // 4
    from_rows = rows_of(z, cut_rows)
    to_rows = rows_of(4 * f + z, cut_rows)

    def quarter(m, i):
        return remote(
            pieces.at[pl.ds(2 * (i + 1), 2), m, from_rows],
            w_hbm.at[:, m, to_rows, :],
            37 + 3 * m + i,
            plane[i],
        )

    def hand_on(m, i):
        quarters[3 * m + i].wait_recv()
        here = w_hbm.at[:, m, rows_of(4 * rel[i] + z, cut_rows), :]
        copies = [remote(here, here, 43 + 9 * m + 3 * i + s, line[s]) for s in range(3)]
        for copy in copies:
            copy.start()
        return copies

    load.wait()
    split(0)
    quarters = [quarter(0, i) for i in range(3)]
    for copy in quarters:
        copy.start()

    tok = tok_ref[...].astype(jnp.float32)
    inv = lax.rsqrt(jnp.mean(tok * tok, axis=-1, keepdims=True) + eps)
    xn_ref[...] = (tok * inv * gain_one_ref[...]).astype(jnp.bfloat16)
    position = z * count + lax.broadcasted_iota(jnp.int32, (count, HEAD_DIM), 0)
    angle = position.astype(jnp.float32) * freq_ref[...]
    cosine = jnp.cos(angle)
    lane = lax.broadcasted_iota(jnp.int32, (count, HEAD_DIM), 1)
    sine = jnp.where(lane < HEAD_DIM // 2, -jnp.sin(angle), jnp.sin(angle))

    top, low = rows_of(2 * fx, cut), rows_of(2 * fy + 1, cut)
    in_x.wait_recv()
    in_xy = remote(wa.at[top, ins], wa.at[top, ins], 5, at(fy))
    in_xy.start()
    in_y.wait_recv()
    in_yx = remote(wa.at[low, ins], wa.at[low, ins], 6, at(fx))
    in_yx.start()
    out_x = remote(attn_hbm.at[:, outs], wa.at[mine, outs], 7, at(fx))
    out_y = remote(attn_hbm.at[:, outs], wa.at[mine, outs], 8, at(fy))
    split(1)
    quarters += [quarter(1, i) for i in range(3)]
    for copy in quarters[3:]:
        copy.start()
    out_x.start()
    out_y.start()
    handed = hand_on(0, 0) + hand_on(0, 1)
    dy_copies = [
        remote(cot_hbm.at[rows_of(c, half)], dy_hbm.at[c, f], 23 + i, plane[i]) for i in range(2)
    ]
    for copy in dy_copies:
        copy.start()
    split(2)
    own_w = pltpu.make_async_copy(pieces.at[pl.ds(0, 2)], w_hbm.at[:, :, mine, :], local.at[1])
    own_w.start()
    owned.wait()
    in_xy.wait_recv()
    in_yx.wait_recv()

    normed = xn_ref[...]
    for h in range(QUERY_PER_GROUP + 2):
        cols = pl.ds(h * HEAD_DIM, HEAD_DIM)
        if h % 2 == 0:
            pair = dot_f32(normed, wa[:, pl.ds(h * HEAD_DIM, 2 * HEAD_DIM)])
        value = pair[:, (h % 2) * HEAD_DIM : (h % 2 + 1) * HEAD_DIM]
        if h <= QUERY_PER_GROUP:
            value = turn(value, cosine, sine)
        if h < QUERY_PER_GROUP:
            q_ref[:, cols] = value.astype(jnp.bfloat16)
        else:
            kv_ref[0, :, pl.ds((h - QUERY_PER_GROUP) * HEAD_DIM, HEAD_DIM)] = value.astype(
                jnp.bfloat16
            )
    kv_copies = [remote(kv_ref.at[0], kv_ref.at[s], 8 + s, line[s - 1]) for s in range(1, 4)]
    for s in range(1, 4):

        @pl.when(z + s < 4)
        def _(s=s):
            kv_copies[s - 1].start()

        @pl.when(z < s)
        def _(s=s):
            kv_ref[s] = jnp.zeros(kv_ref.shape[1:], jnp.bfloat16)

    handed += hand_on(0, 2)
    out_x.wait_recv()
    out_xy = remote(wa.at[top, outs], wa.at[top, outs], 12, at(fy))
    out_xy.start()
    out_y.wait_recv()
    out_yx = remote(wa.at[low, outs], wa.at[low, outs], 13, at(fx))
    out_yx.start()

    w_copies = [
        remote(pieces.at[pl.ds(2 * (i + 1), 2), 2], w_hbm.at[:, 2, mine, :], 14 + i, plane[i])
        for i in range(3)
    ]
    for copy in w_copies:
        copy.start()
    for i in range(3):
        handed += hand_on(1, i)

    for s in range(1, 4):

        @pl.when(z >= s)
        def _(s=s):
            kv_copies[s - 1].wait_recv()

    keys = kv_ref[:, :, pl.ds(0, HEAD_DIM)].reshape(4 * count, HEAD_DIM)
    vals = kv_ref[:, :, pl.ds(HEAD_DIM, HEAD_DIM)].reshape(4 * count, HEAD_DIM)
    for g in range(QUERY_PER_GROUP):
        cols = pl.ds(g * HEAD_DIM, HEAD_DIM)
        probs = block_probs(z, keys, q_ref[:, cols]).astype(jnp.bfloat16)
        mixed_ref[:, cols] = dot_f32(probs, vals, TN).astype(jnp.bfloat16)

    upper, lower = pl.ds(0, half // 2), pl.ds(half // 2, half // 2)

    def pass_on(copies, ref, k):
        copies[0].wait_recv()
        up = ref.at[c, fx, upper]
        passed = [remote(up, up, k, at(fy))]
        passed[0].start()
        copies[1].wait_recv()
        low = ref.at[c, fy, lower]
        passed.append(remote(low, low, k + 1, at(fx)))
        passed[1].start()
        return passed

    out_xy.wait_recv()
    out_yx.wait_recv()
    store_wa = pltpu.make_async_copy(wa, wa_hbm, local.at[4])
    store_wa.start()
    for s in range(width // 256):
        cols = pl.ds(s * 256, 256)
        part[:, cols] = dot_f32(mixed_ref[...], wa[cols, outs], NT)
    swap = remote(part.at[rows_of(1 - c, half)], part_in, 26, sibling)
    swap.start()
    swap.wait_recv()
    my_rows = rows_of(c, half)
    residual = tok_ref[my_rows, :].astype(jnp.float32) + (part[my_rows, :] + part_in[...])
    res_ref[...] = residual
    inv = lax.rsqrt(jnp.mean(residual * residual, axis=-1, keepdims=True) + eps)
    low_half[...] = (residual * inv * gain_two_ref[...]).astype(jnp.bfloat16)
    own_x = pltpu.make_async_copy(low_half, x_hbm.at[c, f], local.at[5])
    own_x.start()
    x_copies = [remote(low_half, x_hbm.at[c, f], 27 + i, plane[i]) for i in range(2)]
    for copy in x_copies:
        copy.start()
    sib_x = [remote(low_half, x_hbm.at[c, f], 30, sibling)]
    sib_x[0].start()

    dy_passed = pass_on(dy_copies, dy_hbm, 61)
    x_passed = pass_on(x_copies, x_hbm, 63)
    sib_dy = []
    for i in range(2):
        sib_dy.append(remote(dy_hbm.at[c, rel[i]], dy_hbm.at[c, rel[i]], 31 + i, sibling))
        sib_x.append(remote(x_hbm.at[c, rel[i]], x_hbm.at[c, rel[i]], 34 + i, sibling))
        sib_dy[i].start()
        sib_x[i + 1].start()
    for copy in dy_passed:
        copy.wait_recv()
    sib_dy.append(remote(dy_hbm.at[c, fd], dy_hbm.at[c, fd], 33, sibling))
    sib_dy[2].start()
    for copy in x_passed:
        copy.wait_recv()
    sib_x.append(remote(x_hbm.at[c, fd], x_hbm.at[c, fd], 36, sibling))
    sib_x[3].start()

    for copy in w_copies + gate_copies + handed + sib_dy + sib_x:
        copy.wait_recv()
    for s in range(1, 4):

        @pl.when(z + s < 4)
        def _(s=s):
            kv_copies[s - 1].wait_send()

    for copy in [in_x, in_y, in_xy, in_yx, out_x, out_y, out_xy, out_yx, swap]:
        copy.wait_send()
    sent = w_copies + quarters + handed + gate_copies + dy_copies + x_copies
    for copy in sent + dy_passed + x_passed + sib_dy + sib_x:
        copy.wait_send()
    for copy in [own_w, own_x, store_wa] + own_dy:
        copy.wait()


def front(tok, gain_one, gain_two, routes, gates, order, attn_own, weights, cot):
    count, width = tok.shape
    half = count // 2
    shard, columns = attn_own.shape
    experts, hidden = EXPERTS // 4, weights.shape[3]
    vmem, hbm = pl.BlockSpec(memory_space=pltpu.VMEM), pl.BlockSpec(memory_space=pl.ANY)
    bf16, f32 = jnp.bfloat16, jnp.float32
    shape = jax.ShapeDtypeStruct
    return pl.pallas_call(
        front_kernel,
        in_specs=[vmem] * 7 + [hbm] * 3,
        out_specs=[vmem] * 6 + [hbm] * 4,
        out_shape=[
            shape((count, width), bf16),
            shape((count, QUERY_PER_GROUP * HEAD_DIM), bf16),
            shape((4, count, 2 * HEAD_DIM), bf16),
            shape((count, QUERY_PER_GROUP * HEAD_DIM), bf16),
            shape((half, width), f32),
            shape((4, EXPERTS, count), f32),
            shape((4 * shard, columns), bf16),
            shape((experts, 3, 4 * shard, hidden), bf16),
            shape((2, 4, half, width), bf16),
            shape((2, 4, half, width), bf16),
        ],
        scratch_shapes=[
            pltpu.VMEM(weights.shape, bf16),
            pltpu.VMEM((EXPERTS, 3, shard, hidden), bf16),
            pltpu.VMEM((4 * shard, columns), bf16),
            pltpu.VMEM((count, width), f32),
            pltpu.VMEM((half, width), f32),
            pltpu.VMEM((half, width), bf16),
            pltpu.SemaphoreType.DMA((65,)),
            pltpu.SemaphoreType.DMA((65,)),
            pltpu.SemaphoreType.DMA((7,)),
        ],
        compiler_params=pltpu.CompilerParams(
            collective_id=0, has_side_effects=True, vmem_limit_bytes=60 * MIB
        ),
        name="front",
    )(tok, gain_one, gain_two, frequencies(), routes, gates, order, attn_own, weights, cot)


def ctx_chunks(mats, shard):
    early = [(0, 0), (1, 0)]
    chunks = [(j, r, 0, shard) for j, r in early]
    chunks += [(j, r, 0, shard) for j in range(mats) for r in range(4) if (j, r) not in early]
    return chunks, [shard // 8] * 8


def rear_kernel(
    res_ref,
    xn_ref,
    q_ref,
    kv_ref,
    mixed_ref,
    gain_one_ref,
    gain_two_ref,
    freq_ref,
    tok_hbm,
    cot_hbm,
    x_hbm,
    dy_hbm,
    w_hbm,
    wl_ref,
    wa_hbm,
    layer_ref,
    tokgrad_ref,
    gains_ref,
    gate_ref,
    attn_hbm,
    fin_hbm,
    xy,
    wgu,
    wd,
    gu,
    hid,
    table,
    ge,
    r1,
    dn_in,
    dn_got,
    mo_in,
    mo_got,
    gg_in,
    gg_sum,
    gg_got,
    dres,
    dattn,
    dmixed,
    dproj,
    dkv,
    dkv_low,
    dkv_got,
    d1,
    d1_low,
    d1_in,
    ra,
    a1,
    gacc,
    gin,
    tok_half,
    cot_half,
    send,
    recv,
    local,
    z_out,
    z_across,
    z_back,
    z_r1,
    z_r2,
    f_out,
    f_in,
    credit,
):
    f, z, c = place()
    fx, fy, fd = plane_peers(f)
    rel = [f, fx, fy, fd]
    f32, bf16 = jnp.float32, jnp.bfloat16
    count, width = tok_hbm.shape
    half = count // 2
    shard = attn_hbm.shape[0]
    in_cols = (QUERY_PER_GROUP + 2) * HEAD_DIM
    q_cols = QUERY_PER_GROUP * HEAD_DIM
    ins = pl.ds(0, in_cols)
    outs = pl.ds(in_cols, attn_hbm.shape[1] - in_cols)
    scale = HEAD_DIM ** (-0.5)

    def at(fsdp=f, ctx=z, tp=c):
        return {"fsdp": fsdp, "ctx": ctx, "tp": tp}

    def copy_to(src, dst, send_sem, recv_sem, device):
        return pltpu.make_async_remote_copy(
            src_ref=src,
            dst_ref=dst,
            send_sem=send_sem,
            recv_sem=recv_sem,
            device_id=device,
            device_id_type=MESH_ID,
        )

    def remote(src, dst, k, device):
        return copy_to(src, dst, send.at[k], recv.at[k], device)

    plane = [at(fx), at(fy), at(fd)]
    line = [at(ctx=lax.rem(z + s, 4)) for s in range(1, 4)]
    sibling = at(tp=1 - c)
    partner = at(ctx=z + 1 - 2 * lax.rem(z, 2))
    opposite = at(ctx=3 - z)
    inner = (z == 1) | (z == 2)
    outer = (z == 0) | (z == 3)

    own = w_hbm.shape[0]
    hidden = w_hbm.shape[3]
    tokens = 8 * half
    tile = 2 * half
    loads = [pltpu.make_async_copy(x_hbm, xy.at[pl.ds(0, tokens)], local.at[0])]
    for e in range(own):
        for m in range(2):
            cols = pl.ds((2 * e + m) * hidden, hidden)
            loads.append(pltpu.make_async_copy(w_hbm.at[e, m], wgu.at[:, cols], local.at[1 + 2 * e + m]))
    loads.append(pltpu.make_async_copy(dy_hbm, xy.at[pl.ds(tokens, tokens)], local.at[5]))
    for e in range(own):
        cols = pl.ds(e * hidden, hidden)
        loads.append(pltpu.make_async_copy(w_hbm.at[e, 2], wd.at[:, cols], local.at[6 + e]))
    my_rows = rows_of(c, half)
    loads.append(pltpu.make_async_copy(tok_hbm.at[my_rows], tok_half, local.at[8]))
    loads.append(pltpu.make_async_copy(cot_hbm.at[my_rows], cot_half, local.at[9]))
    for copy in loads:
        copy.start()
    greet(plane + line + [sibling])
    for b in range(8):
        rows = wl_ref[b % 4, :, pl.ds((b // 4) * half, half)]
        rows = jnp.concatenate([rows, jnp.zeros((128 - EXPERTS, half), f32)], axis=0)
        table[pl.ds(b * half, half), :] = rows.T
    for copy in loads:
        copy.wait()

    lanes = lax.broadcasted_iota(jnp.int32, (tile, 128), 1)

    def act_step(i, _):
        rows = pl.ds(pl.multiple_of(i * tile, tile), tile)
        acts = dot_f32(xy[rows, :], wgu[...])
        plain = dot_f32(xy[pl.ds(pl.multiple_of(tokens + i * tile, tile), tile), :], wd[...])
        scales = table[rows, :]
        sums = jnp.zeros((tile, 128), f32)
        for e in range(own):
            gate_act = acts[:, 2 * e * hidden : (2 * e + 1) * hidden]
            up_act = acts[:, (2 * e + 1) * hidden : (2 * e + 2) * hidden]
            d_plain = plain[:, e * hidden : (e + 1) * hidden]
            here = lanes == own * f + e
            factor = jnp.sum(jnp.where(here, scales, 0.0), axis=1, keepdims=True)
            sigmoid = 1.0 / (1.0 + jnp.exp(-gate_act))
            active = gate_act * sigmoid
            act = active * up_act
            total = jnp.sum(act * d_plain, axis=1, keepdims=True)
            sums = jnp.where(here, jnp.where(factor != 0.0, total, 0.0), sums)
            d_hidden = d_plain * factor
            slope = sigmoid * (1.0 + gate_act * (1.0 - sigmoid))
            hid[rows, pl.ds(e * hidden, hidden)] = (act * factor).astype(bf16)
            gu[rows, pl.ds(2 * e * hidden, hidden)] = (d_hidden * up_act * slope).astype(bf16)
            gu[rows, pl.ds((2 * e + 1) * hidden, hidden)] = (d_hidden * active).astype(bf16)
        table[rows, :] = sums
        return 0

    lax.fori_loop(0, tokens // tile, act_step, 0)
    side, far = rows_of(c, 4 * half), rows_of(1 - c, 4 * half)
    gg_swap = remote(table.at[far], gg_in, 1, sibling)
    gg_swap.start()

    def grad_step(t, _):
        cols = pl.ds(pl.multiple_of(lax.rem(f + t, 4) * shard, 128), shard)
        into_in = dot_f32(xy[pl.ds(0, tokens), cols], gu[...], TN).astype(bf16)
        into_out = dot_f32(xy[pl.ds(tokens, tokens), cols], hid[...], TN).astype(bf16)
        for e in range(own):
            for m in range(2):
                k = 2 * e + m
                ge[3 * e + m, cols, :] = into_in[:, k * hidden : (k + 1) * hidden]
            ge[3 * e + 2, cols, :] = into_out[:, e * hidden : (e + 1) * hidden]
        return 0

    def down_step(i, _):
        rows = pl.ds(pl.multiple_of(i * tile, tile), tile)
        ra[rows, pl.ds(0, width)] = dot_f32(gu[rows, :], wgu[...], NT).astype(bf16)
        return 0

    def out_step(i, _):
        rows = pl.ds(pl.multiple_of(i * tile, tile), tile)
        xy[rows, :] = dot_f32(hid[rows, :], wd[...], NT).astype(bf16)
        return 0

    chunks, attn_rows = ctx_chunks(ge.shape[0], shard)
    n_expert = len(chunks)
    n_all = n_expert + len(attn_rows)

    def chunk(k):
        if k < n_expert:
            j, r, low, size = chunks[k]
            rows = pl.ds(pl.multiple_of(rel[r] * shard + low, 16), size)
            return ge.at[j, rows], r1.at[j, rows]
        rows = pl.ds(sum(attn_rows[: k - n_expert]), attn_rows[k - n_expert])
        return ra.at[rows], a1.at[rows]

    def add_into(dst, left, right):
        size = math.gcd(dst.shape[0], 64)

        def body(i, _):
            rows = pl.ds(pl.multiple_of(i * size, size), size)
            dst[rows, :] = (left[rows, :].astype(f32) + right[rows, :].astype(f32)).astype(bf16)
            return 0

        lax.fori_loop(0, dst.shape[0] // size, body, 0)

    def first(k):
        own, one = chunk(k)
        return copy_to(own, one, z_out.at[k], z_r1.at[k], partner)

    def across(k):
        own, one = chunk(k)
        return copy_to(own, one, z_across.at[k], z_r2.at[k], opposite)

    def back(k):
        _, one = chunk(k)
        return copy_to(one, one, z_back.at[k], z_r1.at[k], partner)

    def final(k):
        _, one = chunk(k)
        j, r, low, size = chunks[k]
        there = fin_hbm.at[r, j, pl.ds(low, size)]
        if r == 0:
            return pltpu.make_async_copy(one, there, f_out.at[k])
        return copy_to(one, there, f_out.at[k], f_in.at[k], plane[r - 1])

    pending, ready = [], []
    pace = 2
    lag_a, lag_b, lag_c, window = 1, 2, 5, 3

    def z_step(i):
        if i < n_all:

            @pl.when(outer)
            def _():
                if i >= window:
                    first(i - window).wait_send()
                first(i).start()

        if lag_a <= i < n_all + lag_a:
            k = i - lag_a

            @pl.when(inner)
            def _():
                own, one = chunk(k)
                first(k).wait_recv()
                add_into(own, own, one)
                pl.semaphore_signal(credit, inc=1, device_id=opposite, device_id_type=MESH_ID)

        if lag_a <= i < n_all + lag_a:
            k = i - lag_a

            @pl.when(inner)
            def _():
                pl.semaphore_wait(credit, 1)
                across(k).start()

        if lag_b <= i < n_all + lag_b:
            k = i - lag_b

            @pl.when(inner)
            def _():
                own, one = chunk(k)
                across(k).wait_recv()
                add_into(one, own, one)
                back(k).start()

        if lag_c <= i < n_all + lag_c:
            k = i - lag_c

            @pl.when(outer)
            def _():
                back(k).wait_recv()

            if k < n_expert:
                ready.append(k)

        for _ in range(pace):
            if pending:
                pending.pop(0).start()
            elif ready:
                final(ready.pop(0)).start()

    steps = iter(range(n_all + max(lag_b, lag_c)))

    def go_on(count=1):
        for _ in range(count):
            z_step(next(steps))

    wide = pl.ds(0, width)
    lax.fori_loop(0, 1, grad_step, 0)
    go_on()
    lax.fori_loop(2 * (1 - c), 2 * (1 - c) + 2, down_step, 0)
    dn_swap = remote(ra.at[far, wide], dn_in, 0, sibling)
    dn_swap.start()
    lax.fori_loop(2 * c, 2 * c + 2, down_step, 0)
    go_on()

    def both(ref, arrived):
        def body(i, _):
            rows = pl.ds(pl.multiple_of(c * 4 * half + i * half, half), half)
            here = pl.ds(pl.multiple_of(i * half, half), half)
            ref[rows, wide] = (ref[rows, wide].astype(f32) + arrived[here, :].astype(f32)).astype(bf16)
            return 0

        lax.fori_loop(0, 4, body, 0)

    def group(i):
        return rows_of(4 * c + i, half)

    gg_swap.wait_recv()
    gg_sum[...] = table[side, :] + gg_in[...]
    dn_swap.wait_recv()
    both(ra, dn_in)
    dn_out = [
        remote(ra.at[group(rel[i + 1]), wide], dn_got.at[i], 3 + i, plane[i]) for i in range(3)
    ]
    gg_out = [
        remote(gg_sum.at[rows_of(rel[i + 1], half)], gg_got.at[i], 6 + i, plane[i])
        for i in range(3)
    ]
    for copy in dn_out + gg_out:
        copy.start()
    lax.fori_loop(1, 4, grad_step, 0)
    go_on()
    lax.fori_loop(2 * (1 - c), 2 * (1 - c) + 2, out_step, 0)
    mo_swap = remote(xy.at[far], mo_in, 2, sibling)
    mo_swap.start()
    lax.fori_loop(2 * c, 2 * c + 2, out_step, 0)
    in_part, out_part = pl.ds(0, in_cols), pl.ds(0, q_cols)
    load_in = pltpu.make_async_copy(wa_hbm.at[:, ins], wgu.at[:, in_part], local.at[0])
    load_out = pltpu.make_async_copy(wa_hbm.at[:, outs], wd, local.at[1])
    load_out.start()
    load_in.start()
    go_on()
    for copy in dn_out:
        copy.wait_recv()
    for copy in dn_out + [dn_swap]:
        copy.wait_send()
    mo_swap.wait_recv()
    both(xy, mo_in)
    d_two = ra[group(f), wide].astype(f32)
    for i in range(3):
        d_two = d_two + dn_got[i].astype(f32)
    residual = res_ref[...]
    inv = lax.rsqrt(jnp.mean(residual * residual, axis=-1, keepdims=True) + eps)
    scaled = d_two * gain_two_ref[...]
    inside = jnp.mean(scaled * residual, axis=-1, keepdims=True)
    d_norm = inv * scaled - residual * (inv * inv * inv * inside)
    gacc[0] = jnp.zeros(gacc.shape[1:], f32)
    gacc[0, 1:2, :] = jnp.sum(d_two * residual * inv, axis=0, keepdims=True)
    d_res = cot_half[...].astype(f32) + d_norm
    dres[...] = d_res
    dattn[my_rows, :] = d_res.astype(bf16)
    da_swap = remote(dattn.at[my_rows], dattn.at[my_rows], 12, sibling)
    da_swap.start()
    mo_out = [remote(xy.at[group(rel[i + 1])], mo_got.at[i], 9 + i, plane[i]) for i in range(3)]
    for copy in mo_out:
        copy.start()
    load_out.wait()
    go_on()
    da_swap.wait_recv()
    dmixed[...] = dot_f32(dattn[...], wd[...]).astype(bf16)
    go_on()

    position = z * count + lax.broadcasted_iota(jnp.int32, (count, HEAD_DIM), 0)
    angle = position.astype(f32) * freq_ref[...]
    cosine = jnp.cos(angle)
    lane = lax.broadcasted_iota(jnp.int32, (count, HEAD_DIM), 1)
    sine = jnp.where(lane < HEAD_DIM // 2, jnp.sin(angle), -jnp.sin(angle))
    keys = kv_ref[:, :, pl.ds(0, HEAD_DIM)].reshape(4 * count, HEAD_DIM)
    vals = kv_ref[:, :, pl.ds(HEAD_DIM, HEAD_DIM)].reshape(4 * count, HEAD_DIM)
    key_cols, val_cols = pl.ds(0, HEAD_DIM), pl.ds(HEAD_DIM, HEAD_DIM)
    dkv[...] = jnp.zeros_like(dkv)
    for g in range(QUERY_PER_GROUP):
        cols = pl.ds(g * HEAD_DIM, HEAD_DIM)
        query = q_ref[:, cols]
        d_mix = dmixed[:, cols]
        probs = block_probs(z, keys, query)
        d_probs = dot_f32(vals, d_mix, NT)
        inside = jnp.sum(probs * d_probs, axis=0, keepdims=True)
        d_scores = (probs * (d_probs - inside)).astype(bf16)
        d_query = dot_f32(d_scores, keys, TN) * scale
        dproj[:, cols] = turn(d_query, cosine, sine).astype(bf16)
        dkv[:, key_cols] += dot_f32(d_scores, query) * scale
        dkv[:, val_cols] += dot_f32(probs.astype(bf16), d_mix)
        if g % 3 == 2:
            go_on()
    dkv_low[...] = dkv[...].reshape(dkv_low.shape).astype(bf16)
    dkv_out = [
        remote(dkv_low.at[s], dkv_got.at[s - 1], 12 + s, at(ctx=lax.rem(z + 4 - s, 4)))
        for s in range(1, 4)
    ]
    for s in range(1, 4):

        @pl.when(z >= s)
        def _(s=s):
            dkv_out[s - 1].start()

    low_rows = pl.ds(4 * shard, shard)

    def weight_grad(left, right, cols):
        def body(i, _):
            rows = pl.ds(pl.multiple_of(i * 256, 256), 256)
            xy[rows, cols] = dot_f32(left[:, rows], right, TN).astype(bf16)
            return 0

        lax.fori_loop(0, width // 256, body, 0)

    def send_grad(cols, into, k):
        third = shard // 3
        copies = []
        for p in range(3):
            for i in range(3):
                rows = pl.ds(pl.multiple_of(rel[i + 1] * shard + p * third, third), third)
                copies.append(
                    remote(
                        xy.at[rows, cols],
                        ra.at[pl.ds(i * shard + p * third, third), into],
                        k + 3 * p + i,
                        plane[i],
                    )
                )
        pending.extend(copies)
        return copies

    for copy in mo_out + gg_out:
        copy.wait_recv()
    moe = xy[group(f), :].astype(f32)
    gates = gg_sum[rows_of(f, half), :]
    for i in range(3):
        moe = moe + mo_got[i].astype(f32)
        gates = gates + gg_got[i]
    layer_ref[my_rows, :] = (res_ref[...] + moe).astype(bf16)
    gate_ref[my_rows, :] = gates
    lo_swap = remote(layer_ref.at[my_rows], layer_ref.at[my_rows], 27, sibling)
    gt_swap = remote(gate_ref.at[my_rows], gate_ref.at[my_rows], 28, sibling)
    lo_swap.start()
    gt_swap.start()
    for copy in mo_out + [mo_swap]:
        copy.wait_send()
    go_on()

    right_half = pl.ds(q_cols, q_cols)
    weight_grad(dattn, mixed_ref[...], right_half)
    ga_copies = send_grad(right_half, outs, 34)
    go_on()
    q_part = pl.ds(0, q_cols)
    weight_grad(xn_ref, dproj[:, q_part], q_part)
    ga_copies += send_grad(q_part, q_part, 43)
    go_on()
    for s in range(1, 4):

        @pl.when(z + s < 4)
        def _(s=s):
            dkv_out[s - 1].wait_recv()
            dkv[0:count, :] += dkv_got[s - 1].astype(f32)

    kv_part = pl.ds(q_cols, 2 * HEAD_DIM)
    dproj[:, pl.ds(q_cols, HEAD_DIM)] = turn(dkv[0:count, key_cols], cosine, sine).astype(bf16)
    dproj[:, pl.ds(q_cols + HEAD_DIM, HEAD_DIM)] = dkv[0:count, val_cols].astype(bf16)
    for s in range(4):
        block = dot_f32(xn_ref[:, pl.ds(s * shard, shard)], dproj[:, kv_part], TN)
        xy[low_rows, pl.ds(s * 2 * HEAD_DIM, 2 * HEAD_DIM)] = block.astype(bf16)
    kv_copies = [
        remote(
            xy.at[low_rows, rows_of(rel[i + 1], 2 * HEAD_DIM)],
            ra.at[pl.ds(i * shard, shard), kv_part],
            16 + i,
            plane[i],
        )
        for i in range(3)
    ]
    pending.extend(kv_copies)
    ga_copies += kv_copies
    go_on()

    load_in.wait()
    for s in range(width // 256):
        rows = pl.ds(s * 256, 256)
        d1[:, rows] = dot_f32(dproj[my_rows, :], wgu[rows, in_part], NT)
        d1_low[:, rows] = dot_f32(
            dproj[rows_of(1 - c, half), :], wgu[rows, in_part], NT
        ).astype(bf16)
    d1_swap = remote(d1_low, d1_in, 25, sibling)
    d1_swap.start()
    go_on()
    d1_swap.wait_recv()
    d_one = d1[...] + d1_in[...].astype(f32)
    tok = tok_half[...].astype(f32)
    inv = lax.rsqrt(jnp.mean(tok * tok, axis=-1, keepdims=True) + eps)
    scaled = d_one * gain_one_ref[...]
    inside = jnp.mean(scaled * tok, axis=-1, keepdims=True)
    d_norm = inv * scaled - tok * (inv * inv * inv * inside)
    gacc[0, 0:1, :] = jnp.sum(d_one * tok * inv, axis=0, keepdims=True)
    tokgrad_ref[my_rows, :] = (dres[...] + d_norm).astype(bf16)
    tg_swap = remote(tokgrad_ref.at[my_rows], tokgrad_ref.at[my_rows], 26, sibling)
    tg_swap.start()
    go_on()

    stages = [sibling, at(fx), at(fy), partner, at(ctx=lax.rem(z + 2, 4))]
    gain_copies = [remote(gacc.at[i], gin.at[i], 29 + i, stages[i]) for i in range(5)]
    for i in range(5):
        gain_copies[i].start()
        go_on()
        gain_copies[i].wait_recv()
        total = gacc[i] + gin[i]
        if i < 4:
            gacc[i + 1] = total
        else:
            gains_ref[...] = total

    while (i := next(steps)) < n_expert - 1:
        z_step(i)
    z_step(i)
    for copy in pending:
        copy.start()
    del pending[:]
    for copy in ga_copies:
        copy.wait_recv()

    def attn_sum(i, _):
        size = shard // 8
        here = pl.ds(pl.multiple_of(i * size, size), size)
        rows = pl.ds(pl.multiple_of(f * shard + i * size, size), size)
        low = pl.ds(pl.multiple_of(4 * shard + i * size, size), size)
        for cols, mine in (
            (q_part, xy[rows, q_part]),
            (kv_part, xy[low, rows_of(f, 2 * HEAD_DIM)]),
            (outs, xy[rows, right_half]),
        ):
            total = mine.astype(f32)
            for r in range(3):
                other = pl.ds(pl.multiple_of(r * shard + i * size, size), size)
                total = total + ra[other, cols].astype(f32)
            ra[here, cols] = total.astype(bf16)
        return 0

    lax.fori_loop(0, 8, attn_sum, 0)
    for i in steps:
        z_step(i)
    store = pltpu.make_async_copy(a1, attn_hbm, local.at[0])
    store.start()

    for k in ready:
        final(k).start()

    store.wait()
    for k in range(n_all):

        @pl.when(outer)
        def _(k=k):
            if k >= n_all - window:
                first(k).wait_send()

        @pl.when(inner)
        def _(k=k):
            across(k).wait_send()
            back(k).wait_send()

    for k in range(n_expert):
        if chunks[k][1] == 0:
            final(k).wait()
        else:
            final(k).wait_send()
            final(k).wait_recv()
    for s in range(1, 4):

        @pl.when(z >= s)
        def _(s=s):
            dkv_out[s - 1].wait_send()

    for copy in [tg_swap, lo_swap, gt_swap]:
        copy.wait_recv()
    swaps = [gg_swap, da_swap, d1_swap, tg_swap, lo_swap, gt_swap]
    for copy in swaps + gg_out + ga_copies + gain_copies:
        copy.wait_send()


def rear(res, xn, q, kv, mixed, gain_one, gain_two, tok, cot, x, dy, weights, gate_table, wa):
    count, width = tok.shape
    half = count // 2
    tokens = 8 * half
    columns = wa.shape[1]
    shard = width // 4
    own, _, _, hidden = weights.shape
    mats = 3 * own
    q_cols = q.shape[1]
    vmem, hbm = pl.BlockSpec(memory_space=pltpu.VMEM), pl.BlockSpec(memory_space=pl.ANY)
    bf16, f32 = jnp.bfloat16, jnp.float32
    shape = jax.ShapeDtypeStruct
    dma = pltpu.SemaphoreType.DMA
    chunks, attn_rows = ctx_chunks(mats, shard)
    n_expert, n_all = len(chunks), len(chunks) + len(attn_rows)
    return pl.pallas_call(
        rear_kernel,
        in_specs=[vmem] * 8 + [hbm] * 5 + [vmem, hbm],
        out_specs=[vmem] * 4 + [hbm] * 2,
        out_shape=[
            shape((count, width), bf16),
            shape((count, width), bf16),
            shape((8, width), f32),
            shape((count, 128), f32),
            shape((shard, columns), bf16),
            shape((4, mats, shard, hidden), bf16),
        ],
        scratch_shapes=[
            pltpu.VMEM((2 * tokens, width), bf16),
            pltpu.VMEM((width, 2 * own * hidden), bf16),
            pltpu.VMEM((width, own * hidden), bf16),
            pltpu.VMEM((tokens, width), bf16),
            pltpu.VMEM((tokens, own * hidden), bf16),
            pltpu.VMEM((tokens, 128), f32),
            pltpu.VMEM((mats, width, hidden), bf16),
            pltpu.VMEM((mats, width, hidden), bf16),
            pltpu.VMEM((4 * half, width), bf16),
            pltpu.VMEM((3, half, width), bf16),
            pltpu.VMEM((4 * half, width), bf16),
            pltpu.VMEM((3, half, width), bf16),
            pltpu.VMEM((4 * half, 128), f32),
            pltpu.VMEM((4 * half, 128), f32),
            pltpu.VMEM((3, half, 128), f32),
            pltpu.VMEM((half, width), f32),
            pltpu.VMEM((count, width), bf16),
            pltpu.VMEM((count, q_cols), bf16),
            pltpu.VMEM((count, q_cols + 2 * HEAD_DIM), bf16),
            pltpu.VMEM((4 * count, 2 * HEAD_DIM), f32),
            pltpu.VMEM((4, count, 2 * HEAD_DIM), bf16),
            pltpu.VMEM((3, count, 2 * HEAD_DIM), bf16),
            pltpu.VMEM((half, width), f32),
            pltpu.VMEM((half, width), bf16),
            pltpu.VMEM((half, width), bf16),
            pltpu.VMEM((3 * shard, columns), bf16),
            pltpu.VMEM((shard, columns), bf16),
            pltpu.VMEM((5, 8, width), f32),
            pltpu.VMEM((5, 8, width), f32),
            pltpu.VMEM((half, width), bf16),
            pltpu.VMEM((half, width), bf16),
            dma((52,)),
            dma((52,)),
            dma((10,)),
            dma((n_all,)),
            dma((n_all,)),
            dma((n_all,)),
            dma((n_all,)),
            dma((n_all,)),
            dma((n_expert,)),
            dma((n_expert,)),
            pltpu.SemaphoreType.REGULAR,
        ],
        compiler_params=pltpu.CompilerParams(
            collective_id=1, has_side_effects=True, vmem_limit_bytes=63 * MIB
        ),
        name="rear",
    )(
        res,
        xn,
        q,
        kv,
        mixed,
        gain_one,
        gain_two,
        frequencies(),
        tok,
        cot,
        x,
        dy,
        weights,
        gate_table,
        wa,
    )


def body_fast(
    tokens,
    attn_norm,
    attention_params,
    ffn_norm,
    expert_weights,
    gate_values,
    routes,
    slot_order,
    cotangent,
):
    sequence_count, block_len, model_width = tokens.shape
    count = sequence_count * block_len
    half = count // 2
    f = lax.axis_index("fsdp")
    shard, hidden = attention_params.shape[0], expert_weights.shape[3]
    tok = tokens.reshape(count, model_width)
    cot = cotangent.reshape(count, model_width)
    gain_one, gain_two = attn_norm[None, :], ffn_norm[None, :]
    route_rows = routes.reshape(count, TOP)
    normed, queries, kv, mixed, residual, gate_table, whole_attn, whole_expert, x, dy = front(
        tok,
        gain_one,
        gain_two,
        route_rows.T,
        gate_values.reshape(count, TOP).T,
        slot_order.reshape(1, count),
        attention_params[:, 0, :],
        jnp.transpose(expert_weights, (0, 2, 1, 3)),
        cot,
    )
    layer_out, tokens_grad, gains, gate_rows, attn_grad, finals = rear(
        residual,
        normed,
        queries,
        kv,
        mixed,
        gain_one,
        gain_two,
        tok,
        cot,
        x.reshape(8 * half, model_width),
        dy.reshape(8 * half, model_width),
        whole_expert,
        gate_table,
        whole_attn,
    )
    picked = route_rows[:, :, None] == jnp.arange(EXPERTS, dtype=jnp.int32)
    gate_grad = jnp.sum(jnp.where(picked, gate_rows[:, None, :EXPERTS], 0.0), axis=-1)
    finals = finals.reshape(EXPERTS, 3, shard, hidden)
    expert_grad, attn_lines = join_experts(finals, attn_grad, expert_order(f).T)
    expert_grad = jnp.transpose(expert_grad, (0, 2, 1, 3))
    return (
        layer_out.reshape(sequence_count, block_len, model_width),
        tokens_grad.reshape(sequence_count, block_len, model_width),
        attn_lines.reshape(shard, 1, attention_params.shape[2]),
        expert_grad,
        gains[0],
        gains[1],
        gate_grad.reshape(sequence_count, block_len, TOP),
    )


def solution(mesh):
    in_specs = (
        P("fsdp", "ctx", None),
        P(),
        P("fsdp", "tp", None),
        P(),
        P("fsdp", None, None, "tp"),
        P("fsdp", "ctx", None),
        P("fsdp", "ctx", None),
        P("fsdp", "ctx"),
        P("fsdp", "ctx", None),
    )
    out_specs = (
        P("fsdp", "ctx", None),
        P("fsdp", "ctx", None),
        P("fsdp", "tp", None),
        P("fsdp", None, None, "tp"),
        P(),
        P(),
        P("fsdp", "ctx", None),
    )
    four = mesh.shape["fsdp"] == 4 and mesh.shape["ctx"] == 4 and mesh.shape["tp"] == 2
    body_fn = body_fast if four else body
    return jax.shard_map(body_fn, mesh=mesh, in_specs=in_specs, out_specs=out_specs, check_vma=False)
```

```python
import jax
import jax.numpy as jnp
from jax import lax
import math
import numpy as np
from jax.experimental import pallas as pl
from jax.experimental.pallas import tpu as pltpu
from jax.sharding import PartitionSpec as P

HEAD_DIM = 128
TOP = 4
EXPERTS = 8
QUERY_PER_GROUP = 6
CAP = 160


eps = 1e-06
theta_base = 1000000.0


def angle_tables(positions):
    frequency = theta_base ** (-(jnp.arange(HEAD_DIM // 2, dtype=jnp.float32) * 2.0) / HEAD_DIM)
    angles = positions.astype(jnp.float32)[:, None] * frequency[None, :]
    return (jnp.cos(angles), jnp.sin(angles))


def rotate(source, cosine_table, sine_table):
    half_size = source.shape[-1] // 2
    front_half = source[..., :half_size]
    back_half = source[..., half_size:]
    return jnp.concatenate(
        [
            front_half * cosine_table - back_half * sine_table,
            back_half * cosine_table + front_half * sine_table,
        ],
        axis=-1,
    )


def norm_back(source, inv_rms, gain_vec, upstream):
    scaled = upstream * gain_vec
    inner_sum = jnp.mean(scaled * source, axis=-1, keepdims=True)
    d_source = inv_rms * scaled - source * inv_rms * inv_rms * inv_rms * inner_sum
    return (d_source, jnp.sum(upstream * source * inv_rms, axis=0))


def slot_tables(route_rows, rank_rows):
    tok_count = route_rows.shape[0]
    inverse = (
        jnp.zeros((tok_count,), jnp.int32).at[rank_rows].set(jnp.arange(tok_count, dtype=jnp.int32))
    )
    ranked = route_rows[inverse].reshape(-1)
    onehot = (ranked[:, None] == jnp.arange(EXPERTS, dtype=jnp.int32)[None, :]).astype(jnp.int32)
    before = jnp.cumsum(onehot, axis=0) - onehot
    slot_ranked = jnp.sum(before * onehot, axis=1).reshape(tok_count, TOP)
    slots = slot_ranked[rank_rows]
    kept_pair = slots < CAP
    pair_slot = jnp.where(kept_pair, route_rows * CAP + slots, EXPERTS * CAP)
    owners = jnp.broadcast_to(jnp.arange(tok_count, dtype=jnp.int32)[:, None], (tok_count, TOP))
    slot_token = (
        jnp.full((EXPERTS * CAP,), tok_count, jnp.int32)
        .at[pair_slot.reshape(-1)]
        .set(owners.reshape(-1), mode="drop")
    )
    return (kept_pair, pair_slot, slot_token)


def attend_forward(queries, key_rows, value_rows, allowed):
    scores = jnp.einsum(
        "qhgd,khd->hgqk", queries, key_rows, preferred_element_type=jnp.float32
    ) * HEAD_DIM ** (-0.5)
    scores = jnp.where(allowed, scores, -1e30)
    row_max = jnp.max(scores, axis=-1, keepdims=True)
    expd = jnp.exp(scores - row_max)
    row_total = jnp.sum(expd, axis=-1, keepdims=True)
    attn_probs = (expd / row_total).astype(jnp.bfloat16)
    mixed_heads = jnp.einsum(
        "hgqk,khd->qhgd", attn_probs, value_rows, preferred_element_type=jnp.float32
    )
    return (mixed_heads.astype(jnp.bfloat16), row_max + jnp.log(row_total))


def attend_backward(queries, key_rows, value_rows, allowed, log_total, d_mixed):
    scores = jnp.einsum(
        "qhgd,khd->hgqk", queries, key_rows, preferred_element_type=jnp.float32
    ) * HEAD_DIM ** (-0.5)
    scores = jnp.where(allowed, scores, -1e30)
    attn_probs = jnp.exp(scores - log_total)
    low_probs = attn_probs.astype(jnp.bfloat16)
    d_probs = jnp.einsum("qhgd,khd->hgqk", d_mixed, value_rows, preferred_element_type=jnp.float32)
    inner_sum = jnp.sum(attn_probs * d_probs, axis=-1, keepdims=True)
    d_scores = (attn_probs * (d_probs - inner_sum)).astype(jnp.bfloat16)
    d_queries = jnp.einsum(
        "hgqk,khd->qhgd", d_scores, key_rows, preferred_element_type=jnp.float32
    ) * HEAD_DIM ** (-0.5)
    d_keys = jnp.einsum(
        "hgqk,qhgd->khd", d_scores, queries, preferred_element_type=jnp.float32
    ) * HEAD_DIM ** (-0.5)
    d_values = jnp.einsum("hgqk,qhgd->khd", low_probs, d_mixed, preferred_element_type=jnp.float32)
    return (d_queries, d_keys, d_values)


def body(
    tokens,
    attn_norm,
    attention_params,
    ffn_norm,
    expert_weights,
    gate_values,
    routes,
    slot_order,
    cotangent,
):
    sequence_count, block_len, model_width = tokens.shape
    tok_count = sequence_count * block_len
    kv_loc = attention_params.shape[1]
    input_columns = (QUERY_PER_GROUP + 2) * HEAD_DIM
    ctx_size = lax.axis_size("ctx")
    ctx_place = lax.axis_index("ctx")
    sequence_length = block_len * ctx_size
    whole_attn, whole_expert = (
        lax.all_gather(attention_params, "fsdp", axis=0, tiled=True),
        lax.all_gather(expert_weights, "fsdp", axis=0, tiled=True),
    )
    positions = ctx_place * block_len + jnp.arange(block_len, dtype=jnp.int32)
    cosine_table, sine_table = angle_tables(positions)
    cosine_table = jnp.tile(cosine_table, (sequence_count, 1))
    sine_table = jnp.tile(sine_table, (sequence_count, 1))
    cos_four = cosine_table[:, None, None, :]
    sin_four = sine_table[:, None, None, :]
    cos_three = cosine_table[:, None, :]
    sin_three = sine_table[:, None, :]
    allowed = (jnp.arange(sequence_length, dtype=jnp.int32) // block_len <= ctx_place)[
        None, None, None, :
    ]
    tok_float = tokens.reshape(tok_count, model_width).astype(jnp.float32)
    inv_one = lax.rsqrt(jnp.mean(tok_float * tok_float, axis=-1, keepdims=True) + eps)
    first_normed = (tok_float * inv_one * attn_norm).astype(jnp.bfloat16)
    projected_rows = jnp.einsum(
        "td,dhc->thc",
        first_normed,
        whole_attn[:, :, :input_columns],
        preferred_element_type=jnp.float32,
    ).reshape(tok_count, kv_loc, QUERY_PER_GROUP + 2, HEAD_DIM)
    queries = rotate(projected_rows[:, :, :QUERY_PER_GROUP], cos_four, sin_four).astype(
        jnp.bfloat16
    )
    key_rows = rotate(projected_rows[:, :, QUERY_PER_GROUP], cos_three, sin_three).astype(
        jnp.bfloat16
    )
    value_rows = projected_rows[:, :, QUERY_PER_GROUP + 1].astype(jnp.bfloat16)
    key_all, value_all = (
        lax.all_gather(
            key_rows.reshape(sequence_count, block_len, kv_loc, HEAD_DIM), "ctx", axis=1, tiled=True
        ),
        lax.all_gather(
            value_rows.reshape(sequence_count, block_len, kv_loc, HEAD_DIM),
            "ctx",
            axis=1,
            tiled=True,
        ),
    )
    query_seq = queries.reshape(sequence_count, block_len, kv_loc, QUERY_PER_GROUP, HEAD_DIM)
    mixed_heads, log_total = lax.map(
        lambda item_args: attend_forward(item_args[0], item_args[1], item_args[2], allowed),
        (query_seq, key_all, value_all),
    )
    mixed_flat = mixed_heads.reshape(tok_count, kv_loc, QUERY_PER_GROUP * HEAD_DIM)
    attn_part = jnp.einsum(
        "thc,dhc->td",
        mixed_flat,
        whole_attn[:, :, input_columns:],
        preferred_element_type=jnp.float32,
    )
    attn_sum = lax.psum(attn_part, "tp")
    residual = tok_float + attn_sum
    inv_two = lax.rsqrt(jnp.mean(residual * residual, axis=-1, keepdims=True) + eps)
    normed_two = (residual * inv_two * ffn_norm).astype(jnp.bfloat16)
    kept_pair, pair_slot, slot_token = slot_tables(
        routes.reshape(tok_count, TOP), slot_order.reshape(tok_count)
    )
    kept_float = kept_pair.astype(jnp.float32)
    gate_kept = gate_values.reshape(tok_count, TOP) * kept_float
    slot_gate = (
        jnp.zeros((EXPERTS * CAP,), jnp.float32)
        .at[pair_slot.reshape(-1)]
        .set(gate_kept.reshape(-1), mode="drop")
    )
    padded = jnp.concatenate([normed_two, jnp.zeros((1, model_width), jnp.bfloat16)], axis=0)
    inputs = padded[slot_token].reshape(EXPERTS, CAP, model_width)
    gate_act = jnp.einsum(
        "ecd,deh->ech", inputs, whole_expert[:, :, 0], preferred_element_type=jnp.float32
    )
    up_act = jnp.einsum(
        "ecd,deh->ech", inputs, whole_expert[:, :, 1], preferred_element_type=jnp.float32
    )
    gate_sigmoid = jax.nn.sigmoid(gate_act)
    active = gate_act * gate_sigmoid
    hidden = (active * up_act).astype(jnp.bfloat16)
    expert_out = jnp.einsum(
        "ech,deh->ecd", hidden, whole_expert[:, :, 2], preferred_element_type=jnp.float32
    )
    out_pad = jnp.concatenate(
        [expert_out.reshape(EXPERTS * CAP, model_width), jnp.zeros((1, model_width), jnp.float32)],
        axis=0,
    )
    picked = out_pad[pair_slot]
    moe_part = jnp.sum(picked * gate_kept[:, :, None], axis=1)
    moe = lax.psum(moe_part.astype(jnp.bfloat16), "tp").astype(jnp.float32)
    layer_out = (
        (residual + moe).astype(jnp.bfloat16).reshape(sequence_count, block_len, model_width)
    )
    grad_out = cotangent.reshape(tok_count, model_width).astype(jnp.float32)
    gate_part = jnp.sum(picked * grad_out[:, None, :], axis=-1) * kept_float
    grad_pad = jnp.concatenate([grad_out, jnp.zeros((1, model_width), jnp.float32)], axis=0)
    d_expert = (
        (grad_pad[slot_token] * slot_gate[:, None])
        .astype(jnp.bfloat16)
        .reshape(EXPERTS, CAP, model_width)
    )
    d_hidden = jnp.einsum(
        "ecd,deh->ech", d_expert, whole_expert[:, :, 2], preferred_element_type=jnp.float32
    )
    silu_slope = gate_sigmoid * (1.0 + gate_act * (1.0 - gate_sigmoid))
    d_gate_act = (d_hidden * up_act * silu_slope).astype(jnp.bfloat16)
    d_up_act = (d_hidden * active).astype(jnp.bfloat16)
    d_inputs = jnp.einsum(
        "ech,deh->ecd", d_gate_act, whole_expert[:, :, 0], preferred_element_type=jnp.float32
    )
    d_inputs = d_inputs + jnp.einsum(
        "ech,deh->ecd", d_up_act, whole_expert[:, :, 1], preferred_element_type=jnp.float32
    )
    d_in_pad = jnp.concatenate(
        [d_inputs.reshape(EXPERTS * CAP, model_width), jnp.zeros((1, model_width), jnp.float32)],
        axis=0,
    )
    d_normed_part = jnp.sum(d_in_pad[pair_slot], axis=1)
    d_normed_two, gate_grad = lax.psum((d_normed_part, gate_part), "tp")
    d_resid_norm, gain_two = norm_back(residual, inv_two, ffn_norm, d_normed_two)
    d_residual = grad_out + d_resid_norm
    d_attn = d_residual.astype(jnp.bfloat16)
    d_mixed = jnp.einsum(
        "td,dhc->thc", d_attn, whole_attn[:, :, input_columns:], preferred_element_type=jnp.float32
    ).astype(jnp.bfloat16)
    d_mixed_seq = d_mixed.reshape(sequence_count, block_len, kv_loc, QUERY_PER_GROUP, HEAD_DIM)
    d_queries, d_key_all, d_value_all = lax.map(
        lambda item_args: attend_backward(
            item_args[0], item_args[1], item_args[2], allowed, item_args[3], item_args[4]
        ),
        (query_seq, key_all, value_all, log_total, d_mixed_seq),
    )
    d_keys, d_values = (
        lax.psum_scatter(
            d_key_all.astype(jnp.bfloat16), "ctx", scatter_dimension=1, tiled=True
        ).astype(jnp.float32),
        lax.psum_scatter(
            d_value_all.astype(jnp.bfloat16), "ctx", scatter_dimension=1, tiled=True
        ).astype(jnp.float32),
    )
    d_queries = rotate(
        d_queries.reshape(tok_count, kv_loc, QUERY_PER_GROUP, HEAD_DIM), cos_four, -sin_four
    )
    d_keys = rotate(d_keys.reshape(tok_count, kv_loc, HEAD_DIM), cos_three, -sin_three)
    d_values = d_values.reshape(tok_count, kv_loc, HEAD_DIM)
    d_projected = jnp.concatenate([d_queries, d_keys[:, :, None], d_values[:, :, None]], axis=2)
    d_projected = d_projected.astype(jnp.bfloat16).reshape(tok_count, kv_loc, input_columns)
    d_normed_local = jnp.einsum(
        "thc,dhc->td",
        d_projected,
        whole_attn[:, :, :input_columns],
        preferred_element_type=jnp.float32,
    )
    d_normed_one = lax.psum(d_normed_local.astype(jnp.bfloat16), "tp").astype(jnp.float32)
    d_tok_norm, gain_one = norm_back(tok_float, inv_one, attn_norm, d_normed_one)
    tokens_grad = (
        (d_residual + d_tok_norm)
        .astype(jnp.bfloat16)
        .reshape(sequence_count, block_len, model_width)
    )
    gain_one, gain_two = lax.psum((gain_one, gain_two), ("fsdp", "ctx"))
    in_term = jnp.einsum(
        "td,thc->dhc", first_normed, d_projected, preferred_element_type=jnp.float32
    )
    out_term = jnp.einsum("td,thc->dhc", d_attn, mixed_flat, preferred_element_type=jnp.float32)
    attn_grad = lax.psum_scatter(
        jnp.concatenate([in_term, out_term], axis=2),
        ("fsdp", "ctx"),
        scatter_dimension=0,
        tiled=True,
    )
    gate_term = jnp.einsum("ecd,ech->deh", inputs, d_gate_act, preferred_element_type=jnp.float32)
    up_term = jnp.einsum("ecd,ech->deh", inputs, d_up_act, preferred_element_type=jnp.float32)
    down_term = jnp.einsum("ecd,ech->deh", d_expert, hidden, preferred_element_type=jnp.float32)
    expert_grad = lax.psum_scatter(
        jnp.stack([gate_term, up_term, down_term], axis=2),
        ("fsdp", "ctx"),
        scatter_dimension=0,
        tiled=True,
    )
    attn_grad, expert_grad = (
        lax.all_gather(attn_grad.astype(jnp.bfloat16), "ctx", axis=0, tiled=True).astype(
            attn_grad.dtype
        ),
        lax.all_gather(expert_grad.astype(jnp.bfloat16), "ctx", axis=0, tiled=True).astype(
            expert_grad.dtype
        ),
    )
    return (
        layer_out,
        tokens_grad,
        attn_grad,
        expert_grad,
        gain_one,
        gain_two,
        gate_grad.reshape(sequence_count, block_len, TOP),
    )


MESH_ID = pl.DeviceIdType.MESH
MIB = 2**20


def expert_order(place):
    row = jnp.arange(128, dtype=jnp.int32)
    expert = (((row // 32) ^ place) * 2) + (row // 16) % 2
    source = (row % 16) * 8 + expert
    return (source[:, None] == row[None, :]).astype(jnp.bfloat16)


def join_kernel(order_ref, in_ref, attn_in_ref, out_ref, attn_out_ref):
    width = in_ref.shape[3]
    for m in range(3):
        for k in range(in_ref.shape[2] // 16):
            block = in_ref[:, m, pl.ds(k * 16, 16), :].reshape(128, width)
            moved = jnp.dot(order_ref[...], block, preferred_element_type=jnp.float32)
            out_ref[pl.ds(k * 16, 16), m] = moved.reshape(16, 8, width)
    rows, columns = attn_in_ref.shape
    parts = columns // 128
    for j in range(parts):
        part = attn_in_ref[:, pl.ds(j * 128, 128)].astype(jnp.float32)
        attn_out_ref[pl.ds(j, rows, stride=parts), :] = part


def join_experts(grads, attn_grad, order):
    experts, _, rows, width = grads.shape
    columns = attn_grad.shape[1]
    step = 128
    lines = step * columns // 128
    return pl.pallas_call(
        join_kernel,
        grid=(rows // step,),
        in_specs=[
            pl.BlockSpec((128, 128), lambda i: (0, 0)),
            pl.BlockSpec((experts, 3, step, width), lambda i: (0, 0, i, 0)),
            pl.BlockSpec((step, columns), lambda i: (i, 0)),
        ],
        out_specs=[
            pl.BlockSpec((step, 3, experts, width), lambda i: (i, 0, 0, 0)),
            pl.BlockSpec((lines, 128), lambda i: (i, 0)),
        ],
        out_shape=[
            jax.ShapeDtypeStruct((rows, 3, experts, width), jnp.float32),
            jax.ShapeDtypeStruct((rows * columns // 128, 128), jnp.float32),
        ],
        compiler_params=pltpu.CompilerParams(vmem_limit_bytes=60 * MIB),
        name="join_experts",
    )(order, grads, attn_grad)


NT = (((1,), (1,)), ((), ()))
TN = (((0,), (0,)), ((), ()))


def dot_f32(a, b, dims=(((1,), (0,)), ((), ()))):
    return lax.dot_general(a, b, dims, preferred_element_type=jnp.float32)


def block_probs(last, keys, query):
    scores = dot_f32(keys, query, NT) * HEAD_DIM ** (-0.5)
    block = lax.broadcasted_iota(jnp.int32, scores.shape, 0) // query.shape[0]
    scores = jnp.where(block <= last, scores, -1e30)
    expd = jnp.exp(scores - jnp.max(scores, axis=0, keepdims=True))
    return expd * (1.0 / jnp.sum(expd, axis=0, keepdims=True))


def place():
    return lax.axis_index("fsdp"), lax.axis_index("ctx"), lax.axis_index("tp")


def plane_peers(f):
    return f + 1 - 2 * lax.rem(f, 2), lax.rem(f + 2, 4), 3 - f


def rows_of(index, size):
    return pl.ds(pl.multiple_of(index * size, size), size)


def greet(devices):
    barrier = pltpu.get_barrier_semaphore()
    for device in devices:
        pl.semaphore_signal(barrier, inc=1, device_id=device, device_id_type=MESH_ID)
    pl.semaphore_wait(barrier, len(devices))


def turn(value, cosine, sine):
    return value * cosine + pltpu.roll(value, HEAD_DIM // 2, 1) * sine


def frequencies():
    i = np.arange(HEAD_DIM // 2, dtype=np.float32)
    freq = (theta_base ** (-(i * 2.0) / HEAD_DIM)).astype(np.float32)
    return jnp.asarray(np.concatenate([freq, freq])[None, :])


def front_kernel(
    tok_ref,
    gain_ref,
    freq_ref,
    routes_ref,
    gates_ref,
    order_ref,
    attn_hbm,
    experts_hbm,
    cot_hbm,
    xn_ref,
    q_ref,
    kv_ref,
    mixed_ref,
    res_ref,
    wl_ref,
    wa_hbm,
    w_hbm,
    x_hbm,
    dy_hbm,
    raw,
    pieces,
    wa,
    part,
    part_in,
    low_half,
    send,
    recv,
    local,
):
    f, z, c = place()
    fx, fy, fd = plane_peers(f)
    count, width = tok_ref.shape
    half = count // 2
    shard = attn_hbm.shape[0]
    cut = shard // 2
    in_cols = (QUERY_PER_GROUP + 2) * HEAD_DIM
    ins = pl.ds(0, in_cols)
    outs = pl.ds(in_cols, attn_hbm.shape[1] - in_cols)

    def at(fsdp=f, ctx=z, tp=c):
        return {"fsdp": fsdp, "ctx": ctx, "tp": tp}

    def remote(src, dst, k, device):
        return pltpu.make_async_remote_copy(
            src_ref=src,
            dst_ref=dst,
            send_sem=send.at[k],
            recv_sem=recv.at[k],
            device_id=device,
            device_id_type=MESH_ID,
        )

    plane = [at(fx), at(fy), at(fd)]
    rel = [fx, fy, fd]
    line = [at(ctx=lax.rem(z + s, 4)) for s in range(1, 4)]
    sibling = at(tp=1 - c)
    mine = rows_of(f, shard)
    load = pltpu.make_async_copy(experts_hbm, raw, local.at[6])
    load.start()
    greet(plane + line + [sibling])

    owned = pltpu.make_async_copy(attn_hbm, wa.at[mine], local.at[0])
    owned.start()
    in_x = remote(attn_hbm.at[:, ins], wa.at[mine, ins], 0, at(fx))
    in_y = remote(attn_hbm.at[:, ins], wa.at[mine, ins], 1, at(fy))
    in_x.start()
    in_y.start()

    rank = jnp.broadcast_to(order_ref[...].astype(jnp.float32), (count, count))
    ahead = jnp.where(rank.T < rank, 1.0, 0.0).astype(jnp.bfloat16)
    expert = lax.broadcasted_iota(jnp.int32, (128, count), 0)
    member = jnp.zeros((128, count), jnp.float32)
    gate = jnp.zeros((128, count), jnp.float32)
    for j in range(TOP):
        hit = jnp.broadcast_to(routes_ref[j : j + 1, :], (128, count)) == expert
        member = jnp.where(hit, 1.0, member)
        gate = jnp.where(hit, jnp.broadcast_to(gates_ref[j : j + 1, :], (128, count)), gate)
    slots = dot_f32(member.astype(jnp.bfloat16), ahead)
    gate = jnp.where(slots < CAP - 0.5, gate, 0.0)
    wl_ref[f] = gate[:EXPERTS]
    gate_copies = [remote(wl_ref.at[f], wl_ref.at[f], 2 + i, plane[i]) for i in range(3)]
    for copy in gate_copies:
        copy.start()

    own_dy = [
        pltpu.make_async_copy(
            cot_hbm.at[pl.ds(i * half, half)], dy_hbm.at[i, f], local.at[2 + i]
        )
        for i in range(2)
    ]
    for copy in own_dy:
        copy.start()

    row = lax.broadcasted_iota(jnp.int32, (128, 128), 0)
    column = lax.broadcasted_iota(jnp.int32, (128, 128), 1)
    owner = jnp.where(row < 64, jnp.where(row < 32, f, fx), jnp.where(row < 96, fy, fd))
    source = (row % 16) * 8 + owner * 2 + (row // 16) % 2
    order = jnp.where(source == column, 1.0, 0.0).astype(jnp.bfloat16)

    def split(m):
        def body(k, _):
            rows = pl.ds(pl.multiple_of(k * 16, 16), 16)
            block = raw[rows, m].reshape(128, raw.shape[3])
            moved = dot_f32(order, block).astype(jnp.bfloat16)
            pieces[:, m, rows, :] = moved.reshape(8, 16, raw.shape[3])
            return 0

        lax.fori_loop(0, shard // 16, body, 0)

    cut_rows = shard // 4
    from_rows = rows_of(z, cut_rows)
    to_rows = rows_of(4 * f + z, cut_rows)

    def quarter(m, i):
        return remote(
            pieces.at[pl.ds(2 * (i + 1), 2), m, from_rows],
            w_hbm.at[:, m, to_rows, :],
            37 + 3 * m + i,
            plane[i],
        )

    def hand_on(m, i):
        quarters[3 * m + i].wait_recv()
        here = w_hbm.at[:, m, rows_of(4 * rel[i] + z, cut_rows), :]
        copies = [remote(here, here, 43 + 9 * m + 3 * i + s, line[s]) for s in range(3)]
        for copy in copies:
            copy.start()
        return copies

    load.wait()
    split(0)
    quarters = [quarter(0, i) for i in range(3)]
    for copy in quarters:
        copy.start()

    tok = tok_ref[...].astype(jnp.float32)
    inv = lax.rsqrt(jnp.mean(tok * tok, axis=-1, keepdims=True) + eps)
    xn_ref[...] = (tok * inv * gain_ref[0:1, :]).astype(jnp.bfloat16)
    position = z * count + lax.broadcasted_iota(jnp.int32, (count, HEAD_DIM), 0)
    angle = position.astype(jnp.float32) * freq_ref[...]
    cosine = jnp.cos(angle)
    lane = lax.broadcasted_iota(jnp.int32, (count, HEAD_DIM), 1)
    sine = jnp.where(lane < HEAD_DIM // 2, -jnp.sin(angle), jnp.sin(angle))

    top, low = rows_of(2 * fx, cut), rows_of(2 * fy + 1, cut)
    in_x.wait_recv()
    in_xy = remote(wa.at[top, ins], wa.at[top, ins], 5, at(fy))
    in_xy.start()
    in_y.wait_recv()
    in_yx = remote(wa.at[low, ins], wa.at[low, ins], 6, at(fx))
    in_yx.start()
    out_x = remote(attn_hbm.at[:, outs], wa.at[mine, outs], 7, at(fx))
    out_y = remote(attn_hbm.at[:, outs], wa.at[mine, outs], 8, at(fy))
    split(1)
    quarters += [quarter(1, i) for i in range(3)]
    for copy in quarters[3:]:
        copy.start()
    out_x.start()
    out_y.start()
    handed = hand_on(0, 0)
    dy_copies = [
        remote(cot_hbm.at[rows_of(c, half)], dy_hbm.at[c, f], 23 + i, plane[i]) for i in range(2)
    ]
    for copy in dy_copies:
        copy.start()
    split(2)
    own_w = pltpu.make_async_copy(pieces.at[pl.ds(0, 2)], w_hbm.at[:, :, mine, :], local.at[1])
    own_w.start()
    owned.wait()
    in_xy.wait_recv()
    in_yx.wait_recv()

    normed = xn_ref[...]
    for h in range(QUERY_PER_GROUP + 2):
        cols = pl.ds(h * HEAD_DIM, HEAD_DIM)
        if h % 2 == 0:
            pair = dot_f32(normed, wa[:, pl.ds(h * HEAD_DIM, 2 * HEAD_DIM)])
        value = pair[:, (h % 2) * HEAD_DIM : (h % 2 + 1) * HEAD_DIM]
        if h <= QUERY_PER_GROUP:
            value = turn(value, cosine, sine)
        if h < QUERY_PER_GROUP:
            q_ref[:, cols] = value.astype(jnp.bfloat16)
        else:
            kv_ref[0, :, pl.ds((h - QUERY_PER_GROUP) * HEAD_DIM, HEAD_DIM)] = value.astype(
                jnp.bfloat16
            )
    kv_copies = [remote(kv_ref.at[0], kv_ref.at[s], 8 + s, line[s - 1]) for s in range(1, 4)]
    for s in range(1, 4):

        @pl.when(z + s < 4)
        def _(s=s):
            kv_copies[s - 1].start()

        @pl.when(z < s)
        def _(s=s):
            kv_ref[s] = jnp.zeros(kv_ref.shape[1:], jnp.bfloat16)

    handed += hand_on(0, 1) + hand_on(0, 2)
    out_x.wait_recv()
    out_xy = remote(wa.at[top, outs], wa.at[top, outs], 12, at(fy))
    out_xy.start()
    out_y.wait_recv()
    out_yx = remote(wa.at[low, outs], wa.at[low, outs], 13, at(fx))
    out_yx.start()

    w_copies = [
        remote(pieces.at[pl.ds(2 * (i + 1), 2), 2], w_hbm.at[:, 2, mine, :], 14 + i, plane[i])
        for i in range(3)
    ]
    for copy in w_copies:
        copy.start()
    for i in range(3):
        handed += hand_on(1, i)

    for s in range(1, 4):

        @pl.when(z >= s)
        def _(s=s):
            kv_copies[s - 1].wait_recv()

    keys = kv_ref[:, :, pl.ds(0, HEAD_DIM)].reshape(4 * count, HEAD_DIM)
    vals = kv_ref[:, :, pl.ds(HEAD_DIM, HEAD_DIM)].reshape(4 * count, HEAD_DIM)
    for g in range(QUERY_PER_GROUP):
        cols = pl.ds(g * HEAD_DIM, HEAD_DIM)
        probs = block_probs(z, keys, q_ref[:, cols]).astype(jnp.bfloat16)
        mixed_ref[:, cols] = dot_f32(probs, vals, TN).astype(jnp.bfloat16)

    upper, lower = pl.ds(0, half // 2), pl.ds(half // 2, half // 2)

    def pass_on(copies, ref, k):
        copies[0].wait_recv()
        up = ref.at[c, fx, upper]
        passed = [remote(up, up, k, at(fy))]
        passed[0].start()
        copies[1].wait_recv()
        low = ref.at[c, fy, lower]
        passed.append(remote(low, low, k + 1, at(fx)))
        passed[1].start()
        return passed

    out_xy.wait_recv()
    out_yx.wait_recv()
    store_wa = pltpu.make_async_copy(wa, wa_hbm, local.at[4])
    store_wa.start()
    for s in range(width // 256):
        cols = pl.ds(s * 256, 256)
        part[:, cols] = dot_f32(mixed_ref[...], wa[cols, outs], NT)
    swap = remote(part.at[rows_of(1 - c, half)], part_in, 26, sibling)
    swap.start()
    swap.wait_recv()
    my_rows = rows_of(c, half)
    residual = tok_ref[my_rows, :].astype(jnp.float32) + (part[my_rows, :] + part_in[...])
    res_ref[...] = residual
    inv = lax.rsqrt(jnp.mean(residual * residual, axis=-1, keepdims=True) + eps)
    low_half[...] = (residual * inv * gain_ref[1:2, :]).astype(jnp.bfloat16)
    own_x = pltpu.make_async_copy(low_half, x_hbm.at[c, f], local.at[5])
    own_x.start()
    x_copies = [remote(low_half, x_hbm.at[c, f], 27 + i, plane[i]) for i in range(2)]
    for copy in x_copies:
        copy.start()
    sib_x = [remote(low_half, x_hbm.at[c, f], 30, sibling)]
    sib_x[0].start()

    dy_passed = pass_on(dy_copies, dy_hbm, 61)
    x_passed = pass_on(x_copies, x_hbm, 63)
    sib_dy = []
    for i in range(2):
        sib_dy.append(remote(dy_hbm.at[c, rel[i]], dy_hbm.at[c, rel[i]], 31 + i, sibling))
        sib_x.append(remote(x_hbm.at[c, rel[i]], x_hbm.at[c, rel[i]], 34 + i, sibling))
        sib_dy[i].start()
        sib_x[i + 1].start()
    for copy in dy_passed:
        copy.wait_recv()
    sib_dy.append(remote(dy_hbm.at[c, fd], dy_hbm.at[c, fd], 33, sibling))
    sib_dy[2].start()
    for copy in x_passed:
        copy.wait_recv()
    sib_x.append(remote(x_hbm.at[c, fd], x_hbm.at[c, fd], 36, sibling))
    sib_x[3].start()

    for copy in w_copies + gate_copies + handed + sib_dy + sib_x:
        copy.wait_recv()
    for s in range(1, 4):

        @pl.when(z + s < 4)
        def _(s=s):
            kv_copies[s - 1].wait_send()

    for copy in [in_x, in_y, in_xy, in_yx, out_x, out_y, out_xy, out_yx, swap]:
        copy.wait_send()
    sent = w_copies + quarters + handed + gate_copies + dy_copies + x_copies
    for copy in sent + dy_passed + x_passed + sib_dy + sib_x:
        copy.wait_send()
    for copy in [own_w, own_x, store_wa] + own_dy:
        copy.wait()


def front(tok, gains, routes, gates, order, attn_own, weights, cot):
    count, width = tok.shape
    half = count // 2
    shard, columns = attn_own.shape
    experts, hidden = EXPERTS // 4, weights.shape[3]
    vmem, hbm = pl.BlockSpec(memory_space=pltpu.VMEM), pl.BlockSpec(memory_space=pl.ANY)
    bf16, f32 = jnp.bfloat16, jnp.float32
    shape = jax.ShapeDtypeStruct
    return pl.pallas_call(
        front_kernel,
        in_specs=[vmem] * 6 + [hbm] * 3,
        out_specs=[vmem] * 6 + [hbm] * 4,
        out_shape=[
            shape((count, width), bf16),
            shape((count, QUERY_PER_GROUP * HEAD_DIM), bf16),
            shape((4, count, 2 * HEAD_DIM), bf16),
            shape((count, QUERY_PER_GROUP * HEAD_DIM), bf16),
            shape((half, width), f32),
            shape((4, EXPERTS, count), f32),
            shape((4 * shard, columns), bf16),
            shape((experts, 3, 4 * shard, hidden), bf16),
            shape((2, 4, half, width), bf16),
            shape((2, 4, half, width), bf16),
        ],
        scratch_shapes=[
            pltpu.VMEM(weights.shape, bf16),
            pltpu.VMEM((EXPERTS, 3, shard, hidden), bf16),
            pltpu.VMEM((4 * shard, columns), bf16),
            pltpu.VMEM((count, width), f32),
            pltpu.VMEM((half, width), f32),
            pltpu.VMEM((half, width), bf16),
            pltpu.SemaphoreType.DMA((65,)),
            pltpu.SemaphoreType.DMA((65,)),
            pltpu.SemaphoreType.DMA((7,)),
        ],
        compiler_params=pltpu.CompilerParams(
            collective_id=0, has_side_effects=True, vmem_limit_bytes=60 * MIB
        ),
        name="front",
    )(tok, gains, frequencies(), routes, gates, order, attn_own, weights, cot)


def ctx_chunks(mats, shard):
    early = [(0, 0), (1, 0)]
    chunks = [(j, r, 0, shard) for j, r in early]
    chunks += [(j, r, 0, shard) for j in range(mats) for r in range(4) if (j, r) not in early]
    return chunks, [shard // 8] * 8


def rear_kernel(
    res_ref,
    xn_ref,
    q_ref,
    kv_ref,
    mixed_ref,
    gain_ref,
    freq_ref,
    tok_hbm,
    cot_hbm,
    x_hbm,
    dy_hbm,
    w_hbm,
    wl_ref,
    wa_hbm,
    layer_ref,
    tokgrad_ref,
    gains_ref,
    gate_ref,
    attn_hbm,
    fin_hbm,
    xy,
    wgu,
    wd,
    gu,
    hid,
    table,
    ge,
    r1,
    dn_in,
    dn_got,
    mo_in,
    mo_got,
    gg_in,
    gg_sum,
    gg_got,
    dres,
    dattn,
    dmixed,
    dproj,
    dkv,
    dkv_low,
    dkv_got,
    d1,
    d1_low,
    d1_in,
    ra,
    a1,
    gacc,
    gin,
    tok_half,
    cot_half,
    send,
    recv,
    local,
    z_out,
    z_across,
    z_back,
    z_r1,
    z_r2,
    f_out,
    f_in,
    credit,
):
    f, z, c = place()
    fx, fy, fd = plane_peers(f)
    rel = [f, fx, fy, fd]
    f32, bf16 = jnp.float32, jnp.bfloat16
    count, width = tok_hbm.shape
    half = count // 2
    shard = attn_hbm.shape[0]
    in_cols = (QUERY_PER_GROUP + 2) * HEAD_DIM
    q_cols = QUERY_PER_GROUP * HEAD_DIM
    ins = pl.ds(0, in_cols)
    outs = pl.ds(in_cols, attn_hbm.shape[1] - in_cols)
    scale = HEAD_DIM ** (-0.5)

    def at(fsdp=f, ctx=z, tp=c):
        return {"fsdp": fsdp, "ctx": ctx, "tp": tp}

    def copy_to(src, dst, send_sem, recv_sem, device):
        return pltpu.make_async_remote_copy(
            src_ref=src,
            dst_ref=dst,
            send_sem=send_sem,
            recv_sem=recv_sem,
            device_id=device,
            device_id_type=MESH_ID,
        )

    def remote(src, dst, k, device):
        return copy_to(src, dst, send.at[k], recv.at[k], device)

    plane = [at(fx), at(fy), at(fd)]
    line = [at(ctx=lax.rem(z + s, 4)) for s in range(1, 4)]
    sibling = at(tp=1 - c)
    partner = at(ctx=z + 1 - 2 * lax.rem(z, 2))
    opposite = at(ctx=3 - z)
    inner = (z == 1) | (z == 2)
    outer = (z == 0) | (z == 3)

    own = w_hbm.shape[0]
    hidden = w_hbm.shape[3]
    tokens = 8 * half
    tile = 2 * half
    loads = [pltpu.make_async_copy(x_hbm, xy.at[pl.ds(0, tokens)], local.at[0])]
    for e in range(own):
        for m in range(2):
            cols = pl.ds((2 * e + m) * hidden, hidden)
            loads.append(pltpu.make_async_copy(w_hbm.at[e, m], wgu.at[:, cols], local.at[1 + 2 * e + m]))
    loads.append(pltpu.make_async_copy(dy_hbm, xy.at[pl.ds(tokens, tokens)], local.at[5]))
    for e in range(own):
        cols = pl.ds(e * hidden, hidden)
        loads.append(pltpu.make_async_copy(w_hbm.at[e, 2], wd.at[:, cols], local.at[6 + e]))
    my_rows = rows_of(c, half)
    loads.append(pltpu.make_async_copy(tok_hbm.at[my_rows], tok_half, local.at[8]))
    loads.append(pltpu.make_async_copy(cot_hbm.at[my_rows], cot_half, local.at[9]))
    for copy in loads:
        copy.start()
    greet(plane + line + [sibling])
    for b in range(8):
        rows = wl_ref[b % 4, :, pl.ds((b // 4) * half, half)]
        rows = jnp.concatenate([rows, jnp.zeros((128 - EXPERTS, half), f32)], axis=0)
        table[pl.ds(b * half, half), :] = rows.T
    for copy in loads[:5]:
        copy.wait()

    lanes = lax.broadcasted_iota(jnp.int32, (tile, 128), 1)

    def act_step(i, _):
        rows = pl.ds(pl.multiple_of(i * tile, tile), tile)
        acts = dot_f32(xy[rows, :], wgu[...])

        @pl.when(i == 0)
        def _():
            for copy in loads[5:]:
                copy.wait()

        plain = dot_f32(xy[pl.ds(pl.multiple_of(tokens + i * tile, tile), tile), :], wd[...])
        scales = table[rows, :]
        sums = jnp.zeros((tile, 128), f32)
        for e in range(own):
            gate_act = acts[:, 2 * e * hidden : (2 * e + 1) * hidden]
            up_act = acts[:, (2 * e + 1) * hidden : (2 * e + 2) * hidden]
            d_plain = plain[:, e * hidden : (e + 1) * hidden]
            here = lanes == own * f + e
            factor = jnp.sum(jnp.where(here, scales, 0.0), axis=1, keepdims=True)
            sigmoid = 1.0 / (1.0 + jnp.exp(-gate_act))
            active = gate_act * sigmoid
            act = active * up_act
            total = jnp.sum(act * d_plain, axis=1, keepdims=True)
            sums = jnp.where(here, jnp.where(factor != 0.0, total, 0.0), sums)
            d_hidden = d_plain * factor
            slope = sigmoid * (1.0 + gate_act * (1.0 - sigmoid))
            hid[rows, pl.ds(e * hidden, hidden)] = (act * factor).astype(bf16)
            gu[rows, pl.ds(2 * e * hidden, hidden)] = (d_hidden * up_act * slope).astype(bf16)
            gu[rows, pl.ds((2 * e + 1) * hidden, hidden)] = (d_hidden * active).astype(bf16)
        table[rows, :] = sums
        return 0

    lax.fori_loop(0, tokens // tile, act_step, 0)
    side, far = rows_of(c, 4 * half), rows_of(1 - c, 4 * half)
    gg_swap = remote(table.at[far], gg_in, 1, sibling)
    gg_swap.start()

    def grad_step(t, _):
        cols = pl.ds(pl.multiple_of(lax.rem(f + t, 4) * shard, 128), shard)
        into_in = dot_f32(xy[pl.ds(0, tokens), cols], gu[...], TN).astype(bf16)
        into_out = dot_f32(xy[pl.ds(tokens, tokens), cols], hid[...], TN).astype(bf16)
        for e in range(own):
            for m in range(2):
                k = 2 * e + m
                ge[3 * e + m, cols, :] = into_in[:, k * hidden : (k + 1) * hidden]
            ge[3 * e + 2, cols, :] = into_out[:, e * hidden : (e + 1) * hidden]
        return 0

    def down_step(i, _):
        rows = pl.ds(pl.multiple_of(i * tile, tile), tile)
        ra[rows, pl.ds(0, width)] = dot_f32(gu[rows, :], wgu[...], NT).astype(bf16)
        return 0

    def out_step(i, _):
        rows = pl.ds(pl.multiple_of(i * tile, tile), tile)
        xy[rows, :] = dot_f32(hid[rows, :], wd[...], NT).astype(bf16)
        return 0

    chunks, attn_rows = ctx_chunks(ge.shape[0], shard)
    n_expert = len(chunks)
    n_all = n_expert + len(attn_rows)

    def chunk(k):
        if k < n_expert:
            j, r, low, size = chunks[k]
            rows = pl.ds(pl.multiple_of(rel[r] * shard + low, 16), size)
            return ge.at[j, rows], r1.at[j, rows]
        rows = pl.ds(sum(attn_rows[: k - n_expert]), attn_rows[k - n_expert])
        return ra.at[rows], a1.at[rows]

    def add_into(dst, left, right):
        size = math.gcd(dst.shape[0], 64)

        def body(i, _):
            rows = pl.ds(pl.multiple_of(i * size, size), size)
            dst[rows, :] = (left[rows, :].astype(f32) + right[rows, :].astype(f32)).astype(bf16)
            return 0

        lax.fori_loop(0, dst.shape[0] // size, body, 0)

    def first(k):
        own, one = chunk(k)
        return copy_to(own, one, z_out.at[k], z_r1.at[k], partner)

    def across(k):
        own, one = chunk(k)
        return copy_to(own, one, z_across.at[k], z_r2.at[k], opposite)

    def back(k):
        _, one = chunk(k)
        return copy_to(one, one, z_back.at[k], z_r1.at[k], partner)

    def final(k):
        _, one = chunk(k)
        j, r, low, size = chunks[k]
        there = fin_hbm.at[r, j, pl.ds(low, size)]
        if r == 0:
            return pltpu.make_async_copy(one, there, f_out.at[k])
        return copy_to(one, there, f_out.at[k], f_in.at[k], plane[r - 1])

    pending, ready = [], []
    pace = 2
    lag_a, lag_b, lag_c, window = 1, 2, 5, 3

    def z_step(i):
        if i < n_all:

            @pl.when(outer)
            def _():
                if i >= window:
                    first(i - window).wait_send()
                first(i).start()

        if lag_a <= i < n_all + lag_a:
            k = i - lag_a

            @pl.when(inner)
            def _():
                own, one = chunk(k)
                first(k).wait_recv()
                add_into(own, own, one)
                pl.semaphore_signal(credit, inc=1, device_id=opposite, device_id_type=MESH_ID)

        if lag_a <= i < n_all + lag_a:
            k = i - lag_a

            @pl.when(inner)
            def _():
                pl.semaphore_wait(credit, 1)
                across(k).start()

        if lag_b <= i < n_all + lag_b:
            k = i - lag_b

            @pl.when(inner)
            def _():
                own, one = chunk(k)
                across(k).wait_recv()
                add_into(one, own, one)
                back(k).start()

        if lag_c <= i < n_all + lag_c:
            k = i - lag_c

            @pl.when(outer)
            def _():
                back(k).wait_recv()

            if k < n_expert:
                ready.append(k)

        for _ in range(pace):
            if pending:
                pending.pop(0).start()
            elif ready:
                final(ready.pop(0)).start()

    steps = iter(range(n_all + max(lag_b, lag_c)))

    def go_on(count=1):
        for _ in range(count):
            z_step(next(steps))

    wide = pl.ds(0, width)
    lax.fori_loop(0, 1, grad_step, 0)
    go_on()
    lax.fori_loop(2 * (1 - c), 2 * (1 - c) + 2, down_step, 0)
    dn_swap = remote(ra.at[far, wide], dn_in, 0, sibling)
    dn_swap.start()
    lax.fori_loop(2 * c, 2 * c + 2, down_step, 0)
    go_on()

    def both(ref, arrived):
        def body(i, _):
            rows = pl.ds(pl.multiple_of(c * 4 * half + i * half, half), half)
            here = pl.ds(pl.multiple_of(i * half, half), half)
            ref[rows, wide] = (ref[rows, wide].astype(f32) + arrived[here, :].astype(f32)).astype(bf16)
            return 0

        lax.fori_loop(0, 4, body, 0)

    def group(i):
        return rows_of(4 * c + i, half)

    gg_swap.wait_recv()
    gg_sum[...] = table[side, :] + gg_in[...]
    dn_swap.wait_recv()
    both(ra, dn_in)
    dn_out = [
        remote(ra.at[group(rel[i + 1]), wide], dn_got.at[i], 3 + i, plane[i]) for i in range(3)
    ]
    gg_out = [
        remote(gg_sum.at[rows_of(rel[i + 1], half)], gg_got.at[i], 6 + i, plane[i])
        for i in range(3)
    ]
    for copy in dn_out + gg_out:
        copy.start()
    lax.fori_loop(1, 4, grad_step, 0)
    go_on()
    lax.fori_loop(2 * (1 - c), 2 * (1 - c) + 2, out_step, 0)
    mo_swap = remote(xy.at[far], mo_in, 2, sibling)
    mo_swap.start()
    lax.fori_loop(2 * c, 2 * c + 2, out_step, 0)
    in_part, out_part = pl.ds(0, in_cols), pl.ds(0, q_cols)
    load_in = pltpu.make_async_copy(wa_hbm.at[:, ins], wgu.at[:, in_part], local.at[0])
    load_out = pltpu.make_async_copy(wa_hbm.at[:, outs], wd, local.at[1])
    load_out.start()
    load_in.start()
    go_on()
    for copy in dn_out:
        copy.wait_recv()
    for copy in dn_out + [dn_swap]:
        copy.wait_send()
    mo_swap.wait_recv()
    both(xy, mo_in)
    d_two = ra[group(f), wide].astype(f32)
    for i in range(3):
        d_two = d_two + dn_got[i].astype(f32)
    residual = res_ref[...]
    inv = lax.rsqrt(jnp.mean(residual * residual, axis=-1, keepdims=True) + eps)
    scaled = d_two * gain_ref[1:2, :]
    inside = jnp.mean(scaled * residual, axis=-1, keepdims=True)
    d_norm = inv * scaled - residual * (inv * inv * inv * inside)
    gacc[0] = jnp.zeros(gacc.shape[1:], f32)
    gacc[0, 1:2, :] = jnp.sum(d_two * residual * inv, axis=0, keepdims=True)
    d_res = cot_half[...].astype(f32) + d_norm
    dres[...] = d_res
    dattn[my_rows, :] = d_res.astype(bf16)
    da_swap = remote(dattn.at[my_rows], dattn.at[my_rows], 12, sibling)
    da_swap.start()
    mo_out = [remote(xy.at[group(rel[i + 1])], mo_got.at[i], 9 + i, plane[i]) for i in range(3)]
    for copy in mo_out:
        copy.start()
    load_out.wait()
    go_on()
    da_swap.wait_recv()
    dmixed[...] = dot_f32(dattn[...], wd[...]).astype(bf16)
    go_on()

    position = z * count + lax.broadcasted_iota(jnp.int32, (count, HEAD_DIM), 0)
    angle = position.astype(f32) * freq_ref[...]
    cosine = jnp.cos(angle)
    lane = lax.broadcasted_iota(jnp.int32, (count, HEAD_DIM), 1)
    sine = jnp.where(lane < HEAD_DIM // 2, jnp.sin(angle), -jnp.sin(angle))
    keys = kv_ref[:, :, pl.ds(0, HEAD_DIM)].reshape(4 * count, HEAD_DIM)
    vals = kv_ref[:, :, pl.ds(HEAD_DIM, HEAD_DIM)].reshape(4 * count, HEAD_DIM)
    key_cols, val_cols = pl.ds(0, HEAD_DIM), pl.ds(HEAD_DIM, HEAD_DIM)
    dkv[...] = jnp.zeros_like(dkv)
    for g in range(QUERY_PER_GROUP):
        cols = pl.ds(g * HEAD_DIM, HEAD_DIM)
        query = q_ref[:, cols]
        d_mix = dmixed[:, cols]
        probs = block_probs(z, keys, query)
        d_probs = dot_f32(vals, d_mix, NT)
        inside = jnp.sum(probs * d_probs, axis=0, keepdims=True)
        d_scores = (probs * (d_probs - inside)).astype(bf16)
        d_query = dot_f32(d_scores, keys, TN) * scale
        dproj[:, cols] = turn(d_query, cosine, sine).astype(bf16)
        dkv[:, key_cols] += dot_f32(d_scores, query) * scale
        dkv[:, val_cols] += dot_f32(probs.astype(bf16), d_mix)
        if g % 3 == 2:
            go_on()
    dkv_low[...] = dkv[...].reshape(dkv_low.shape).astype(bf16)
    dkv_out = [
        remote(dkv_low.at[s], dkv_got.at[s - 1], 12 + s, at(ctx=lax.rem(z + 4 - s, 4)))
        for s in range(1, 4)
    ]
    for s in range(1, 4):

        @pl.when(z >= s)
        def _(s=s):
            dkv_out[s - 1].start()

    low_rows = pl.ds(4 * shard, shard)

    def weight_grad(left, right, cols):
        def body(i, _):
            rows = pl.ds(pl.multiple_of(i * 256, 256), 256)
            xy[rows, cols] = dot_f32(left[:, rows], right, TN).astype(bf16)
            return 0

        lax.fori_loop(0, width // 256, body, 0)

    def send_grad(cols, into, k):
        third = shard // 3
        copies = []
        for p in range(3):
            for i in range(3):
                rows = pl.ds(pl.multiple_of(rel[i + 1] * shard + p * third, third), third)
                copies.append(
                    remote(
                        xy.at[rows, cols],
                        ra.at[pl.ds(i * shard + p * third, third), into],
                        k + 3 * p + i,
                        plane[i],
                    )
                )
        pending.extend(copies)
        return copies

    for copy in mo_out + gg_out:
        copy.wait_recv()
    moe = xy[group(f), :].astype(f32)
    gates = gg_sum[rows_of(f, half), :]
    for i in range(3):
        moe = moe + mo_got[i].astype(f32)
        gates = gates + gg_got[i]
    layer_ref[my_rows, :] = (res_ref[...] + moe).astype(bf16)
    gate_ref[my_rows, :] = gates
    lo_swap = remote(layer_ref.at[my_rows], layer_ref.at[my_rows], 27, sibling)
    gt_swap = remote(gate_ref.at[my_rows], gate_ref.at[my_rows], 28, sibling)
    lo_swap.start()
    gt_swap.start()
    for copy in mo_out + [mo_swap]:
        copy.wait_send()
    go_on()

    right_half = pl.ds(q_cols, q_cols)
    weight_grad(dattn, mixed_ref[...], right_half)
    ga_copies = send_grad(right_half, outs, 34)
    go_on()
    q_part = pl.ds(0, q_cols)
    weight_grad(xn_ref, dproj[:, q_part], q_part)
    ga_copies += send_grad(q_part, q_part, 43)
    go_on()
    for s in range(1, 4):

        @pl.when(z + s < 4)
        def _(s=s):
            dkv_out[s - 1].wait_recv()
            dkv[0:count, :] += dkv_got[s - 1].astype(f32)

    kv_part = pl.ds(q_cols, 2 * HEAD_DIM)
    dproj[:, pl.ds(q_cols, HEAD_DIM)] = turn(dkv[0:count, key_cols], cosine, sine).astype(bf16)
    dproj[:, pl.ds(q_cols + HEAD_DIM, HEAD_DIM)] = dkv[0:count, val_cols].astype(bf16)
    for s in range(4):
        block = dot_f32(xn_ref[:, pl.ds(s * shard, shard)], dproj[:, kv_part], TN)
        xy[low_rows, pl.ds(s * 2 * HEAD_DIM, 2 * HEAD_DIM)] = block.astype(bf16)
    kv_copies = [
        remote(
            xy.at[low_rows, rows_of(rel[i + 1], 2 * HEAD_DIM)],
            ra.at[pl.ds(i * shard, shard), kv_part],
            16 + i,
            plane[i],
        )
        for i in range(3)
    ]
    pending.extend(kv_copies)
    ga_copies += kv_copies
    go_on()

    load_in.wait()
    for s in range(width // 256):
        rows = pl.ds(s * 256, 256)
        d1[:, rows] = dot_f32(dproj[my_rows, :], wgu[rows, in_part], NT)
        d1_low[:, rows] = dot_f32(
            dproj[rows_of(1 - c, half), :], wgu[rows, in_part], NT
        ).astype(bf16)
    d1_swap = remote(d1_low, d1_in, 25, sibling)
    d1_swap.start()
    go_on()
    d1_swap.wait_recv()
    d_one = d1[...] + d1_in[...].astype(f32)
    tok = tok_half[...].astype(f32)
    inv = lax.rsqrt(jnp.mean(tok * tok, axis=-1, keepdims=True) + eps)
    scaled = d_one * gain_ref[0:1, :]
    inside = jnp.mean(scaled * tok, axis=-1, keepdims=True)
    d_norm = inv * scaled - tok * (inv * inv * inv * inside)
    gacc[0, 0:1, :] = jnp.sum(d_one * tok * inv, axis=0, keepdims=True)
    tokgrad_ref[my_rows, :] = (dres[...] + d_norm).astype(bf16)
    tg_swap = remote(tokgrad_ref.at[my_rows], tokgrad_ref.at[my_rows], 26, sibling)
    tg_swap.start()
    go_on()

    stages = [sibling, at(fx), at(fy), partner, at(ctx=lax.rem(z + 2, 4))]
    gain_copies = [remote(gacc.at[i], gin.at[i], 29 + i, stages[i]) for i in range(5)]
    for i in range(5):
        gain_copies[i].start()
        go_on()
        gain_copies[i].wait_recv()
        total = gacc[i] + gin[i]
        if i < 4:
            gacc[i + 1] = total
        else:
            gains_ref[...] = total

    while (i := next(steps)) < n_expert - 1:
        z_step(i)
    z_step(i)
    for copy in pending:
        copy.start()
    del pending[:]
    for copy in ga_copies:
        copy.wait_recv()

    def attn_sum(i, _):
        size = shard // 8
        here = pl.ds(pl.multiple_of(i * size, size), size)
        rows = pl.ds(pl.multiple_of(f * shard + i * size, size), size)
        low = pl.ds(pl.multiple_of(4 * shard + i * size, size), size)
        for cols, mine in (
            (q_part, xy[rows, q_part]),
            (kv_part, xy[low, rows_of(f, 2 * HEAD_DIM)]),
            (outs, xy[rows, right_half]),
        ):
            total = mine.astype(f32)
            for r in range(3):
                other = pl.ds(pl.multiple_of(r * shard + i * size, size), size)
                total = total + ra[other, cols].astype(f32)
            ra[here, cols] = total.astype(bf16)
        return 0

    lax.fori_loop(0, 8, attn_sum, 0)
    for i in steps:
        z_step(i)
    store = pltpu.make_async_copy(a1, attn_hbm, local.at[0])
    store.start()

    for k in ready:
        final(k).start()

    store.wait()
    for k in range(n_all):

        @pl.when(outer)
        def _(k=k):
            if k >= n_all - window:
                first(k).wait_send()

        @pl.when(inner)
        def _(k=k):
            across(k).wait_send()
            back(k).wait_send()

    for k in range(n_expert):
        if chunks[k][1] == 0:
            final(k).wait()
        else:
            final(k).wait_send()
            final(k).wait_recv()
    for s in range(1, 4):

        @pl.when(z >= s)
        def _(s=s):
            dkv_out[s - 1].wait_send()

    for copy in [tg_swap, lo_swap, gt_swap]:
        copy.wait_recv()
    swaps = [gg_swap, da_swap, d1_swap, tg_swap, lo_swap, gt_swap]
    for copy in swaps + gg_out + ga_copies + gain_copies:
        copy.wait_send()


def rear(res, xn, q, kv, mixed, gains, tok, cot, x, dy, weights, gate_table, wa):
    count, width = tok.shape
    half = count // 2
    tokens = 8 * half
    columns = wa.shape[1]
    shard = width // 4
    own, _, _, hidden = weights.shape
    mats = 3 * own
    q_cols = q.shape[1]
    vmem, hbm = pl.BlockSpec(memory_space=pltpu.VMEM), pl.BlockSpec(memory_space=pl.ANY)
    bf16, f32 = jnp.bfloat16, jnp.float32
    shape = jax.ShapeDtypeStruct
    dma = pltpu.SemaphoreType.DMA
    chunks, attn_rows = ctx_chunks(mats, shard)
    n_expert, n_all = len(chunks), len(chunks) + len(attn_rows)
    return pl.pallas_call(
        rear_kernel,
        in_specs=[vmem] * 7 + [hbm] * 5 + [vmem, hbm],
        out_specs=[vmem] * 4 + [hbm] * 2,
        out_shape=[
            shape((count, width), bf16),
            shape((count, width), bf16),
            shape((8, width), f32),
            shape((count, 128), f32),
            shape((shard, columns), bf16),
            shape((4, mats, shard, hidden), bf16),
        ],
        scratch_shapes=[
            pltpu.VMEM((2 * tokens, width), bf16),
            pltpu.VMEM((width, 2 * own * hidden), bf16),
            pltpu.VMEM((width, own * hidden), bf16),
            pltpu.VMEM((tokens, width), bf16),
            pltpu.VMEM((tokens, own * hidden), bf16),
            pltpu.VMEM((tokens, 128), f32),
            pltpu.VMEM((mats, width, hidden), bf16),
            pltpu.VMEM((mats, width, hidden), bf16),
            pltpu.VMEM((4 * half, width), bf16),
            pltpu.VMEM((3, half, width), bf16),
            pltpu.VMEM((4 * half, width), bf16),
            pltpu.VMEM((3, half, width), bf16),
            pltpu.VMEM((4 * half, 128), f32),
            pltpu.VMEM((4 * half, 128), f32),
            pltpu.VMEM((3, half, 128), f32),
            pltpu.VMEM((half, width), f32),
            pltpu.VMEM((count, width), bf16),
            pltpu.VMEM((count, q_cols), bf16),
            pltpu.VMEM((count, q_cols + 2 * HEAD_DIM), bf16),
            pltpu.VMEM((4 * count, 2 * HEAD_DIM), f32),
            pltpu.VMEM((4, count, 2 * HEAD_DIM), bf16),
            pltpu.VMEM((3, count, 2 * HEAD_DIM), bf16),
            pltpu.VMEM((half, width), f32),
            pltpu.VMEM((half, width), bf16),
            pltpu.VMEM((half, width), bf16),
            pltpu.VMEM((3 * shard, columns), bf16),
            pltpu.VMEM((shard, columns), bf16),
            pltpu.VMEM((5, 8, width), f32),
            pltpu.VMEM((5, 8, width), f32),
            pltpu.VMEM((half, width), bf16),
            pltpu.VMEM((half, width), bf16),
            dma((52,)),
            dma((52,)),
            dma((10,)),
            dma((n_all,)),
            dma((n_all,)),
            dma((n_all,)),
            dma((n_all,)),
            dma((n_all,)),
            dma((n_expert,)),
            dma((n_expert,)),
            pltpu.SemaphoreType.REGULAR,
        ],
        compiler_params=pltpu.CompilerParams(
            collective_id=1, has_side_effects=True, vmem_limit_bytes=63 * MIB
        ),
        name="rear",
    )(
        res,
        xn,
        q,
        kv,
        mixed,
        gains,
        frequencies(),
        tok,
        cot,
        x,
        dy,
        weights,
        gate_table,
        wa,
    )


def body_fast(
    tokens,
    attn_norm,
    attention_params,
    ffn_norm,
    expert_weights,
    gate_values,
    routes,
    slot_order,
    cotangent,
):
    sequence_count, block_len, model_width = tokens.shape
    count = sequence_count * block_len
    half = count // 2
    f = lax.axis_index("fsdp")
    shard, hidden = attention_params.shape[0], expert_weights.shape[3]
    tok = tokens.reshape(count, model_width)
    cot = cotangent.reshape(count, model_width)
    norm_gains = jnp.stack([attn_norm, ffn_norm])
    route_rows = routes.reshape(count, TOP)
    normed, queries, kv, mixed, residual, gate_table, whole_attn, whole_expert, x, dy = front(
        tok,
        norm_gains,
        route_rows.T,
        gate_values.reshape(count, TOP).T,
        slot_order.reshape(1, count),
        attention_params[:, 0, :],
        jnp.transpose(expert_weights, (0, 2, 1, 3)),
        cot,
    )
    layer_out, tokens_grad, gains, gate_rows, attn_grad, finals = rear(
        residual,
        normed,
        queries,
        kv,
        mixed,
        norm_gains,
        tok,
        cot,
        x.reshape(8 * half, model_width),
        dy.reshape(8 * half, model_width),
        whole_expert,
        gate_table,
        whole_attn,
    )
    picked = route_rows[:, :, None] == jnp.arange(EXPERTS, dtype=jnp.int32)
    gate_grad = jnp.sum(jnp.where(picked, gate_rows[:, None, :EXPERTS], 0.0), axis=-1)
    finals = finals.reshape(EXPERTS, 3, shard, hidden)
    expert_grad, attn_lines = join_experts(finals, attn_grad, expert_order(f).T)
    expert_grad = jnp.transpose(expert_grad, (0, 2, 1, 3))
    return (
        layer_out.reshape(sequence_count, block_len, model_width),
        tokens_grad.reshape(sequence_count, block_len, model_width),
        attn_lines.reshape(shard, 1, attention_params.shape[2]),
        expert_grad,
        gains[0],
        gains[1],
        gate_grad.reshape(sequence_count, block_len, TOP),
    )


def solution(mesh):
    in_specs = (
        P("fsdp", "ctx", None),
        P(),
        P("fsdp", "tp", None),
        P(),
        P("fsdp", None, None, "tp"),
        P("fsdp", "ctx", None),
        P("fsdp", "ctx", None),
        P("fsdp", "ctx"),
        P("fsdp", "ctx", None),
    )
    out_specs = (
        P("fsdp", "ctx", None),
        P("fsdp", "ctx", None),
        P("fsdp", "tp", None),
        P("fsdp", None, None, "tp"),
        P(),
        P(),
        P("fsdp", "ctx", None),
    )
    four = mesh.shape["fsdp"] == 4 and mesh.shape["ctx"] == 4 and mesh.shape["tp"] == 2
    body_fn = body_fast if four else body
    return jax.shard_map(body_fn, mesh=mesh, in_specs=in_specs, out_specs=out_specs, check_vma=False)
```

```python
import jax
import jax.numpy as jnp
from jax import lax
import math
import numpy as np
from jax.experimental import pallas as pl
from jax.experimental.pallas import tpu as pltpu
from jax.sharding import PartitionSpec as P

HEAD_DIM = 128
TOP = 4
EXPERTS = 8
QUERY_PER_GROUP = 6
CAP = 160


eps = 1e-06
theta_base = 1000000.0


def angle_tables(positions):
    frequency = theta_base ** (-(jnp.arange(HEAD_DIM // 2, dtype=jnp.float32) * 2.0) / HEAD_DIM)
    angles = positions.astype(jnp.float32)[:, None] * frequency[None, :]
    return (jnp.cos(angles), jnp.sin(angles))


def rotate(source, cosine_table, sine_table):
    half_size = source.shape[-1] // 2
    front_half = source[..., :half_size]
    back_half = source[..., half_size:]
    return jnp.concatenate(
        [
            front_half * cosine_table - back_half * sine_table,
            back_half * cosine_table + front_half * sine_table,
        ],
        axis=-1,
    )


def norm_back(source, inv_rms, gain_vec, upstream):
    scaled = upstream * gain_vec
    inner_sum = jnp.mean(scaled * source, axis=-1, keepdims=True)
    d_source = inv_rms * scaled - source * inv_rms * inv_rms * inv_rms * inner_sum
    return (d_source, jnp.sum(upstream * source * inv_rms, axis=0))


def slot_tables(route_rows, rank_rows):
    tok_count = route_rows.shape[0]
    inverse = (
        jnp.zeros((tok_count,), jnp.int32).at[rank_rows].set(jnp.arange(tok_count, dtype=jnp.int32))
    )
    ranked = route_rows[inverse].reshape(-1)
    onehot = (ranked[:, None] == jnp.arange(EXPERTS, dtype=jnp.int32)[None, :]).astype(jnp.int32)
    before = jnp.cumsum(onehot, axis=0) - onehot
    slot_ranked = jnp.sum(before * onehot, axis=1).reshape(tok_count, TOP)
    slots = slot_ranked[rank_rows]
    kept_pair = slots < CAP
    pair_slot = jnp.where(kept_pair, route_rows * CAP + slots, EXPERTS * CAP)
    owners = jnp.broadcast_to(jnp.arange(tok_count, dtype=jnp.int32)[:, None], (tok_count, TOP))
    slot_token = (
        jnp.full((EXPERTS * CAP,), tok_count, jnp.int32)
        .at[pair_slot.reshape(-1)]
        .set(owners.reshape(-1), mode="drop")
    )
    return (kept_pair, pair_slot, slot_token)


def attend_forward(queries, key_rows, value_rows, allowed):
    scores = jnp.einsum(
        "qhgd,khd->hgqk", queries, key_rows, preferred_element_type=jnp.float32
    ) * HEAD_DIM ** (-0.5)
    scores = jnp.where(allowed, scores, -1e30)
    row_max = jnp.max(scores, axis=-1, keepdims=True)
    expd = jnp.exp(scores - row_max)
    row_total = jnp.sum(expd, axis=-1, keepdims=True)
    attn_probs = (expd / row_total).astype(jnp.bfloat16)
    mixed_heads = jnp.einsum(
        "hgqk,khd->qhgd", attn_probs, value_rows, preferred_element_type=jnp.float32
    )
    return (mixed_heads.astype(jnp.bfloat16), row_max + jnp.log(row_total))


def attend_backward(queries, key_rows, value_rows, allowed, log_total, d_mixed):
    scores = jnp.einsum(
        "qhgd,khd->hgqk", queries, key_rows, preferred_element_type=jnp.float32
    ) * HEAD_DIM ** (-0.5)
    scores = jnp.where(allowed, scores, -1e30)
    attn_probs = jnp.exp(scores - log_total)
    low_probs = attn_probs.astype(jnp.bfloat16)
    d_probs = jnp.einsum("qhgd,khd->hgqk", d_mixed, value_rows, preferred_element_type=jnp.float32)
    inner_sum = jnp.sum(attn_probs * d_probs, axis=-1, keepdims=True)
    d_scores = (attn_probs * (d_probs - inner_sum)).astype(jnp.bfloat16)
    d_queries = jnp.einsum(
        "hgqk,khd->qhgd", d_scores, key_rows, preferred_element_type=jnp.float32
    ) * HEAD_DIM ** (-0.5)
    d_keys = jnp.einsum(
        "hgqk,qhgd->khd", d_scores, queries, preferred_element_type=jnp.float32
    ) * HEAD_DIM ** (-0.5)
    d_values = jnp.einsum("hgqk,qhgd->khd", low_probs, d_mixed, preferred_element_type=jnp.float32)
    return (d_queries, d_keys, d_values)


def body(
    tokens,
    attn_norm,
    attention_params,
    ffn_norm,
    expert_weights,
    gate_values,
    routes,
    slot_order,
    cotangent,
):
    sequence_count, block_len, model_width = tokens.shape
    tok_count = sequence_count * block_len
    kv_loc = attention_params.shape[1]
    input_columns = (QUERY_PER_GROUP + 2) * HEAD_DIM
    ctx_size = lax.axis_size("ctx")
    ctx_place = lax.axis_index("ctx")
    sequence_length = block_len * ctx_size
    whole_attn, whole_expert = (
        lax.all_gather(attention_params, "fsdp", axis=0, tiled=True),
        lax.all_gather(expert_weights, "fsdp", axis=0, tiled=True),
    )
    positions = ctx_place * block_len + jnp.arange(block_len, dtype=jnp.int32)
    cosine_table, sine_table = angle_tables(positions)
    cosine_table = jnp.tile(cosine_table, (sequence_count, 1))
    sine_table = jnp.tile(sine_table, (sequence_count, 1))
    cos_four = cosine_table[:, None, None, :]
    sin_four = sine_table[:, None, None, :]
    cos_three = cosine_table[:, None, :]
    sin_three = sine_table[:, None, :]
    allowed = (jnp.arange(sequence_length, dtype=jnp.int32) // block_len <= ctx_place)[
        None, None, None, :
    ]
    tok_float = tokens.reshape(tok_count, model_width).astype(jnp.float32)
    inv_one = lax.rsqrt(jnp.mean(tok_float * tok_float, axis=-1, keepdims=True) + eps)
    first_normed = (tok_float * inv_one * attn_norm).astype(jnp.bfloat16)
    projected_rows = jnp.einsum(
        "td,dhc->thc",
        first_normed,
        whole_attn[:, :, :input_columns],
        preferred_element_type=jnp.float32,
    ).reshape(tok_count, kv_loc, QUERY_PER_GROUP + 2, HEAD_DIM)
    queries = rotate(projected_rows[:, :, :QUERY_PER_GROUP], cos_four, sin_four).astype(
        jnp.bfloat16
    )
    key_rows = rotate(projected_rows[:, :, QUERY_PER_GROUP], cos_three, sin_three).astype(
        jnp.bfloat16
    )
    value_rows = projected_rows[:, :, QUERY_PER_GROUP + 1].astype(jnp.bfloat16)
    key_all, value_all = (
        lax.all_gather(
            key_rows.reshape(sequence_count, block_len, kv_loc, HEAD_DIM), "ctx", axis=1, tiled=True
        ),
        lax.all_gather(
            value_rows.reshape(sequence_count, block_len, kv_loc, HEAD_DIM),
            "ctx",
            axis=1,
            tiled=True,
        ),
    )
    query_seq = queries.reshape(sequence_count, block_len, kv_loc, QUERY_PER_GROUP, HEAD_DIM)
    mixed_heads, log_total = lax.map(
        lambda item_args: attend_forward(item_args[0], item_args[1], item_args[2], allowed),
        (query_seq, key_all, value_all),
    )
    mixed_flat = mixed_heads.reshape(tok_count, kv_loc, QUERY_PER_GROUP * HEAD_DIM)
    attn_part = jnp.einsum(
        "thc,dhc->td",
        mixed_flat,
        whole_attn[:, :, input_columns:],
        preferred_element_type=jnp.float32,
    )
    attn_sum = lax.psum(attn_part, "tp")
    residual = tok_float + attn_sum
    inv_two = lax.rsqrt(jnp.mean(residual * residual, axis=-1, keepdims=True) + eps)
    normed_two = (residual * inv_two * ffn_norm).astype(jnp.bfloat16)
    kept_pair, pair_slot, slot_token = slot_tables(
        routes.reshape(tok_count, TOP), slot_order.reshape(tok_count)
    )
    kept_float = kept_pair.astype(jnp.float32)
    gate_kept = gate_values.reshape(tok_count, TOP) * kept_float
    slot_gate = (
        jnp.zeros((EXPERTS * CAP,), jnp.float32)
        .at[pair_slot.reshape(-1)]
        .set(gate_kept.reshape(-1), mode="drop")
    )
    padded = jnp.concatenate([normed_two, jnp.zeros((1, model_width), jnp.bfloat16)], axis=0)
    inputs = padded[slot_token].reshape(EXPERTS, CAP, model_width)
    gate_act = jnp.einsum(
        "ecd,deh->ech", inputs, whole_expert[:, :, 0], preferred_element_type=jnp.float32
    )
    up_act = jnp.einsum(
        "ecd,deh->ech", inputs, whole_expert[:, :, 1], preferred_element_type=jnp.float32
    )
    gate_sigmoid = jax.nn.sigmoid(gate_act)
    active = gate_act * gate_sigmoid
    hidden = (active * up_act).astype(jnp.bfloat16)
    expert_out = jnp.einsum(
        "ech,deh->ecd", hidden, whole_expert[:, :, 2], preferred_element_type=jnp.float32
    )
    out_pad = jnp.concatenate(
        [expert_out.reshape(EXPERTS * CAP, model_width), jnp.zeros((1, model_width), jnp.float32)],
        axis=0,
    )
    picked = out_pad[pair_slot]
    moe_part = jnp.sum(picked * gate_kept[:, :, None], axis=1)
    moe = lax.psum(moe_part.astype(jnp.bfloat16), "tp").astype(jnp.float32)
    layer_out = (
        (residual + moe).astype(jnp.bfloat16).reshape(sequence_count, block_len, model_width)
    )
    grad_out = cotangent.reshape(tok_count, model_width).astype(jnp.float32)
    gate_part = jnp.sum(picked * grad_out[:, None, :], axis=-1) * kept_float
    grad_pad = jnp.concatenate([grad_out, jnp.zeros((1, model_width), jnp.float32)], axis=0)
    d_expert = (
        (grad_pad[slot_token] * slot_gate[:, None])
        .astype(jnp.bfloat16)
        .reshape(EXPERTS, CAP, model_width)
    )
    d_hidden = jnp.einsum(
        "ecd,deh->ech", d_expert, whole_expert[:, :, 2], preferred_element_type=jnp.float32
    )
    silu_slope = gate_sigmoid * (1.0 + gate_act * (1.0 - gate_sigmoid))
    d_gate_act = (d_hidden * up_act * silu_slope).astype(jnp.bfloat16)
    d_up_act = (d_hidden * active).astype(jnp.bfloat16)
    d_inputs = jnp.einsum(
        "ech,deh->ecd", d_gate_act, whole_expert[:, :, 0], preferred_element_type=jnp.float32
    )
    d_inputs = d_inputs + jnp.einsum(
        "ech,deh->ecd", d_up_act, whole_expert[:, :, 1], preferred_element_type=jnp.float32
    )
    d_in_pad = jnp.concatenate(
        [d_inputs.reshape(EXPERTS * CAP, model_width), jnp.zeros((1, model_width), jnp.float32)],
        axis=0,
    )
    d_normed_part = jnp.sum(d_in_pad[pair_slot], axis=1)
    d_normed_two, gate_grad = lax.psum((d_normed_part, gate_part), "tp")
    d_resid_norm, gain_two = norm_back(residual, inv_two, ffn_norm, d_normed_two)
    d_residual = grad_out + d_resid_norm
    d_attn = d_residual.astype(jnp.bfloat16)
    d_mixed = jnp.einsum(
        "td,dhc->thc", d_attn, whole_attn[:, :, input_columns:], preferred_element_type=jnp.float32
    ).astype(jnp.bfloat16)
    d_mixed_seq = d_mixed.reshape(sequence_count, block_len, kv_loc, QUERY_PER_GROUP, HEAD_DIM)
    d_queries, d_key_all, d_value_all = lax.map(
        lambda item_args: attend_backward(
            item_args[0], item_args[1], item_args[2], allowed, item_args[3], item_args[4]
        ),
        (query_seq, key_all, value_all, log_total, d_mixed_seq),
    )
    d_keys, d_values = (
        lax.psum_scatter(
            d_key_all.astype(jnp.bfloat16), "ctx", scatter_dimension=1, tiled=True
        ).astype(jnp.float32),
        lax.psum_scatter(
            d_value_all.astype(jnp.bfloat16), "ctx", scatter_dimension=1, tiled=True
        ).astype(jnp.float32),
    )
    d_queries = rotate(
        d_queries.reshape(tok_count, kv_loc, QUERY_PER_GROUP, HEAD_DIM), cos_four, -sin_four
    )
    d_keys = rotate(d_keys.reshape(tok_count, kv_loc, HEAD_DIM), cos_three, -sin_three)
    d_values = d_values.reshape(tok_count, kv_loc, HEAD_DIM)
    d_projected = jnp.concatenate([d_queries, d_keys[:, :, None], d_values[:, :, None]], axis=2)
    d_projected = d_projected.astype(jnp.bfloat16).reshape(tok_count, kv_loc, input_columns)
    d_normed_local = jnp.einsum(
        "thc,dhc->td",
        d_projected,
        whole_attn[:, :, :input_columns],
        preferred_element_type=jnp.float32,
    )
    d_normed_one = lax.psum(d_normed_local.astype(jnp.bfloat16), "tp").astype(jnp.float32)
    d_tok_norm, gain_one = norm_back(tok_float, inv_one, attn_norm, d_normed_one)
    tokens_grad = (
        (d_residual + d_tok_norm)
        .astype(jnp.bfloat16)
        .reshape(sequence_count, block_len, model_width)
    )
    gain_one, gain_two = lax.psum((gain_one, gain_two), ("fsdp", "ctx"))
    in_term = jnp.einsum(
        "td,thc->dhc", first_normed, d_projected, preferred_element_type=jnp.float32
    )
    out_term = jnp.einsum("td,thc->dhc", d_attn, mixed_flat, preferred_element_type=jnp.float32)
    attn_grad = lax.psum_scatter(
        jnp.concatenate([in_term, out_term], axis=2),
        ("fsdp", "ctx"),
        scatter_dimension=0,
        tiled=True,
    )
    gate_term = jnp.einsum("ecd,ech->deh", inputs, d_gate_act, preferred_element_type=jnp.float32)
    up_term = jnp.einsum("ecd,ech->deh", inputs, d_up_act, preferred_element_type=jnp.float32)
    down_term = jnp.einsum("ecd,ech->deh", d_expert, hidden, preferred_element_type=jnp.float32)
    expert_grad = lax.psum_scatter(
        jnp.stack([gate_term, up_term, down_term], axis=2),
        ("fsdp", "ctx"),
        scatter_dimension=0,
        tiled=True,
    )
    attn_grad, expert_grad = (
        lax.all_gather(attn_grad.astype(jnp.bfloat16), "ctx", axis=0, tiled=True).astype(
            attn_grad.dtype
        ),
        lax.all_gather(expert_grad.astype(jnp.bfloat16), "ctx", axis=0, tiled=True).astype(
            expert_grad.dtype
        ),
    )
    return (
        layer_out,
        tokens_grad,
        attn_grad,
        expert_grad,
        gain_one,
        gain_two,
        gate_grad.reshape(sequence_count, block_len, TOP),
    )


MESH_ID = pl.DeviceIdType.MESH
MIB = 2**20


def expert_order(place):
    row = jnp.arange(128, dtype=jnp.int32)
    expert = (((row // 32) ^ place) * 2) + (row // 16) % 2
    source = (row % 16) * 8 + expert
    return (source[:, None] == row[None, :]).astype(jnp.bfloat16)


def join_kernel(order_ref, in_ref, attn_in_ref, out_ref, attn_out_ref):
    width = in_ref.shape[3]
    for m in range(3):
        for k in range(in_ref.shape[2] // 16):
            block = in_ref[:, m, pl.ds(k * 16, 16), :].reshape(128, width)
            moved = jnp.dot(order_ref[...], block, preferred_element_type=jnp.float32)
            out_ref[pl.ds(k * 16, 16), m] = moved.reshape(16, 8, width)
    rows, columns = attn_in_ref.shape
    parts = columns // 128
    for j in range(parts):
        part = attn_in_ref[:, pl.ds(j * 128, 128)].astype(jnp.float32)
        attn_out_ref[pl.ds(j, rows, stride=parts), :] = part


def join_experts(grads, attn_grad, order):
    experts, _, rows, width = grads.shape
    columns = attn_grad.shape[1]
    step = 128
    lines = step * columns // 128
    return pl.pallas_call(
        join_kernel,
        grid=(rows // step,),
        in_specs=[
            pl.BlockSpec((128, 128), lambda i: (0, 0)),
            pl.BlockSpec((experts, 3, step, width), lambda i: (0, 0, i, 0)),
            pl.BlockSpec((step, columns), lambda i: (i, 0)),
        ],
        out_specs=[
            pl.BlockSpec((step, 3, experts, width), lambda i: (i, 0, 0, 0)),
            pl.BlockSpec((lines, 128), lambda i: (i, 0)),
        ],
        out_shape=[
            jax.ShapeDtypeStruct((rows, 3, experts, width), jnp.float32),
            jax.ShapeDtypeStruct((rows * columns // 128, 128), jnp.float32),
        ],
        compiler_params=pltpu.CompilerParams(vmem_limit_bytes=60 * MIB),
        name="join_experts",
    )(order, grads, attn_grad)


NT = (((1,), (1,)), ((), ()))
TN = (((0,), (0,)), ((), ()))


def dot_f32(a, b, dims=(((1,), (0,)), ((), ()))):
    return lax.dot_general(a, b, dims, preferred_element_type=jnp.float32)


def block_probs(last, keys, query):
    scores = dot_f32(keys, query, NT) * HEAD_DIM ** (-0.5)
    block = lax.broadcasted_iota(jnp.int32, scores.shape, 0) // query.shape[0]
    scores = jnp.where(block <= last, scores, -1e30)
    expd = jnp.exp(scores - jnp.max(scores, axis=0, keepdims=True))
    return expd * (1.0 / jnp.sum(expd, axis=0, keepdims=True))


def place():
    return lax.axis_index("fsdp"), lax.axis_index("ctx"), lax.axis_index("tp")


def plane_peers(f):
    return f + 1 - 2 * lax.rem(f, 2), lax.rem(f + 2, 4), 3 - f


def rows_of(index, size):
    return pl.ds(pl.multiple_of(index * size, size), size)


def greet(devices):
    barrier = pltpu.get_barrier_semaphore()
    for device in devices:
        pl.semaphore_signal(barrier, inc=1, device_id=device, device_id_type=MESH_ID)
    pl.semaphore_wait(barrier, len(devices))


def turn(value, cosine, sine):
    return value * cosine + pltpu.roll(value, HEAD_DIM // 2, 1) * sine


def frequencies():
    i = np.arange(HEAD_DIM // 2, dtype=np.float32)
    freq = (theta_base ** (-(i * 2.0) / HEAD_DIM)).astype(np.float32)
    return jnp.asarray(np.concatenate([freq, freq])[None, :])


def front_kernel(
    tok_ref,
    gain_ref,
    freq_ref,
    routes_ref,
    gates_ref,
    order_ref,
    attn_hbm,
    experts_hbm,
    cot_hbm,
    xn_ref,
    q_ref,
    kv_ref,
    mixed_ref,
    res_ref,
    wl_ref,
    wa_hbm,
    w_hbm,
    x_hbm,
    dy_hbm,
    raw,
    pieces,
    wa,
    part,
    part_in,
    low_half,
    send,
    recv,
    local,
):
    f, z, c = place()
    fx, fy, fd = plane_peers(f)
    count, width = tok_ref.shape
    half = count // 2
    shard = attn_hbm.shape[0]
    cut = shard // 2
    in_cols = (QUERY_PER_GROUP + 2) * HEAD_DIM
    ins = pl.ds(0, in_cols)
    outs = pl.ds(in_cols, attn_hbm.shape[1] - in_cols)

    def at(fsdp=f, ctx=z, tp=c):
        return {"fsdp": fsdp, "ctx": ctx, "tp": tp}

    def remote(src, dst, k, device):
        return pltpu.make_async_remote_copy(
            src_ref=src,
            dst_ref=dst,
            send_sem=send.at[k],
            recv_sem=recv.at[k],
            device_id=device,
            device_id_type=MESH_ID,
        )

    plane = [at(fx), at(fy), at(fd)]
    rel = [fx, fy, fd]
    line = [at(ctx=lax.rem(z + s, 4)) for s in range(1, 4)]
    sibling = at(tp=1 - c)
    mine = rows_of(f, shard)
    load = pltpu.make_async_copy(experts_hbm, raw, local.at[6])
    load.start()
    greet(plane + line + [sibling])

    owned = pltpu.make_async_copy(attn_hbm, wa.at[mine], local.at[0])
    owned.start()
    in_x = remote(attn_hbm.at[:, ins], wa.at[mine, ins], 0, at(fx))
    in_y = remote(attn_hbm.at[:, ins], wa.at[mine, ins], 1, at(fy))
    in_x.start()
    in_y.start()

    rank = jnp.broadcast_to(order_ref[...].astype(jnp.float32), (count, count))
    ahead = jnp.where(rank.T < rank, 1.0, 0.0).astype(jnp.bfloat16)
    expert = lax.broadcasted_iota(jnp.int32, (128, count), 0)
    member = jnp.zeros((128, count), jnp.float32)
    gate = jnp.zeros((128, count), jnp.float32)
    for j in range(TOP):
        hit = jnp.broadcast_to(routes_ref[j : j + 1, :], (128, count)) == expert
        member = jnp.where(hit, 1.0, member)
        gate = jnp.where(hit, jnp.broadcast_to(gates_ref[j : j + 1, :], (128, count)), gate)
    slots = dot_f32(member.astype(jnp.bfloat16), ahead)
    gate = jnp.where(slots < CAP - 0.5, gate, 0.0)
    wl_ref[f] = gate[:EXPERTS]
    gate_copies = [remote(wl_ref.at[f], wl_ref.at[f], 2 + i, plane[i]) for i in range(3)]
    for copy in gate_copies:
        copy.start()

    own_dy = [
        pltpu.make_async_copy(
            cot_hbm.at[pl.ds(i * half, half)], dy_hbm.at[i, f], local.at[2 + i]
        )
        for i in range(2)
    ]
    for copy in own_dy:
        copy.start()

    row = lax.broadcasted_iota(jnp.int32, (128, 128), 0)
    column = lax.broadcasted_iota(jnp.int32, (128, 128), 1)
    owner = jnp.where(row < 64, jnp.where(row < 32, f, fx), jnp.where(row < 96, fy, fd))
    source = (row % 16) * 8 + owner * 2 + (row // 16) % 2
    order = jnp.where(source == column, 1.0, 0.0).astype(jnp.bfloat16)

    def split(m):
        def body(k, _):
            rows = pl.ds(pl.multiple_of(k * 16, 16), 16)
            block = raw[rows, m].reshape(128, raw.shape[3])
            moved = dot_f32(order, block).astype(jnp.bfloat16)
            pieces[:, m, rows, :] = moved.reshape(8, 16, raw.shape[3])
            return 0

        lax.fori_loop(0, shard // 16, body, 0)

    cut_rows = shard // 4
    from_rows = rows_of(z, cut_rows)
    to_rows = rows_of(4 * f + z, cut_rows)

    def quarter(m, i):
        return remote(
            pieces.at[pl.ds(2 * (i + 1), 2), m, from_rows],
            w_hbm.at[:, m, to_rows, :],
            37 + 3 * m + i,
            plane[i],
        )

    def hand_on(m, i):
        quarters[3 * m + i].wait_recv()
        here = w_hbm.at[:, m, rows_of(4 * rel[i] + z, cut_rows), :]
        copies = [remote(here, here, 43 + 9 * m + 3 * i + s, line[s]) for s in range(3)]
        for copy in copies:
            copy.start()
        return copies

    load.wait()
    split(0)
    quarters = [quarter(0, i) for i in range(3)]
    for copy in quarters:
        copy.start()

    tok = tok_ref[...].astype(jnp.float32)
    inv = lax.rsqrt(jnp.mean(tok * tok, axis=-1, keepdims=True) + eps)
    xn_ref[...] = (tok * inv * gain_ref[0:1, :]).astype(jnp.bfloat16)
    position = z * count + lax.broadcasted_iota(jnp.int32, (count, HEAD_DIM), 0)
    angle = position.astype(jnp.float32) * freq_ref[...]
    cosine = jnp.cos(angle)
    lane = lax.broadcasted_iota(jnp.int32, (count, HEAD_DIM), 1)
    sine = jnp.where(lane < HEAD_DIM // 2, -jnp.sin(angle), jnp.sin(angle))

    top, low = rows_of(2 * fx, cut), rows_of(2 * fy + 1, cut)
    in_x.wait_recv()
    in_xy = remote(wa.at[top, ins], wa.at[top, ins], 5, at(fy))
    in_xy.start()
    in_y.wait_recv()
    in_yx = remote(wa.at[low, ins], wa.at[low, ins], 6, at(fx))
    in_yx.start()
    out_x = remote(attn_hbm.at[:, outs], wa.at[mine, outs], 7, at(fx))
    out_y = remote(attn_hbm.at[:, outs], wa.at[mine, outs], 8, at(fy))
    split(1)
    quarters += [quarter(1, i) for i in range(3)]
    for copy in quarters[3:]:
        copy.start()
    out_x.start()
    out_y.start()
    handed = hand_on(0, 0) + hand_on(0, 1)
    dy_copies = [
        remote(cot_hbm.at[rows_of(c, half)], dy_hbm.at[c, f], 23 + i, plane[i]) for i in range(2)
    ]
    for copy in dy_copies:
        copy.start()
    split(2)
    own_w = pltpu.make_async_copy(pieces.at[pl.ds(0, 2)], w_hbm.at[:, :, mine, :], local.at[1])
    own_w.start()
    owned.wait()
    in_xy.wait_recv()
    in_yx.wait_recv()

    normed = xn_ref[...]
    for h in range(QUERY_PER_GROUP + 2):
        cols = pl.ds(h * HEAD_DIM, HEAD_DIM)
        if h % 2 == 0:
            pair = dot_f32(normed, wa[:, pl.ds(h * HEAD_DIM, 2 * HEAD_DIM)])
        value = pair[:, (h % 2) * HEAD_DIM : (h % 2 + 1) * HEAD_DIM]
        if h <= QUERY_PER_GROUP:
            value = turn(value, cosine, sine)
        if h < QUERY_PER_GROUP:
            q_ref[:, cols] = value.astype(jnp.bfloat16)
        else:
            kv_ref[0, :, pl.ds((h - QUERY_PER_GROUP) * HEAD_DIM, HEAD_DIM)] = value.astype(
                jnp.bfloat16
            )
    kv_copies = [remote(kv_ref.at[0], kv_ref.at[s], 8 + s, line[s - 1]) for s in range(1, 4)]
    for s in range(1, 4):

        @pl.when(z + s < 4)
        def _(s=s):
            kv_copies[s - 1].start()

        @pl.when(z < s)
        def _(s=s):
            kv_ref[s] = jnp.zeros(kv_ref.shape[1:], jnp.bfloat16)

    handed += hand_on(0, 2)
    out_x.wait_recv()
    out_xy = remote(wa.at[top, outs], wa.at[top, outs], 12, at(fy))
    out_xy.start()
    out_y.wait_recv()
    out_yx = remote(wa.at[low, outs], wa.at[low, outs], 13, at(fx))
    out_yx.start()

    w_copies = [
        remote(pieces.at[pl.ds(2 * (i + 1), 2), 2], w_hbm.at[:, 2, mine, :], 14 + i, plane[i])
        for i in range(3)
    ]
    for copy in w_copies:
        copy.start()
    for i in range(3):
        handed += hand_on(1, i)

    for s in range(1, 4):

        @pl.when(z >= s)
        def _(s=s):
            kv_copies[s - 1].wait_recv()

    keys = kv_ref[:, :, pl.ds(0, HEAD_DIM)].reshape(4 * count, HEAD_DIM)
    vals = kv_ref[:, :, pl.ds(HEAD_DIM, HEAD_DIM)].reshape(4 * count, HEAD_DIM)
    for g in range(QUERY_PER_GROUP):
        cols = pl.ds(g * HEAD_DIM, HEAD_DIM)
        probs = block_probs(z, keys, q_ref[:, cols]).astype(jnp.bfloat16)
        mixed_ref[:, cols] = dot_f32(probs, vals, TN).astype(jnp.bfloat16)

    upper, lower = pl.ds(0, half // 2), pl.ds(half // 2, half // 2)

    def pass_on(copies, ref, k):
        copies[0].wait_recv()
        up = ref.at[c, fx, upper]
        passed = [remote(up, up, k, at(fy))]
        passed[0].start()
        copies[1].wait_recv()
        low = ref.at[c, fy, lower]
        passed.append(remote(low, low, k + 1, at(fx)))
        passed[1].start()
        return passed

    out_xy.wait_recv()
    out_yx.wait_recv()
    store_wa = pltpu.make_async_copy(wa, wa_hbm, local.at[4])
    store_wa.start()
    for s in range(width // 256):
        cols = pl.ds(s * 256, 256)
        part[:, cols] = dot_f32(mixed_ref[...], wa[cols, outs], NT)
    swap = remote(part.at[rows_of(1 - c, half)], part_in, 26, sibling)
    swap.start()
    swap.wait_recv()
    my_rows = rows_of(c, half)
    residual = tok_ref[my_rows, :].astype(jnp.float32) + (part[my_rows, :] + part_in[...])
    res_ref[...] = residual
    inv = lax.rsqrt(jnp.mean(residual * residual, axis=-1, keepdims=True) + eps)
    low_half[...] = (residual * inv * gain_ref[1:2, :]).astype(jnp.bfloat16)
    own_x = pltpu.make_async_copy(low_half, x_hbm.at[c, f], local.at[5])
    own_x.start()
    x_copies = [remote(low_half, x_hbm.at[c, f], 27 + i, plane[i]) for i in range(2)]
    for copy in x_copies:
        copy.start()
    sib_x = [remote(low_half, x_hbm.at[c, f], 30, sibling)]
    sib_x[0].start()

    dy_passed = pass_on(dy_copies, dy_hbm, 61)
    x_passed = pass_on(x_copies, x_hbm, 63)
    sib_dy = []
    for i in range(2):
        sib_dy.append(remote(dy_hbm.at[c, rel[i]], dy_hbm.at[c, rel[i]], 31 + i, sibling))
        sib_x.append(remote(x_hbm.at[c, rel[i]], x_hbm.at[c, rel[i]], 34 + i, sibling))
        sib_dy[i].start()
        sib_x[i + 1].start()
    for copy in dy_passed:
        copy.wait_recv()
    sib_dy.append(remote(dy_hbm.at[c, fd], dy_hbm.at[c, fd], 33, sibling))
    sib_dy[2].start()
    for copy in x_passed:
        copy.wait_recv()
    sib_x.append(remote(x_hbm.at[c, fd], x_hbm.at[c, fd], 36, sibling))
    sib_x[3].start()

    for copy in w_copies + gate_copies + handed + sib_dy + sib_x:
        copy.wait_recv()
    for s in range(1, 4):

        @pl.when(z + s < 4)
        def _(s=s):
            kv_copies[s - 1].wait_send()

    for copy in [in_x, in_y, in_xy, in_yx, out_x, out_y, out_xy, out_yx, swap]:
        copy.wait_send()
    sent = w_copies + quarters + handed + gate_copies + dy_copies + x_copies
    for copy in sent + dy_passed + x_passed + sib_dy + sib_x:
        copy.wait_send()
    for copy in [own_w, own_x, store_wa] + own_dy:
        copy.wait()


def front(tok, gains, routes, gates, order, attn_own, weights, cot):
    count, width = tok.shape
    half = count // 2
    shard, columns = attn_own.shape
    experts, hidden = EXPERTS // 4, weights.shape[3]
    vmem, hbm = pl.BlockSpec(memory_space=pltpu.VMEM), pl.BlockSpec(memory_space=pl.ANY)
    bf16, f32 = jnp.bfloat16, jnp.float32
    shape = jax.ShapeDtypeStruct
    return pl.pallas_call(
        front_kernel,
        in_specs=[vmem] * 6 + [hbm] * 3,
        out_specs=[vmem] * 6 + [hbm] * 4,
        out_shape=[
            shape((count, width), bf16),
            shape((count, QUERY_PER_GROUP * HEAD_DIM), bf16),
            shape((4, count, 2 * HEAD_DIM), bf16),
            shape((count, QUERY_PER_GROUP * HEAD_DIM), bf16),
            shape((half, width), f32),
            shape((4, EXPERTS, count), f32),
            shape((4 * shard, columns), bf16),
            shape((experts, 3, 4 * shard, hidden), bf16),
            shape((2, 4, half, width), bf16),
            shape((2, 4, half, width), bf16),
        ],
        scratch_shapes=[
            pltpu.VMEM(weights.shape, bf16),
            pltpu.VMEM((EXPERTS, 3, shard, hidden), bf16),
            pltpu.VMEM((4 * shard, columns), bf16),
            pltpu.VMEM((count, width), f32),
            pltpu.VMEM((half, width), f32),
            pltpu.VMEM((half, width), bf16),
            pltpu.SemaphoreType.DMA((65,)),
            pltpu.SemaphoreType.DMA((65,)),
            pltpu.SemaphoreType.DMA((7,)),
        ],
        compiler_params=pltpu.CompilerParams(
            collective_id=0, has_side_effects=True, vmem_limit_bytes=60 * MIB
        ),
        name="front",
    )(tok, gains, frequencies(), routes, gates, order, attn_own, weights, cot)


def ctx_chunks(mats, shard):
    early = [(0, 0), (1, 0)]
    chunks = [(j, r, 0, shard) for j, r in early]
    chunks += [(j, r, 0, shard) for j in range(mats) for r in range(4) if (j, r) not in early]
    return chunks, [shard // 8] * 8


def rear_kernel(
    res_ref,
    xn_ref,
    q_ref,
    kv_ref,
    mixed_ref,
    gain_ref,
    freq_ref,
    tok_hbm,
    cot_hbm,
    x_hbm,
    dy_hbm,
    w_hbm,
    wl_ref,
    wa_hbm,
    layer_ref,
    tokgrad_ref,
    gains_ref,
    gate_ref,
    attn_hbm,
    fin_hbm,
    xy,
    wgu,
    wd,
    gu,
    hid,
    table,
    ge,
    r1,
    dn_in,
    dn_got,
    mo_in,
    mo_got,
    gg_in,
    gg_sum,
    gg_got,
    dres,
    dattn,
    dmixed,
    dproj,
    dkv,
    dkv_low,
    dkv_got,
    d1,
    d1_low,
    d1_in,
    ra,
    a1,
    gacc,
    gin,
    tok_half,
    cot_half,
    send,
    recv,
    local,
    z_out,
    z_across,
    z_back,
    z_r1,
    z_r2,
    f_out,
    f_in,
    credit,
):
    f, z, c = place()
    fx, fy, fd = plane_peers(f)
    rel = [f, fx, fy, fd]
    f32, bf16 = jnp.float32, jnp.bfloat16
    count, width = tok_hbm.shape
    half = count // 2
    shard = attn_hbm.shape[0]
    in_cols = (QUERY_PER_GROUP + 2) * HEAD_DIM
    q_cols = QUERY_PER_GROUP * HEAD_DIM
    ins = pl.ds(0, in_cols)
    outs = pl.ds(in_cols, attn_hbm.shape[1] - in_cols)
    scale = HEAD_DIM ** (-0.5)

    def at(fsdp=f, ctx=z, tp=c):
        return {"fsdp": fsdp, "ctx": ctx, "tp": tp}

    def copy_to(src, dst, send_sem, recv_sem, device):
        return pltpu.make_async_remote_copy(
            src_ref=src,
            dst_ref=dst,
            send_sem=send_sem,
            recv_sem=recv_sem,
            device_id=device,
            device_id_type=MESH_ID,
        )

    def remote(src, dst, k, device):
        return copy_to(src, dst, send.at[k], recv.at[k], device)

    plane = [at(fx), at(fy), at(fd)]
    line = [at(ctx=lax.rem(z + s, 4)) for s in range(1, 4)]
    sibling = at(tp=1 - c)
    partner = at(ctx=z + 1 - 2 * lax.rem(z, 2))
    opposite = at(ctx=3 - z)
    inner = (z == 1) | (z == 2)
    outer = (z == 0) | (z == 3)

    own = w_hbm.shape[0]
    hidden = w_hbm.shape[3]
    tokens = 8 * half
    tile = 2 * half
    loads = [pltpu.make_async_copy(x_hbm, xy.at[pl.ds(0, tokens)], local.at[0])]
    for e in range(own):
        for m in range(2):
            cols = pl.ds((2 * e + m) * hidden, hidden)
            loads.append(pltpu.make_async_copy(w_hbm.at[e, m], wgu.at[:, cols], local.at[1 + 2 * e + m]))
    loads.append(pltpu.make_async_copy(dy_hbm, xy.at[pl.ds(tokens, tokens)], local.at[5]))
    for e in range(own):
        cols = pl.ds(e * hidden, hidden)
        loads.append(pltpu.make_async_copy(w_hbm.at[e, 2], wd.at[:, cols], local.at[6 + e]))
    my_rows = rows_of(c, half)
    loads.append(pltpu.make_async_copy(tok_hbm.at[my_rows], tok_half, local.at[8]))
    loads.append(pltpu.make_async_copy(cot_hbm.at[my_rows], cot_half, local.at[9]))
    for copy in loads:
        copy.start()
    greet(plane + line + [sibling])
    for b in range(8):
        rows = wl_ref[b % 4, :, pl.ds((b // 4) * half, half)]
        rows = jnp.concatenate([rows, jnp.zeros((128 - EXPERTS, half), f32)], axis=0)
        table[pl.ds(b * half, half), :] = rows.T
    for copy in loads:
        copy.wait()

    lanes = lax.broadcasted_iota(jnp.int32, (tile, 128), 1)

    def act_step(i, _):
        rows = pl.ds(pl.multiple_of(i * tile, tile), tile)
        acts = dot_f32(xy[rows, :], wgu[...])
        plain = dot_f32(xy[pl.ds(pl.multiple_of(tokens + i * tile, tile), tile), :], wd[...])
        scales = table[rows, :]
        sums = jnp.zeros((tile, 128), f32)
        for e in range(own):
            gate_act = acts[:, 2 * e * hidden : (2 * e + 1) * hidden]
            up_act = acts[:, (2 * e + 1) * hidden : (2 * e + 2) * hidden]
            d_plain = plain[:, e * hidden : (e + 1) * hidden]
            here = lanes == own * f + e
            factor = jnp.sum(jnp.where(here, scales, 0.0), axis=1, keepdims=True)
            sigmoid = 1.0 / (1.0 + jnp.exp(-gate_act))
            active = gate_act * sigmoid
            act = active * up_act
            total = jnp.sum(act * d_plain, axis=1, keepdims=True)
            sums = jnp.where(here, jnp.where(factor != 0.0, total, 0.0), sums)
            d_hidden = d_plain * factor
            slope = sigmoid * (1.0 + gate_act * (1.0 - sigmoid))
            hid[rows, pl.ds(e * hidden, hidden)] = (act * factor).astype(bf16)
            gu[rows, pl.ds(2 * e * hidden, hidden)] = (d_hidden * up_act * slope).astype(bf16)
            gu[rows, pl.ds((2 * e + 1) * hidden, hidden)] = (d_hidden * active).astype(bf16)
        table[rows, :] = sums
        return 0

    lax.fori_loop(0, tokens // tile, act_step, 0)
    side, far = rows_of(c, 4 * half), rows_of(1 - c, 4 * half)
    gg_swap = remote(table.at[far], gg_in, 1, sibling)
    gg_swap.start()

    def grad_step(t, _):
        cols = pl.ds(pl.multiple_of(lax.rem(f + t, 4) * shard, 128), shard)
        into_in = dot_f32(xy[pl.ds(0, tokens), cols], gu[...], TN).astype(bf16)
        into_out = dot_f32(xy[pl.ds(tokens, tokens), cols], hid[...], TN).astype(bf16)
        for e in range(own):
            for m in range(2):
                k = 2 * e + m
                ge[3 * e + m, cols, :] = into_in[:, k * hidden : (k + 1) * hidden]
            ge[3 * e + 2, cols, :] = into_out[:, e * hidden : (e + 1) * hidden]
        return 0

    def down_step(i, _):
        rows = pl.ds(pl.multiple_of(i * tile, tile), tile)
        ra[rows, pl.ds(0, width)] = dot_f32(gu[rows, :], wgu[...], NT).astype(bf16)
        return 0

    def out_step(i, _):
        rows = pl.ds(pl.multiple_of(i * tile, tile), tile)
        xy[rows, :] = dot_f32(hid[rows, :], wd[...], NT).astype(bf16)
        return 0

    chunks, attn_rows = ctx_chunks(ge.shape[0], shard)
    n_expert = len(chunks)
    n_all = n_expert + len(attn_rows)

    def chunk(k):
        if k < n_expert:
            j, r, low, size = chunks[k]
            rows = pl.ds(pl.multiple_of(rel[r] * shard + low, 16), size)
            return ge.at[j, rows], r1.at[j, rows]
        rows = pl.ds(sum(attn_rows[: k - n_expert]), attn_rows[k - n_expert])
        return ra.at[rows], a1.at[rows]

    def add_into(dst, left, right):
        size = math.gcd(dst.shape[0], 64)

        def body(i, _):
            rows = pl.ds(pl.multiple_of(i * size, size), size)
            dst[rows, :] = (left[rows, :].astype(f32) + right[rows, :].astype(f32)).astype(bf16)
            return 0

        lax.fori_loop(0, dst.shape[0] // size, body, 0)

    def first(k):
        own, one = chunk(k)
        return copy_to(own, one, z_out.at[k], z_r1.at[k], partner)

    def across(k):
        own, one = chunk(k)
        return copy_to(own, one, z_across.at[k], z_r2.at[k], opposite)

    def back(k):
        _, one = chunk(k)
        return copy_to(one, one, z_back.at[k], z_r1.at[k], partner)

    def final(k):
        _, one = chunk(k)
        j, r, low, size = chunks[k]
        there = fin_hbm.at[r, j, pl.ds(low, size)]
        if r == 0:
            return pltpu.make_async_copy(one, there, f_out.at[k])
        return copy_to(one, there, f_out.at[k], f_in.at[k], plane[r - 1])

    pending, ready = [], []
    pace = 2
    lag_a, lag_b, lag_c, window = 1, 2, 5, 3

    def z_step(i):
        if i < n_all:

            @pl.when(outer)
            def _():
                if i >= window:
                    first(i - window).wait_send()
                first(i).start()

        if lag_a <= i < n_all + lag_a:
            k = i - lag_a

            @pl.when(inner)
            def _():
                own, one = chunk(k)
                first(k).wait_recv()
                add_into(own, own, one)
                pl.semaphore_signal(credit, inc=1, device_id=opposite, device_id_type=MESH_ID)

        if lag_a <= i < n_all + lag_a:
            k = i - lag_a

            @pl.when(inner)
            def _():
                pl.semaphore_wait(credit, 1)
                across(k).start()

        if lag_b <= i < n_all + lag_b:
            k = i - lag_b

            @pl.when(inner)
            def _():
                own, one = chunk(k)
                across(k).wait_recv()
                add_into(one, own, one)
                back(k).start()

        if lag_c <= i < n_all + lag_c:
            k = i - lag_c

            @pl.when(outer)
            def _():
                back(k).wait_recv()

            if k < n_expert:
                ready.append(k)

        for _ in range(pace):
            if pending:
                pending.pop(0).start()
            elif ready:
                final(ready.pop(0)).start()

    steps = iter(range(n_all + max(lag_b, lag_c)))

    def go_on(count=1):
        for _ in range(count):
            z_step(next(steps))

    wide = pl.ds(0, width)
    lax.fori_loop(0, 1, grad_step, 0)
    go_on()
    lax.fori_loop(2 * (1 - c), 2 * (1 - c) + 2, down_step, 0)
    dn_swap = remote(ra.at[far, wide], dn_in, 0, sibling)
    dn_swap.start()
    lax.fori_loop(2 * c, 2 * c + 2, down_step, 0)
    go_on()

    def both(ref, arrived):
        def body(i, _):
            rows = pl.ds(pl.multiple_of(c * 4 * half + i * half, half), half)
            here = pl.ds(pl.multiple_of(i * half, half), half)
            ref[rows, wide] = (ref[rows, wide].astype(f32) + arrived[here, :].astype(f32)).astype(bf16)
            return 0

        lax.fori_loop(0, 4, body, 0)

    def group(i):
        return rows_of(4 * c + i, half)

    gg_swap.wait_recv()
    gg_sum[...] = table[side, :] + gg_in[...]
    dn_swap.wait_recv()
    both(ra, dn_in)
    dn_out = [
        remote(ra.at[group(rel[i + 1]), wide], dn_got.at[i], 3 + i, plane[i]) for i in range(3)
    ]
    gg_out = [
        remote(gg_sum.at[rows_of(rel[i + 1], half)], gg_got.at[i], 6 + i, plane[i])
        for i in range(3)
    ]
    for copy in dn_out + gg_out:
        copy.start()
    lax.fori_loop(1, 4, grad_step, 0)
    go_on()
    lax.fori_loop(2 * (1 - c), 2 * (1 - c) + 2, out_step, 0)
    mo_swap = remote(xy.at[far], mo_in, 2, sibling)
    mo_swap.start()
    lax.fori_loop(2 * c, 2 * c + 2, out_step, 0)
    in_part, out_part = pl.ds(0, in_cols), pl.ds(0, q_cols)
    load_in = pltpu.make_async_copy(wa_hbm.at[:, ins], wgu.at[:, in_part], local.at[0])
    load_out = pltpu.make_async_copy(wa_hbm.at[:, outs], wd, local.at[1])
    load_out.start()
    load_in.start()
    go_on()
    for copy in dn_out:
        copy.wait_recv()
    for copy in dn_out + [dn_swap]:
        copy.wait_send()
    mo_swap.wait_recv()
    both(xy, mo_in)
    d_two = ra[group(f), wide].astype(f32)
    for i in range(3):
        d_two = d_two + dn_got[i].astype(f32)
    residual = res_ref[...]
    inv = lax.rsqrt(jnp.mean(residual * residual, axis=-1, keepdims=True) + eps)
    scaled = d_two * gain_ref[1:2, :]
    inside = jnp.mean(scaled * residual, axis=-1, keepdims=True)
    d_norm = inv * scaled - residual * (inv * inv * inv * inside)
    gacc[0] = jnp.zeros(gacc.shape[1:], f32)
    gacc[0, 1:2, :] = jnp.sum(d_two * residual * inv, axis=0, keepdims=True)
    d_res = cot_half[...].astype(f32) + d_norm
    dres[...] = d_res
    dattn[my_rows, :] = d_res.astype(bf16)
    da_swap = remote(dattn.at[my_rows], dattn.at[my_rows], 12, sibling)
    da_swap.start()
    mo_out = [remote(xy.at[group(rel[i + 1])], mo_got.at[i], 9 + i, plane[i]) for i in range(3)]
    for copy in mo_out:
        copy.start()
    load_out.wait()
    go_on()
    da_swap.wait_recv()
    dmixed[...] = dot_f32(dattn[...], wd[...]).astype(bf16)
    go_on()

    position = z * count + lax.broadcasted_iota(jnp.int32, (count, HEAD_DIM), 0)
    angle = position.astype(f32) * freq_ref[...]
    cosine = jnp.cos(angle)
    lane = lax.broadcasted_iota(jnp.int32, (count, HEAD_DIM), 1)
    sine = jnp.where(lane < HEAD_DIM // 2, jnp.sin(angle), -jnp.sin(angle))
    keys = kv_ref[:, :, pl.ds(0, HEAD_DIM)].reshape(4 * count, HEAD_DIM)
    vals = kv_ref[:, :, pl.ds(HEAD_DIM, HEAD_DIM)].reshape(4 * count, HEAD_DIM)
    key_cols, val_cols = pl.ds(0, HEAD_DIM), pl.ds(HEAD_DIM, HEAD_DIM)
    dkv[...] = jnp.zeros_like(dkv)
    for g in range(QUERY_PER_GROUP):
        cols = pl.ds(g * HEAD_DIM, HEAD_DIM)
        query = q_ref[:, cols]
        d_mix = dmixed[:, cols]
        probs = block_probs(z, keys, query)
        d_probs = dot_f32(vals, d_mix, NT)
        inside = jnp.sum(probs * d_probs, axis=0, keepdims=True)
        d_scores = (probs * (d_probs - inside)).astype(bf16)
        d_query = dot_f32(d_scores, keys, TN) * scale
        dproj[:, cols] = turn(d_query, cosine, sine).astype(bf16)
        dkv[:, key_cols] += dot_f32(d_scores, query) * scale
        dkv[:, val_cols] += dot_f32(probs.astype(bf16), d_mix)
        if g % 3 == 2:
            go_on()
    dkv_low[...] = dkv[...].reshape(dkv_low.shape).astype(bf16)
    dkv_out = [
        remote(dkv_low.at[s], dkv_got.at[s - 1], 12 + s, at(ctx=lax.rem(z + 4 - s, 4)))
        for s in range(1, 4)
    ]
    for s in range(1, 4):

        @pl.when(z >= s)
        def _(s=s):
            dkv_out[s - 1].start()

    low_rows = pl.ds(4 * shard, shard)

    def weight_grad(left, right, cols):
        def body(i, _):
            rows = pl.ds(pl.multiple_of(i * 256, 256), 256)
            xy[rows, cols] = dot_f32(left[:, rows], right, TN).astype(bf16)
            return 0

        lax.fori_loop(0, width // 256, body, 0)

    def send_grad(cols, into, k):
        third = shard // 3
        copies = []
        for p in range(3):
            for i in range(3):
                rows = pl.ds(pl.multiple_of(rel[i + 1] * shard + p * third, third), third)
                copies.append(
                    remote(
                        xy.at[rows, cols],
                        ra.at[pl.ds(i * shard + p * third, third), into],
                        k + 3 * p + i,
                        plane[i],
                    )
                )
        pending.extend(copies)
        return copies

    for copy in mo_out + gg_out:
        copy.wait_recv()
    moe = xy[group(f), :].astype(f32)
    gates = gg_sum[rows_of(f, half), :]
    for i in range(3):
        moe = moe + mo_got[i].astype(f32)
        gates = gates + gg_got[i]
    layer_ref[my_rows, :] = (res_ref[...] + moe).astype(bf16)
    gate_ref[my_rows, :] = gates
    lo_swap = remote(layer_ref.at[my_rows], layer_ref.at[my_rows], 27, sibling)
    gt_swap = remote(gate_ref.at[my_rows], gate_ref.at[my_rows], 28, sibling)
    lo_swap.start()
    gt_swap.start()
    for copy in mo_out + [mo_swap]:
        copy.wait_send()
    go_on()

    right_half = pl.ds(q_cols, q_cols)
    weight_grad(dattn, mixed_ref[...], right_half)
    ga_copies = send_grad(right_half, outs, 34)
    go_on()
    q_part = pl.ds(0, q_cols)
    weight_grad(xn_ref, dproj[:, q_part], q_part)
    ga_copies += send_grad(q_part, q_part, 43)
    go_on()
    for s in range(1, 4):

        @pl.when(z + s < 4)
        def _(s=s):
            dkv_out[s - 1].wait_recv()
            dkv[0:count, :] += dkv_got[s - 1].astype(f32)

    kv_part = pl.ds(q_cols, 2 * HEAD_DIM)
    dproj[:, pl.ds(q_cols, HEAD_DIM)] = turn(dkv[0:count, key_cols], cosine, sine).astype(bf16)
    dproj[:, pl.ds(q_cols + HEAD_DIM, HEAD_DIM)] = dkv[0:count, val_cols].astype(bf16)
    for s in range(4):
        block = dot_f32(xn_ref[:, pl.ds(s * shard, shard)], dproj[:, kv_part], TN)
        xy[low_rows, pl.ds(s * 2 * HEAD_DIM, 2 * HEAD_DIM)] = block.astype(bf16)
    kv_copies = [
        remote(
            xy.at[low_rows, rows_of(rel[i + 1], 2 * HEAD_DIM)],
            ra.at[pl.ds(i * shard, shard), kv_part],
            16 + i,
            plane[i],
        )
        for i in range(3)
    ]
    pending.extend(kv_copies)
    ga_copies += kv_copies
    go_on()

    load_in.wait()
    for s in range(width // 256):
        rows = pl.ds(s * 256, 256)
        d1[:, rows] = dot_f32(dproj[my_rows, :], wgu[rows, in_part], NT)
        d1_low[:, rows] = dot_f32(
            dproj[rows_of(1 - c, half), :], wgu[rows, in_part], NT
        ).astype(bf16)
    d1_swap = remote(d1_low, d1_in, 25, sibling)
    d1_swap.start()
    go_on()
    d1_swap.wait_recv()
    d_one = d1[...] + d1_in[...].astype(f32)
    tok = tok_half[...].astype(f32)
    inv = lax.rsqrt(jnp.mean(tok * tok, axis=-1, keepdims=True) + eps)
    scaled = d_one * gain_ref[0:1, :]
    inside = jnp.mean(scaled * tok, axis=-1, keepdims=True)
    d_norm = inv * scaled - tok * (inv * inv * inv * inside)
    gacc[0, 0:1, :] = jnp.sum(d_one * tok * inv, axis=0, keepdims=True)
    tokgrad_ref[my_rows, :] = (dres[...] + d_norm).astype(bf16)
    tg_swap = remote(tokgrad_ref.at[my_rows], tokgrad_ref.at[my_rows], 26, sibling)
    tg_swap.start()
    go_on()

    stages = [sibling, at(fx), at(fy), partner, at(ctx=lax.rem(z + 2, 4))]
    gain_copies = [remote(gacc.at[i], gin.at[i], 29 + i, stages[i]) for i in range(5)]
    for i in range(5):
        gain_copies[i].start()
        go_on()
        gain_copies[i].wait_recv()
        total = gacc[i] + gin[i]
        if i < 4:
            gacc[i + 1] = total
        else:
            gains_ref[...] = total

    while (i := next(steps)) < n_expert - 1:
        z_step(i)
    z_step(i)
    for copy in pending:
        copy.start()
    del pending[:]
    for copy in ga_copies:
        copy.wait_recv()

    def attn_sum(i, _):
        size = shard // 8
        here = pl.ds(pl.multiple_of(i * size, size), size)
        rows = pl.ds(pl.multiple_of(f * shard + i * size, size), size)
        low = pl.ds(pl.multiple_of(4 * shard + i * size, size), size)
        for cols, mine in (
            (q_part, xy[rows, q_part]),
            (kv_part, xy[low, rows_of(f, 2 * HEAD_DIM)]),
            (outs, xy[rows, right_half]),
        ):
            total = mine.astype(f32)
            for r in range(3):
                other = pl.ds(pl.multiple_of(r * shard + i * size, size), size)
                total = total + ra[other, cols].astype(f32)
            ra[here, cols] = total.astype(bf16)
        return 0

    lax.fori_loop(0, 8, attn_sum, 0)
    for i in steps:
        z_step(i)
    store = pltpu.make_async_copy(a1, attn_hbm, local.at[0])
    store.start()

    for k in ready:
        final(k).start()

    store.wait()
    for k in range(n_all):

        @pl.when(outer)
        def _(k=k):
            if k >= n_all - window:
                first(k).wait_send()

        @pl.when(inner)
        def _(k=k):
            across(k).wait_send()
            back(k).wait_send()

    for k in range(n_expert):
        if chunks[k][1] == 0:
            final(k).wait()
        else:
            final(k).wait_send()
            final(k).wait_recv()
    for s in range(1, 4):

        @pl.when(z >= s)
        def _(s=s):
            dkv_out[s - 1].wait_send()

    for copy in [tg_swap, lo_swap, gt_swap]:
        copy.wait_recv()
    swaps = [gg_swap, da_swap, d1_swap, tg_swap, lo_swap, gt_swap]
    for copy in swaps + gg_out + ga_copies + gain_copies:
        copy.wait_send()


def rear(res, xn, q, kv, mixed, gains, tok, cot, x, dy, weights, gate_table, wa):
    count, width = tok.shape
    half = count // 2
    tokens = 8 * half
    columns = wa.shape[1]
    shard = width // 4
    own, _, _, hidden = weights.shape
    mats = 3 * own
    q_cols = q.shape[1]
    vmem, hbm = pl.BlockSpec(memory_space=pltpu.VMEM), pl.BlockSpec(memory_space=pl.ANY)
    bf16, f32 = jnp.bfloat16, jnp.float32
    shape = jax.ShapeDtypeStruct
    dma = pltpu.SemaphoreType.DMA
    chunks, attn_rows = ctx_chunks(mats, shard)
    n_expert, n_all = len(chunks), len(chunks) + len(attn_rows)
    return pl.pallas_call(
        rear_kernel,
        in_specs=[vmem] * 7 + [hbm] * 5 + [vmem, hbm],
        out_specs=[vmem] * 4 + [hbm] * 2,
        out_shape=[
            shape((count, width), bf16),
            shape((count, width), bf16),
            shape((8, width), f32),
            shape((count, 128), f32),
            shape((shard, columns), bf16),
            shape((4, mats, shard, hidden), bf16),
        ],
        scratch_shapes=[
            pltpu.VMEM((2 * tokens, width), bf16),
            pltpu.VMEM((width, 2 * own * hidden), bf16),
            pltpu.VMEM((width, own * hidden), bf16),
            pltpu.VMEM((tokens, width), bf16),
            pltpu.VMEM((tokens, own * hidden), bf16),
            pltpu.VMEM((tokens, 128), f32),
            pltpu.VMEM((mats, width, hidden), bf16),
            pltpu.VMEM((mats, width, hidden), bf16),
            pltpu.VMEM((4 * half, width), bf16),
            pltpu.VMEM((3, half, width), bf16),
            pltpu.VMEM((4 * half, width), bf16),
            pltpu.VMEM((3, half, width), bf16),
            pltpu.VMEM((4 * half, 128), f32),
            pltpu.VMEM((4 * half, 128), f32),
            pltpu.VMEM((3, half, 128), f32),
            pltpu.VMEM((half, width), f32),
            pltpu.VMEM((count, width), bf16),
            pltpu.VMEM((count, q_cols), bf16),
            pltpu.VMEM((count, q_cols + 2 * HEAD_DIM), bf16),
            pltpu.VMEM((4 * count, 2 * HEAD_DIM), f32),
            pltpu.VMEM((4, count, 2 * HEAD_DIM), bf16),
            pltpu.VMEM((3, count, 2 * HEAD_DIM), bf16),
            pltpu.VMEM((half, width), f32),
            pltpu.VMEM((half, width), bf16),
            pltpu.VMEM((half, width), bf16),
            pltpu.VMEM((3 * shard, columns), bf16),
            pltpu.VMEM((shard, columns), bf16),
            pltpu.VMEM((5, 8, width), f32),
            pltpu.VMEM((5, 8, width), f32),
            pltpu.VMEM((half, width), bf16),
            pltpu.VMEM((half, width), bf16),
            dma((52,)),
            dma((52,)),
            dma((10,)),
            dma((n_all,)),
            dma((n_all,)),
            dma((n_all,)),
            dma((n_all,)),
            dma((n_all,)),
            dma((n_expert,)),
            dma((n_expert,)),
            pltpu.SemaphoreType.REGULAR,
        ],
        compiler_params=pltpu.CompilerParams(
            collective_id=1, has_side_effects=True, vmem_limit_bytes=63 * MIB
        ),
        name="rear",
    )(
        res,
        xn,
        q,
        kv,
        mixed,
        gains,
        frequencies(),
        tok,
        cot,
        x,
        dy,
        weights,
        gate_table,
        wa,
    )


def body_fast(
    tokens,
    attn_norm,
    attention_params,
    ffn_norm,
    expert_weights,
    gate_values,
    routes,
    slot_order,
    cotangent,
):
    sequence_count, block_len, model_width = tokens.shape
    count = sequence_count * block_len
    half = count // 2
    f = lax.axis_index("fsdp")
    shard, hidden = attention_params.shape[0], expert_weights.shape[3]
    tok = tokens.reshape(count, model_width)
    cot = cotangent.reshape(count, model_width)
    norm_gains = jnp.stack([attn_norm, ffn_norm])
    route_rows = routes.reshape(count, TOP)
    normed, queries, kv, mixed, residual, gate_table, whole_attn, whole_expert, x, dy = front(
        tok,
        norm_gains,
        route_rows.T,
        gate_values.reshape(count, TOP).T,
        slot_order.reshape(1, count),
        attention_params[:, 0, :],
        jnp.transpose(expert_weights, (0, 2, 1, 3)),
        cot,
    )
    layer_out, tokens_grad, gains, gate_rows, attn_grad, finals = rear(
        residual,
        normed,
        queries,
        kv,
        mixed,
        norm_gains,
        tok,
        cot,
        x.reshape(8 * half, model_width),
        dy.reshape(8 * half, model_width),
        whole_expert,
        gate_table,
        whole_attn,
    )
    picked = route_rows[:, :, None] == jnp.arange(EXPERTS, dtype=jnp.int32)
    gate_grad = jnp.sum(jnp.where(picked, gate_rows[:, None, :EXPERTS], 0.0), axis=-1)
    finals = finals.reshape(EXPERTS, 3, shard, hidden)
    expert_grad, attn_lines = join_experts(finals, attn_grad, expert_order(f).T)
    expert_grad = jnp.transpose(expert_grad, (0, 2, 1, 3))
    return (
        layer_out.reshape(sequence_count, block_len, model_width),
        tokens_grad.reshape(sequence_count, block_len, model_width),
        attn_lines.reshape(shard, 1, attention_params.shape[2]),
        expert_grad,
        gains[0],
        gains[1],
        gate_grad.reshape(sequence_count, block_len, TOP),
    )


def solution(mesh):
    in_specs = (
        P("fsdp", "ctx", None),
        P(),
        P("fsdp", "tp", None),
        P(),
        P("fsdp", None, None, "tp"),
        P("fsdp", "ctx", None),
        P("fsdp", "ctx", None),
        P("fsdp", "ctx"),
        P("fsdp", "ctx", None),
    )
    out_specs = (
        P("fsdp", "ctx", None),
        P("fsdp", "ctx", None),
        P("fsdp", "tp", None),
        P("fsdp", None, None, "tp"),
        P(),
        P(),
        P("fsdp", "ctx", None),
    )
    four = mesh.shape["fsdp"] == 4 and mesh.shape["ctx"] == 4 and mesh.shape["tp"] == 2
    body_fn = body_fast if four else body
    return jax.shard_map(body_fn, mesh=mesh, in_specs=in_specs, out_specs=out_specs, check_vma=False)
```
